128 devices in a mesh: dp: 32 (over y, x, z_lo), tensor: 4 (over z_hi, core).
Axes of the slice: x: 4, y: 4, z: 4 (z_hi: 2, z_lo: 2; z = z_hi * 2 + z_lo), core: 2. Of those that a mesh axis runs over, the one named last changes fastest.
Arguments:
- hidden_in: bfloat16 [32768, 1536], P(('dp', 'tensor')), may hold values from -6 to 6
- norm_gain: float32 [1536], replicated, may hold values from 0.1 to 1.9
- proj_zx: bfloat16 [1536, 2, 3072], P('dp', None, 'tensor'), may hold values from -0.15625 to 0.15625
- proj_shared: bfloat16 [1536, 256], P(('dp', 'tensor')), may hold values from -0.15625 to 0.15625
- proj_step: bfloat16 [1536, 48], P('dp', 'tensor'), may hold values from -0.15625 to 0.15625
- conv_inner: float32 [5, 3072], P(None, 'tensor'), may hold values from -0.5 to 0.5
- conv_shared: float32 [5, 256], replicated, may hold values from -0.5 to 0.5
- step_bias: float32 [48], P('tensor'), may hold values from -6 to -2
- decay_log: float32 [48], P('tensor'), may hold values from 0 to 2.7
- skip_gain: float32 [48], P('tensor'), may hold values from 0.5 to 1.5
- gated_gain: float32 [3072], P('tensor'), may hold values from 0.1 to 1.9
- proj_out: bfloat16 [3072, 1536], P('tensor', 'dp'), may hold values from -0.109375 to 0.109375
- out_grad: bfloat16 [32768, 1536], P(('dp', 'tensor')), may hold values from -6 to 6
- segments: int32 [32768], P('dp'), may hold values from 0 to 6, as said below
Outputs:
- hidden_out: bfloat16 [32768, 1536], P(('dp', 'tensor'))
- grad_hidden: bfloat16 [32768, 1536], P(('dp', 'tensor'))
- grad_norm_gain: float32 [1536], replicated
- grad_proj_zx: float32 [1536, 2, 3072], P('dp', None, 'tensor')
- grad_proj_shared: float32 [1536, 256], P(('dp', 'tensor'))
- grad_proj_step: float32 [1536, 48], P('dp', 'tensor')
- grad_conv_inner: float32 [5, 3072], P(None, 'tensor')
- grad_conv_shared: float32 [5, 256], replicated
- grad_step_bias: float32 [48], P('tensor')
- grad_decay_log: float32 [48], P('tensor')
- grad_skip_gain: float32 [48], P('tensor')
- grad_gated_gain: float32 [3072], P('tensor')
- grad_proj_out: float32 [3072, 1536], P('tensor', 'dp')
The draws below stay inside these ranges and needn't reach their ends.
Inputs may be any that keep to these rules, and one draw needn't show every extreme that they name: `segments`: within each sequence of 1024 tokens the ids start at 0 and never fall; a document is a run of equal ids.
All inputs are finite; a program needn't handle non-finite values.
Results may differ from the reference program's by a relative error of at most 0.024.
Values may be sent and summed in bfloat16 or wider, within the bound.
No kernel may reach another device: no remote copies, remote signals or barrier semaphores. Data moves between devices by JAX's collectives and lax.ppermute only.
A program may use at most 256 MiB of HBM per device.

```python
import jax
import jax.numpy as jnp
from jax import lax

D = 1536
H = 48
N = 128
SPAN = 256
LEN = 1024
DI = 3072
TOKENS = 32768


def draw_segments(key, part):
    key = jax.random.fold_in(key, 17)
    length_key, offset_key, edge_key, pick_key = jax.random.split(key, 4)
    seq_count = TOKENS // LEN
    shortest = SPAN * 25 // 32
    longest = SPAN * 125 // 16 - SPAN
    doc_count = (LEN + SPAN) // shortest + 2
    doc_lengths = jax.random.randint(length_key, (seq_count, doc_count), shortest, longest + 1)
    offsets = jax.random.randint(offset_key, (seq_count,), 0, doc_lengths[:, 0])
    chosen = jax.random.randint(pick_key, (), 0, seq_count)
    is_chosen = jnp.arange(seq_count) == chosen
    doc_lengths = jnp.where(is_chosen[:, None], shortest, doc_lengths)
    offsets = jnp.where(is_chosen, shortest - 1, offsets)
    doc_ends = jnp.cumsum(doc_lengths, axis=1) - offsets[:, None]
    first_end = doc_ends[:, 0]
    snap_flag = jax.random.randint(edge_key, (seq_count,), 0, 2)
    snapped = jnp.where((snap_flag == 1) & (first_end >= SPAN), first_end // SPAN * SPAN, first_end)
    doc_ends = jnp.concatenate([snapped[:, None], doc_ends[:, 1:]], axis=1)
    places = jnp.arange(LEN)
    doc_ids = jnp.sum((places[None, :, None] >= doc_ends[:, None, :]).astype(jnp.int32), axis=2)
    return doc_ids.reshape(TOKENS).astype(jnp.int32)


def shard_levels(own_key, shape, cuts, smallest, largest):
    loudness, own = 1.0, jax.random.fold_in(own_key, 6)
    for position, parts in cuts:
        heights = jnp.exp(jax.random.uniform(jax.random.fold_in(own, position), (parts,), jnp.float32, smallest / len(cuts), largest / len(cuts)))
        loudness = loudness * jnp.repeat(heights, shape[position] // parts).reshape([-1 if axis == position else 1 for axis in range(len(shape))])
    return loudness


def bell_draw(key, extent, scale, reach, shards=(), held_as=jnp.bfloat16):
    gain = shard_levels(key, extent, shards, -0.22, 0.18) if shards else 1.0
    drawn = jax.random.normal(key, extent, jnp.float32) * scale * gain
    return jnp.minimum(jnp.maximum(drawn, -reach), reach).astype(held_as)


def setup_inputs(seed: int = 0) -> dict:
    splits = jax.random.split(jax.random.key(seed), 15)
    hidden_in = bell_draw(splits[0], (TOKENS, D), 1.0, 6.0, ((0, 128),))
    norm_gain = jnp.clip(1.0 + 0.18 * jax.random.normal(splits[1], (D,), jnp.float32), 0.1, 1.9)
    proj_zx = bell_draw(splits[2], (D, 2, DI), D ** -0.5, 0.15625, ((0, 32), (2, 4)))
    proj_shared = bell_draw(splits[3], (D, 2 * N), D ** -0.5, 0.15625, ((0, 128),))
    proj_step = bell_draw(splits[4], (D, H), D ** -0.5, 0.15625, ((0, 32), (1, 4)))
    conv_inner = jnp.clip(jax.random.uniform(splits[5], (5, DI), jnp.float32, -0.5, 0.5) * shard_levels(splits[5], (5, DI), ((1, 4),), -0.4, 0.0), -0.5, 0.5)
    conv_shared = jnp.clip(jax.random.uniform(splits[6], (5, 2 * N), jnp.float32, -0.5, 0.5), -0.5, 0.5)
    step_bias = jnp.clip(-6.0 + 4.0 * jax.random.uniform(splits[7], (H,), jnp.float32) ** shard_levels(splits[7], (H,), ((0, 4),), -0.2, 0.2), -6.0, -2.0)
    decay_log = jnp.clip(2.7 * jax.random.uniform(splits[8], (H,), jnp.float32) ** shard_levels(splits[8], (H,), ((0, 4),), -0.2, 0.2), 0.0, 2.7)
    skip_gain = jnp.clip(0.5 + 1.0 * jax.random.uniform(splits[9], (H,), jnp.float32) ** shard_levels(splits[9], (H,), ((0, 4),), -0.2, 0.2), 0.5, 1.5)
    gated_gain = jnp.clip(1.0 + 0.18 * jax.random.normal(splits[10], (DI,), jnp.float32), 0.1, 1.9)
    proj_out = bell_draw(splits[11], (DI, D), DI ** -0.5, 0.109375, ((0, 4), (1, 32)))
    out_grad = bell_draw(splits[12], (TOKENS, D), 1.0, 6.0, ((0, 128),))
    segments = draw_segments(jax.random.fold_in(splits[14], 71), 0)
    return dict(hidden_in=hidden_in, norm_gain=norm_gain, proj_zx=proj_zx, proj_shared=proj_shared, proj_step=proj_step, conv_inner=conv_inner, conv_shared=conv_shared, step_bias=step_bias, decay_log=decay_log, skip_gain=skip_gain, gated_gain=gated_gain, proj_out=proj_out, out_grad=out_grad, segments=segments)


EPS = 1e-05
HIGH = lax.Precision.HIGHEST

@jax.custom_vjp
def low(v):
    return lax.optimization_barrier(v.astype(jnp.bfloat16)).astype(jnp.float32)

@jax.custom_vjp
def low_back(v):
    return v

def low_keep(v):
    return (low(v), None)

def low_pass(kept, grad):
    return (grad,)

def back_keep(v):
    return (v, None)

def back_low(kept, grad):
    return (low(grad),)
low.defvjp(low_keep, low_pass)
low_back.defvjp(back_keep, back_low)

def causal_conv(values, conv_taps, segment_ids):
    length = values.shape[0]
    padded = jnp.concatenate([jnp.zeros((3, values.shape[1]), values.dtype), values], 0)
    seg_pad = jnp.concatenate([jnp.full((3,), -1, jnp.int32), segment_ids.astype(jnp.int32)], 0)
    summed = conv_taps[4] + jnp.zeros_like(values)
    for offset in range(4):
        same_doc = (seg_pad[offset:offset + length] == segment_ids)[:, None]
        summed = summed + conv_taps[offset] * jnp.where(same_doc, padded[offset:offset + length], 0.0)
    return jax.nn.silu(summed)

def scan_heads(cumulative, step_sizes, inner_heads, write_vectors, read_vectors, segment_ids):
    length = segment_ids.shape[0]
    places = jnp.arange(length)
    allowed = (places[:, None] >= places[None, :]) & (segment_ids[:, None] == segment_ids[None, :])
    inner_prod = jnp.dot(read_vectors, write_vectors.T, precision=HIGH)

    def one_head(operands):
        head_cumul, head_step, head_inner = operands
        spread = jnp.where(allowed, head_cumul[:, None] - head_cumul[None, :], -jnp.inf)
        weights = jnp.exp(spread) * inner_prod * head_step[None, :]
        return jnp.dot(weights, head_inner, precision=HIGH)
    return lax.map(jax.checkpoint(one_head), (cumulative.T, step_sizes.T, inner_heads))

def mixer_forward(gate_pre, inner_pre, shared_pre, step_pre, conv_inner, conv_shared, step_bias, decay_log, skip_gain, segment_ids):
    inner_conv = causal_conv(inner_pre, conv_inner, segment_ids)
    shared_conv = causal_conv(shared_pre, conv_shared, segment_ids)
    length, inner_width = inner_conv.shape
    head_count = step_bias.shape[0]
    head_size = inner_width // head_count
    states = shared_conv.shape[1] // 2
    step_sizes = jax.nn.softplus(step_pre + step_bias)
    cumulative = jnp.cumsum(-step_sizes * jnp.exp(decay_log), axis=0)
    inner_heads = inner_conv.reshape(length, head_count, head_size).transpose(1, 0, 2)
    scanned = scan_heads(cumulative, step_sizes, inner_heads, shared_conv[:, :states], shared_conv[:, states:], segment_ids)
    scanned = scanned + inner_heads * skip_gain[:, None, None]
    flat = scanned.transpose(1, 0, 2).reshape(length, inner_width)
    return flat * jax.nn.silu(gate_pre)

def layer_forward(layer_in, weights, segment_ids):
    norm_gain, proj_zx, proj_shared, proj_step, conv_inner, conv_shared, step_bias, decay_log, skip_gain, gated_gain, proj_out = weights
    scale_in = lax.rsqrt(lax.optimization_barrier(jnp.mean(layer_in * layer_in, axis=-1, keepdims=True)) + EPS)
    normed = low(layer_in * scale_in * norm_gain)
    gate_pre = low_back(jnp.dot(normed, proj_zx[:, 0, :], precision=HIGH))
    inner_pre = low_back(jnp.dot(normed, proj_zx[:, 1, :], precision=HIGH))
    shared_pre = low_back(jnp.dot(normed, proj_shared, precision=HIGH))
    step_pre = low_back(jnp.dot(normed, proj_step, precision=HIGH))
    gated = mixer_forward(gate_pre, inner_pre, shared_pre, step_pre, conv_inner, conv_shared, step_bias, decay_log, skip_gain, segment_ids)
    scale_mix = lax.rsqrt(lax.optimization_barrier(jnp.mean(gated * gated, axis=-1, keepdims=True)) + EPS)
    mixed = low(gated * scale_mix * gated_gain)
    return layer_in + jnp.dot(mixed, proj_out, precision=HIGH)

def reference(hidden_in, norm_gain, proj_zx, proj_shared, proj_step, conv_inner, conv_shared, step_bias, decay_log, skip_gain, gated_gain, proj_out, out_grad, segments):
    params = tuple((item.astype(jnp.float32) for item in (norm_gain, proj_zx, proj_shared, proj_step, conv_inner, conv_shared, step_bias, decay_log, skip_gain, gated_gain, proj_out)))
    seq_count = segments.shape[0] // LEN
    inputs = hidden_in.astype(jnp.float32).reshape(seq_count, LEN, D)
    cotangents = out_grad.astype(jnp.float32).reshape(seq_count, LEN, D)
    doc_ids = segments.reshape(seq_count, LEN)

    def per_sequence(totals, operands):
        seq_in, seq_grad, seq_ids = operands

        def forward_fn(layer_in, weights):
            return layer_forward(layer_in, weights, seq_ids)
        layer_out, pullback = jax.vjp(forward_fn, seq_in, params)
        grad_in, grad_params = pullback(seq_grad)
        totals = jax.tree.map(jnp.add, totals, grad_params)
        return (totals, (layer_out, grad_in))
    initial = jax.tree.map(jnp.zeros_like, params)
    totals, (layer_outs, grad_ins) = lax.scan(per_sequence, initial, (inputs, cotangents, doc_ids))
    hidden_out = layer_outs.reshape(seq_count * LEN, D).astype(jnp.bfloat16)
    grad_hidden = grad_ins.reshape(seq_count * LEN, D).astype(jnp.bfloat16)
    return (hidden_out, grad_hidden, totals[0], totals[1], totals[2], totals[3], totals[4], totals[5], totals[6], totals[7], totals[8], totals[9], totals[10])
```

```python
from functools import partial

import jax
import jax.numpy as jnp
from jax import lax
from jax.sharding import Mesh
from jax.sharding import PartitionSpec as P

SPAN = 256
EPS = 1e-05
HIGH = lax.Precision.HIGHEST
F32 = jnp.float32
BF16 = jnp.bfloat16
DP = ("y", "x", "zl")
TENSOR = ("zh", "c")
SIZES = {"y": 4, "x": 4, "zl": 2, "zh": 2, "c": 2}


def shift(value, axis, by):
    n = SIZES[axis]
    return lax.ppermute(value, axis, [(i, (i - by) % n) for i in range(n)])


def swap(value, axis):
    return shift(value, axis, 1)


def ordered_pair(own, other, axis):
    first = lax.axis_index(axis) == 0
    return jnp.stack([jnp.where(first, own, other), jnp.where(first, other, own)], 0)


def gather_pair(value, axis):
    return ordered_pair(value, swap(value, axis), axis)


def gather_ring(value, axis):
    parts = [value, shift(value, axis, 1), shift(value, axis, 2), shift(value, axis, -1)]
    turned = jnp.stack(parts + parts[:3], 0)
    start = (4 - lax.axis_index(axis)) % 4
    return lax.dynamic_slice_in_dim(turned, start, 4, 0)


def gather_dp(value):
    pair = gather_pair(value, "zl")
    rows = gather_ring(pair, "x")
    full = gather_ring(rows, "y")
    return full.reshape((32 * value.shape[0],) + value.shape[1:])


def scatter_ring(value, axis):
    me = lax.axis_index(axis)

    def entry(by):
        return lax.dynamic_index_in_dim(value, (me + by) % 4, 0, keepdims=False)

    ahead = shift(entry(-1), axis, 1)
    behind = shift(entry(1), axis, -1)
    across = shift(entry(2), axis, 2)
    return (entry(0).astype(F32) + across.astype(F32)) + (ahead.astype(F32) + behind.astype(F32))


def scatter_pair(value, axis):
    me = lax.axis_index(axis)
    keep = lax.dynamic_index_in_dim(value, me, 0, keepdims=False)
    give = lax.dynamic_index_in_dim(value, 1 - me, 0, keepdims=False)
    return keep.astype(F32) + swap(give, axis).astype(F32)


def scatter_dp(value):
    width = value.shape[1]
    blocks = value.reshape(4, 4, 2, 48, width)
    mine = scatter_ring(blocks, "y").astype(BF16)
    mine = scatter_ring(mine, "x").astype(BF16)
    return scatter_pair(mine, "zl")


def sum_ring(value, axis):
    ahead, behind, across = shift(value, axis, 1), shift(value, axis, -1), shift(value, axis, 2)
    return (value + across) + (ahead + behind)


def sum_pair(value, axis):
    return value + swap(value, axis)


def gather_tokens(value):
    far = swap(value, "zh")
    near_pair = gather_pair(value, "c")
    far_pair = gather_pair(far, "c")
    both = ordered_pair(near_pair, far_pair, "zh")
    return both.reshape((4 * value.shape[0],) + value.shape[1:])


def scatter_tensor(value):
    by_zh = value.reshape((2, 2) + value.shape[1:])
    half = scatter_pair(jnp.swapaxes(by_zh, 0, 1), "c").astype(BF16)
    return scatter_pair(half, "zh")


def causal_conv(values, conv_taps, segment_ids):
    length = values.shape[0]
    padded = jnp.concatenate([jnp.zeros((3, values.shape[1]), values.dtype), values], 0)
    seg_pad = jnp.concatenate([jnp.full((3,), -1, jnp.int32), segment_ids], 0)
    summed = conv_taps[4] + jnp.zeros_like(values)
    for offset in range(4):
        same_doc = (seg_pad[offset : offset + length] == segment_ids)[:, None]
        summed = summed + conv_taps[offset] * jnp.where(
            same_doc, padded[offset : offset + length], 0.0
        )
    return jax.nn.silu(summed)


def block_mixer(
    inner_pre,
    shared_pre,
    step_pre,
    conv_inner,
    conv_shared,
    step_bias,
    decay_log,
    skip_gain,
    segment_ids=None,
    block_len=None,
):
    inner_conv = causal_conv(inner_pre, conv_inner, segment_ids)
    shared_conv = causal_conv(shared_pre, conv_shared, segment_ids)
    length, inner_width = inner_conv.shape
    head_count = step_bias.shape[0]
    head_size = inner_width // head_count
    states = shared_conv.shape[1] // 2
    blocks = length // block_len
    step_sizes = jax.nn.softplus(step_pre + step_bias)
    log_decay = -step_sizes * jnp.exp(decay_log)
    inner_blocks = inner_conv.reshape(blocks, block_len, head_count, head_size)
    write_blocks = shared_conv[:, :states].reshape(blocks, block_len, states)
    read_blocks = shared_conv[:, states:].reshape(blocks, block_len, states)
    step_blocks = step_sizes.reshape(blocks, block_len, head_count)
    log_blocks = log_decay.reshape(blocks, block_len, head_count)
    doc_blocks = segment_ids.reshape(blocks, block_len)
    doc_before = jnp.concatenate([jnp.full((1,), -1, jnp.int32), doc_blocks[:-1, -1]], 0)
    places = jnp.arange(block_len)
    lower_tri = places[:, None] >= places[None, :]

    def advance(carried, operands):
        inner_here, write_here, read_here, step_here, log_here, doc_here, prior_doc = operands
        cumulative = jnp.cumsum(log_here, axis=0)
        allowed = lower_tri & (doc_here[:, None] == doc_here[None, :])
        inner_prod = jnp.dot(read_here, write_here.T, precision=HIGH)
        spread = jnp.where(
            allowed[None], cumulative.T[:, :, None] - cumulative.T[:, None, :], -jnp.inf
        )
        weights = jnp.exp(spread) * inner_prod[None] * step_here.T[:, None, :]
        within = jnp.einsum("hts,shp->thp", weights, inner_here, precision=HIGH)
        enters = jnp.where((doc_here == prior_doc)[:, None], jnp.exp(cumulative), 0.0)
        from_state = (
            jnp.einsum("tn,hnp->thp", read_here, carried, precision=HIGH) * enters[:, :, None]
        )
        result = within + from_state + inner_here * skip_gain[None, :, None]
        to_end = (
            jnp.where(
                (doc_here == doc_here[-1])[:, None],
                jnp.exp(cumulative[-1][None, :] - cumulative),
                0.0,
            )
            * step_here
        )
        carry_keep = jnp.where(doc_here[-1] == prior_doc, jnp.exp(cumulative[-1]), 0.0)
        updated = carried * carry_keep[:, None, None] + jnp.einsum(
            "sn,shp->hnp", write_here, inner_here * to_end[:, :, None], precision=HIGH
        )
        return (updated, result)

    initial = jnp.zeros((head_count, states, head_size), F32)
    unused, outputs = lax.scan(
        advance,
        initial,
        (inner_blocks, write_blocks, read_blocks, step_blocks, log_blocks, doc_blocks, doc_before),
    )
    return outputs.reshape(length, inner_width)


def per_device(
    hidden_in,
    norm_gain,
    proj_zx,
    proj_shared,
    proj_step,
    conv_inner,
    conv_shared,
    step_bias,
    decay_log,
    skip_gain,
    gated_gain,
    proj_out,
    out_grad,
    segments,
):
    model_width = hidden_in.shape[1]
    width = proj_zx.shape[2]
    inner_width = width * 4
    heads = step_bias.shape[0]
    residual_in = hidden_in.astype(F32)
    scale_in = lax.rsqrt(jnp.mean(residual_in * residual_in, axis=-1, keepdims=True) + EPS)
    normed_low = (residual_in * scale_in * norm_gain).astype(BF16)

    shared_rows = gather_tokens(proj_shared)
    first_rows = jnp.concatenate(
        [proj_zx[:, 1, :], shared_rows, jnp.pad(proj_step, ((0, 0), (0, 128 - heads)))], 1
    )
    first_full = gather_dp(first_rows)
    tokens = gather_tokens(normed_low)
    second_rows = jnp.concatenate([proj_zx[:, 0, :], proj_out.T], 1)
    second_rows, first_done = lax.optimization_barrier((second_rows, first_full))
    second_full = gather_dp(second_rows)
    out_grad_late, tokens = lax.optimization_barrier((out_grad, tokens))
    grad_rows = gather_tokens(out_grad_late)

    first_pre = jnp.dot(tokens, first_full, preferred_element_type=F32)
    inner_pre = first_pre[:, :width]
    shared_pre = first_pre[:, width : width + 256]
    step_pre = first_pre[:, width + 256 : width + 256 + heads]
    mixer_fn = partial(block_mixer, segment_ids=segments, block_len=SPAN)
    scanned, mixer_back = jax.vjp(
        mixer_fn,
        inner_pre,
        shared_pre,
        step_pre,
        conv_inner,
        conv_shared,
        step_bias,
        decay_log,
        skip_gain,
    )
    gate_full = second_full[:, :width]
    out_full = second_full[:, width:]
    gate_pre = jnp.dot(tokens, gate_full, preferred_element_type=F32)
    grad_mixed = jnp.dot(grad_rows, out_full, preferred_element_type=F32)
    gate_sig = jax.nn.sigmoid(gate_pre)
    gate_act = gate_pre * gate_sig
    gated = scanned * gate_act
    sums = jnp.stack(
        [jnp.sum(gated * gated, axis=-1), jnp.sum(grad_mixed * gated_gain * gated, axis=-1)], 0
    )
    sums = sum_pair(sum_pair(sums, "c"), "zh")
    scale_mix = lax.rsqrt(sums[0] / inner_width + EPS)[:, None]
    norm_dot = (sums[1] / inner_width)[:, None]
    gated_scaled = gated * scale_mix
    mixed_low = (gated_scaled * gated_gain).astype(BF16)
    grad_gain_mix = jnp.sum(grad_mixed * gated_scaled, axis=0)
    grad_gated = scale_mix * gated_gain * grad_mixed - gated * scale_mix**3 * norm_dot
    grad_scanned = grad_gated * gate_act
    grad_gate = grad_gated * scanned * gate_sig * (1 + gate_pre * (1 - gate_sig))
    gate_grad_low = grad_gate.astype(BF16)

    mixed_sum = scatter_tensor(
        lax.dot_general(
            mixed_low, out_full, (((1,), (1,)), ((), ())), preferred_element_type=F32
        )
        .astype(BF16)
        .reshape(4, -1, model_width)
    )
    hidden_out = (residual_in + mixed_sum).astype(BF16)
    to_model = (((0,), (0,)), ((), ()))
    second_grad = jnp.concatenate(
        [
            lax.dot_general(tokens, gate_grad_low, to_model, preferred_element_type=F32),
            lax.dot_general(grad_rows, mixed_low, to_model, preferred_element_type=F32),
        ],
        1,
    ).astype(BF16)
    second_mine = scatter_dp(second_grad)
    grad_proj_gate = second_mine[:, :width]
    grad_proj_out = second_mine[:, width:].T

    (
        grad_inner,
        grad_shared,
        grad_step,
        grad_conv_in,
        grad_conv_sh,
        grad_bias,
        grad_decay,
        grad_skip,
    ) = mixer_back(grad_scanned)
    first_grad_low = jnp.concatenate(
        [grad_inner, grad_shared, jnp.pad(grad_step, ((0, 0), (0, 128 - heads)))], 1
    ).astype(BF16)
    to_tokens = (((1,), (1,)), ((), ()))
    grad_tokens = lax.dot_general(
        gate_grad_low, gate_full, to_tokens, preferred_element_type=F32
    ) + lax.dot_general(first_grad_low, first_full, to_tokens, preferred_element_type=F32)
    grad_gain_in = jnp.sum(grad_tokens * tokens.astype(F32), axis=0) / norm_gain
    grad_normed = scatter_tensor(grad_tokens.astype(BF16).reshape(4, -1, model_width))
    weighted = jnp.sum(grad_normed * norm_gain * residual_in, axis=-1, keepdims=True)
    grad_hidden = (
        out_grad.astype(F32)
        + scale_in * norm_gain * grad_normed
        - residual_in * scale_in**3 * weighted / model_width
    ).astype(BF16)

    first_grad = lax.dot_general(tokens, first_grad_low, to_model, preferred_element_type=F32).astype(BF16)
    shared_parts = first_grad[:, width : width + 256].reshape(32, 4, 12, 256).swapaxes(0, 1)
    shared_part = scatter_tensor(shared_parts).astype(BF16).reshape(1536, 64)
    first_pack = jnp.concatenate(
        [first_grad[:, :width], shared_part, first_grad[:, width + 256 : width + 256 + 64]], 1
    )
    first_mine = scatter_dp(first_pack)
    grad_proj_inner = first_mine[:, :width]
    grad_proj_shared = first_mine[:, width : width + 64].reshape(12, 256)
    grad_proj_step = first_mine[:, width + 64 : width + 64 + heads]
    grad_proj_zx = jnp.stack([grad_proj_gate, grad_proj_inner], 1)

    everywhere = jnp.concatenate([grad_gain_in, grad_conv_sh.reshape(-1)])
    everywhere = sum_pair(sum_pair(everywhere, "c"), "zh")
    small = jnp.concatenate(
        [everywhere, grad_conv_in.reshape(-1), grad_gain_mix, grad_bias, grad_decay, grad_skip]
    )
    count = small.shape[0]
    small = jnp.pad(small, (0, 8192 - count)).reshape(8, 1024)
    small = sum_pair(sum_ring(sum_ring(small, "y"), "x"), "zl").reshape(-1)
    cuts = [model_width, 5 * 256, 5 * width, width, heads, heads, heads]
    parts, place = [], 0
    for size in cuts:
        parts.append(small[place : place + size])
        place += size
    return (
        hidden_out,
        grad_hidden,
        parts[0],
        grad_proj_zx,
        grad_proj_shared,
        grad_proj_step,
        parts[2].reshape(5, width),
        parts[1].reshape(5, 256),
        parts[4],
        parts[5],
        parts[6],
        parts[3],
        grad_proj_out,
    )


def solution(mesh):
    fine = Mesh(mesh.devices.reshape(4, 4, 2, 2, 2), DP + TENSOR)
    both = DP + TENSOR
    return jax.shard_map(
        per_device,
        mesh=fine,
        in_specs=(
            P(both, None),
            P(),
            P(DP, None, TENSOR),
            P(both, None),
            P(DP, TENSOR),
            P(None, TENSOR),
            P(),
            P(TENSOR),
            P(TENSOR),
            P(TENSOR),
            P(TENSOR),
            P(TENSOR, DP),
            P(both, None),
            P(DP),
        ),
        out_specs=(
            P(both, None),
            P(both, None),
            P(),
            P(DP, None, TENSOR),
            P(both, None),
            P(DP, TENSOR),
            P(None, TENSOR),
            P(),
            P(TENSOR),
            P(TENSOR),
            P(TENSOR),
            P(TENSOR),
            P(TENSOR, DP),
        ),
        check_vma=False,
    )
```

```python
import jax
import jax.numpy as jnp
from jax import lax
from jax.experimental import pallas as pl
from jax.experimental.pallas import tpu as pltpu
from jax.sharding import Mesh
from jax.sharding import PartitionSpec as P

EPS = 1e-05
DP = ("y", "x", "zl")
TENSOR = ("zh", "c")
SIZES = {"y": 4, "x": 4, "zl": 2, "zh": 2, "c": 2}

F32 = jnp.float32
BF16 = jnp.bfloat16
HIGH = lax.Precision.HIGHEST
BLOCK = 128
VMEM = 56 * 1024 * 1024
NT = (((1,), (1,)), ((), ()))


def dot(a, b):
    return jnp.dot(a, b, preferred_element_type=F32)


def dot_nt(a, b):
    return lax.dot_general(a, b, NT, preferred_element_type=F32)


def sigmoid(a):
    return 0.5 * jnp.tanh(0.5 * a) + 0.5


def softplus(a):
    return jnp.maximum(a, 0.0) + jnp.log1p(jnp.exp(-jnp.abs(a)))


def conv_strip(ext, taps, aux, j):
    n = ext.shape[0] - 8
    lanes = slice(j * 128, (j + 1) * 128)
    total = taps[4:5, lanes] + taps[3:4, lanes] * ext[8 : 8 + n, lanes]
    for back in (1, 2, 3):
        total += taps[3 - back : 4 - back, lanes] * (
            aux[:, back - 1 : back] * ext[8 - back : 8 - back + n, lanes]
        )
    return total


def spread_heads(cols, j, low_half):
    return jnp.where(low_half, cols[:, 2 * j : 2 * j + 1], cols[:, 2 * j + 1 : 2 * j + 2])


def scan_forward_kernel(tok, weights_a, weights_b, taps, heads, chan, aux, segrow, pre_out, scan_out, state_out, ext, act, carry, fed):
    n = tok.shape[0]
    pairs = carry.shape[1] // 128

    @pl.when(pl.program_id(0) == 0)
    def _():
        carry[...] = jnp.zeros_like(carry)
        ext[0:8, :] = jnp.zeros((8, ext.shape[1]), F32)

    pre = jnp.concatenate([dot(tok[...], weights_a[...]), dot(tok[...], weights_b[...])], 1)
    pre_out[...] = pre
    wide = ext.shape[1]
    ext[8:, :] = pre[:, :wide]
    marks = aux[...]
    for j in range(wide // 128):
        total = conv_strip(ext, taps, marks, j)
        act[:, j * 128 : (j + 1) * 128] = total * sigmoid(total)
    ext[0:8, :] = ext[n : n + 8, :]

    step = softplus(pre[:, wide:] + heads[0:1, :])
    log_step = -step * heads[1:2, :]
    row = lax.broadcasted_iota(jnp.int32, (n, n), 0)
    col = lax.broadcasted_iota(jnp.int32, (n, n), 1)
    lower = (row >= col).astype(F32)
    cum = jnp.dot(lower, log_step, precision=HIGH, preferred_element_type=F32)
    cum_t = cum.T
    write = act[:, pairs * 128 : (pairs + 1) * 128]
    read = act[:, (pairs + 1) * 128 : (pairs + 2) * 128].astype(BF16)
    write_t = write.T.astype(BF16)
    allowed = (row >= col) & (marks[:, 8:9] == segrow[0:1, :])
    inner = jnp.where(allowed, dot(read, write_t), 0.0)
    last = cum[n - 1 : n, :]
    enters = jnp.exp(cum) * marks[:, 3:4]
    to_end = jnp.exp(last - cum) * marks[:, 4:5]
    keep = jnp.exp(last) * marks[n - 1 : n, 3:4]
    held = carry[...]
    held_low = held.astype(BF16)
    state_out[0] = held_low
    from_state = dot(read, held_low)
    low_half = lax.broadcasted_iota(jnp.int32, (1, 128), 1) < 64
    for j in range(pairs):
        lanes = slice(j * 128, (j + 1) * 128)
        x = act[:, lanes]
        xdt = x * spread_heads(step, j, low_half)
        parts = []
        for h in (2 * j, 2 * j + 1):
            decay = jnp.exp(jnp.minimum(cum[:, h : h + 1] - cum_t[h : h + 1, :], 0.0))
            parts.append((decay * inner).astype(BF16))
        xdt_low = xdt.astype(BF16)
        zero = jnp.zeros_like(xdt_low)
        pair = jnp.concatenate([jnp.where(low_half, xdt_low, zero), jnp.where(low_half, zero, xdt_low)], 0)
        y = dot(jnp.concatenate(parts, 1), pair)
        y += spread_heads(enters, j, low_half) * from_state[:, lanes] + chan[0:1, lanes] * x
        scan_out[:, lanes] = y
        fed[:, lanes] = (xdt * spread_heads(to_end, j, low_half)).astype(BF16)
        carry[:, lanes] = held[:, lanes] * spread_heads(keep, j, low_half)
    carry[...] += dot(write_t, fed[...])


def scan_backward_kernel(pre, pre_before, taps, heads, chan, sums, aux, segrow, grad, state, low_out, taps_out, heads_out, ext, gext, act, slope, carry, fed, back, rows):
    n = pre.shape[0]
    pairs = carry.shape[1] // 128
    wide = ext.shape[1]

    @pl.when(pl.program_id(0) == 0)
    def _():
        carry[...] = jnp.zeros_like(carry)
        gext[n:, :] = jnp.zeros((8, wide), F32)
        taps_out[...] = jnp.zeros_like(taps_out)
        heads_out[...] = jnp.zeros_like(heads_out)
        rows[...] = jnp.zeros_like(rows)

    marks = aux[...]
    ext[0:8, :] = pre_before[:, :wide]
    ext[8:, :] = pre[:, :wide]
    for j in range(wide // 128):
        lanes = slice(j * 128, (j + 1) * 128)
        total = conv_strip(ext, taps, marks, j)
        sig = sigmoid(total)
        value = total * sig
        act[:, lanes] = value
        slope[:, lanes] = sig + value * (1.0 - sig)

    step_arg = pre[:, wide:] + heads[0:1, :]
    step = softplus(step_arg)
    rate = heads[1:2, :]
    row = lax.broadcasted_iota(jnp.int32, (n, n), 0)
    col = lax.broadcasted_iota(jnp.int32, (n, n), 1)
    lower = (row >= col).astype(F32)
    cum = jnp.dot(lower, -step * rate, precision=HIGH, preferred_element_type=F32)
    cum_t = cum.T
    write = act[:, pairs * 128 : (pairs + 1) * 128]
    read = act[:, (pairs + 1) * 128 : (pairs + 2) * 128]
    read_t = read.T.astype(BF16)
    write_low = write.astype(BF16)
    read_low = read.astype(BF16)
    allowed = (row <= col) & (marks[:, 8:9] == segrow[0:1, :])
    inner_t = jnp.where(allowed, dot(write_low, read_t), 0.0)
    last = cum[n - 1 : n, :]
    enters = jnp.exp(cum) * marks[:, 3:4]
    to_end = jnp.exp(last - cum) * marks[:, 4:5]
    keep = jnp.exp(last) * marks[n - 1 : n, 3:4]
    held = state[0]
    later = carry[...]
    later_low = later.astype(BF16)
    from_state = dot(read_low, held)
    from_later = dot(write_low, later_low)
    low_half = lax.broadcasted_iota(jnp.int32, (1, 128), 1) < 64
    head_lane = lax.broadcasted_iota(jnp.int32, (1, 128), 1)
    grad_inner = jnp.zeros((n, n), F32)
    col_sums = jnp.zeros((n, 128), F32)
    to_end_part = jnp.zeros((n, 128), F32)
    enter_part = jnp.zeros((n, 128), F32)
    step_part = jnp.zeros((n, 128), F32)
    skip_part = jnp.zeros((n, 128), F32)
    keep_part = jnp.zeros((8, 128), F32)

    def head_sums(value, j):
        high = value.astype(BF16)
        rest = (value - high.astype(F32)).astype(BF16)
        return dot(jnp.concatenate([high, rest], 1), sums[j])

    for j in range(pairs):
        lanes = slice(j * 128, (j + 1) * 128)
        x = act[:, lanes]
        dy = grad[:, lanes].astype(F32)
        step_wide = spread_heads(step, j, low_half)
        xdt = x * step_wide
        xdt_low = xdt.astype(BF16)
        dy_low = dy.astype(BF16)
        zero = jnp.zeros_like(xdt_low)
        products = dot_nt(
            jnp.concatenate([jnp.where(low_half, xdt_low, zero), jnp.where(low_half, zero, xdt_low)], 0),
            dy_low,
        )
        parts = []
        for k, h in enumerate((2 * j, 2 * j + 1)):
            product = products[k * n : (k + 1) * n, :]
            decay = jnp.exp(jnp.minimum(cum_t[h : h + 1, :] - cum[:, h : h + 1], 0.0))
            scaled = decay * product
            grad_inner += scaled
            weighted = scaled * inner_t
            rows[h : h + 1, :] = jnp.sum(weighted, axis=0, keepdims=True)
            col_sums += jnp.where(head_lane == h, jnp.sum(weighted, axis=1, keepdims=True), 0.0)
            parts.append((decay * inner_t).astype(BF16))
        grad_pair = jnp.concatenate([jnp.where(low_half, dy_low, zero), jnp.where(low_half, zero, dy_low)], 0)
        grad_xdt = dot(jnp.concatenate(parts, 1), grad_pair)
        end_wide = spread_heads(to_end, j, low_half)
        enter_wide = spread_heads(enters, j, low_half)
        later_part = end_wide * from_later[:, lanes]
        grad_xdt += later_part
        to_end_part += head_sums(later_part * xdt, j)
        fed[:, lanes] = (xdt * end_wide).astype(BF16)
        grad_enter = dy * enter_wide
        back[:, lanes] = grad_enter.astype(BF16)
        enter_part += head_sums(grad_enter * from_state[:, lanes], j)
        step_part += head_sums(grad_xdt * x, j)
        skip_part += head_sums(dy * x, j)
        kept = jnp.sum(held[:, lanes].astype(F32) * later[:, lanes], axis=0, keepdims=True)
        keep_part += head_sums(jnp.broadcast_to(kept, (8, 128)), j)
        act[:, lanes] = grad_xdt * step_wide + chan[0:1, lanes] * dy
        carry[:, lanes] = later[:, lanes] * spread_heads(keep, j, low_half)

    grad_cum = rows[...].T - col_sums + enter_part - to_end_part
    grad_last = jnp.sum(to_end_part, axis=0, keepdims=True) + keep * keep_part[0:1, :]
    upper = (row <= col).astype(F32)
    grad_log = jnp.dot(upper, grad_cum, precision=HIGH, preferred_element_type=F32) + grad_last
    grad_step = (step_part - rate * grad_log) * sigmoid(step_arg)
    heads_out[0:1, :] += jnp.sum(grad_step, axis=0, keepdims=True)
    heads_out[1:2, :] += -rate * jnp.sum(step * grad_log, axis=0, keepdims=True)
    heads_out[2:3, :] += jnp.sum(skip_part, axis=0, keepdims=True)
    low_out[:, wide:] = grad_step.astype(BF16)

    grad_inner = jnp.where(allowed, grad_inner, 0.0)
    act[:, pairs * 128 : (pairs + 1) * 128] = dot(grad_inner.astype(BF16), read_low) + dot_nt(fed[...], later_low)
    act[:, (pairs + 1) * 128 : (pairs + 2) * 128] = dot(grad_inner.T.astype(BF16), write_low) + dot_nt(back[...], held)
    carry[...] += dot(read_t, back[...])

    for j in range(wide // 128):
        lanes = slice(j * 128, (j + 1) * 128)
        grad_pre = act[:, lanes] * slope[:, lanes]
        gext[0:n, lanes] = grad_pre
        total = taps[3:4, lanes] * grad_pre
        taps_out[3:4, lanes] += jnp.sum(grad_pre * ext[8 : 8 + n, lanes], axis=0, keepdims=True)
        taps_out[4:5, lanes] += jnp.sum(grad_pre, axis=0, keepdims=True)
        for by in (1, 2, 3):
            total += taps[3 - by : 4 - by, lanes] * (marks[:, 4 + by : 5 + by] * gext[by : by + n, lanes])
            taps_out[3 - by : 4 - by, lanes] += jnp.sum(
                grad_pre * (marks[:, by - 1 : by] * ext[8 - by : 8 - by + n, lanes]), axis=0, keepdims=True
            )
        low_out[:, lanes] = total.astype(BF16)
    gext[n:, :] = gext[0:8, :]


def scan_marks(segments):
    length = segments.shape[0]
    blocks = segments.reshape(-1, BLOCK)
    before = jnp.concatenate([jnp.full((1,), -1, jnp.int32), blocks[:-1, -1]], 0)

    def same(by):
        if by > 0:
            other = jnp.concatenate([jnp.full((by,), -1, jnp.int32), segments[:-by]], 0)
        else:
            other = jnp.concatenate([segments[-by:], jnp.full((-by,), -1, jnp.int32)], 0)
        return other == segments

    cols = [same(1), same(2), same(3), (blocks == before[:, None]).reshape(-1), (blocks == blocks[:, -1:]).reshape(-1)]
    cols += [same(-1), same(-2), same(-3), segments]
    marks = jnp.stack([c.astype(F32) for c in cols], 1)
    return jnp.pad(marks, ((0, 0), (0, 128 - len(cols)))), jnp.broadcast_to(segments.astype(F32), (8, length))


def scan_forward(tokens, weights_a, weights_b, taps, heads, chan, marks, segrow):
    length, model = tokens.shape
    cols = weights_a.shape[1] + weights_b.shape[1]
    inner = cols - 384
    wide = cols - 128
    n = BLOCK
    blocks = length // n

    def whole(shape):
        return pl.BlockSpec(shape, lambda i: (0,) * len(shape))

    return pl.pallas_call(
        scan_forward_kernel,
        grid=(blocks,),
        in_specs=[
            pl.BlockSpec((n, model), lambda i: (i, 0)),
            whole(weights_a.shape),
            whole(weights_b.shape),
            whole((8, wide)),
            whole((8, 128)),
            whole((8, inner)),
            pl.BlockSpec((n, 128), lambda i: (i, 0)),
            pl.BlockSpec((8, n), lambda i: (0, i)),
        ],
        out_specs=[
            pl.BlockSpec((n, cols), lambda i: (i, 0)),
            pl.BlockSpec((n, inner), lambda i: (i, 0)),
            pl.BlockSpec((1, 128, inner), lambda i: (i, 0, 0)),
        ],
        out_shape=[
            jax.ShapeDtypeStruct((length, cols), F32),
            jax.ShapeDtypeStruct((length, inner), F32),
            jax.ShapeDtypeStruct((blocks, 128, inner), BF16),
        ],
        scratch_shapes=[
            pltpu.VMEM((n + 8, wide), F32),
            pltpu.VMEM((n, wide), F32),
            pltpu.VMEM((128, inner), F32),
            pltpu.VMEM((n, inner), BF16),
        ],
        compiler_params=pltpu.CompilerParams(vmem_limit_bytes=VMEM),
        name="scan_forward",
    )(tokens, weights_a, weights_b, taps, heads, chan, marks, segrow)


def scan_backward(pre, taps, heads, chan, sums, marks, segrow, grad, states):
    length, cols = pre.shape
    inner = cols - 384
    wide = cols - 128
    n = BLOCK
    blocks = length // n

    def whole(shape):
        return pl.BlockSpec(shape, lambda i: (0,) * len(shape))

    def rev(i):
        return blocks - 1 - i

    return pl.pallas_call(
        scan_backward_kernel,
        grid=(blocks,),
        in_specs=[
            pl.BlockSpec((n, cols), lambda i: (rev(i), 0)),
            pl.BlockSpec((8, cols), lambda i: (jnp.maximum(rev(i) * (n // 8) - 1, 0), 0)),
            whole((8, wide)),
            whole((8, 128)),
            whole((8, inner)),
            whole((inner // 128, 256, 128)),
            pl.BlockSpec((n, 128), lambda i: (rev(i), 0)),
            pl.BlockSpec((8, n), lambda i: (0, rev(i))),
            pl.BlockSpec((n, inner), lambda i: (rev(i), 0)),
            pl.BlockSpec((1, 128, inner), lambda i: (rev(i), 0, 0)),
        ],
        out_specs=[
            pl.BlockSpec((n, cols), lambda i: (rev(i), 0)),
            whole((8, wide)),
            whole((8, 128)),
        ],
        out_shape=[
            jax.ShapeDtypeStruct((length, cols), BF16),
            jax.ShapeDtypeStruct((8, wide), F32),
            jax.ShapeDtypeStruct((8, 128), F32),
        ],
        scratch_shapes=[
            pltpu.VMEM((n + 8, wide), F32),
            pltpu.VMEM((n + 8, wide), F32),
            pltpu.VMEM((n, wide), F32),
            pltpu.VMEM((n, wide), F32),
            pltpu.VMEM((128, inner), F32),
            pltpu.VMEM((n, inner), BF16),
            pltpu.VMEM((n, inner), BF16),
            pltpu.VMEM((128, n), F32),
        ],
        compiler_params=pltpu.CompilerParams(vmem_limit_bytes=VMEM),
        name="scan_backward",
    )(pre, pre, taps, heads, chan, sums, marks, segrow, grad, states)


def head_sum_table(inner):
    pairs = inner // 128
    lane = jnp.arange(256) % 128
    head = 2 * jnp.arange(pairs)[:, None] + (lane >= 64)[None, :]
    return (head[:, :, None] == jnp.arange(128)[None, None, :]).astype(BF16)


def mix_first_kernel(tok, rows, gate_w, out_w, scanned, gain, gate_out, mixed_out, sums_out):
    gate_pre = dot(tok[...], gate_w[...])
    grad_mixed = dot(rows[...], out_w[...])
    gate_out[...] = gate_pre
    mixed_out[...] = grad_mixed
    gated = scanned[...] * (gate_pre * sigmoid(gate_pre))
    square = jnp.sum(gated * gated, axis=1, keepdims=True)
    inner = jnp.sum(grad_mixed * gain[0:1, :] * gated, axis=1, keepdims=True)
    lane = lax.broadcasted_iota(jnp.int32, (1, 128), 1)
    cols = jnp.where(lane == 0, square, jnp.where(lane == 1, inner, 0.0))
    sums_out[...] = cols.T[0:8, :]


def mix_first(tokens, grad_rows, gate_w, out_w, scanned, gain):
    length, model = tokens.shape
    width = scanned.shape[1]
    n = 256

    def whole(shape):
        return pl.BlockSpec(shape, lambda i: (0,) * len(shape))

    def rows(cols):
        return pl.BlockSpec((n, cols), lambda i: (i, 0))

    return pl.pallas_call(
        mix_first_kernel,
        grid=(length // n,),
        in_specs=[rows(model), rows(model), whole(gate_w.shape), whole(out_w.shape), rows(width), whole((8, width))],
        out_specs=[rows(width), rows(width), pl.BlockSpec((8, n), lambda i: (0, i))],
        out_shape=[
            jax.ShapeDtypeStruct((length, width), F32),
            jax.ShapeDtypeStruct((length, width), F32),
            jax.ShapeDtypeStruct((8, length), F32),
        ],
        compiler_params=pltpu.CompilerParams(vmem_limit_bytes=VMEM),
        name="mix_first",
    )(tokens, grad_rows, gate_w, out_w, scanned, gain)


def mix_second_kernel(channels, sums, gate, grad_mixed_in, scanned_in, out_w, gain, low_out, projected, grad_scan, grad_gate, gain_out):
    n = gate.shape[0]

    @pl.when(pl.program_id(0) == 0)
    def _():
        gain_out[...] = jnp.zeros_like(gain_out)

    cols = jnp.concatenate([sums[...], jnp.zeros((120, n), F32)], 0).T
    scale = lax.rsqrt(cols[:, 0:1] / channels + EPS)
    pull = scale * scale * scale * (cols[:, 1:2] / channels)
    gate_pre = gate[...]
    grad_mixed = grad_mixed_in[...]
    scanned = scanned_in[...]
    sig = sigmoid(gate_pre)
    silu = gate_pre * sig
    gated = scanned * silu
    scaled = gated * scale
    mixed = (scaled * gain[0:1, :]).astype(BF16)
    low_out[...] = mixed
    gain_out[0:1, :] += jnp.sum(grad_mixed * scaled, axis=0, keepdims=True)
    grad_gated = scale * gain[0:1, :] * grad_mixed - gated * pull
    grad_scan[...] = grad_gated * silu
    grad_gate[...] = (grad_gated * scanned * (sig + silu * (1.0 - sig))).astype(BF16)
    projected[...] = dot_nt(mixed, out_w[...]).astype(BF16)


def mix_second(sums, gate, grad_mixed, scanned, out_w, gain, channels):
    length, width = gate.shape
    model = out_w.shape[0]
    n = 256

    def whole(shape):
        return pl.BlockSpec(shape, lambda i: (0,) * len(shape))

    def rows(cols):
        return pl.BlockSpec((n, cols), lambda i: (i, 0))

    return pl.pallas_call(
        lambda *refs: mix_second_kernel(channels, *refs),
        grid=(length // n,),
        in_specs=[pl.BlockSpec((8, n), lambda i: (0, i)), rows(width), rows(width), rows(width), whole(out_w.shape), whole((8, width))],
        out_specs=[rows(width), rows(model), rows(width), rows(width), whole((8, width))],
        out_shape=[
            jax.ShapeDtypeStruct((length, width), BF16),
            jax.ShapeDtypeStruct((length, model), BF16),
            jax.ShapeDtypeStruct((length, width), F32),
            jax.ShapeDtypeStruct((length, width), BF16),
            jax.ShapeDtypeStruct((8, width), F32),
        ],
        compiler_params=pltpu.CompilerParams(vmem_limit_bytes=VMEM),
        name="mix_second",
    )(sums, gate, grad_mixed, scanned, out_w, gain)


def token_grads_kernel(tok, grad_gate, low, gate_w, weights_a, weights_b, rows_out, sums_out):
    @pl.when(pl.program_id(0) == 0)
    def _():
        sums_out[...] = jnp.zeros_like(sums_out)

    cut = weights_a.shape[1]
    total = dot_nt(grad_gate[...], gate_w[...])
    total += dot_nt(low[:, :cut], weights_a[...])
    total += dot_nt(low[:, cut:], weights_b[...])
    rows_out[...] = total.astype(BF16)
    sums_out[0:1, :] += jnp.sum(total * tok[...].astype(F32), axis=0, keepdims=True)


def token_grads(tokens, grad_gate, low, gate_w, weights_a, weights_b):
    length, model = tokens.shape
    n = 256

    def whole(shape):
        return pl.BlockSpec(shape, lambda i: (0,) * len(shape))

    def rows(cols):
        return pl.BlockSpec((n, cols), lambda i: (i, 0))

    return pl.pallas_call(
        token_grads_kernel,
        grid=(length // n,),
        in_specs=[rows(model), rows(grad_gate.shape[1]), rows(low.shape[1]), whole(gate_w.shape), whole(weights_a.shape), whole(weights_b.shape)],
        out_specs=[rows(model), whole((8, model))],
        out_shape=[jax.ShapeDtypeStruct((length, model), BF16), jax.ShapeDtypeStruct((8, model), F32)],
        compiler_params=pltpu.CompilerParams(vmem_limit_bytes=VMEM),
        name="token_grads",
    )(tokens, grad_gate, low, gate_w, weights_a, weights_b)


def shift(value, axis, by):
    n = SIZES[axis]
    return lax.ppermute(value, axis, [(i, (i - by) % n) for i in range(n)])


def swap(value, axis):
    return shift(value, axis, 1)


def ordered_pair(own, other, axis):
    first = lax.axis_index(axis) == 0
    return jnp.stack([jnp.where(first, own, other), jnp.where(first, other, own)], 0)


def gather_pair(value, axis):
    return ordered_pair(value, swap(value, axis), axis)


def place_kernel(me, *refs):
    for k, part in enumerate(refs[:4]):

        @pl.when(pl.program_id(0) == k)
        def _():
            refs[4][...] = part[...].reshape(refs[4].shape)


def gather_ring(value, axis, position):
    parts = [value, shift(value, axis, 1), shift(value, axis, 2), shift(value, axis, -1)]
    shape = value.shape[:position] + (4,) + value.shape[position:]
    block = value.shape[:position] + (1,) + value.shape[position:]

    def out_index(i, me):
        return tuple((me[0] + i) % 4 if d == position else 0 for d in range(len(shape)))

    return pl.pallas_call(
        place_kernel,
        grid_spec=pltpu.PrefetchScalarGridSpec(
            num_scalar_prefetch=1,
            grid=(4,),
            in_specs=[pl.BlockSpec(value.shape, lambda i, me: (0,) * value.ndim)] * 4,
            out_specs=pl.BlockSpec(block, out_index),
        ),
        out_shape=jax.ShapeDtypeStruct(shape, value.dtype),
        compiler_params=pltpu.CompilerParams(vmem_limit_bytes=VMEM),
        name="place_" + axis,
    )(lax.axis_index(axis).reshape(1).astype(jnp.int32), *parts)


def gather_halves(a, b):
    pair_a, pair_b = gather_pair(a, "zl"), gather_pair(b, "zl")
    pair_a = pair_a.reshape(96, a.shape[1])
    pair_b = pair_b.reshape(96, b.shape[1])
    rows_a = gather_ring(pair_a, "x", 0)
    rows_b = gather_ring(pair_b, "y", 0)
    full_a = gather_ring(rows_a, "y", 0)
    full_b = gather_ring(rows_b, "x", 1)
    return full_a.reshape(1536, -1), full_b.reshape(1536, -1)


def scatter_ring(value, axis, position):
    me = lax.axis_index(axis)

    def entry(by):
        return lax.dynamic_index_in_dim(value, (me + by) % 4, position, keepdims=False)

    ahead = shift(entry(-1), axis, 1)
    behind = shift(entry(1), axis, -1)
    across = shift(entry(2), axis, 2)
    return (entry(0).astype(F32) + across.astype(F32)) + (ahead.astype(F32) + behind.astype(F32))


def scatter_pair(value, axis):
    me = lax.axis_index(axis)
    keep = lax.dynamic_index_in_dim(value, me, 0, keepdims=False)
    give = lax.dynamic_index_in_dim(value, 1 - me, 0, keepdims=False)
    return keep.astype(F32) + swap(give, axis).astype(F32)


def scatter_halves(a, b):
    blocks_a = a.reshape(4, 4, 96, a.shape[1])
    blocks_b = b.reshape(4, 4, 96, b.shape[1])
    half_a = scatter_ring(blocks_a, "y", 0).astype(BF16)
    half_b = scatter_ring(blocks_b, "x", 1).astype(BF16)
    mine_a = scatter_ring(half_a, "x", 0).astype(BF16)
    mine_b = scatter_ring(half_b, "y", 0).astype(BF16)
    both = jnp.concatenate([mine_a, mine_b], 1)
    return scatter_pair(both.reshape(2, 48, -1), "zl")


def sum_ring(value, axis):
    ahead, behind, across = shift(value, axis, 1), shift(value, axis, -1), shift(value, axis, 2)
    return (value + across) + (ahead + behind)


def sum_pair(value, axis):
    return value + swap(value, axis)


def gather_tokens(value):
    far = swap(value, "zh")
    near_pair = gather_pair(value, "c")
    far_pair = gather_pair(far, "c")
    both = ordered_pair(near_pair, far_pair, "zh")
    return both.reshape((4 * value.shape[0],) + value.shape[1:])


def scatter_tensor(value):
    by_zh = value.reshape((2, 2) + value.shape[1:])
    half = scatter_pair(jnp.swapaxes(by_zh, 0, 1), "c").astype(BF16)
    return scatter_pair(half, "zh")


def per_device(
    hidden_in,
    norm_gain,
    proj_zx,
    proj_shared,
    proj_step,
    conv_inner,
    conv_shared,
    step_bias,
    decay_log,
    skip_gain,
    gated_gain,
    proj_out,
    out_grad,
    segments,
):
    model_width = hidden_in.shape[1]
    width = proj_zx.shape[2]
    heads = step_bias.shape[0]
    cut = 640
    residual_in = hidden_in.astype(F32)
    scale_in = lax.rsqrt(jnp.mean(residual_in * residual_in, axis=-1, keepdims=True) + EPS)
    normed_low = (residual_in * scale_in * norm_gain).astype(BF16)

    shared_rows = gather_tokens(proj_shared)
    first_rows = jnp.concatenate(
        [proj_zx[:, 1, :], shared_rows, jnp.pad(proj_step, ((0, 0), (0, 128 - heads)))], 1
    )
    first_a, first_b = gather_halves(first_rows[:, :cut], first_rows[:, cut:])
    tokens = gather_tokens(normed_low)
    second_rows = jnp.concatenate([proj_zx[:, 0, :], proj_out.T], 1)
    second_full = lax.all_gather(gather_pair(second_rows, "zl"), ("y", "x"), axis=0, tiled=True)
    second_full = second_full.reshape(1536, 2 * width)
    gate_full = second_full[:, :width]
    out_full = second_full[:, width:]
    out_grad_late, tokens = lax.optimization_barrier((out_grad, tokens))
    grad_rows = gather_tokens(out_grad_late)

    pad = (0, 128 - heads)
    head_rows = jnp.stack([jnp.pad(step_bias, pad), jnp.pad(jnp.exp(decay_log), pad)], 0)
    head_rows = jnp.pad(head_rows, ((0, 6), (0, 0)))
    taps = jnp.pad(jnp.concatenate([conv_inner, conv_shared], 1), ((0, 3), (0, 0)))
    chan = jnp.broadcast_to(jnp.repeat(skip_gain, width // heads), (8, width))
    gain = jnp.broadcast_to(gated_gain, (8, width))
    marks, segrow = scan_marks(segments)
    pre, scanned, states = scan_forward(tokens, first_a, first_b, taps, head_rows, chan, marks, segrow)

    gate_pre, grad_mixed, sums = mix_first(tokens, grad_rows, gate_full, out_full, scanned, gain)
    sums = sum_pair(sum_pair(sums, "c"), "zh")
    mixed_low, projected, grad_scanned, gate_grad_low, gain_sums = mix_second(
        sums, gate_pre, grad_mixed, scanned, out_full, gain, 4 * width
    )
    mixed_sum = scatter_tensor(projected.reshape(4, -1, model_width))
    hidden_out = (residual_in + mixed_sum).astype(BF16)

    to_model = (((0,), (0,)), ((), ()))
    second_grad = jnp.concatenate(
        [
            lax.dot_general(tokens, gate_grad_low, to_model, preferred_element_type=F32).astype(BF16),
            lax.dot_general(grad_rows, mixed_low, to_model, preferred_element_type=F32).astype(BF16),
        ],
        1,
    )
    second_mine = lax.psum_scatter(second_grad, ("y", "x"), scatter_dimension=0, tiled=True)
    second_mine = scatter_pair(second_mine.reshape(2, 48, -1), "zl")
    grad_proj_gate = second_mine[:, :width]
    grad_proj_out = second_mine[:, width:].T

    sum_table = head_sum_table(width)
    low, tap_sums, head_sums = scan_backward(
        pre, taps, head_rows, chan, sum_table, marks, segrow, grad_scanned, states
    )
    token_rows, gain_in = token_grads(tokens, gate_grad_low, low, gate_full, first_a, first_b)
    grad_gain_in = gain_in[0] / norm_gain
    grad_normed = scatter_tensor(token_rows.reshape(4, -1, model_width))
    weighted = jnp.sum(grad_normed * norm_gain * residual_in, axis=-1, keepdims=True)
    grad_hidden = (
        out_grad.astype(F32)
        + scale_in * norm_gain * grad_normed
        - residual_in * scale_in**3 * weighted / model_width
    ).astype(BF16)

    first_grad = lax.dot_general(tokens, low, to_model, preferred_element_type=F32).astype(BF16)
    shared_parts = first_grad[:, width : width + 256].reshape(32, 4, 12, 256).swapaxes(0, 1)
    shared_part = scatter_tensor(shared_parts).astype(BF16).reshape(1536, 64)
    rest = jnp.concatenate(
        [first_grad[:, 512:width], shared_part, first_grad[:, width + 256 : width + 256 + 64]], 1
    )
    first_mine = scatter_halves(first_grad[:, :512], rest)
    grad_proj_inner = first_mine[:, :width]
    grad_proj_shared = first_mine[:, width : width + 64].reshape(12, 256)
    grad_proj_step = first_mine[:, width + 64 : width + 64 + heads]
    grad_proj_zx = jnp.stack([grad_proj_gate, grad_proj_inner], 1)

    everywhere = jnp.concatenate([grad_gain_in, tap_sums[:5, width:].reshape(-1)])
    everywhere = sum_pair(sum_pair(everywhere, "c"), "zh")
    small = jnp.concatenate(
        [everywhere, tap_sums[:5, :width].reshape(-1), gain_sums[0], head_sums[:3, :heads].reshape(-1)]
    )
    count = small.shape[0]
    small = jnp.pad(small, (0, 8192 - count)).reshape(8, 1024)
    small = sum_pair(sum_ring(sum_ring(small, "y"), "x"), "zl").reshape(-1)
    cuts = [model_width, 5 * 256, 5 * width, width, heads, heads, heads]
    parts, place = [], 0
    for size in cuts:
        parts.append(small[place : place + size])
        place += size
    return (
        hidden_out,
        grad_hidden,
        parts[0],
        grad_proj_zx,
        grad_proj_shared,
        grad_proj_step,
        parts[2].reshape(5, width),
        parts[1].reshape(5, 256),
        parts[4],
        parts[5],
        parts[6],
        parts[3],
        grad_proj_out,
    )


def solution(mesh):
    fine = Mesh(mesh.devices.reshape(4, 4, 2, 2, 2), DP + TENSOR)
    both = DP + TENSOR
    return jax.shard_map(
        per_device,
        mesh=fine,
        in_specs=(
            P(both, None),
            P(),
            P(DP, None, TENSOR),
            P(both, None),
            P(DP, TENSOR),
            P(None, TENSOR),
            P(),
            P(TENSOR),
            P(TENSOR),
            P(TENSOR),
            P(TENSOR),
            P(TENSOR, DP),
            P(both, None),
            P(DP),
        ),
        out_specs=(
            P(both, None),
            P(both, None),
            P(),
            P(DP, None, TENSOR),
            P(both, None),
            P(DP, TENSOR),
            P(None, TENSOR),
            P(),
            P(TENSOR),
            P(TENSOR),
            P(TENSOR),
            P(TENSOR),
            P(TENSOR, DP),
        ),
        check_vma=False,
    )
```

```python
import jax
import jax.numpy as jnp
from jax import lax
from jax.experimental import pallas as pl
from jax.experimental.pallas import tpu as pltpu
from jax.sharding import Mesh
from jax.sharding import PartitionSpec as P

EPS = 1e-05
DP = ("y", "x", "zl")
TENSOR = ("zh", "c")
SIZES = {"y": 4, "x": 4, "zl": 2, "zh": 2, "c": 2}

F32 = jnp.float32
BF16 = jnp.bfloat16
HIGH = lax.Precision.HIGHEST
BLOCK = 128
VMEM = 56 * 1024 * 1024
PARAMS = pltpu.CompilerParams(vmem_limit_bytes=VMEM)
NT = (((1,), (1,)), ((), ()))
TN = (((0,), (0,)), ((), ()))
VMEM_SPEC = pl.BlockSpec(memory_space=pltpu.VMEM)


def cost(us):
    return pl.CostEstimate(flops=int(us * 1e9), transcendentals=0, bytes_accessed=int(us * 3e6))


def whole(shape):
    return pl.BlockSpec(shape, lambda *i: (0,) * len(shape))


def dot(a, b):
    return jnp.dot(a, b, preferred_element_type=F32)


def dot_nt(a, b):
    return lax.dot_general(a, b, NT, preferred_element_type=F32)


def sigmoid(a):
    return 0.5 * jnp.tanh(0.5 * a) + 0.5


def softplus(a):
    return jnp.maximum(a, 0.0) + jnp.log1p(jnp.exp(-jnp.abs(a)))


def conv_strip(ext, taps, aux, j):
    n = ext.shape[0] - 8
    lanes = slice(j * 128, (j + 1) * 128)
    total = taps[4:5, lanes] + taps[3:4, lanes] * ext[8 : 8 + n, lanes]
    for back in (1, 2, 3):
        total += taps[3 - back : 4 - back, lanes] * (
            aux[:, back - 1 : back] * ext[8 - back : 8 - back + n, lanes]
        )
    return total


def spread_heads(cols, j, low_half):
    return jnp.where(low_half, cols[:, 2 * j : 2 * j + 1], cols[:, 2 * j + 1 : 2 * j + 2])


def scan_forward_kernel(tok, weights, taps, heads, chan, aux, segrow, pre_out, scan_out, state_out, ext, act, carry, fed):
    n = tok.shape[0]
    pairs = carry.shape[1] // 128

    @pl.when(pl.program_id(0) == 0)
    def _():
        carry[...] = jnp.zeros_like(carry)
        ext[0:8, :] = jnp.zeros((8, ext.shape[1]), F32)

    pre = dot(tok[...], weights[...])
    pre_out[...] = pre
    wide = ext.shape[1]
    ext[8:, :] = pre[:, :wide]
    marks = aux[...]
    for j in range(wide // 128):
        total = conv_strip(ext, taps, marks, j)
        act[:, j * 128 : (j + 1) * 128] = total * sigmoid(total)
    ext[0:8, :] = ext[n : n + 8, :]

    step = softplus(pre[:, wide:] + heads[0:1, :])
    log_step = -step * heads[1:2, :]
    row = lax.broadcasted_iota(jnp.int32, (n, n), 0)
    col = lax.broadcasted_iota(jnp.int32, (n, n), 1)
    lower = (row >= col).astype(F32)
    cum = jnp.dot(lower, log_step, precision=HIGH, preferred_element_type=F32)
    cum_t = cum.T
    write = act[:, pairs * 128 : (pairs + 1) * 128]
    read = act[:, (pairs + 1) * 128 : (pairs + 2) * 128].astype(BF16)
    write_t = write.T.astype(BF16)
    allowed = (row >= col) & (marks[:, 8:9] == segrow[0:1, :])
    inner = jnp.where(allowed, dot(read, write_t), 0.0)
    last = cum[n - 1 : n, :]
    enters = jnp.exp(cum) * marks[:, 3:4]
    to_end = jnp.exp(last - cum) * marks[:, 4:5]
    keep = jnp.exp(last) * marks[n - 1 : n, 3:4]
    held = carry[...]
    held_low = held.astype(BF16)
    state_out[0] = held_low
    from_state = dot(read, held_low)
    low_half = lax.broadcasted_iota(jnp.int32, (1, 128), 1) < 64
    for j in range(pairs):
        lanes = slice(j * 128, (j + 1) * 128)
        x = act[:, lanes]
        xdt = x * spread_heads(step, j, low_half)
        parts = []
        for h in (2 * j, 2 * j + 1):
            decay = jnp.exp(jnp.minimum(cum[:, h : h + 1] - cum_t[h : h + 1, :], 0.0))
            parts.append((decay * inner).astype(BF16))
        xdt_low = xdt.astype(BF16)
        zero = jnp.zeros_like(xdt_low)
        pair = jnp.concatenate([jnp.where(low_half, xdt_low, zero), jnp.where(low_half, zero, xdt_low)], 0)
        y = dot(jnp.concatenate(parts, 1), pair)
        y += spread_heads(enters, j, low_half) * from_state[:, lanes] + chan[0:1, lanes] * x
        scan_out[:, lanes] = y
        fed[:, lanes] = (xdt * spread_heads(to_end, j, low_half)).astype(BF16)
        carry[:, lanes] = held[:, lanes] * spread_heads(keep, j, low_half)
    carry[...] += dot(write_t, fed[...])


def scan_backward_kernel(pre, pre_before, taps, heads, chan, sums, aux, segrow, grad, state, low_out, taps_out, heads_out, ext, gext, act, slope, carry, fed, back, rows):
    n = pre.shape[0]
    pairs = carry.shape[1] // 128
    wide = ext.shape[1]

    @pl.when(pl.program_id(0) == 0)
    def _():
        carry[...] = jnp.zeros_like(carry)
        gext[n:, :] = jnp.zeros((8, wide), F32)
        taps_out[...] = jnp.zeros_like(taps_out)
        heads_out[...] = jnp.zeros_like(heads_out)
        rows[...] = jnp.zeros_like(rows)

    marks = aux[...]
    ext[0:8, :] = pre_before[:, :wide]
    ext[8:, :] = pre[:, :wide]
    for j in range(wide // 128):
        lanes = slice(j * 128, (j + 1) * 128)
        total = conv_strip(ext, taps, marks, j)
        sig = sigmoid(total)
        value = total * sig
        act[:, lanes] = value
        slope[:, lanes] = sig + value * (1.0 - sig)

    step_arg = pre[:, wide:] + heads[0:1, :]
    step = softplus(step_arg)
    rate = heads[1:2, :]
    row = lax.broadcasted_iota(jnp.int32, (n, n), 0)
    col = lax.broadcasted_iota(jnp.int32, (n, n), 1)
    lower = (row >= col).astype(F32)
    cum = jnp.dot(lower, -step * rate, precision=HIGH, preferred_element_type=F32)
    cum_t = cum.T
    write = act[:, pairs * 128 : (pairs + 1) * 128]
    read = act[:, (pairs + 1) * 128 : (pairs + 2) * 128]
    read_t = read.T.astype(BF16)
    write_low = write.astype(BF16)
    read_low = read.astype(BF16)
    allowed = (row <= col) & (marks[:, 8:9] == segrow[0:1, :])
    inner_t = jnp.where(allowed, dot(write_low, read_t), 0.0)
    last = cum[n - 1 : n, :]
    enters = jnp.exp(cum) * marks[:, 3:4]
    to_end = jnp.exp(last - cum) * marks[:, 4:5]
    keep = jnp.exp(last) * marks[n - 1 : n, 3:4]
    held = state[0]
    later = carry[...]
    later_low = later.astype(BF16)
    from_state = dot(read_low, held)
    from_later = dot(write_low, later_low)
    low_half = lax.broadcasted_iota(jnp.int32, (1, 128), 1) < 64
    head_lane = lax.broadcasted_iota(jnp.int32, (1, 128), 1)
    grad_inner = jnp.zeros((n, n), F32)
    col_sums = jnp.zeros((n, 128), F32)
    to_end_part = jnp.zeros((n, 128), F32)
    enter_part = jnp.zeros((n, 128), F32)
    step_part = jnp.zeros((n, 128), F32)
    skip_part = jnp.zeros((n, 128), F32)
    keep_part = jnp.zeros((8, 128), F32)

    def head_sums(value, j):
        high = value.astype(BF16)
        rest = (value - high.astype(F32)).astype(BF16)
        return dot(jnp.concatenate([high, rest], 1), sums[j])

    for j in range(pairs):
        lanes = slice(j * 128, (j + 1) * 128)
        x = act[:, lanes]
        dy = grad[:, lanes].astype(F32)
        step_wide = spread_heads(step, j, low_half)
        xdt = x * step_wide
        xdt_low = xdt.astype(BF16)
        dy_low = dy.astype(BF16)
        zero = jnp.zeros_like(xdt_low)
        products = dot_nt(
            jnp.concatenate([jnp.where(low_half, xdt_low, zero), jnp.where(low_half, zero, xdt_low)], 0),
            dy_low,
        )
        parts = []
        for k, h in enumerate((2 * j, 2 * j + 1)):
            product = products[k * n : (k + 1) * n, :]
            decay = jnp.exp(jnp.minimum(cum_t[h : h + 1, :] - cum[:, h : h + 1], 0.0))
            scaled = decay * product
            grad_inner += scaled
            weighted = scaled * inner_t
            rows[h : h + 1, :] = jnp.sum(weighted, axis=0, keepdims=True)
            col_sums += jnp.where(head_lane == h, jnp.sum(weighted, axis=1, keepdims=True), 0.0)
            parts.append((decay * inner_t).astype(BF16))
        grad_pair = jnp.concatenate([jnp.where(low_half, dy_low, zero), jnp.where(low_half, zero, dy_low)], 0)
        grad_xdt = dot(jnp.concatenate(parts, 1), grad_pair)
        end_wide = spread_heads(to_end, j, low_half)
        enter_wide = spread_heads(enters, j, low_half)
        later_part = end_wide * from_later[:, lanes]
        grad_xdt += later_part
        to_end_part += head_sums(later_part * xdt, j)
        fed[:, lanes] = (xdt * end_wide).astype(BF16)
        grad_enter = dy * enter_wide
        back[:, lanes] = grad_enter.astype(BF16)
        enter_part += head_sums(grad_enter * from_state[:, lanes], j)
        step_part += head_sums(grad_xdt * x, j)
        skip_part += head_sums(dy * x, j)
        kept = jnp.sum(held[:, lanes].astype(F32) * later[:, lanes], axis=0, keepdims=True)
        keep_part += head_sums(jnp.broadcast_to(kept, (8, 128)), j)
        act[:, lanes] = grad_xdt * step_wide + chan[0:1, lanes] * dy
        carry[:, lanes] = later[:, lanes] * spread_heads(keep, j, low_half)

    grad_cum = rows[...].T - col_sums + enter_part - to_end_part
    grad_last = jnp.sum(to_end_part, axis=0, keepdims=True) + keep * keep_part[0:1, :]
    upper = (row <= col).astype(F32)
    grad_log = jnp.dot(upper, grad_cum, precision=HIGH, preferred_element_type=F32) + grad_last
    grad_step = (step_part - rate * grad_log) * sigmoid(step_arg)
    heads_out[0:1, :] += jnp.sum(grad_step, axis=0, keepdims=True)
    heads_out[1:2, :] += -rate * jnp.sum(step * grad_log, axis=0, keepdims=True)
    heads_out[2:3, :] += jnp.sum(skip_part, axis=0, keepdims=True)
    low_out[:, wide:] = grad_step.astype(BF16)

    grad_inner = jnp.where(allowed, grad_inner, 0.0)
    act[:, pairs * 128 : (pairs + 1) * 128] = dot(grad_inner.astype(BF16), read_low) + dot_nt(fed[...], later_low)
    act[:, (pairs + 1) * 128 : (pairs + 2) * 128] = dot(grad_inner.T.astype(BF16), write_low) + dot_nt(back[...], held)
    carry[...] += dot(read_t, back[...])

    for j in range(wide // 128):
        lanes = slice(j * 128, (j + 1) * 128)
        grad_pre = act[:, lanes] * slope[:, lanes]
        gext[0:n, lanes] = grad_pre
        total = taps[3:4, lanes] * grad_pre
        taps_out[3:4, lanes] += jnp.sum(grad_pre * ext[8 : 8 + n, lanes], axis=0, keepdims=True)
        taps_out[4:5, lanes] += jnp.sum(grad_pre, axis=0, keepdims=True)
        for by in (1, 2, 3):
            total += taps[3 - by : 4 - by, lanes] * (marks[:, 4 + by : 5 + by] * gext[by : by + n, lanes])
            taps_out[3 - by : 4 - by, lanes] += jnp.sum(
                grad_pre * (marks[:, by - 1 : by] * ext[8 - by : 8 - by + n, lanes]), axis=0, keepdims=True
            )
        low_out[:, lanes] = total.astype(BF16)
    gext[n:, :] = gext[0:8, :]


def scan_marks(segments):
    length = segments.shape[0]
    blocks = segments.reshape(-1, BLOCK)
    before = jnp.concatenate([jnp.full((1,), -1, jnp.int32), blocks[:-1, -1]], 0)

    def same(by):
        if by > 0:
            other = jnp.concatenate([jnp.full((by,), -1, jnp.int32), segments[:-by]], 0)
        else:
            other = jnp.concatenate([segments[-by:], jnp.full((-by,), -1, jnp.int32)], 0)
        return other == segments

    cols = [same(1), same(2), same(3), (blocks == before[:, None]).reshape(-1), (blocks == blocks[:, -1:]).reshape(-1)]
    cols += [same(-1), same(-2), same(-3), segments]
    marks = jnp.stack([c.astype(F32) for c in cols], 1)
    return jnp.pad(marks, ((0, 0), (0, 128 - len(cols)))), jnp.broadcast_to(segments.astype(F32), (8, length))


def scan_forward(tokens, weights, taps, heads, chan, marks, segrow):
    length, model = tokens.shape
    cols = weights.shape[1]
    inner = cols - 384
    wide = cols - 128
    n = BLOCK
    blocks = length // n


    return pl.pallas_call(
        scan_forward_kernel,
        grid=(blocks,),
        in_specs=[
            pl.BlockSpec((n, model), lambda i: (i, 0)),
            whole(weights.shape),
            whole((8, wide)),
            whole((8, 128)),
            whole((8, inner)),
            pl.BlockSpec((n, 128), lambda i: (i, 0)),
            pl.BlockSpec((8, n), lambda i: (0, i)),
        ],
        out_specs=[
            pl.BlockSpec((n, cols), lambda i: (i, 0)),
            pl.BlockSpec((n, inner), lambda i: (i, 0)),
            pl.BlockSpec((1, 128, inner), lambda i: (i, 0, 0)),
        ],
        out_shape=[
            jax.ShapeDtypeStruct((length, cols), F32),
            jax.ShapeDtypeStruct((length, inner), F32),
            jax.ShapeDtypeStruct((blocks, 128, inner), BF16),
        ],
        scratch_shapes=[
            pltpu.VMEM((n + 8, wide), F32),
            pltpu.VMEM((n, wide), F32),
            pltpu.VMEM((128, inner), F32),
            pltpu.VMEM((n, inner), BF16),
        ],
        compiler_params=PARAMS,
        cost_estimate=cost(20),
        name="scan_forward",
    )(tokens, weights, taps, heads, chan, marks, segrow)


def scan_backward(pre, taps, heads, chan, sums, marks, segrow, grad, states):
    length, cols = pre.shape
    inner = cols - 384
    wide = cols - 128
    n = BLOCK
    blocks = length // n


    def rev(i):
        return blocks - 1 - i

    return pl.pallas_call(
        scan_backward_kernel,
        grid=(blocks,),
        in_specs=[
            pl.BlockSpec((n, cols), lambda i: (rev(i), 0)),
            pl.BlockSpec((8, cols), lambda i: (jnp.maximum(rev(i) * (n // 8) - 1, 0), 0)),
            whole((8, wide)),
            whole((8, 128)),
            whole((8, inner)),
            whole((inner // 128, 256, 128)),
            pl.BlockSpec((n, 128), lambda i: (rev(i), 0)),
            pl.BlockSpec((8, n), lambda i: (0, rev(i))),
            pl.BlockSpec((n, inner), lambda i: (rev(i), 0)),
            pl.BlockSpec((1, 128, inner), lambda i: (rev(i), 0, 0)),
        ],
        out_specs=[
            pl.BlockSpec((n, cols), lambda i: (rev(i), 0)),
            whole((8, wide)),
            whole((8, 128)),
        ],
        out_shape=[
            jax.ShapeDtypeStruct((length, cols), BF16),
            jax.ShapeDtypeStruct((8, wide), F32),
            jax.ShapeDtypeStruct((8, 128), F32),
        ],
        scratch_shapes=[
            pltpu.VMEM((n + 8, wide), F32),
            pltpu.VMEM((n + 8, wide), F32),
            pltpu.VMEM((n, wide), F32),
            pltpu.VMEM((n, wide), F32),
            pltpu.VMEM((128, inner), F32),
            pltpu.VMEM((n, inner), BF16),
            pltpu.VMEM((n, inner), BF16),
            pltpu.VMEM((128, n), F32),
        ],
        compiler_params=PARAMS,
        cost_estimate=cost(30),
        name="scan_backward",
    )(pre, pre, taps, heads, chan, sums, marks, segrow, grad, states)


def head_sum_table(inner):
    pairs = inner // 128
    lane = jnp.arange(256) % 128
    head = 2 * jnp.arange(pairs)[:, None] + (lane >= 64)[None, :]
    return (head[:, :, None] == jnp.arange(128)[None, None, :]).astype(BF16)


def mix_first_kernel(tok, rows, gate_w, out_w, scanned, gain, gate_out, mixed_out, sums_out):
    gate_pre = dot(tok[...], gate_w[...])
    grad_mixed = dot(rows[...], out_w[...])
    gate_out[...] = gate_pre
    mixed_out[...] = grad_mixed
    gated = scanned[...] * (gate_pre * sigmoid(gate_pre))
    square = jnp.sum(gated * gated, axis=1, keepdims=True)
    inner = jnp.sum(grad_mixed * gain[0:1, :] * gated, axis=1, keepdims=True)
    lane = lax.broadcasted_iota(jnp.int32, (1, 128), 1)
    cols = jnp.where(lane == 0, square, jnp.where(lane == 1, inner, 0.0))
    sums_out[...] = cols.T[0:8, :]


def mix_first(tokens, grad_rows, second, scanned, gain):
    length, model = tokens.shape
    width = scanned.shape[1]
    n = 256

    def rows(cols):
        return pl.BlockSpec((n, cols), lambda i: (i, 0))

    return pl.pallas_call(
        mix_first_kernel,
        grid=(length // n,),
        in_specs=[
            rows(model),
            rows(model),
            pl.BlockSpec((model, width), lambda i: (0, 0)),
            pl.BlockSpec((model, width), lambda i: (0, 1)),
            rows(width),
            whole((8, width)),
        ],
        out_specs=[rows(width), rows(width), pl.BlockSpec((8, n), lambda i: (0, i))],
        out_shape=[
            jax.ShapeDtypeStruct((length, width), F32),
            jax.ShapeDtypeStruct((length, width), F32),
            jax.ShapeDtypeStruct((8, length), F32),
        ],
        compiler_params=PARAMS,
        cost_estimate=cost(10),
        name="mix_first",
    )(tokens, grad_rows, second, second, scanned, gain)


def block_of(i, me):
    return jnp.where(i < 2, 2 * i + 1 - me[0], 2 * (i - 2) + me[0])


def give_spec(n, model):
    return pl.BlockSpec((1, n, model), lambda i, me: (jnp.minimum(i, 1), 0, 0))


def keep_spec(n, model):
    return pl.BlockSpec((1, n, model), lambda i, me: (jnp.maximum(i - 2, 0), 0, 0))


def store_block(value, give, keep):
    @pl.when(pl.program_id(0) < 2)
    def _():
        give[0] = value

    @pl.when(pl.program_id(0) >= 2)
    def _():
        keep[0] = value


def mix_second_kernel(channels, me, sums, gate, grad_mixed_in, scanned_in, out_w, gain, low_out, give, keep, grad_scan, grad_gate, gain_out):
    n = gate.shape[0]

    @pl.when(pl.program_id(0) == 0)
    def _():
        gain_out[...] = jnp.zeros_like(gain_out)

    cols = jnp.concatenate([sums[...], jnp.zeros((120, n), F32)], 0).T
    scale = lax.rsqrt(cols[:, 0:1] / channels + EPS)
    pull = scale * scale * scale * (cols[:, 1:2] / channels)
    gate_pre = gate[...]
    grad_mixed = grad_mixed_in[...]
    scanned = scanned_in[...]
    sig = sigmoid(gate_pre)
    silu = gate_pre * sig
    gated = scanned * silu
    scaled = gated * scale
    mixed = (scaled * gain[0:1, :]).astype(BF16)
    low_out[...] = mixed
    gain_out[0:1, :] += jnp.sum(grad_mixed * scaled, axis=0, keepdims=True)
    grad_gated = scale * gain[0:1, :] * grad_mixed - gated * pull
    grad_scan[...] = grad_gated * silu
    grad_gate[...] = (grad_gated * scanned * (sig + silu * (1.0 - sig))).astype(BF16)
    store_block(dot_nt(mixed, out_w[...]).astype(BF16), give, keep)


def mix_second(sums, gate, grad_mixed, scanned, second, gain, channels, core):
    length, width = gate.shape
    model = second.shape[0]
    n = 256

    def rows(cols):
        return pl.BlockSpec((n, cols), lambda i, me: (block_of(i, me), 0))

    return pl.pallas_call(
        lambda *refs: mix_second_kernel(channels, *refs),
        grid_spec=pltpu.PrefetchScalarGridSpec(
            num_scalar_prefetch=1,
            grid=(4,),
            in_specs=[
                pl.BlockSpec((8, n), lambda i, me: (0, block_of(i, me))),
                rows(width),
                rows(width),
                rows(width),
                pl.BlockSpec((model, width), lambda i, me: (0, 1)),
                whole((8, width)),
            ],
            out_specs=[
                rows(width),
                give_spec(n, model),
                keep_spec(n, model),
                rows(width),
                rows(width),
                whole((8, width)),
            ],
        ),
        out_shape=[
            jax.ShapeDtypeStruct((length, width), BF16),
            jax.ShapeDtypeStruct((2, n, model), BF16),
            jax.ShapeDtypeStruct((2, n, model), BF16),
            jax.ShapeDtypeStruct((length, width), F32),
            jax.ShapeDtypeStruct((length, width), BF16),
            jax.ShapeDtypeStruct((8, width), F32),
        ],
        compiler_params=PARAMS,
        cost_estimate=cost(11),
        name="mix_second",
    )(core, sums, gate, grad_mixed, scanned, second, gain)


def token_grads_kernel(me, tok, grad_gate, low, gate_w, weights, norm_gain, taps, heads, gain, give, keep, packed, total_sums):
    step = pl.program_id(0)

    @pl.when(step == 0)
    def _():
        total_sums[...] = jnp.zeros_like(total_sums)

    total = dot_nt(grad_gate[...], gate_w[...]) + dot_nt(low[...], weights[...])
    store_block(total.astype(BF16), give, keep)
    total_sums[0:1, :] += jnp.sum(total * tok[...].astype(F32), axis=0, keepdims=True)

    @pl.when(step == 3)
    def _():
        width = gain.shape[1]
        by_gain = total_sums[0:1, :] / norm_gain[0:1, :]
        packed[0:5, :] = taps[0:5, :]
        packed[5:6, :width] = gain[0:1, :]
        packed[5:6, width:] = jnp.zeros((1, 1024 - width), F32)
        packed[6:7, :] = by_gain[:, :1024]
        packed[7:8, :512] = by_gain[:, 1024:]
        for r in range(3):
            packed[7:8, 512 + 128 * r : 640 + 128 * r] = heads[r : r + 1, :]
        packed[7:8, 896:] = jnp.zeros((1, 128), F32)


def token_grads(tokens, grad_gate, low, second, weights, norm_gain, taps, heads, gain, core):
    length, model = tokens.shape
    width = gain.shape[1]
    n = 256

    def rows(cols):
        return pl.BlockSpec((n, cols), lambda i, me: (block_of(i, me), 0))

    return pl.pallas_call(
        token_grads_kernel,
        grid_spec=pltpu.PrefetchScalarGridSpec(
            num_scalar_prefetch=1,
            grid=(4,),
            in_specs=[
                rows(model),
                rows(grad_gate.shape[1]),
                rows(low.shape[1]),
                pl.BlockSpec((model, width), lambda i, me: (0, 0)),
                whole(weights.shape),
                whole((8, model)),
                whole(taps.shape),
                whole(heads.shape),
                whole(gain.shape),
            ],
            out_specs=[give_spec(n, model), keep_spec(n, model), whole((8, 1024))],
            scratch_shapes=[pltpu.VMEM((8, model), F32)],
        ),
        out_shape=[
            jax.ShapeDtypeStruct((2, n, model), BF16),
            jax.ShapeDtypeStruct((2, n, model), BF16),
            jax.ShapeDtypeStruct((8, 1024), F32),
        ],
        compiler_params=PARAMS,
        cost_estimate=cost(12),
        name="token_grads",
    )(core, tokens, grad_gate, low, second, weights, norm_gain, taps, heads, gain)


def second_grads_kernel(tok, rows, grad_gate, mixed, out):
    width = grad_gate.shape[1]
    gate_part = lax.dot_general(tok[...], grad_gate[...], TN, preferred_element_type=F32)
    out_part = lax.dot_general(rows[...], mixed[...], TN, preferred_element_type=F32)
    out[:, :width] = gate_part.astype(BF16)
    out[:, width:] = out_part.astype(BF16)


def second_grads(tokens, grad_rows, grad_gate, mixed):
    length, model = tokens.shape
    width = grad_gate.shape[1]
    n = model // 4
    cols = pl.BlockSpec((length, n), lambda i: (0, i))
    return pl.pallas_call(
        second_grads_kernel,
        grid=(4,),
        in_specs=[cols, cols, whole((length, width)), whole((length, width))],
        out_specs=pl.BlockSpec((n, 2 * width), lambda i: (i, 0)),
        out_shape=jax.ShapeDtypeStruct((model, 2 * width), BF16),
        compiler_params=PARAMS,
        cost_estimate=cost(8),
        name="second_grads",
    )(tokens, grad_rows, grad_gate, mixed)


def first_grads_kernel(me, tok, low, *outs):
    y = pl.program_id(0)
    grad = lax.dot_general(tok[...], low[...], TN, preferred_element_type=F32).astype(BF16)
    for x in range(4):
        for k in range(4):

            @pl.when((x - me[0] + 4) % 4 == k)
            def _():
                outs[k][y] = grad[96 * x : 96 * (x + 1), :]


def first_grads(tokens, low, me):
    length, model = tokens.shape
    width = low.shape[1]
    n = model // 4
    shape = (4, n // 4, width)
    return pl.pallas_call(
        first_grads_kernel,
        grid_spec=pltpu.PrefetchScalarGridSpec(
            num_scalar_prefetch=1,
            grid=(4,),
            in_specs=[pl.BlockSpec((length, n), lambda i, me: (0, i)), whole((length, width))],
            out_specs=[whole(shape)] * 4,
        ),
        out_shape=[jax.ShapeDtypeStruct(shape, BF16)] * 4,
        compiler_params=PARAMS,
        cost_estimate=cost(6),
        name="first_grads",
    )(me, tokens, low)


def add_split_kernel(me, own, ahead, across, behind, *outs):
    for d in range(4):
        e = (me[0] + d) % 4
        total = (own[e].astype(F32) + across[e].astype(F32)) + (ahead[e].astype(F32) + behind[e].astype(F32))
        outs[d][...] = total.astype(BF16)


def add_split(parts, me):
    shape = parts[0].shape[1:]
    return pl.pallas_call(
        add_split_kernel,
        in_specs=[pl.BlockSpec(memory_space=pltpu.SMEM)] + [VMEM_SPEC] * 4,
        out_specs=[VMEM_SPEC] * 4,
        out_shape=[jax.ShapeDtypeStruct(shape, BF16)] * 4,
        compiler_params=PARAMS,
        name="add_split",
    )(me, *parts)


def add_halve_kernel(me, own, ahead, across, behind, keep, give, total):
    total[...] = (own[...].astype(F32) + across[...].astype(F32)) + (ahead[...].astype(F32) + behind[...].astype(F32))
    n = keep.shape[0]
    keep[...] = total[pl.ds(pl.multiple_of(me[0] * n, 16), n), :]
    give[...] = total[pl.ds(pl.multiple_of((1 - me[0]) * n, 16), n), :].astype(BF16)


def add_halve(parts, me):
    rows, width = parts[0].shape
    return pl.pallas_call(
        add_halve_kernel,
        in_specs=[pl.BlockSpec(memory_space=pltpu.SMEM)] + [VMEM_SPEC] * 4,
        out_specs=[VMEM_SPEC] * 2,
        out_shape=[
            jax.ShapeDtypeStruct((rows // 2, width), F32),
            jax.ShapeDtypeStruct((rows // 2, width), BF16),
        ],
        scratch_shapes=[pltpu.VMEM((rows, width), F32)],
        compiler_params=PARAMS,
        name="add_halve",
    )(me, *parts)


def place_kernel(me, *refs):
    out = refs[-1]
    for k, part in enumerate(refs[:-1]):

        @pl.when(pl.program_id(0) == k)
        def _():
            out[...] = part[...].reshape(out.shape)


def place(parts, index, me, shape, block, name):
    return pl.pallas_call(
        place_kernel,
        grid_spec=pltpu.PrefetchScalarGridSpec(
            num_scalar_prefetch=1,
            grid=(len(parts),),
            in_specs=[whole(p.shape) for p in parts],
            out_specs=pl.BlockSpec(block, lambda i, me: index(i, me[0])),
        ),
        out_shape=jax.ShapeDtypeStruct(shape, parts[0].dtype),
        compiler_params=PARAMS,
        cost_estimate=cost(2),
        name=name,
    )(me, *parts)


def place_halves_kernel(me, own, right, left, low, high, out):
    step = pl.program_id(0)
    for k, part in enumerate((own, right, left)):
        for half in range(2):

            @pl.when(step == 2 * k + half)
            def _():
                out[...] = part[2 * half : 2 * half + 2].reshape(out.shape)

    @pl.when(step == 6)
    def _():
        out[...] = low[...].reshape(out.shape)

    @pl.when(step == 7)
    def _():
        out[...] = high[...].reshape(out.shape)


def place_halves(parts, me, position):
    deep, width = parts[0].shape[1:]

    def index(i, me):
        by = jnp.where(i < 2, 0, jnp.where(i < 4, 1, jnp.where(i < 6, 3, 2)))
        ring = (me[0] + by) % 4
        return (ring, i % 2, 0, 0) if position == 0 else (i % 2, ring, 0, 0)

    return pl.pallas_call(
        place_halves_kernel,
        grid_spec=pltpu.PrefetchScalarGridSpec(
            num_scalar_prefetch=1,
            grid=(8,),
            in_specs=[whole(p.shape) for p in parts],
            out_specs=pl.BlockSpec((1, 2, deep, width) if position == 0 else (2, 1, deep, width), index),
        ),
        out_shape=jax.ShapeDtypeStruct((4, 4, deep, width), BF16),
        compiler_params=PARAMS,
        cost_estimate=cost(3),
        name="place_halves",
    )(me, *parts)


def shift(value, axis, by):
    n = SIZES[axis]
    return lax.ppermute(value, axis, [(i, (i - by) % n) for i in range(n)])


def swap(value, axis):
    return shift(value, axis, 1)


def ring(value, axis):
    return [value, shift(value, axis, 1), shift(value, axis, 2), shift(value, axis, -1)]


def sends(blocks, axis):
    return [blocks[0], shift(blocks[1], axis, -1), shift(blocks[2], axis, 2), shift(blocks[3], axis, 1)]


def tensor_xor(value, by):
    return lax.ppermute(value, TENSOR, [(i, i ^ by) for i in range(4)])


def sum_ring(value, axis):
    own, ahead, across, behind = ring(value, axis)
    return (own + across) + (ahead + behind)


def sum_pair(value, axis):
    return value + swap(value, axis)


def after(value, *others):
    return lax.optimization_barrier((value,) + others)[0]


def index_of(axis):
    return lax.axis_index(axis).reshape(1).astype(jnp.int32)


def pair_rows(value):
    rows, width = value.shape
    parts = [value, swap(value, "zl")]
    return place(parts, lambda i, me: ((me + i) % 2, 0), index_of("zl"), (2 * rows, width), (rows, width), "place_zl")


def ring_rows(value, axis):
    rows, width = value.shape
    return place(
        ring(value, axis), lambda i, me: ((me + i) % 4, 0, 0), index_of(axis), (4, rows, width), (1, rows, width), "place_" + axis
    )


def token_place(own, near, far, both, me):
    rows, width = own.shape
    return place([own, near, far, both], lambda i, me: (me ^ i, 0), me, (4 * rows, width), (rows, width), "place_tokens")


def per_device(
    hidden_in,
    norm_gain,
    proj_zx,
    proj_shared,
    proj_step,
    conv_inner,
    conv_shared,
    step_bias,
    decay_log,
    skip_gain,
    gated_gain,
    proj_out,
    out_grad,
    segments,
):
    model_width = hidden_in.shape[1]
    width = proj_zx.shape[2]
    heads = step_bias.shape[0]
    me = {axis: index_of(axis) for axis in DP + TENSOR}
    spot = 2 * me["zh"] + me["c"]

    shared_parts = [proj_shared] + [tensor_xor(proj_shared, by) for by in (1, 2, 3)]
    shared_rows = jnp.zeros((48, 256), BF16)
    for by, part in enumerate(shared_parts):
        shared_rows = lax.dynamic_update_slice(shared_rows, part, (((spot[0] ^ by) * 12), jnp.int32(0)))
    first_rows = jnp.concatenate(
        [proj_zx[:, 1, :], shared_rows, jnp.pad(proj_step, ((0, 0), (0, 128 - heads)))], 1
    )
    second_rows = jnp.concatenate([proj_zx[:, 0, :], proj_out.T], 1)
    second_pair = pair_rows(second_rows)
    first_pair = pair_rows(first_rows)

    residual_in = hidden_in.astype(F32)
    scale_in = lax.rsqrt(jnp.mean(residual_in * residual_in, axis=-1, keepdims=True) + EPS)
    normed_low = (residual_in * scale_in * norm_gain).astype(BF16)
    normed_far = swap(normed_low, "zh")
    normed_near = swap(normed_low, "c")

    first_x = ring_rows(first_pair, "x")
    second_y = ring_rows(after(second_pair, first_x), "y")
    first_right, first_left = shift(first_x, "y", 1), shift(first_x, "y", -1)
    second_right, second_left = shift(second_y, "x", 1), shift(second_y, "x", -1)
    normed_both = swap(normed_far, "c")
    tokens = token_place(normed_low, normed_near, normed_far, normed_both, spot)
    grad_far = swap(after(out_grad, normed_far), "zh")
    grad_near = swap(after(out_grad, normed_far), "c")
    first_low = shift(first_left[0:2], "y", -1)
    first_high = shift(first_right[2:4], "y", 1)
    first_full = place_halves([first_x, first_right, first_left, first_low, first_high], me["y"], 0)
    first_full = first_full.reshape(model_width, -1)
    second_low = shift(second_left[0:2], "x", -1)
    second_high = shift(second_right[2:4], "x", 1)
    grad_both = swap(grad_far, "c")

    pad = (0, 128 - heads)
    head_rows = jnp.stack([jnp.pad(step_bias, pad), jnp.pad(jnp.exp(decay_log), pad)], 0)
    head_rows = jnp.pad(head_rows, ((0, 6), (0, 0)))
    taps = jnp.pad(jnp.concatenate([conv_inner, conv_shared], 1), ((0, 3), (0, 0)))
    chan = jnp.broadcast_to(jnp.repeat(skip_gain, width // heads), (8, width))
    gain = jnp.broadcast_to(gated_gain, (8, width))
    norm_rows = jnp.broadcast_to(norm_gain, (8, model_width))
    marks, segrow = scan_marks(segments)
    tokens_now = after(tokens, first_full, second_left, second_right)
    pre, scanned, states = scan_forward(tokens_now, first_full, taps, head_rows, chan, marks, segrow)
    second_full = place_halves([second_y, second_right, second_left, second_low, second_high], me["x"], 1)
    second_full = second_full.reshape(model_width, -1)
    grad_rows = token_place(out_grad, grad_near, grad_far, grad_both, spot)

    gate_pre, grad_mixed, sums = mix_first(tokens, grad_rows, second_full, scanned, gain)
    sums = (sums + tensor_xor(sums, 1)) + (tensor_xor(sums, 2) + tensor_xor(sums, 3))
    mixed_low, out_give, out_keep, grad_scanned, gate_grad_low, gain_sums = mix_second(
        sums, gate_pre, grad_mixed, scanned, second_full, gain, 4 * width, me["c"]
    )
    out_got = swap(out_give, "c")

    def entry(value, index):
        return lax.dynamic_index_in_dim(value, index[0], 0, keepdims=False).astype(F32)

    out_far = (entry(out_keep, 1 - me["zh"]) + entry(out_got, 1 - me["zh"])).astype(BF16)
    second_total = second_grads(tokens, grad_rows, gate_grad_low, mixed_low)
    second_sum = lax.psum_scatter(second_total, ("y", "x"), scatter_dimension=0, tiled=True)
    out_far_got = swap(out_far, "zh")

    sum_table = head_sum_table(width)
    grad_scanned = after(grad_scanned, out_far, second_total)
    low, tap_sums, head_sums = scan_backward(
        pre, taps, head_rows, chan, sum_table, marks, segrow, grad_scanned, states
    )
    low = after(low, out_far_got)
    first_blocks = first_grads(tokens, low, me["x"])
    first_parts = sends(first_blocks, "x")
    low_late = after(low, *first_blocks)
    row_give, row_keep, small = token_grads(
        tokens, gate_grad_low, low_late, second_full, first_full, norm_rows, tap_sums, head_sums, gain_sums, me["c"]
    )
    row_got = swap(row_give, "c")
    row_far = (entry(row_keep, 1 - me["zh"]) + entry(row_got, 1 - me["zh"])).astype(BF16)
    row_far_got = swap(row_far, "zh")

    small = sum_ring(after(small, row_far), "y")
    small = sum_ring(small, "x")
    first_parts = [after(part, row_far) for part in first_parts]
    first_parts = sends(add_split(first_parts, me["y"]), "y")
    small = sum_pair(small, "zl")
    first_keep, first_give = add_halve(first_parts, me["zl"])
    first_give = after(first_give, row_far_got)
    first_mine = first_keep + swap(first_give, "zl").astype(F32)
    second_pairs = second_sum.reshape(2, 48, 2 * width)
    second_mine = entry(second_pairs, me["zl"]) + swap(
        lax.dynamic_index_in_dim(second_pairs, 1 - me["zl"][0], 0, keepdims=False), "zl"
    ).astype(F32)

    hidden_out = (
        residual_in + (entry(out_keep, me["zh"]) + entry(out_got, me["zh"]) + out_far_got.astype(F32))
    ).astype(BF16)
    grad_normed = entry(row_keep, me["zh"]) + entry(row_got, me["zh"]) + row_far_got.astype(F32)
    weighted = jnp.sum(grad_normed * norm_gain * residual_in, axis=-1, keepdims=True)
    grad_hidden = (
        out_grad.astype(F32)
        + scale_in * norm_gain * grad_normed
        - residual_in * scale_in**3 * weighted / model_width
    ).astype(BF16)
    grad_proj_out = second_mine[:, width:].T
    grad_proj_zx = jnp.stack([second_mine[:, :width], first_mine[:, :width]], 1)
    grad_proj_step = first_mine[:, width + 256 : width + 256 + heads]

    def quarter(by):
        return lax.dynamic_slice(first_mine, ((spot[0] ^ by) * 12, jnp.int32(width)), (12, 256))

    grad_proj_shared = (quarter(0) + tensor_xor(quarter(1), 1)) + (
        tensor_xor(quarter(2), 2) + tensor_xor(quarter(3), 3)
    )

    summed = (small + tensor_xor(small, 1)) + (tensor_xor(small, 2) + tensor_xor(small, 3))
    grad_norm_gain = jnp.concatenate([summed[6], summed[7, :512]])
    return (
        hidden_out,
        grad_hidden,
        grad_norm_gain,
        grad_proj_zx,
        grad_proj_shared,
        grad_proj_step,
        small[:5, :width],
        summed[:5, width:],
        small[7, 512 : 512 + heads],
        small[7, 640 : 640 + heads],
        small[7, 768 : 768 + heads],
        small[5, :width],
        grad_proj_out,
    )


def solution(mesh):
    fine = Mesh(mesh.devices.reshape(4, 4, 2, 2, 2), DP + TENSOR)
    both = DP + TENSOR
    return jax.shard_map(
        per_device,
        mesh=fine,
        in_specs=(
            P(both, None),
            P(),
            P(DP, None, TENSOR),
            P(both, None),
            P(DP, TENSOR),
            P(None, TENSOR),
            P(),
            P(TENSOR),
            P(TENSOR),
            P(TENSOR),
            P(TENSOR),
            P(TENSOR, DP),
            P(both, None),
            P(DP),
        ),
        out_specs=(
            P(both, None),
            P(both, None),
            P(),
            P(DP, None, TENSOR),
            P(both, None),
            P(DP, TENSOR),
            P(None, TENSOR),
            P(),
            P(TENSOR),
            P(TENSOR),
            P(TENSOR),
            P(TENSOR),
            P(TENSOR, DP),
        ),
        check_vma=False,
    )
```

```python
import jax
import jax.numpy as jnp
from jax import lax
from jax.experimental import pallas as pl
from jax.experimental.pallas import tpu as pltpu
from jax.sharding import Mesh
from jax.sharding import PartitionSpec as P

EPS = 1e-05
DP = ("y", "x", "zl")
TENSOR = ("zh", "c")
SIZES = {"y": 4, "x": 4, "zl": 2, "zh": 2, "c": 2}

F32 = jnp.float32
BF16 = jnp.bfloat16
HIGH = lax.Precision.HIGHEST
BLOCK = 128
VMEM = 56 * 1024 * 1024
PARAMS = pltpu.CompilerParams(vmem_limit_bytes=VMEM)
NT = (((1,), (1,)), ((), ()))
TN = (((0,), (0,)), ((), ()))
VMEM_SPEC = pl.BlockSpec(memory_space=pltpu.VMEM)


def cost(us):
    return pl.CostEstimate(flops=int(us * 1e6), transcendentals=0, bytes_accessed=int(us * 3e3))


def whole(shape):
    return pl.BlockSpec(shape, lambda *i: (0,) * len(shape))


def column_block(rows, width, index):
    return pl.BlockSpec((rows, width), lambda *i: (0, index))


def first_specs(rows):
    return [column_block(rows, 384, index) for index in (4, 5, 6)]


def dot(a, b):
    return jnp.dot(a, b, preferred_element_type=F32)


def dot_nt(a, b):
    return lax.dot_general(a, b, NT, preferred_element_type=F32)


def sigmoid(a):
    return 0.5 * jnp.tanh(0.5 * a) + 0.5


def softplus(a):
    return jnp.maximum(a, 0.0) + jnp.log1p(jnp.exp(-jnp.abs(a)))


def conv_strip(ext, taps, aux, j):
    n = ext.shape[0] - 8
    lanes = slice(j * 128, (j + 1) * 128)
    total = taps[4:5, lanes] + taps[3:4, lanes] * ext[8 : 8 + n, lanes]
    for back in (1, 2, 3):
        total += taps[3 - back : 4 - back, lanes] * (
            aux[:, back - 1 : back] * ext[8 - back : 8 - back + n, lanes]
        )
    return total


def spread_heads(cols, j, low_half):
    return jnp.where(low_half, cols[:, 2 * j : 2 * j + 1], cols[:, 2 * j + 1 : 2 * j + 2])


def scan_forward_kernel(tok, weights_a, weights_b, weights_c, taps, heads, chan, aux, segrow, pre_out, scan_out, state_out, ext, act, carry, fed):
    n = tok.shape[0]
    pairs = carry.shape[1] // 128

    @pl.when(pl.program_id(0) == 0)
    def _():
        carry[...] = jnp.zeros_like(carry)
        ext[0:8, :] = jnp.zeros((8, ext.shape[1]), F32)

    pre = jnp.concatenate([dot(tok[...], w[...]) for w in (weights_a, weights_b, weights_c)], 1)
    pre_out[...] = pre
    wide = ext.shape[1]
    ext[8:, :] = pre[:, :wide]
    marks = aux[...]
    for j in range(wide // 128):
        total = conv_strip(ext, taps, marks, j)
        act[:, j * 128 : (j + 1) * 128] = total * sigmoid(total)
    ext[0:8, :] = ext[n : n + 8, :]

    step = softplus(pre[:, wide:] + heads[0:1, :])
    log_step = -step * heads[1:2, :]
    row = lax.broadcasted_iota(jnp.int32, (n, n), 0)
    col = lax.broadcasted_iota(jnp.int32, (n, n), 1)
    lower = (row >= col).astype(F32)
    cum = jnp.dot(lower, log_step, precision=HIGH, preferred_element_type=F32)
    cum_t = cum.T
    write = act[:, pairs * 128 : (pairs + 1) * 128]
    read = act[:, (pairs + 1) * 128 : (pairs + 2) * 128].astype(BF16)
    write_t = write.T.astype(BF16)
    allowed = (row >= col) & (marks[:, 8:9] == segrow[0:1, :])
    inner = jnp.where(allowed, dot(read, write_t), 0.0)
    last = cum[n - 1 : n, :]
    enters = jnp.exp(cum) * marks[:, 3:4]
    to_end = jnp.exp(last - cum) * marks[:, 4:5]
    keep = jnp.exp(last) * marks[n - 1 : n, 3:4]
    held = carry[...]
    held_low = held.astype(BF16)
    state_out[0] = held_low
    from_state = dot(read, held_low)
    low_half = lax.broadcasted_iota(jnp.int32, (1, 128), 1) < 64
    for j in range(pairs):
        lanes = slice(j * 128, (j + 1) * 128)
        x = act[:, lanes]
        xdt = x * spread_heads(step, j, low_half)
        parts = []
        for h in (2 * j, 2 * j + 1):
            decay = jnp.exp(jnp.minimum(cum[:, h : h + 1] - cum_t[h : h + 1, :], 0.0))
            parts.append((decay * inner).astype(BF16))
        xdt_low = xdt.astype(BF16)
        zero = jnp.zeros_like(xdt_low)
        pair = jnp.concatenate([jnp.where(low_half, xdt_low, zero), jnp.where(low_half, zero, xdt_low)], 0)
        y = dot(jnp.concatenate(parts, 1), pair)
        y += spread_heads(enters, j, low_half) * from_state[:, lanes] + chan[0:1, lanes] * x
        scan_out[:, lanes] = y
        fed[:, lanes] = (xdt * spread_heads(to_end, j, low_half)).astype(BF16)
        carry[:, lanes] = held[:, lanes] * spread_heads(keep, j, low_half)
    carry[...] += dot(write_t, fed[...])


def scan_backward_kernel(pre, pre_before, taps, heads, chan, sums, aux, segrow, grad, state, low_out, taps_out, heads_out, ext, gext, act, slope, carry, fed, back, rows):
    n = pre.shape[0]
    pairs = carry.shape[1] // 128
    wide = ext.shape[1]

    @pl.when(pl.program_id(0) == 0)
    def _():
        carry[...] = jnp.zeros_like(carry)
        gext[n:, :] = jnp.zeros((8, wide), F32)
        taps_out[...] = jnp.zeros_like(taps_out)
        heads_out[...] = jnp.zeros_like(heads_out)
        rows[...] = jnp.zeros_like(rows)

    marks = aux[...]
    ext[0:8, :] = pre_before[:, :wide]
    ext[8:, :] = pre[:, :wide]
    for j in range(wide // 128):
        lanes = slice(j * 128, (j + 1) * 128)
        total = conv_strip(ext, taps, marks, j)
        sig = sigmoid(total)
        value = total * sig
        act[:, lanes] = value
        slope[:, lanes] = sig + value * (1.0 - sig)

    step_arg = pre[:, wide:] + heads[0:1, :]
    step = softplus(step_arg)
    rate = heads[1:2, :]
    row = lax.broadcasted_iota(jnp.int32, (n, n), 0)
    col = lax.broadcasted_iota(jnp.int32, (n, n), 1)
    lower = (row >= col).astype(F32)
    cum = jnp.dot(lower, -step * rate, precision=HIGH, preferred_element_type=F32)
    cum_t = cum.T
    write = act[:, pairs * 128 : (pairs + 1) * 128]
    read = act[:, (pairs + 1) * 128 : (pairs + 2) * 128]
    read_t = read.T.astype(BF16)
    write_low = write.astype(BF16)
    read_low = read.astype(BF16)
    allowed = (row <= col) & (marks[:, 8:9] == segrow[0:1, :])
    inner_t = jnp.where(allowed, dot(write_low, read_t), 0.0)
    last = cum[n - 1 : n, :]
    enters = jnp.exp(cum) * marks[:, 3:4]
    to_end = jnp.exp(last - cum) * marks[:, 4:5]
    keep = jnp.exp(last) * marks[n - 1 : n, 3:4]
    held = state[0]
    later = carry[...]
    later_low = later.astype(BF16)
    from_state = dot(read_low, held)
    from_later = dot(write_low, later_low)
    low_half = lax.broadcasted_iota(jnp.int32, (1, 128), 1) < 64
    head_lane = lax.broadcasted_iota(jnp.int32, (1, 128), 1)
    grad_inner = jnp.zeros((n, n), F32)
    col_sums = jnp.zeros((n, 128), F32)
    to_end_part = jnp.zeros((n, 128), F32)
    enter_part = jnp.zeros((n, 128), F32)
    step_part = jnp.zeros((n, 128), F32)
    skip_part = jnp.zeros((n, 128), F32)
    keep_part = jnp.zeros((8, 128), F32)

    def head_sums(value, j):
        high = value.astype(BF16)
        rest = (value - high.astype(F32)).astype(BF16)
        return dot(jnp.concatenate([high, rest], 1), sums[j])

    for j in range(pairs):
        lanes = slice(j * 128, (j + 1) * 128)
        x = act[:, lanes]
        dy = grad[:, lanes].astype(F32)
        step_wide = spread_heads(step, j, low_half)
        xdt = x * step_wide
        xdt_low = xdt.astype(BF16)
        dy_low = dy.astype(BF16)
        zero = jnp.zeros_like(xdt_low)
        products = dot_nt(
            jnp.concatenate([jnp.where(low_half, xdt_low, zero), jnp.where(low_half, zero, xdt_low)], 0),
            dy_low,
        )
        parts = []
        for k, h in enumerate((2 * j, 2 * j + 1)):
            product = products[k * n : (k + 1) * n, :]
            decay = jnp.exp(jnp.minimum(cum_t[h : h + 1, :] - cum[:, h : h + 1], 0.0))
            scaled = decay * product
            grad_inner += scaled
            weighted = scaled * inner_t
            rows[h : h + 1, :] = jnp.sum(weighted, axis=0, keepdims=True)
            col_sums += jnp.where(head_lane == h, jnp.sum(weighted, axis=1, keepdims=True), 0.0)
            parts.append((decay * inner_t).astype(BF16))
        grad_pair = jnp.concatenate([jnp.where(low_half, dy_low, zero), jnp.where(low_half, zero, dy_low)], 0)
        grad_xdt = dot(jnp.concatenate(parts, 1), grad_pair)
        end_wide = spread_heads(to_end, j, low_half)
        enter_wide = spread_heads(enters, j, low_half)
        later_part = end_wide * from_later[:, lanes]
        grad_xdt += later_part
        to_end_part += head_sums(later_part * xdt, j)
        fed[:, lanes] = (xdt * end_wide).astype(BF16)
        grad_enter = dy * enter_wide
        back[:, lanes] = grad_enter.astype(BF16)
        enter_part += head_sums(grad_enter * from_state[:, lanes], j)
        step_part += head_sums(grad_xdt * x, j)
        skip_part += head_sums(dy * x, j)
        kept = jnp.sum(held[:, lanes].astype(F32) * later[:, lanes], axis=0, keepdims=True)
        keep_part += head_sums(jnp.broadcast_to(kept, (8, 128)), j)
        act[:, lanes] = grad_xdt * step_wide + chan[0:1, lanes] * dy
        carry[:, lanes] = later[:, lanes] * spread_heads(keep, j, low_half)

    grad_cum = rows[...].T - col_sums + enter_part - to_end_part
    grad_last = jnp.sum(to_end_part, axis=0, keepdims=True) + keep * keep_part[0:1, :]
    upper = (row <= col).astype(F32)
    grad_log = jnp.dot(upper, grad_cum, precision=HIGH, preferred_element_type=F32) + grad_last
    grad_step = (step_part - rate * grad_log) * sigmoid(step_arg)
    heads_out[0:1, :] += jnp.sum(grad_step, axis=0, keepdims=True)
    heads_out[1:2, :] += -rate * jnp.sum(step * grad_log, axis=0, keepdims=True)
    heads_out[2:3, :] += jnp.sum(skip_part, axis=0, keepdims=True)
    low_out[:, wide:] = grad_step.astype(BF16)

    grad_inner = jnp.where(allowed, grad_inner, 0.0)
    act[:, pairs * 128 : (pairs + 1) * 128] = dot(grad_inner.astype(BF16), read_low) + dot_nt(fed[...], later_low)
    act[:, (pairs + 1) * 128 : (pairs + 2) * 128] = dot(grad_inner.T.astype(BF16), write_low) + dot_nt(back[...], held)
    carry[...] += dot(read_t, back[...])

    for j in range(wide // 128):
        lanes = slice(j * 128, (j + 1) * 128)
        grad_pre = act[:, lanes] * slope[:, lanes]
        gext[0:n, lanes] = grad_pre
        total = taps[3:4, lanes] * grad_pre
        taps_out[3:4, lanes] += jnp.sum(grad_pre * ext[8 : 8 + n, lanes], axis=0, keepdims=True)
        taps_out[4:5, lanes] += jnp.sum(grad_pre, axis=0, keepdims=True)
        for by in (1, 2, 3):
            total += taps[3 - by : 4 - by, lanes] * (marks[:, 4 + by : 5 + by] * gext[by : by + n, lanes])
            taps_out[3 - by : 4 - by, lanes] += jnp.sum(
                grad_pre * (marks[:, by - 1 : by] * ext[8 - by : 8 - by + n, lanes]), axis=0, keepdims=True
            )
        low_out[:, lanes] = total.astype(BF16)
    gext[n:, :] = gext[0:8, :]


def scan_marks(segments):
    length = segments.shape[0]
    blocks = segments.reshape(-1, BLOCK)
    before = jnp.concatenate([jnp.full((1,), -1, jnp.int32), blocks[:-1, -1]], 0)

    def same(by):
        if by > 0:
            other = jnp.concatenate([jnp.full((by,), -1, jnp.int32), segments[:-by]], 0)
        else:
            other = jnp.concatenate([segments[-by:], jnp.full((-by,), -1, jnp.int32)], 0)
        return other == segments

    cols = [same(1), same(2), same(3), (blocks == before[:, None]).reshape(-1), (blocks == blocks[:, -1:]).reshape(-1)]
    cols += [same(-1), same(-2), same(-3), segments]
    marks = jnp.stack([c.astype(F32) for c in cols], 1)
    return jnp.pad(marks, ((0, 0), (0, 128 - len(cols)))), jnp.broadcast_to(segments.astype(F32), (8, length))


def scan_forward(tokens, weights, taps, heads, chan, marks, segrow):
    length, model = tokens.shape
    cols = 1152
    inner = cols - 384
    wide = cols - 128
    n = BLOCK
    blocks = length // n


    return pl.pallas_call(
        scan_forward_kernel,
        grid=(blocks,),
        in_specs=[
            pl.BlockSpec((n, model), lambda i: (i, 0)),
            *first_specs(model),
            whole((8, wide)),
            whole((8, 128)),
            whole((8, inner)),
            pl.BlockSpec((n, 128), lambda i: (i, 0)),
            pl.BlockSpec((8, n), lambda i: (0, i)),
        ],
        out_specs=[
            pl.BlockSpec((n, cols), lambda i: (i, 0)),
            pl.BlockSpec((n, inner), lambda i: (i, 0)),
            pl.BlockSpec((1, 128, inner), lambda i: (i, 0, 0)),
        ],
        out_shape=[
            jax.ShapeDtypeStruct((length, cols), F32),
            jax.ShapeDtypeStruct((length, inner), F32),
            jax.ShapeDtypeStruct((blocks, 128, inner), BF16),
        ],
        scratch_shapes=[
            pltpu.VMEM((n + 8, wide), F32),
            pltpu.VMEM((n, wide), F32),
            pltpu.VMEM((128, inner), F32),
            pltpu.VMEM((n, inner), BF16),
        ],
        compiler_params=PARAMS,
        cost_estimate=cost(20),
        name="scan_forward",
    )(tokens, weights, weights, weights, taps, heads, chan, marks, segrow)


def scan_backward(pre, taps, heads, chan, sums, marks, segrow, grad, states):
    length, cols = pre.shape
    inner = cols - 384
    wide = cols - 128
    n = BLOCK
    blocks = length // n


    def rev(i):
        return blocks - 1 - i

    return pl.pallas_call(
        scan_backward_kernel,
        grid=(blocks,),
        in_specs=[
            pl.BlockSpec((n, cols), lambda i: (rev(i), 0)),
            pl.BlockSpec((8, cols), lambda i: (jnp.maximum(rev(i) * (n // 8) - 1, 0), 0)),
            whole((8, wide)),
            whole((8, 128)),
            whole((8, inner)),
            whole((inner // 128, 256, 128)),
            pl.BlockSpec((n, 128), lambda i: (rev(i), 0)),
            pl.BlockSpec((8, n), lambda i: (0, rev(i))),
            pl.BlockSpec((n, inner), lambda i: (rev(i), 0)),
            pl.BlockSpec((1, 128, inner), lambda i: (rev(i), 0, 0)),
        ],
        out_specs=[
            pl.BlockSpec((n, cols), lambda i: (rev(i), 0)),
            whole((8, wide)),
            whole((8, 128)),
        ],
        out_shape=[
            jax.ShapeDtypeStruct((length, cols), BF16),
            jax.ShapeDtypeStruct((8, wide), F32),
            jax.ShapeDtypeStruct((8, 128), F32),
        ],
        scratch_shapes=[
            pltpu.VMEM((n + 8, wide), F32),
            pltpu.VMEM((n + 8, wide), F32),
            pltpu.VMEM((n, wide), F32),
            pltpu.VMEM((n, wide), F32),
            pltpu.VMEM((128, inner), F32),
            pltpu.VMEM((n, inner), BF16),
            pltpu.VMEM((n, inner), BF16),
            pltpu.VMEM((128, n), F32),
        ],
        compiler_params=PARAMS,
        cost_estimate=cost(30),
        name="scan_backward",
    )(pre, pre, taps, heads, chan, sums, marks, segrow, grad, states)


def head_sum_table(inner):
    pairs = inner // 128
    lane = jnp.arange(256) % 128
    head = 2 * jnp.arange(pairs)[:, None] + (lane >= 64)[None, :]
    return (head[:, :, None] == jnp.arange(128)[None, None, :]).astype(BF16)


def mix_first_kernel(tok, rows, gate_w, out_w, scanned, gain, gate_out, mixed_out, sums_out):
    gate_pre = dot(tok[...], gate_w[...])
    grad_mixed = dot(rows[...], out_w[...])
    gate_out[...] = gate_pre
    mixed_out[...] = grad_mixed
    gated = scanned[...] * (gate_pre * sigmoid(gate_pre))
    square = jnp.sum(gated * gated, axis=1, keepdims=True)
    inner = jnp.sum(grad_mixed * gain[0:1, :] * gated, axis=1, keepdims=True)
    lane = lax.broadcasted_iota(jnp.int32, (1, 128), 1)
    cols = jnp.where(lane == 0, square, jnp.where(lane == 1, inner, 0.0))
    sums_out[...] = cols.T[0:8, :]


def mix_first(tokens, grad_rows, second, scanned, gain):
    length, model = tokens.shape
    width = scanned.shape[1]
    n = 256

    def rows(cols):
        return pl.BlockSpec((n, cols), lambda i: (i, 0))

    return pl.pallas_call(
        mix_first_kernel,
        grid=(length // n,),
        in_specs=[
            rows(model),
            rows(model),
            pl.BlockSpec((model, width), lambda i: (0, 0)),
            pl.BlockSpec((model, width), lambda i: (0, 1)),
            rows(width),
            whole((8, width)),
        ],
        out_specs=[rows(width), rows(width), pl.BlockSpec((8, n), lambda i: (0, i))],
        out_shape=[
            jax.ShapeDtypeStruct((length, width), F32),
            jax.ShapeDtypeStruct((length, width), F32),
            jax.ShapeDtypeStruct((8, length), F32),
        ],
        compiler_params=PARAMS,
        cost_estimate=cost(10),
        name="mix_first",
    )(tokens, grad_rows, second, second, scanned, gain)


def store_block(value, outs):
    for k, out in enumerate(outs):

        @pl.when(pl.program_id(0) == k)
        def _():
            out[...] = value


def mix_second_kernel(channels, me, sums, gate, grad_mixed_in, scanned_in, out_w, gain, low_out, grad_scan, grad_gate, gain_out, *outs):
    n = gate.shape[0]

    @pl.when(pl.program_id(0) == 0)
    def _():
        gain_out[...] = jnp.zeros_like(gain_out)

    cols = jnp.concatenate([sums[...], jnp.zeros((120, n), F32)], 0).T
    scale = lax.rsqrt(cols[:, 0:1] / channels + EPS)
    pull = scale * scale * scale * (cols[:, 1:2] / channels)
    gate_pre = gate[...]
    grad_mixed = grad_mixed_in[...]
    scanned = scanned_in[...]
    sig = sigmoid(gate_pre)
    silu = gate_pre * sig
    gated = scanned * silu
    scaled = gated * scale
    mixed = (scaled * gain[0:1, :]).astype(BF16)
    low_out[...] = mixed
    gain_out[0:1, :] += jnp.sum(grad_mixed * scaled, axis=0, keepdims=True)
    grad_gated = scale * gain[0:1, :] * grad_mixed - gated * pull
    grad_scan[...] = grad_gated * silu
    grad_gate[...] = (grad_gated * scanned * (sig + silu * (1.0 - sig))).astype(BF16)
    store_block(dot_nt(mixed, out_w[...]).astype(BF16), outs)


def mix_second(sums, gate, grad_mixed, scanned, second, gain, channels, spot):
    length, width = gate.shape
    model = second.shape[0]
    n = 256

    def rows(cols):
        return pl.BlockSpec((n, cols), lambda i, me: (me[0] ^ (3 - i), 0))

    return pl.pallas_call(
        lambda *refs: mix_second_kernel(channels, *refs),
        grid_spec=pltpu.PrefetchScalarGridSpec(
            num_scalar_prefetch=1,
            grid=(4,),
            in_specs=[
                pl.BlockSpec((8, n), lambda i, me: (0, me[0] ^ (3 - i))),
                rows(width),
                rows(width),
                rows(width),
                pl.BlockSpec((model, width), lambda i, me: (0, 1)),
                whole((8, width)),
            ],
            out_specs=[rows(width), rows(width), rows(width), whole((8, width))] + [whole((n, model))] * 4,
        ),
        out_shape=[
            jax.ShapeDtypeStruct((length, width), BF16),
            jax.ShapeDtypeStruct((length, width), F32),
            jax.ShapeDtypeStruct((length, width), BF16),
            jax.ShapeDtypeStruct((8, width), F32),
        ]
        + [jax.ShapeDtypeStruct((n, model), BF16)] * 4,
        compiler_params=PARAMS,
        cost_estimate=cost(11),
        name="mix_second",
    )(spot, sums, gate, grad_mixed, scanned, second, gain)


def token_grads_kernel(me, grad_gate, low, gate_w, weights_a, weights_b, weights_c, *outs):
    total = dot_nt(grad_gate[...], gate_w[...])
    for n, w in enumerate((weights_a, weights_b, weights_c)):
        total += dot_nt(low[:, 384 * n : 384 * (n + 1)], w[...])
    store_block(total.astype(BF16), outs)


def token_grads(grad_gate, low, weights, spot, first):
    model = weights.shape[0]
    width = grad_gate.shape[1]
    n = 256

    def rows(cols):
        return pl.BlockSpec((n, cols), lambda i, me: (me[0] ^ (first - i), 0))

    return pl.pallas_call(
        token_grads_kernel,
        grid_spec=pltpu.PrefetchScalarGridSpec(
            num_scalar_prefetch=1,
            grid=(2,),
            in_specs=[rows(width), rows(low.shape[1]), column_block(model, width, 0), *first_specs(model)],
            out_specs=[whole((n, model))] * 2,
        ),
        out_shape=[jax.ShapeDtypeStruct((n, model), BF16)] * 2,
        compiler_params=PARAMS,
        cost_estimate=cost(6),
        name="token_grads",
    )(spot, grad_gate, low, weights, weights, weights, weights)


def row_sums(product):
    sums = jnp.sum(product, axis=1, keepdims=True)
    return jnp.broadcast_to(sums, (product.shape[0], 128)).T[0:1, :]


def second_grads_kernel(tok, rows, grad_gate, mixed, gate_w, out, gains):
    width = grad_gate.shape[1]
    gate_part = lax.dot_general(tok[...], grad_gate[...], TN, preferred_element_type=F32)
    out_part = lax.dot_general(rows[...], mixed[...], TN, preferred_element_type=F32)
    out[:, :width] = gate_part.astype(BF16)
    out[:, width:] = out_part.astype(BF16)
    gains[...] = jnp.broadcast_to(row_sums(gate_part * gate_w[...].astype(F32)), gains.shape)


def second_grads(tokens, grad_rows, grad_gate, mixed, weights):
    length, model = tokens.shape
    width = grad_gate.shape[1]
    n = model // 4
    cols = pl.BlockSpec((length, n), lambda i: (0, i))
    return pl.pallas_call(
        second_grads_kernel,
        grid=(4,),
        in_specs=[cols, cols, whole((length, width)), whole((length, width)), pl.BlockSpec((n, width), lambda i: (i, 0))],
        out_specs=[pl.BlockSpec((n, 2 * width), lambda i: (i, 0)), pl.BlockSpec((8, n), lambda i: (0, i))],
        out_shape=[jax.ShapeDtypeStruct((model, 2 * width), BF16), jax.ShapeDtypeStruct((8, model), F32)],
        compiler_params=PARAMS,
        cost_estimate=cost(8),
        name="second_grads",
    )(tokens, grad_rows, grad_gate, mixed, weights)


def first_grads_kernel(me, tok, low, weights_a, weights_b, weights_c, gate_gains, norm_gain, taps, heads, gain, *rest):
    *outs, packed, gains = rest
    step = pl.program_id(0)
    grad = lax.dot_general(tok[...], low[...], TN, preferred_element_type=F32)
    total = jnp.zeros((grad.shape[0], 128), F32)
    for n, w in enumerate((weights_a, weights_b, weights_c)):
        for m in range(3):
            product = grad[:, 384 * n + 128 * m : 384 * n + 128 * (m + 1)] * w[:, 128 * m : 128 * (m + 1)].astype(F32)
            total += product
    spot = pl.ds(pl.multiple_of(((me[0] + step) % 4) * grad.shape[0], 128), grad.shape[0])
    gains[0:1, spot] = row_sums(total)
    for k in range(4):

        @pl.when(step == k)
        def _():
            outs[k][...] = grad.astype(BF16).reshape(outs[k].shape)

    @pl.when(step == 3)
    def _():
        width = gain.shape[1]
        by_gain = (gains[0:1, :] + gate_gains[0:1, :]) / norm_gain[0:1, :]
        packed[0:5, :] = taps[0:5, :]
        packed[5:6, :width] = gain[0:1, :]
        packed[5:6, width:] = jnp.zeros((1, 1024 - width), F32)
        packed[6:7, :] = by_gain[:, :1024]
        packed[7:8, :512] = by_gain[:, 1024:]
        for r in range(3):
            packed[7:8, 512 + 128 * r : 640 + 128 * r] = heads[r : r + 1, :]
        packed[7:8, 896:] = jnp.zeros((1, 128), F32)


def first_grads(tokens, low, weights, gate_gains, norm_gain, taps, heads, gain, me):
    length, model = tokens.shape
    width = low.shape[1]
    n = model // 4
    shape = (4, n // 4, width)

    def spot(i, me):
        return (me[0] + i) % 4

    return pl.pallas_call(
        first_grads_kernel,
        grid_spec=pltpu.PrefetchScalarGridSpec(
            num_scalar_prefetch=1,
            grid=(4,),
            in_specs=[
                pl.BlockSpec((length, n), lambda i, me: (0, spot(i, me))),
                whole((length, width)),
                pl.BlockSpec((n, 384), lambda i, me: (spot(i, me), 4)),
                pl.BlockSpec((n, 384), lambda i, me: (spot(i, me), 5)),
                pl.BlockSpec((n, 384), lambda i, me: (spot(i, me), 6)),
                whole(gate_gains.shape),
                whole(norm_gain.shape),
                whole(taps.shape),
                whole(heads.shape),
                whole(gain.shape),
            ],
            out_specs=[whole(shape)] * 4 + [whole((8, 1024))],
            scratch_shapes=[pltpu.VMEM((8, model), F32)],
        ),
        out_shape=[jax.ShapeDtypeStruct(shape, BF16)] * 4 + [jax.ShapeDtypeStruct((8, 1024), F32)],
        compiler_params=PARAMS,
        cost_estimate=cost(6),
        name="first_grads",
    )(me, tokens, low, weights, weights, weights, gate_gains, norm_gain, taps, heads, gain)


def add_split_kernel(me, own, ahead, across, behind, *outs):
    for d in range(4):
        e = (me[0] + d) % 4
        total = (own[e].astype(F32) + across[e].astype(F32)) + (ahead[e].astype(F32) + behind[e].astype(F32))
        outs[d][...] = total.astype(BF16)


def add_split(parts, me):
    shape = parts[0].shape[1:]
    return pl.pallas_call(
        add_split_kernel,
        in_specs=[pl.BlockSpec(memory_space=pltpu.SMEM)] + [VMEM_SPEC] * 4,
        out_specs=[VMEM_SPEC] * 4,
        out_shape=[jax.ShapeDtypeStruct(shape, BF16)] * 4,
        compiler_params=PARAMS,
        name="add_split",
    )(me, *parts)


def add_halve_kernel(me, own, ahead, across, behind, keep, give, total):
    total[...] = (own[...].astype(F32) + across[...].astype(F32)) + (ahead[...].astype(F32) + behind[...].astype(F32))
    n = keep.shape[0]
    keep[...] = total[pl.ds(pl.multiple_of(me[0] * n, 16), n), :]
    give[...] = total[pl.ds(pl.multiple_of((1 - me[0]) * n, 16), n), :].astype(BF16)


def add_halve(parts, me):
    rows, width = parts[0].shape
    return pl.pallas_call(
        add_halve_kernel,
        in_specs=[pl.BlockSpec(memory_space=pltpu.SMEM)] + [VMEM_SPEC] * 4,
        out_specs=[VMEM_SPEC] * 2,
        out_shape=[
            jax.ShapeDtypeStruct((rows // 2, width), F32),
            jax.ShapeDtypeStruct((rows // 2, width), BF16),
        ],
        scratch_shapes=[pltpu.VMEM((rows, width), F32)],
        compiler_params=PARAMS,
        name="add_halve",
    )(me, *parts)


def place_kernel(me, *refs):
    out = refs[-1]
    for k, part in enumerate(refs[:-1]):

        @pl.when(pl.program_id(0) == k)
        def _():
            out[...] = part[...].reshape(out.shape)


def place(parts, index, me, shape, block, name):
    return pl.pallas_call(
        place_kernel,
        grid_spec=pltpu.PrefetchScalarGridSpec(
            num_scalar_prefetch=1,
            grid=(len(parts),),
            in_specs=[whole(p.shape) for p in parts],
            out_specs=pl.BlockSpec(block, lambda i, me: index(i, me[0])),
        ),
        out_shape=jax.ShapeDtypeStruct(shape, parts[0].dtype),
        compiler_params=PARAMS,
        cost_estimate=cost(2),
        name=name,
    )(me, *parts)


def shift(value, axis, by):
    n = SIZES[axis]
    return lax.ppermute(value, axis, [(i, (i - by) % n) for i in range(n)])


def swap(value, axis):
    return shift(value, axis, 1)


def ring(value, axis):
    return [value, shift(value, axis, 1), shift(value, axis, 2), shift(value, axis, -1)]


def sends(blocks, axis):
    return [blocks[0], shift(blocks[1], axis, -1), shift(blocks[2], axis, 2), shift(blocks[3], axis, 1)]


def tensor_xor(value, by):
    return lax.ppermute(value, TENSOR, [(i, i ^ by) for i in range(4)])


def sum_ring(value, axis):
    own, ahead, across, behind = ring(value, axis)
    return (own + across) + (ahead + behind)


def sum_pair(value, axis):
    return value + swap(value, axis)


def after(value, *others):
    return lax.optimization_barrier((value,) + others)[0]


def index_of(axis):
    return lax.axis_index(axis).reshape(1).astype(jnp.int32)


def pair_rows(value):
    rows, width = value.shape
    parts = [value, swap(value, "zl")]
    return place(parts, lambda i, me: ((me + i) % 2, 0), index_of("zl"), (2 * rows, width), (rows, width), "place_zl")


def token_place(own, near, far, both, me):
    rows, width = own.shape
    return place([own, near, far, both], lambda i, me: (me ^ i, 0), me, (4 * rows, width), (rows, width), "place_tokens")


def per_device(
    hidden_in,
    norm_gain,
    proj_zx,
    proj_shared,
    proj_step,
    conv_inner,
    conv_shared,
    step_bias,
    decay_log,
    skip_gain,
    gated_gain,
    proj_out,
    out_grad,
    segments,
):
    model_width = hidden_in.shape[1]
    width = proj_zx.shape[2]
    heads = step_bias.shape[0]
    me = {axis: index_of(axis) for axis in DP + TENSOR}
    spot = 2 * me["zh"] + me["c"]

    shared_parts = [proj_shared] + [tensor_xor(proj_shared, by) for by in (1, 2, 3)]
    shared_rows = jnp.zeros((48, 256), BF16)
    for by, part in enumerate(shared_parts):
        shared_rows = lax.dynamic_update_slice(shared_rows, part, (((spot[0] ^ by) * 12), jnp.int32(0)))
    first_rows = jnp.concatenate(
        [proj_zx[:, 1, :], shared_rows, jnp.pad(proj_step, ((0, 0), (0, 128 - heads)))], 1
    )
    all_rows = jnp.concatenate([proj_zx[:, 0, :], proj_out.T, first_rows], 1)
    weights = lax.all_gather(pair_rows(all_rows), ("y", "x"), axis=0, tiled=True)

    residual_in = hidden_in.astype(F32)
    scale_in = lax.rsqrt(jnp.mean(residual_in * residual_in, axis=-1, keepdims=True) + EPS)
    normed_low = (residual_in * scale_in * norm_gain).astype(BF16)
    normed_far = swap(normed_low, "zh")
    normed_near = swap(normed_low, "c")

    normed_both = swap(normed_far, "c")
    tokens = token_place(normed_low, normed_near, normed_far, normed_both, spot)
    grad_far = swap(after(out_grad, normed_far), "zh")
    grad_near = swap(after(out_grad, normed_far), "c")
    grad_both = swap(grad_far, "c")
    grad_rows = token_place(out_grad, grad_near, grad_far, grad_both, spot)

    pad = (0, 128 - heads)
    head_rows = jnp.stack([jnp.pad(step_bias, pad), jnp.pad(jnp.exp(decay_log), pad)], 0)
    head_rows = jnp.pad(head_rows, ((0, 6), (0, 0)))
    taps = jnp.pad(jnp.concatenate([conv_inner, conv_shared], 1), ((0, 3), (0, 0)))
    chan = jnp.broadcast_to(jnp.repeat(skip_gain, width // heads), (8, width))
    gain = jnp.broadcast_to(gated_gain, (8, width))
    norm_rows = jnp.broadcast_to(norm_gain, (8, model_width))
    marks, segrow = scan_marks(segments)
    tokens, grad_rows = lax.optimization_barrier((tokens, grad_rows))
    pre, scanned, states = scan_forward(tokens, weights, taps, head_rows, chan, marks, segrow)

    gate_pre, grad_mixed, sums = mix_first(tokens, grad_rows, weights, scanned, gain)
    sums = (sums + tensor_xor(sums, 1)) + (tensor_xor(sums, 2) + tensor_xor(sums, 3))
    mixed_low, grad_scanned, gate_grad_low, gain_sums, *out_blocks = mix_second(
        sums, gate_pre, grad_mixed, scanned, weights, gain, 4 * width, spot
    )
    out_far = (out_blocks[1].astype(F32) + swap(out_blocks[0], "c").astype(F32)).astype(BF16)
    out_near = swap(out_blocks[2], "c")
    second_total, gate_gains = second_grads(tokens, grad_rows, gate_grad_low, mixed_low, weights)
    second_sum = lax.psum_scatter(second_total, ("y", "x"), scatter_dimension=0, tiled=True)
    out_far_got = swap(out_far, "zh")

    sum_table = head_sum_table(width)
    grad_scanned = after(grad_scanned, out_far, second_total)
    low, tap_sums, head_sums = scan_backward(
        pre, taps, head_rows, chan, sum_table, marks, segrow, grad_scanned, states
    )
    low = after(low, out_far_got)
    *first_blocks, small = first_grads(
        tokens, low, weights, gate_gains, norm_rows, tap_sums, head_sums, gain_sums, me["y"]
    )
    first_parts = sends(first_blocks, "y")
    low_late = after(low, *first_blocks)
    far_give, far_keep = token_grads(gate_grad_low, low_late, weights, spot, 3)
    far_got = jnp.concatenate([swap(far_give[:128], "c"), swap(far_give[128:], "c")], 0)
    near_give, near_keep = token_grads(gate_grad_low, after(low_late, far_give), weights, spot, 1)
    near_got = swap(near_give, "c")
    row_far = (far_keep.astype(F32) + far_got.astype(F32)).astype(BF16)
    row_far_got = swap(row_far, "zh")

    first_parts = [after(part, row_far_got, near_give) for part in first_parts]
    first_halves = add_split(first_parts, me["x"])
    first_parts = sends(first_halves, "x")
    small = sum_ring(after(small, *first_halves), "y")
    first_keep, first_give = add_halve(first_parts, me["zl"])
    small = sum_ring(after(small, first_give), "x")
    small = sum_pair(small, "zl")
    first_mine = first_keep + swap(first_give, "zl").astype(F32)
    second_pairs = second_sum.reshape(2, 48, 2 * width)
    second_keep = lax.dynamic_index_in_dim(second_pairs, me["zl"][0], 0, keepdims=False)
    second_mine = second_keep.astype(F32) + swap(
        lax.dynamic_index_in_dim(second_pairs, 1 - me["zl"][0], 0, keepdims=False), "zl"
    ).astype(F32)

    hidden_out = (
        residual_in + (out_blocks[3].astype(F32) + out_near.astype(F32) + out_far_got.astype(F32))
    ).astype(BF16)
    grad_normed = near_keep.astype(F32) + near_got.astype(F32) + row_far_got.astype(F32)
    weighted = jnp.sum(grad_normed * norm_gain * residual_in, axis=-1, keepdims=True)
    grad_hidden = (
        out_grad.astype(F32)
        + scale_in * norm_gain * grad_normed
        - residual_in * scale_in**3 * weighted / model_width
    ).astype(BF16)
    grad_proj_out = second_mine[:, width:].T
    grad_proj_zx = jnp.stack([second_mine[:, :width], first_mine[:, :width]], 1)
    grad_proj_step = first_mine[:, width + 256 : width + 256 + heads]

    def quarter(by):
        return lax.dynamic_slice(first_mine, ((spot[0] ^ by) * 12, jnp.int32(width)), (12, 256))

    grad_proj_shared = (quarter(0) + tensor_xor(quarter(1), 1)) + (
        tensor_xor(quarter(2), 2) + tensor_xor(quarter(3), 3)
    )

    summed = (small + tensor_xor(small, 1)) + (tensor_xor(small, 2) + tensor_xor(small, 3))
    grad_norm_gain = jnp.concatenate([summed[6], summed[7, :512]])
    return (
        hidden_out,
        grad_hidden,
        grad_norm_gain,
        grad_proj_zx,
        grad_proj_shared,
        grad_proj_step,
        small[:5, :width],
        summed[:5, width:],
        small[7, 512 : 512 + heads],
        small[7, 640 : 640 + heads],
        small[7, 768 : 768 + heads],
        small[5, :width],
        grad_proj_out,
    )


def solution(mesh):
    fine = Mesh(mesh.devices.reshape(4, 4, 2, 2, 2), DP + TENSOR)
    both = DP + TENSOR
    return jax.shard_map(
        per_device,
        mesh=fine,
        in_specs=(
            P(both, None),
            P(),
            P(DP, None, TENSOR),
            P(both, None),
            P(DP, TENSOR),
            P(None, TENSOR),
            P(),
            P(TENSOR),
            P(TENSOR),
            P(TENSOR),
            P(TENSOR),
            P(TENSOR, DP),
            P(both, None),
            P(DP),
        ),
        out_specs=(
            P(both, None),
            P(both, None),
            P(),
            P(DP, None, TENSOR),
            P(both, None),
            P(DP, TENSOR),
            P(None, TENSOR),
            P(),
            P(TENSOR),
            P(TENSOR),
            P(TENSOR),
            P(TENSOR),
            P(TENSOR, DP),
        ),
        check_vma=False,
    )
```

```python
import jax
import jax.numpy as jnp
from jax import lax
from jax.experimental import pallas as pl
from jax.experimental.pallas import tpu as pltpu
from jax.sharding import Mesh
from jax.sharding import PartitionSpec as P

EPS = 1e-05
DP = ("y", "x", "zl")
TENSOR = ("zh", "c")
SIZES = {"y": 4, "x": 4, "zl": 2, "zh": 2, "c": 2}

F32 = jnp.float32
BF16 = jnp.bfloat16
HIGH = lax.Precision.HIGHEST
BLOCK = 128
VMEM = 56 * 1024 * 1024
PARAMS = pltpu.CompilerParams(vmem_limit_bytes=VMEM)
NT = (((1,), (1,)), ((), ()))
TN = (((0,), (0,)), ((), ()))
VMEM_SPEC = pl.BlockSpec(memory_space=pltpu.VMEM)


def cost(us):
    return pl.CostEstimate(flops=int(us * 1e6), transcendentals=0, bytes_accessed=int(us * 3e3))


def whole(shape):
    return pl.BlockSpec(shape, lambda *i: (0,) * len(shape))


def column_block(rows, width, index):
    return pl.BlockSpec((rows, width), lambda *i: (0, index))


def first_specs(rows):
    return [column_block(rows, 384, index) for index in (4, 5, 6)]


def dot(a, b):
    return jnp.dot(a, b, preferred_element_type=F32)


def dot_nt(a, b):
    return lax.dot_general(a, b, NT, preferred_element_type=F32)


def sigmoid(a):
    return 0.5 * jnp.tanh(0.5 * a) + 0.5


def softplus(a):
    return jnp.maximum(a, 0.0) + jnp.log1p(jnp.exp(-jnp.abs(a)))


def conv_strip(ext, taps, aux, j):
    n = ext.shape[0] - 8
    lanes = slice(j * 128, (j + 1) * 128)
    total = taps[4:5, lanes] + taps[3:4, lanes] * ext[8 : 8 + n, lanes]
    for back in (1, 2, 3):
        total += taps[3 - back : 4 - back, lanes] * (
            aux[:, back - 1 : back] * ext[8 - back : 8 - back + n, lanes]
        )
    return total


def two_parts(value):
    high = value.astype(BF16)
    return jnp.concatenate([high, (value - high.astype(F32)).astype(BF16)], 1)


def spread_heads(cols, table):
    return dot(two_parts(cols), table)


def scan_forward_kernel(tok, weights_a, weights_b, weights_c, taps, heads, chan, spread, aux, segrow, pre_out, scan_out, state_out, ext, act, carry, fed):
    n = tok.shape[0]
    pairs = carry.shape[1] // 128

    @pl.when(pl.program_id(0) == 0)
    def _():
        carry[...] = jnp.zeros_like(carry)
        ext[0:8, :] = jnp.zeros((8, ext.shape[1]), F32)

    pre = jnp.concatenate([dot(tok[...], w[...]) for w in (weights_a, weights_b, weights_c)], 1)
    pre_out[...] = pre
    wide = ext.shape[1]
    ext[8:, :] = pre[:, :wide]
    marks = aux[...]
    for j in range(wide // 128):
        total = conv_strip(ext, taps, marks, j)
        act[:, j * 128 : (j + 1) * 128] = total * sigmoid(total)
    ext[0:8, :] = ext[n : n + 8, :]

    step = softplus(pre[:, wide:] + heads[0:1, :])
    log_step = -step * heads[1:2, :]
    row = lax.broadcasted_iota(jnp.int32, (n, n), 0)
    col = lax.broadcasted_iota(jnp.int32, (n, n), 1)
    lower = (row >= col).astype(F32)
    cum = jnp.dot(lower, log_step, precision=HIGH, preferred_element_type=F32)
    cum_t = cum.T
    write = act[:, pairs * 128 : (pairs + 1) * 128]
    read = act[:, (pairs + 1) * 128 : (pairs + 2) * 128].astype(BF16)
    write_t = write.T.astype(BF16)
    allowed = (row >= col) & (marks[:, 8:9] == segrow[0:1, :])
    inner = jnp.where(allowed, dot(read, write_t), 0.0)
    last = cum[n - 1 : n, :]
    enters = jnp.exp(cum) * marks[:, 3:4]
    to_end = jnp.exp(last - cum) * marks[:, 4:5]
    keep = jnp.exp(last) * marks[n - 1 : n, 3:4]
    wide_cols = spread_heads(jnp.concatenate([step, enters, to_end, jnp.broadcast_to(keep, (8, 128))], 0), spread[...])
    held = carry[...]
    held_low = held.astype(BF16)
    state_out[0] = held_low
    from_state = dot(read, held_low)
    low_half = lax.broadcasted_iota(jnp.int32, (1, 128), 1) < 64
    for j in range(pairs):
        lanes = slice(j * 128, (j + 1) * 128)
        x = act[:, lanes]
        xdt = x * wide_cols[:n, lanes]
        parts = []
        for h in (2 * j, 2 * j + 1):
            decay = jnp.exp(jnp.minimum(cum[:, h : h + 1] - cum_t[h : h + 1, :], 0.0))
            parts.append((decay * inner).astype(BF16))
        xdt_low = xdt.astype(BF16)
        zero = jnp.zeros_like(xdt_low)
        pair = jnp.concatenate([jnp.where(low_half, xdt_low, zero), jnp.where(low_half, zero, xdt_low)], 0)
        y = dot(jnp.concatenate(parts, 1), pair)
        y += wide_cols[n : 2 * n, lanes] * from_state[:, lanes] + chan[0:1, lanes] * x
        scan_out[:, lanes] = y
        fed[:, lanes] = (xdt * wide_cols[2 * n : 3 * n, lanes]).astype(BF16)
        carry[:, lanes] = held[:, lanes] * wide_cols[3 * n : 3 * n + 1, lanes]
    carry[...] += dot(write_t, fed[...])


def scan_backward_kernel(pre, pre_before, taps, heads, chan, sums, spread, aux, segrow, grad, state, low_out, taps_out, heads_out, ext, gext, act, slope, carry, fed, back, rows):
    n = pre.shape[0]
    pairs = carry.shape[1] // 128
    wide = ext.shape[1]

    @pl.when(pl.program_id(0) == 0)
    def _():
        carry[...] = jnp.zeros_like(carry)
        gext[n:, :] = jnp.zeros((8, wide), F32)
        taps_out[...] = jnp.zeros_like(taps_out)
        heads_out[...] = jnp.zeros_like(heads_out)
        rows[...] = jnp.zeros_like(rows)

    marks = aux[...]
    ext[0:8, :] = pre_before[:, :wide]
    ext[8:, :] = pre[:, :wide]
    for j in range(wide // 128):
        lanes = slice(j * 128, (j + 1) * 128)
        total = conv_strip(ext, taps, marks, j)
        sig = sigmoid(total)
        value = total * sig
        act[:, lanes] = value
        slope[:, lanes] = sig + value * (1.0 - sig)

    step_arg = pre[:, wide:] + heads[0:1, :]
    step = softplus(step_arg)
    rate = heads[1:2, :]
    row = lax.broadcasted_iota(jnp.int32, (n, n), 0)
    col = lax.broadcasted_iota(jnp.int32, (n, n), 1)
    lower = (row >= col).astype(F32)
    cum = jnp.dot(lower, -step * rate, precision=HIGH, preferred_element_type=F32)
    cum_t = cum.T
    write = act[:, pairs * 128 : (pairs + 1) * 128]
    read = act[:, (pairs + 1) * 128 : (pairs + 2) * 128]
    read_t = read.T.astype(BF16)
    write_low = write.astype(BF16)
    read_low = read.astype(BF16)
    allowed = (row <= col) & (marks[:, 8:9] == segrow[0:1, :])
    inner_t = jnp.where(allowed, dot(write_low, read_t), 0.0)
    last = cum[n - 1 : n, :]
    enters = jnp.exp(cum) * marks[:, 3:4]
    to_end = jnp.exp(last - cum) * marks[:, 4:5]
    keep = jnp.exp(last) * marks[n - 1 : n, 3:4]
    wide_cols = spread_heads(jnp.concatenate([step, enters, to_end, jnp.broadcast_to(keep, (8, 128))], 0), spread[...])
    held = state[0]
    later = carry[...]
    later_low = later.astype(BF16)
    from_state = dot(read_low, held)
    from_later = dot(write_low, later_low)
    low_half = lax.broadcasted_iota(jnp.int32, (1, 128), 1) < 64
    head_lane = lax.broadcasted_iota(jnp.int32, (1, 128), 1)
    grad_inner = jnp.zeros((n, n), F32)
    col_sums = jnp.zeros((n, 128), F32)
    to_end_part = jnp.zeros((n, 128), F32)
    enter_part = jnp.zeros((n, 128), F32)
    step_part = jnp.zeros((n, 128), F32)
    skip_part = jnp.zeros((n, 128), F32)
    keep_part = jnp.zeros((8, 128), F32)

    def head_sums(value, j):
        return dot(two_parts(value), sums[j])

    for j in range(pairs):
        lanes = slice(j * 128, (j + 1) * 128)
        x = act[:, lanes]
        dy = grad[:, lanes].astype(F32)
        step_wide = wide_cols[:n, lanes]
        xdt = x * step_wide
        xdt_low = xdt.astype(BF16)
        dy_low = dy.astype(BF16)
        zero = jnp.zeros_like(xdt_low)
        products = dot_nt(
            jnp.concatenate([jnp.where(low_half, xdt_low, zero), jnp.where(low_half, zero, xdt_low)], 0),
            dy_low,
        )
        parts = []
        for k, h in enumerate((2 * j, 2 * j + 1)):
            product = products[k * n : (k + 1) * n, :]
            decay = jnp.exp(jnp.minimum(cum_t[h : h + 1, :] - cum[:, h : h + 1], 0.0))
            scaled = decay * product
            grad_inner += scaled
            weighted = scaled * inner_t
            rows[h : h + 1, :] = jnp.sum(weighted, axis=0, keepdims=True)
            col_sums += jnp.where(head_lane == h, jnp.sum(weighted, axis=1, keepdims=True), 0.0)
            parts.append((decay * inner_t).astype(BF16))
        grad_pair = jnp.concatenate([jnp.where(low_half, dy_low, zero), jnp.where(low_half, zero, dy_low)], 0)
        grad_xdt = dot(jnp.concatenate(parts, 1), grad_pair)
        end_wide = wide_cols[2 * n : 3 * n, lanes]
        enter_wide = wide_cols[n : 2 * n, lanes]
        later_part = end_wide * from_later[:, lanes]
        grad_xdt += later_part
        to_end_part += head_sums(later_part * xdt, j)
        fed[:, lanes] = (xdt * end_wide).astype(BF16)
        grad_enter = dy * enter_wide
        back[:, lanes] = grad_enter.astype(BF16)
        enter_part += head_sums(grad_enter * from_state[:, lanes], j)
        step_part += head_sums(grad_xdt * x, j)
        skip_part += head_sums(dy * x, j)
        kept = jnp.sum(held[:, lanes].astype(F32) * later[:, lanes], axis=0, keepdims=True)
        keep_part += head_sums(jnp.broadcast_to(kept, (8, 128)), j)
        act[:, lanes] = grad_xdt * step_wide + chan[0:1, lanes] * dy
        carry[:, lanes] = later[:, lanes] * wide_cols[3 * n : 3 * n + 1, lanes]

    grad_cum = rows[...].T - col_sums + enter_part - to_end_part
    grad_last = jnp.sum(to_end_part, axis=0, keepdims=True) + keep * keep_part[0:1, :]
    upper = (row <= col).astype(F32)
    grad_log = jnp.dot(upper, grad_cum, precision=HIGH, preferred_element_type=F32) + grad_last
    grad_step = (step_part - rate * grad_log) * sigmoid(step_arg)
    heads_out[0:1, :] += jnp.sum(grad_step, axis=0, keepdims=True)
    heads_out[1:2, :] += -rate * jnp.sum(step * grad_log, axis=0, keepdims=True)
    heads_out[2:3, :] += jnp.sum(skip_part, axis=0, keepdims=True)
    low_out[:, wide:] = grad_step.astype(BF16)

    grad_inner = jnp.where(allowed, grad_inner, 0.0)
    act[:, pairs * 128 : (pairs + 1) * 128] = dot(grad_inner.astype(BF16), read_low) + dot_nt(fed[...], later_low)
    act[:, (pairs + 1) * 128 : (pairs + 2) * 128] = dot(grad_inner.T.astype(BF16), write_low) + dot_nt(back[...], held)
    carry[...] += dot(read_t, back[...])

    for j in range(wide // 128):
        lanes = slice(j * 128, (j + 1) * 128)
        grad_pre = act[:, lanes] * slope[:, lanes]
        gext[0:n, lanes] = grad_pre
        total = taps[3:4, lanes] * grad_pre
        taps_out[3:4, lanes] += jnp.sum(grad_pre * ext[8 : 8 + n, lanes], axis=0, keepdims=True)
        taps_out[4:5, lanes] += jnp.sum(grad_pre, axis=0, keepdims=True)
        for by in (1, 2, 3):
            total += taps[3 - by : 4 - by, lanes] * (marks[:, 4 + by : 5 + by] * gext[by : by + n, lanes])
            taps_out[3 - by : 4 - by, lanes] += jnp.sum(
                grad_pre * (marks[:, by - 1 : by] * ext[8 - by : 8 - by + n, lanes]), axis=0, keepdims=True
            )
        low_out[:, lanes] = total.astype(BF16)
    gext[n:, :] = gext[0:8, :]


def scan_marks(segments):
    length = segments.shape[0]
    blocks = segments.reshape(-1, BLOCK)
    before = jnp.concatenate([jnp.full((1,), -1, jnp.int32), blocks[:-1, -1]], 0)

    def same(by):
        if by > 0:
            other = jnp.concatenate([jnp.full((by,), -1, jnp.int32), segments[:-by]], 0)
        else:
            other = jnp.concatenate([segments[-by:], jnp.full((-by,), -1, jnp.int32)], 0)
        return other == segments

    cols = [same(1), same(2), same(3), (blocks == before[:, None]).reshape(-1), (blocks == blocks[:, -1:]).reshape(-1)]
    cols += [same(-1), same(-2), same(-3), segments]
    marks = jnp.stack([c.astype(F32) for c in cols], 1)
    return jnp.pad(marks, ((0, 0), (0, 128 - len(cols)))), jnp.broadcast_to(segments.astype(F32), (8, length))


def scan_forward(tokens, weights, taps, heads, chan, spread, marks, segrow):
    length, model = tokens.shape
    cols = 1152
    inner = cols - 384
    wide = cols - 128
    n = BLOCK
    blocks = length // n


    return pl.pallas_call(
        scan_forward_kernel,
        grid=(blocks,),
        in_specs=[
            pl.BlockSpec((n, model), lambda i: (i, 0)),
            *first_specs(model),
            whole((8, wide)),
            whole((8, 128)),
            whole((8, inner)),
            whole((256, inner)),
            pl.BlockSpec((n, 128), lambda i: (i, 0)),
            pl.BlockSpec((8, n), lambda i: (0, i)),
        ],
        out_specs=[
            pl.BlockSpec((n, cols), lambda i: (i, 0)),
            pl.BlockSpec((n, inner), lambda i: (i, 0)),
            pl.BlockSpec((1, 128, inner), lambda i: (i, 0, 0)),
        ],
        out_shape=[
            jax.ShapeDtypeStruct((length, cols), F32),
            jax.ShapeDtypeStruct((length, inner), F32),
            jax.ShapeDtypeStruct((blocks, 128, inner), BF16),
        ],
        scratch_shapes=[
            pltpu.VMEM((n + 8, wide), F32),
            pltpu.VMEM((n, wide), F32),
            pltpu.VMEM((128, inner), F32),
            pltpu.VMEM((n, inner), BF16),
        ],
        compiler_params=PARAMS,
        cost_estimate=cost(20),
        name="scan_forward",
    )(tokens, weights, weights, weights, taps, heads, chan, spread, marks, segrow)


def scan_backward(pre, taps, heads, chan, sums, spread, marks, segrow, grad, states):
    length, cols = pre.shape
    inner = cols - 384
    wide = cols - 128
    n = BLOCK
    blocks = length // n


    def rev(i):
        return blocks - 1 - i

    return pl.pallas_call(
        scan_backward_kernel,
        grid=(blocks,),
        in_specs=[
            pl.BlockSpec((n, cols), lambda i: (rev(i), 0)),
            pl.BlockSpec((8, cols), lambda i: (jnp.maximum(rev(i) * (n // 8) - 1, 0), 0)),
            whole((8, wide)),
            whole((8, 128)),
            whole((8, inner)),
            whole((inner // 128, 256, 128)),
            whole((256, inner)),
            pl.BlockSpec((n, 128), lambda i: (rev(i), 0)),
            pl.BlockSpec((8, n), lambda i: (0, rev(i))),
            pl.BlockSpec((n, inner), lambda i: (rev(i), 0)),
            pl.BlockSpec((1, 128, inner), lambda i: (rev(i), 0, 0)),
        ],
        out_specs=[
            pl.BlockSpec((n, cols), lambda i: (rev(i), 0)),
            whole((8, wide)),
            whole((8, 128)),
        ],
        out_shape=[
            jax.ShapeDtypeStruct((length, cols), BF16),
            jax.ShapeDtypeStruct((8, wide), F32),
            jax.ShapeDtypeStruct((8, 128), F32),
        ],
        scratch_shapes=[
            pltpu.VMEM((n + 8, wide), F32),
            pltpu.VMEM((n + 8, wide), F32),
            pltpu.VMEM((n, wide), F32),
            pltpu.VMEM((n, wide), F32),
            pltpu.VMEM((128, inner), F32),
            pltpu.VMEM((n, inner), BF16),
            pltpu.VMEM((n, inner), BF16),
            pltpu.VMEM((128, n), F32),
        ],
        compiler_params=PARAMS,
        cost_estimate=cost(30),
        name="scan_backward",
    )(pre, pre, taps, heads, chan, sums, spread, marks, segrow, grad, states)


def spread_table(inner):
    head = jnp.arange(inner) // 64
    return (jnp.arange(256)[:, None] % 128 == head[None, :]).astype(BF16)


def head_sum_table(inner):
    pairs = inner // 128
    lane = jnp.arange(256) % 128
    head = 2 * jnp.arange(pairs)[:, None] + (lane >= 64)[None, :]
    return (head[:, :, None] == jnp.arange(128)[None, None, :]).astype(BF16)


def mix_first_kernel(tok, rows, gate_w, out_w, scanned, gain, gate_out, mixed_out, sums_out):
    gate_pre = dot(tok[...], gate_w[...])
    grad_mixed = dot(rows[...], out_w[...])
    gate_out[...] = gate_pre
    mixed_out[...] = grad_mixed
    gated = scanned[...] * (gate_pre * sigmoid(gate_pre))
    square = jnp.sum(gated * gated, axis=1, keepdims=True)
    inner = jnp.sum(grad_mixed * gain[0:1, :] * gated, axis=1, keepdims=True)
    lane = lax.broadcasted_iota(jnp.int32, (1, 128), 1)
    cols = jnp.where(lane == 0, square, jnp.where(lane == 1, inner, 0.0))
    sums_out[...] = cols.T[0:8, :]


def mix_first(tokens, grad_rows, second, scanned, gain):
    length, model = tokens.shape
    width = scanned.shape[1]
    n = 256

    def rows(cols):
        return pl.BlockSpec((n, cols), lambda i: (i, 0))

    return pl.pallas_call(
        mix_first_kernel,
        grid=(length // n,),
        in_specs=[
            rows(model),
            rows(model),
            pl.BlockSpec((model, width), lambda i: (0, 0)),
            pl.BlockSpec((model, width), lambda i: (0, 1)),
            rows(width),
            whole((8, width)),
        ],
        out_specs=[rows(width), rows(width), pl.BlockSpec((8, n), lambda i: (0, i))],
        out_shape=[
            jax.ShapeDtypeStruct((length, width), F32),
            jax.ShapeDtypeStruct((length, width), F32),
            jax.ShapeDtypeStruct((8, length), F32),
        ],
        compiler_params=PARAMS,
        cost_estimate=cost(10),
        name="mix_first",
    )(tokens, grad_rows, second, second, scanned, gain)


def store_block(value, outs):
    for k, out in enumerate(outs):

        @pl.when(pl.program_id(0) == k)
        def _():
            out[...] = value


def mix_second_kernel(channels, me, sums, gate, grad_mixed_in, scanned_in, out_w, gain, low_out, grad_scan, grad_gate, gain_out, *outs):
    n = gate.shape[0]

    @pl.when(pl.program_id(0) == 0)
    def _():
        gain_out[...] = jnp.zeros_like(gain_out)

    cols = jnp.concatenate([sums[...], jnp.zeros((120, n), F32)], 0).T
    scale = lax.rsqrt(cols[:, 0:1] / channels + EPS)
    pull = scale * scale * scale * (cols[:, 1:2] / channels)
    gate_pre = gate[...]
    grad_mixed = grad_mixed_in[...]
    scanned = scanned_in[...]
    sig = sigmoid(gate_pre)
    silu = gate_pre * sig
    gated = scanned * silu
    scaled = gated * scale
    mixed = (scaled * gain[0:1, :]).astype(BF16)
    low_out[...] = mixed
    gain_out[0:1, :] += jnp.sum(grad_mixed * scaled, axis=0, keepdims=True)
    grad_gated = scale * gain[0:1, :] * grad_mixed - gated * pull
    grad_scan[...] = grad_gated * silu
    grad_gate[...] = (grad_gated * scanned * (sig + silu * (1.0 - sig))).astype(BF16)
    store_block(dot_nt(mixed, out_w[...]).astype(BF16), outs)


def mix_second(sums, gate, grad_mixed, scanned, second, gain, channels, spot):
    length, width = gate.shape
    model = second.shape[0]
    n = 256

    def rows(cols):
        return pl.BlockSpec((n, cols), lambda i, me: (me[0] ^ (3 - i), 0))

    return pl.pallas_call(
        lambda *refs: mix_second_kernel(channels, *refs),
        grid_spec=pltpu.PrefetchScalarGridSpec(
            num_scalar_prefetch=1,
            grid=(4,),
            in_specs=[
                pl.BlockSpec((8, n), lambda i, me: (0, me[0] ^ (3 - i))),
                rows(width),
                rows(width),
                rows(width),
                pl.BlockSpec((model, width), lambda i, me: (0, 1)),
                whole((8, width)),
            ],
            out_specs=[rows(width), rows(width), rows(width), whole((8, width))] + [whole((n, model))] * 4,
        ),
        out_shape=[
            jax.ShapeDtypeStruct((length, width), BF16),
            jax.ShapeDtypeStruct((length, width), F32),
            jax.ShapeDtypeStruct((length, width), BF16),
            jax.ShapeDtypeStruct((8, width), F32),
        ]
        + [jax.ShapeDtypeStruct((n, model), BF16)] * 4,
        compiler_params=PARAMS,
        cost_estimate=cost(11),
        name="mix_second",
    )(spot, sums, gate, grad_mixed, scanned, second, gain)


def token_grads_kernel(me, grad_gate, low, gate_w, weights_a, weights_b, weights_c, *outs):
    total = dot_nt(grad_gate[...], gate_w[...])
    for n, w in enumerate((weights_a, weights_b, weights_c)):
        total += dot_nt(low[:, 384 * n : 384 * (n + 1)], w[...])
    store_block(total.astype(BF16), outs)


def token_grads(grad_gate, low, weights, spot):
    model = weights.shape[0]
    width = grad_gate.shape[1]
    n = 256

    def rows(cols):
        return pl.BlockSpec((n, cols), lambda i, me: (me[0] ^ (3 - i), 0))

    return pl.pallas_call(
        token_grads_kernel,
        grid_spec=pltpu.PrefetchScalarGridSpec(
            num_scalar_prefetch=1,
            grid=(4,),
            in_specs=[rows(width), rows(low.shape[1]), column_block(model, width, 0), *first_specs(model)],
            out_specs=[whole((n, model))] * 4,
        ),
        out_shape=[jax.ShapeDtypeStruct((n, model), BF16)] * 4,
        compiler_params=PARAMS,
        cost_estimate=cost(6),
        name="token_grads",
    )(spot, grad_gate, low, weights, weights, weights, weights)


def row_sums(product):
    sums = jnp.sum(product, axis=1, keepdims=True)
    return jnp.broadcast_to(sums, (product.shape[0], 128)).T[0:1, :]


def second_grads_kernel(tok, rows, grad_gate, mixed, gate_w, out, gains):
    width = grad_gate.shape[1]
    gate_part = lax.dot_general(tok[...], grad_gate[...], TN, preferred_element_type=F32)
    out_part = lax.dot_general(rows[...], mixed[...], TN, preferred_element_type=F32)
    out[:, :width] = gate_part.astype(BF16)
    out[:, width:] = out_part.astype(BF16)
    gains[...] = jnp.broadcast_to(row_sums(gate_part * gate_w[...].astype(F32)), gains.shape)


def second_grads(tokens, grad_rows, grad_gate, mixed, weights):
    length, model = tokens.shape
    width = grad_gate.shape[1]
    n = model // 4
    cols = pl.BlockSpec((length, n), lambda i: (0, i))
    return pl.pallas_call(
        second_grads_kernel,
        grid=(4,),
        in_specs=[cols, cols, whole((length, width)), whole((length, width)), pl.BlockSpec((n, width), lambda i: (i, 0))],
        out_specs=[pl.BlockSpec((n, 2 * width), lambda i: (i, 0)), pl.BlockSpec((8, n), lambda i: (0, i))],
        out_shape=[jax.ShapeDtypeStruct((model, 2 * width), BF16), jax.ShapeDtypeStruct((8, model), F32)],
        compiler_params=PARAMS,
        cost_estimate=cost(8),
        name="second_grads",
    )(tokens, grad_rows, grad_gate, mixed, weights)


def first_grads_kernel(me, tok, low, weights_a, weights_b, weights_c, gate_gains, norm_gain, taps, heads, gain, *rest):
    outs_a, outs_b = rest[:4], rest[4:8]
    packed, gains, held = rest[8:]
    step = pl.program_id(0)
    y = (me[0] + step) % 4
    n = tok.shape[1]
    cut = outs_a[0].shape[2]
    deep = n // 4
    grad = lax.dot_general(tok[...], low[...], TN, preferred_element_type=F32)
    total = jnp.zeros((n, 128), F32)
    for block, w in enumerate((weights_a, weights_b, weights_c)):
        for m in range(3):
            lanes = slice(384 * block + 128 * m, 384 * block + 128 * (m + 1))
            total += grad[:, lanes] * w[:, 128 * m : 128 * (m + 1)].astype(F32)
    gains[0:1, pl.ds(pl.multiple_of(y * n, 128), n)] = row_sums(total)
    for k in range(4):

        @pl.when(step == k)
        def _():
            outs_a[k][...] = grad[:, :cut].astype(BF16).reshape(outs_a[k].shape)

    held[...] = grad[:, cut:].astype(BF16)
    for k in range(4):
        outs_b[k][y] = held[pl.ds(pl.multiple_of(((me[1] + k) % 4) * deep, 16), deep), :]

    @pl.when(step == 3)
    def _():
        width = gain.shape[1]
        by_gain = (gains[0:1, :] + gate_gains[0:1, :]) / norm_gain[0:1, :]
        packed[0:5, :] = taps[0:5, :]
        packed[5:6, :width] = gain[0:1, :]
        packed[5:6, width:] = jnp.zeros((1, 1024 - width), F32)
        packed[6:7, :] = by_gain[:, :1024]
        packed[7:8, :512] = by_gain[:, 1024:]
        for r in range(3):
            packed[7:8, 512 + 128 * r : 640 + 128 * r] = heads[r : r + 1, :]
        packed[7:8, 896:] = jnp.zeros((1, 128), F32)


def first_grads(tokens, low, weights, gate_gains, norm_gain, taps, heads, gain, me):
    length, model = tokens.shape
    width = low.shape[1]
    cut = 640
    n = model // 4
    shape_a, shape_b = (4, n // 4, cut), (4, n // 4, width - cut)

    def spot(i, me):
        return (me[0] + i) % 4

    return pl.pallas_call(
        first_grads_kernel,
        grid_spec=pltpu.PrefetchScalarGridSpec(
            num_scalar_prefetch=1,
            grid=(4,),
            in_specs=[
                pl.BlockSpec((length, n), lambda i, me: (0, spot(i, me))),
                whole((length, width)),
                pl.BlockSpec((n, 384), lambda i, me: (spot(i, me), 4)),
                pl.BlockSpec((n, 384), lambda i, me: (spot(i, me), 5)),
                pl.BlockSpec((n, 384), lambda i, me: (spot(i, me), 6)),
                whole(gate_gains.shape),
                whole(norm_gain.shape),
                whole(taps.shape),
                whole(heads.shape),
                whole(gain.shape),
            ],
            out_specs=[whole(shape_a)] * 4 + [whole(shape_b)] * 4 + [whole((8, 1024))],
            scratch_shapes=[pltpu.VMEM((8, model), F32), pltpu.VMEM((n, width - cut), BF16)],
        ),
        out_shape=[jax.ShapeDtypeStruct(shape_a, BF16)] * 4
        + [jax.ShapeDtypeStruct(shape_b, BF16)] * 4
        + [jax.ShapeDtypeStruct((8, 1024), F32)],
        compiler_params=PARAMS,
        cost_estimate=cost(6),
        name="first_grads",
    )(me, tokens, low, weights, weights, weights, gate_gains, norm_gain, taps, heads, gain)


def four_sum(own, ahead, across, behind):
    return (own.astype(F32) + across.astype(F32)) + (ahead.astype(F32) + behind.astype(F32))


def add_split_kernel(me, *refs):
    ins, outs = refs[:8], refs[8:]
    for half in range(2):
        for d in range(4):
            e = (me[half] + d) % 4
            outs[4 * half + d][...] = four_sum(*[part[e] for part in ins[4 * half : 4 * half + 4]]).astype(BF16)


def add_split(parts_a, parts_b, me):
    shapes = [jax.ShapeDtypeStruct(parts[0].shape[1:], BF16) for parts in (parts_a, parts_b) for _ in range(4)]
    outs = pl.pallas_call(
        add_split_kernel,
        in_specs=[pl.BlockSpec(memory_space=pltpu.SMEM)] + [VMEM_SPEC] * 8,
        out_specs=[VMEM_SPEC] * 8,
        out_shape=shapes,
        compiler_params=PARAMS,
        name="add_split",
    )(me, *parts_a, *parts_b)
    return outs[:4], outs[4:]


def add_halve_kernel(me, *refs):
    ins, (keep, give, total) = refs[:8], refs[8:]
    cut = ins[0].shape[1]
    total[:, :cut] = four_sum(*[part[...] for part in ins[:4]])
    total[:, cut:] = four_sum(*[part[...] for part in ins[4:]])
    n = keep.shape[0]
    keep[...] = total[pl.ds(pl.multiple_of(me[0] * n, 16), n), :]
    give[...] = total[pl.ds(pl.multiple_of((1 - me[0]) * n, 16), n), :].astype(BF16)


def add_halve(parts_a, parts_b, me):
    rows = parts_a[0].shape[0]
    width = parts_a[0].shape[1] + parts_b[0].shape[1]
    return pl.pallas_call(
        add_halve_kernel,
        in_specs=[pl.BlockSpec(memory_space=pltpu.SMEM)] + [VMEM_SPEC] * 8,
        out_specs=[VMEM_SPEC] * 2,
        out_shape=[
            jax.ShapeDtypeStruct((rows // 2, width), F32),
            jax.ShapeDtypeStruct((rows // 2, width), BF16),
        ],
        scratch_shapes=[pltpu.VMEM((rows, width), F32)],
        compiler_params=PARAMS,
        name="add_halve",
    )(me, *parts_a, *parts_b)


def place_kernel(me, *refs):
    out = refs[-1]
    for k, part in enumerate(refs[:-1]):

        @pl.when(pl.program_id(0) == k)
        def _():
            out[...] = part[...].reshape(out.shape)


def place(parts, index, me, shape, block, name):
    return pl.pallas_call(
        place_kernel,
        grid_spec=pltpu.PrefetchScalarGridSpec(
            num_scalar_prefetch=1,
            grid=(len(parts),),
            in_specs=[whole(p.shape) for p in parts],
            out_specs=pl.BlockSpec(block, lambda i, me: index(i, me[0])),
        ),
        out_shape=jax.ShapeDtypeStruct(shape, parts[0].dtype),
        compiler_params=PARAMS,
        cost_estimate=cost(2),
        name=name,
    )(me, *parts)


def shift(value, axis, by):
    n = SIZES[axis]
    return lax.ppermute(value, axis, [(i, (i - by) % n) for i in range(n)])


def swap(value, axis):
    return shift(value, axis, 1)


def ring(value, axis):
    return [value, shift(value, axis, 1), shift(value, axis, 2), shift(value, axis, -1)]


def sends(blocks, axis):
    return [blocks[0], shift(blocks[1], axis, -1), shift(blocks[2], axis, 2), shift(blocks[3], axis, 1)]


def tensor_xor(value, by):
    return lax.ppermute(value, TENSOR, [(i, i ^ by) for i in range(4)])


def sum_ring(value, axis):
    own, ahead, across, behind = ring(value, axis)
    return (own + across) + (ahead + behind)


def sum_pair(value, axis):
    return value + swap(value, axis)


def after(value, *others):
    return lax.optimization_barrier((value,) + others)[0]


def index_of(axis):
    return lax.axis_index(axis).reshape(1).astype(jnp.int32)


def pair_rows(value):
    rows, width = value.shape
    parts = [value, swap(value, "zl")]
    return place(parts, lambda i, me: ((me + i) % 2, 0), index_of("zl"), (2 * rows, width), (rows, width), "place_zl")


def token_place(own, near, far, both, me):
    rows, width = own.shape
    return place([own, near, far, both], lambda i, me: (me ^ i, 0), me, (4 * rows, width), (rows, width), "place_tokens")


def per_device(
    hidden_in,
    norm_gain,
    proj_zx,
    proj_shared,
    proj_step,
    conv_inner,
    conv_shared,
    step_bias,
    decay_log,
    skip_gain,
    gated_gain,
    proj_out,
    out_grad,
    segments,
):
    model_width = hidden_in.shape[1]
    width = proj_zx.shape[2]
    heads = step_bias.shape[0]
    me = {axis: index_of(axis) for axis in DP + TENSOR}
    spot = 2 * me["zh"] + me["c"]

    shared_parts = [proj_shared] + [tensor_xor(proj_shared, by) for by in (1, 2, 3)]
    shared_rows = jnp.zeros((48, 256), BF16)
    for by, part in enumerate(shared_parts):
        shared_rows = lax.dynamic_update_slice(shared_rows, part, (((spot[0] ^ by) * 12), jnp.int32(0)))
    first_rows = jnp.concatenate(
        [proj_zx[:, 1, :], shared_rows, jnp.pad(proj_step, ((0, 0), (0, 128 - heads)))], 1
    )
    all_rows = jnp.concatenate([proj_zx[:, 0, :], proj_out.T, first_rows], 1)
    weights = lax.all_gather(pair_rows(all_rows), ("y", "x"), axis=0, tiled=True)

    residual_in = hidden_in.astype(F32)
    scale_in = lax.rsqrt(jnp.mean(residual_in * residual_in, axis=-1, keepdims=True) + EPS)
    normed_low = (residual_in * scale_in * norm_gain).astype(BF16)
    normed_far = swap(normed_low, "zh")
    normed_near = swap(normed_low, "c")

    normed_both = swap(normed_far, "c")
    tokens = token_place(normed_low, normed_near, normed_far, normed_both, spot)
    grad_far = swap(after(out_grad, normed_far), "zh")
    grad_near = swap(after(out_grad, normed_far), "c")
    grad_both = swap(grad_far, "c")
    grad_rows = token_place(out_grad, grad_near, grad_far, grad_both, spot)

    pad = (0, 128 - heads)
    head_rows = jnp.stack([jnp.pad(step_bias, pad), jnp.pad(jnp.exp(decay_log), pad)], 0)
    head_rows = jnp.pad(head_rows, ((0, 6), (0, 0)))
    taps = jnp.pad(jnp.concatenate([conv_inner, conv_shared], 1), ((0, 3), (0, 0)))
    chan = jnp.broadcast_to(jnp.repeat(skip_gain, width // heads), (8, width))
    gain = jnp.broadcast_to(gated_gain, (8, width))
    norm_rows = jnp.broadcast_to(norm_gain, (8, model_width))
    marks, segrow = scan_marks(segments)
    spread = spread_table(width)
    sum_table = head_sum_table(width)
    tokens, grad_rows = lax.optimization_barrier((tokens, grad_rows))
    pre, scanned, states = scan_forward(tokens, weights, taps, head_rows, chan, spread, marks, segrow)

    gate_pre, grad_mixed, sums = mix_first(tokens, grad_rows, weights, scanned, gain)
    sums = (sums + tensor_xor(sums, 1)) + (tensor_xor(sums, 2) + tensor_xor(sums, 3))
    mixed_low, grad_scanned, gate_grad_low, gain_sums, *out_blocks = mix_second(
        sums, gate_pre, grad_mixed, scanned, weights, gain, 4 * width, spot
    )
    out_far = (out_blocks[1].astype(F32) + swap(out_blocks[0], "c").astype(F32)).astype(BF16)
    out_near = swap(out_blocks[2], "c")
    second_total, gate_gains = second_grads(tokens, grad_rows, gate_grad_low, mixed_low, weights)
    second_sum = lax.psum_scatter(second_total, ("y", "x"), scatter_dimension=0, tiled=True)
    out_far_got = swap(out_far, "zh")

    grad_scanned = after(grad_scanned, out_far, second_total)
    low, tap_sums, head_sums = scan_backward(
        pre, taps, head_rows, chan, sum_table, spread, marks, segrow, grad_scanned, states
    )
    low = after(low, out_far_got)
    *first_blocks, small = first_grads(
        tokens,
        low,
        weights,
        gate_gains,
        norm_rows,
        tap_sums,
        head_sums,
        gain_sums,
        jnp.concatenate([me["y"], me["x"]]),
    )
    parts_a = sends(first_blocks[:4], "y")
    parts_b = sends(first_blocks[4:], "x")
    low_late = after(low, *first_blocks)
    row_blocks = token_grads(gate_grad_low, low_late, weights, spot)
    parts_a = [after(part, *row_blocks) for part in parts_a]
    parts_b = [after(part, *row_blocks) for part in parts_b]
    half_a, half_b = add_split(parts_a, parts_b, jnp.concatenate([me["x"], me["y"]]))
    far_got = swap(after(row_blocks[0], *half_a), "c")
    near_got = swap(row_blocks[2], "c")
    row_far = (row_blocks[1].astype(F32) + far_got.astype(F32)).astype(BF16)
    row_far_got = swap(row_far, "zh")
    parts_a = [after(part, row_far) for part in sends(half_a, "x")]
    parts_b = [after(part, row_far) for part in sends(half_b, "y")]
    small = sum_ring(after(small, *half_a), "y")
    first_keep, first_give = add_halve(parts_a, parts_b, me["zl"])
    first_mine = first_keep + swap(first_give, "zl").astype(F32)
    small = sum_ring(after(small, first_give), "x")
    small = sum_pair(small, "zl")
    second_pairs = second_sum.reshape(2, 48, 2 * width)
    second_keep = lax.dynamic_index_in_dim(second_pairs, me["zl"][0], 0, keepdims=False)
    second_mine = second_keep.astype(F32) + swap(
        lax.dynamic_index_in_dim(second_pairs, 1 - me["zl"][0], 0, keepdims=False), "zl"
    ).astype(F32)

    hidden_out = (
        residual_in + (out_blocks[3].astype(F32) + out_near.astype(F32) + out_far_got.astype(F32))
    ).astype(BF16)
    grad_normed = row_blocks[3].astype(F32) + near_got.astype(F32) + row_far_got.astype(F32)
    weighted = jnp.sum(grad_normed * norm_gain * residual_in, axis=-1, keepdims=True)
    grad_hidden = (
        out_grad.astype(F32)
        + scale_in * norm_gain * grad_normed
        - residual_in * scale_in**3 * weighted / model_width
    ).astype(BF16)
    grad_proj_out = second_mine[:, width:].T
    grad_proj_zx = jnp.stack([second_mine[:, :width], first_mine[:, :width]], 1)
    grad_proj_step = first_mine[:, width + 256 : width + 256 + heads]

    def quarter(by):
        return lax.dynamic_slice(first_mine, ((spot[0] ^ by) * 12, jnp.int32(width)), (12, 256))

    grad_proj_shared = (quarter(0) + tensor_xor(quarter(1), 1)) + (
        tensor_xor(quarter(2), 2) + tensor_xor(quarter(3), 3)
    )

    small = after(small, row_far_got, second_mine)
    summed = (small + tensor_xor(small, 1)) + (tensor_xor(small, 2) + tensor_xor(small, 3))
    grad_norm_gain = jnp.concatenate([summed[6], summed[7, :512]])
    return (
        hidden_out,
        grad_hidden,
        grad_norm_gain,
        grad_proj_zx,
        grad_proj_shared,
        grad_proj_step,
        small[:5, :width],
        summed[:5, width:],
        small[7, 512 : 512 + heads],
        small[7, 640 : 640 + heads],
        small[7, 768 : 768 + heads],
        small[5, :width],
        grad_proj_out,
    )


def solution(mesh):
    fine = Mesh(mesh.devices.reshape(4, 4, 2, 2, 2), DP + TENSOR)
    both = DP + TENSOR
    return jax.shard_map(
        per_device,
        mesh=fine,
        in_specs=(
            P(both, None),
            P(),
            P(DP, None, TENSOR),
            P(both, None),
            P(DP, TENSOR),
            P(None, TENSOR),
            P(),
            P(TENSOR),
            P(TENSOR),
            P(TENSOR),
            P(TENSOR),
            P(TENSOR, DP),
            P(both, None),
            P(DP),
        ),
        out_specs=(
            P(both, None),
            P(both, None),
            P(),
            P(DP, None, TENSOR),
            P(both, None),
            P(DP, TENSOR),
            P(None, TENSOR),
            P(),
            P(TENSOR),
            P(TENSOR),
            P(TENSOR),
            P(TENSOR),
            P(TENSOR, DP),
        ),
        check_vma=False,
    )
```

```python
import jax
import jax.numpy as jnp
from jax import lax
from jax.experimental import pallas as pl
from jax.experimental.pallas import tpu as pltpu
from jax.sharding import Mesh
from jax.sharding import PartitionSpec as P

EPS = 1e-05
DP = ("y", "x", "zl")
TENSOR = ("zh", "c")
SIZES = {"y": 4, "x": 4, "zl": 2, "zh": 2, "c": 2}

F32 = jnp.float32
BF16 = jnp.bfloat16
HIGH = lax.Precision.HIGHEST
BLOCK = 256
VMEM = 56 * 1024 * 1024
PARAMS = pltpu.CompilerParams(vmem_limit_bytes=VMEM)
NT = (((1,), (1,)), ((), ()))
TN = (((0,), (0,)), ((), ()))
VMEM_SPEC = pl.BlockSpec(memory_space=pltpu.VMEM)


def cost(us):
    return pl.CostEstimate(flops=int(us * 1e6), transcendentals=0, bytes_accessed=int(us * 3e3))


def whole(shape):
    return pl.BlockSpec(shape, lambda *i: (0,) * len(shape))


def column_block(rows, width, index):
    return pl.BlockSpec((rows, width), lambda *i: (0, index))


def first_specs(rows):
    return [column_block(rows, 384, index) for index in (2, 3, 4)]


def out_specs_of(rows):
    return [column_block(rows, 384, index) for index in (5, 6)]


def dot(a, b):
    return jnp.dot(a, b, preferred_element_type=F32)


def dot_nt(a, b):
    return lax.dot_general(a, b, NT, preferred_element_type=F32)


def sigmoid(a):
    return 0.5 * jnp.tanh(0.5 * a) + 0.5


def softplus(a):
    return jnp.maximum(a, 0.0) + jnp.log1p(jnp.exp(-jnp.abs(a)))


def conv_strip(ext, taps, aux, j):
    n = ext.shape[0] - 8
    lanes = slice(j * 128, (j + 1) * 128)
    total = taps[4:5, lanes] + taps[3:4, lanes] * ext[8 : 8 + n, lanes]
    for back in (1, 2, 3):
        total += taps[3 - back : 4 - back, lanes] * (
            aux[:, back - 1 : back] * ext[8 - back : 8 - back + n, lanes]
        )
    return total


def two_parts(value):
    high = value.astype(BF16)
    return jnp.concatenate([high, (value - high.astype(F32)).astype(BF16)], 1)


def spread_heads(cols, table):
    return dot(two_parts(cols), table)


def scan_forward_kernel(tok, rows, gate_w, out_a, out_b, weights_a, weights_b, weights_c, taps, heads, chan, gain, spread, aux, segrow, pre_out, scan_out, state_out, gate_out, mixed_out, sums_out, ext, act, carry, fed):
    n = tok.shape[0]
    pairs = carry.shape[1] // 128

    @pl.when(pl.program_id(0) == 0)
    def _():
        carry[...] = jnp.zeros_like(carry)
        ext[0:8, :] = jnp.zeros((8, ext.shape[1]), F32)

    pre = jnp.concatenate([dot(tok[...], w[...]) for w in (weights_a, weights_b, weights_c)], 1)
    pre_out[...] = pre
    wide = ext.shape[1]
    ext[8:, :] = pre[:, :wide]
    marks = aux[...]
    for j in range(wide // 128):
        total = conv_strip(ext, taps, marks, j)
        act[:, j * 128 : (j + 1) * 128] = total * sigmoid(total)
    ext[0:8, :] = ext[n : n + 8, :]

    step = softplus(pre[:, wide:] + heads[0:1, :])
    log_step = -step * heads[1:2, :]
    row = lax.broadcasted_iota(jnp.int32, (n, n), 0)
    col = lax.broadcasted_iota(jnp.int32, (n, n), 1)
    lower = (row >= col).astype(F32)
    cum = jnp.dot(lower, log_step, precision=HIGH, preferred_element_type=F32)
    cum_t = cum.T
    write = act[:, pairs * 128 : (pairs + 1) * 128]
    read = act[:, (pairs + 1) * 128 : (pairs + 2) * 128].astype(BF16)
    write_t = write.T.astype(BF16)
    allowed = (row >= col) & (marks[:, 8:9] == segrow[0:1, :])
    inner = jnp.where(allowed, dot(read, write_t), 0.0)
    last = cum[n - 1 : n, :]
    enters = jnp.exp(cum) * marks[:, 3:4]
    to_end = jnp.exp(last - cum) * marks[:, 4:5]
    keep = jnp.exp(last) * marks[n - 1 : n, 3:4]
    wide_cols = spread_heads(jnp.concatenate([step, enters, to_end, jnp.broadcast_to(keep, (8, 128))], 0), spread[...])
    held = carry[...]
    held_low = held.astype(BF16)
    state_out[0] = held_low
    from_state = dot(read, held_low)
    low_half = lax.broadcasted_iota(jnp.int32, (1, 128), 1) < 64
    for j in range(pairs):
        lanes = slice(j * 128, (j + 1) * 128)
        x = act[:, lanes]
        xdt = x * wide_cols[:n, lanes]
        parts = []
        for h in (2 * j, 2 * j + 1):
            decay = jnp.exp(jnp.minimum(cum[:, h : h + 1] - cum_t[h : h + 1, :], 0.0))
            parts.append((decay * inner).astype(BF16))
        xdt_low = xdt.astype(BF16)
        zero = jnp.zeros_like(xdt_low)
        pair = jnp.concatenate([jnp.where(low_half, xdt_low, zero), jnp.where(low_half, zero, xdt_low)], 0)
        y = dot(jnp.concatenate(parts, 1), pair)
        if j % 2 == 0:
            block = slice(128 * j, 128 * j + 256)
            gate_out[:, block] = dot(tok[...], gate_w[:, block])
        else:
            spot = 256 * (j // 2)
            out_w = (out_a[:, 0:256], jnp.concatenate([out_a[:, 256:], out_b[:, :128]], 1), out_b[:, 128:])[j // 2]
            mixed_out[:, spot : spot + 256] = dot(rows[...], out_w)
        y += wide_cols[n : 2 * n, lanes] * from_state[:, lanes] + chan[0:1, lanes] * x
        scan_out[:, lanes] = y
        fed[:, lanes] = (xdt * wide_cols[2 * n : 3 * n, lanes]).astype(BF16)
        carry[:, lanes] = held[:, lanes] * wide_cols[3 * n : 3 * n + 1, lanes]
    carry[...] += dot(write_t, fed[...])

    gate_pre = gate_out[...]
    grad_mixed = mixed_out[...]
    gated = scan_out[...] * (gate_pre * sigmoid(gate_pre))
    square = jnp.sum(gated * gated, axis=1, keepdims=True)
    inner = jnp.sum(grad_mixed * gain[0:1, :] * gated, axis=1, keepdims=True)
    lane = lax.broadcasted_iota(jnp.int32, (1, 128), 1)
    cols = jnp.where(lane == 0, square, jnp.where(lane == 1, inner, 0.0))
    sums_out[...] = cols.T[0:8, :]


def scan_backward_kernel(me, pre, pre_before, taps, heads, chan, sums, spread, aux, segrow, grad, state, tok, grad_gate, weights, norm_gain, gain_sums, *rest):
    row_outs, outs_a, outs_b = rest[:4], rest[4:8], rest[8:12]
    packed, ext, gext, act, slope, carry, fed, back, rows, low_out, taps_out, heads_out, gains, all_tok, all_low, split = rest[12:]
    n = pre.shape[0]
    pairs = carry.shape[1] // 128
    wide = ext.shape[1]
    gate_width = grad_gate.shape[1]

    @pl.when(pl.program_id(0) == 0)
    def _():
        carry[...] = jnp.zeros_like(carry)
        gext[n:, :] = jnp.zeros((8, wide), F32)
        taps_out[...] = jnp.zeros_like(taps_out)
        heads_out[...] = jnp.zeros_like(heads_out)
        rows[...] = jnp.zeros_like(rows)
        gains[...] = jnp.zeros_like(gains)

    marks = aux[...]
    ext[0:8, :] = pre_before[:, :wide]
    ext[8:, :] = pre[:, :wide]
    for j in range(wide // 128):
        lanes = slice(j * 128, (j + 1) * 128)
        total = conv_strip(ext, taps, marks, j)
        sig = sigmoid(total)
        value = total * sig
        act[:, lanes] = value
        slope[:, lanes] = sig + value * (1.0 - sig)

    step_arg = pre[:, wide:] + heads[0:1, :]
    step = softplus(step_arg)
    rate = heads[1:2, :]
    row = lax.broadcasted_iota(jnp.int32, (n, n), 0)
    col = lax.broadcasted_iota(jnp.int32, (n, n), 1)
    lower = (row >= col).astype(F32)
    cum = jnp.dot(lower, -step * rate, precision=HIGH, preferred_element_type=F32)
    cum_t = cum.T
    write = act[:, pairs * 128 : (pairs + 1) * 128]
    read = act[:, (pairs + 1) * 128 : (pairs + 2) * 128]
    read_t = read.T.astype(BF16)
    write_low = write.astype(BF16)
    read_low = read.astype(BF16)
    allowed = (row <= col) & (marks[:, 8:9] == segrow[0:1, :])
    inner_t = jnp.where(allowed, dot(write_low, read_t), 0.0)
    last = cum[n - 1 : n, :]
    enters = jnp.exp(cum) * marks[:, 3:4]
    to_end = jnp.exp(last - cum) * marks[:, 4:5]
    keep = jnp.exp(last) * marks[n - 1 : n, 3:4]
    wide_cols = spread_heads(jnp.concatenate([step, enters, to_end, jnp.broadcast_to(keep, (8, 128))], 0), spread[...])
    held = state[0]
    later = carry[...]
    later_low = later.astype(BF16)
    from_state = dot(read_low, held)
    from_later = dot(write_low, later_low)
    low_half = lax.broadcasted_iota(jnp.int32, (1, 128), 1) < 64
    head_lane = lax.broadcasted_iota(jnp.int32, (1, 128), 1)
    grad_inner = jnp.zeros((n, n), F32)
    col_sums = jnp.zeros((n, 128), F32)
    to_end_part = jnp.zeros((n, 128), F32)
    enter_part = jnp.zeros((n, 128), F32)
    step_part = jnp.zeros((n, 128), F32)
    skip_part = jnp.zeros((n, 128), F32)
    keep_part = jnp.zeros((8, 128), F32)

    def head_sums(value, j):
        return dot(two_parts(value), sums[j])

    for j in range(pairs):
        lanes = slice(j * 128, (j + 1) * 128)
        x = act[:, lanes]
        dy = grad[:, lanes].astype(F32)
        step_wide = wide_cols[:n, lanes]
        xdt = x * step_wide
        xdt_low = xdt.astype(BF16)
        dy_low = dy.astype(BF16)
        zero = jnp.zeros_like(xdt_low)
        products = dot_nt(
            jnp.concatenate([jnp.where(low_half, xdt_low, zero), jnp.where(low_half, zero, xdt_low)], 0),
            dy_low,
        )
        parts = []
        for k, h in enumerate((2 * j, 2 * j + 1)):
            product = products[k * n : (k + 1) * n, :]
            decay = jnp.exp(jnp.minimum(cum_t[h : h + 1, :] - cum[:, h : h + 1], 0.0))
            scaled = decay * product
            grad_inner += scaled
            weighted = scaled * inner_t
            rows[h : h + 1, :] = jnp.sum(weighted, axis=0, keepdims=True)
            col_sums += jnp.where(head_lane == h, jnp.sum(weighted, axis=1, keepdims=True), 0.0)
            parts.append((decay * inner_t).astype(BF16))
        grad_pair = jnp.concatenate([jnp.where(low_half, dy_low, zero), jnp.where(low_half, zero, dy_low)], 0)
        grad_xdt = dot(jnp.concatenate(parts, 1), grad_pair)
        end_wide = wide_cols[2 * n : 3 * n, lanes]
        enter_wide = wide_cols[n : 2 * n, lanes]
        later_part = end_wide * from_later[:, lanes]
        grad_xdt += later_part
        to_end_part += head_sums(later_part * xdt, j)
        fed[:, lanes] = (xdt * end_wide).astype(BF16)
        grad_enter = dy * enter_wide
        back[:, lanes] = grad_enter.astype(BF16)
        enter_part += head_sums(grad_enter * from_state[:, lanes], j)
        step_part += head_sums(grad_xdt * x, j)
        skip_part += head_sums(dy * x, j)
        kept = jnp.sum(held[:, lanes].astype(F32) * later[:, lanes], axis=0, keepdims=True)
        keep_part += head_sums(jnp.broadcast_to(kept, (8, 128)), j)
        act[:, lanes] = grad_xdt * step_wide + chan[0:1, lanes] * dy
        carry[:, lanes] = later[:, lanes] * wide_cols[3 * n : 3 * n + 1, lanes]

    grad_cum = rows[...].T - col_sums + enter_part - to_end_part
    grad_last = jnp.sum(to_end_part, axis=0, keepdims=True) + keep * keep_part[0:1, :]
    upper = (row <= col).astype(F32)
    grad_log = jnp.dot(upper, grad_cum, precision=HIGH, preferred_element_type=F32) + grad_last
    grad_step = (step_part - rate * grad_log) * sigmoid(step_arg)
    heads_out[0:1, :] += jnp.sum(grad_step, axis=0, keepdims=True)
    heads_out[1:2, :] += -rate * jnp.sum(step * grad_log, axis=0, keepdims=True)
    heads_out[2:3, :] += jnp.sum(skip_part, axis=0, keepdims=True)
    low_out[:, gate_width + wide :] = grad_step.astype(BF16)

    grad_inner = jnp.where(allowed, grad_inner, 0.0)
    act[:, pairs * 128 : (pairs + 1) * 128] = dot(grad_inner.astype(BF16), read_low) + dot_nt(fed[...], later_low)
    act[:, (pairs + 1) * 128 : (pairs + 2) * 128] = dot(grad_inner.T.astype(BF16), write_low) + dot_nt(back[...], held)
    carry[...] += dot(read_t, back[...])

    for j in range(wide // 128):
        lanes = slice(j * 128, (j + 1) * 128)
        grad_pre = act[:, lanes] * slope[:, lanes]
        gext[0:n, lanes] = grad_pre
        total = taps[3:4, lanes] * grad_pre
        taps_out[3:4, lanes] += jnp.sum(grad_pre * ext[8 : 8 + n, lanes], axis=0, keepdims=True)
        taps_out[4:5, lanes] += jnp.sum(grad_pre, axis=0, keepdims=True)
        for by in (1, 2, 3):
            total += taps[3 - by : 4 - by, lanes] * (marks[:, 4 + by : 5 + by] * gext[by : by + n, lanes])
            taps_out[3 - by : 4 - by, lanes] += jnp.sum(
                grad_pre * (marks[:, by - 1 : by] * ext[8 - by : 8 - by + n, lanes]), axis=0, keepdims=True
            )
        low_out[:, gate_width + j * 128 : gate_width + (j + 1) * 128] = total.astype(BF16)
    gext[n:, :] = gext[0:8, :]

    step_id = pl.program_id(0)
    low_out[:, : grad_gate.shape[1]] = grad_gate[...]
    token_grad = dot_nt(low_out[...], weights[...])
    gains[0:1, :] += jnp.sum(token_grad * tok[...].astype(F32), axis=0, keepdims=True)
    place = pl.ds(pl.multiple_of((3 - step_id) * n, n), n)
    all_tok[place, :] = tok[...]
    all_low[place, :] = low_out[:, grad_gate.shape[1] :]
    token_low = token_grad.astype(BF16)
    for k in range(4):

        @pl.when((me[0] ^ (3 - k)) == 3 - step_id)
        def _():
            row_outs[k][...] = token_low

    @pl.when(step_id == 3)
    def _():
        cut = outs_a[0].shape[2]
        deep = outs_a[0].shape[1]
        for k in range(4):
            first = pl.multiple_of(((me[1] + k) % 4) * (4 * deep), 128)
            grad_rows = lax.dot_general(
                all_tok[:, pl.ds(first, 4 * deep)], all_low[...], TN, preferred_element_type=F32
            ).astype(BF16)
            outs_a[k][...] = grad_rows[:, :cut].reshape(outs_a[k].shape)
            split[...] = grad_rows[:, cut:]
            y = (me[1] + k) % 4
            for d in range(4):
                start = pl.multiple_of(((me[2] + d) % 4) * deep, 16)
                outs_b[d][y] = split[pl.ds(start, deep), :]
        width = gain_sums.shape[1]
        by_gain = gains[0:1, :] / norm_gain[0:1, :]
        packed[0:5, :] = taps_out[0:5, :]
        packed[5:6, :width] = gain_sums[0:1, :]
        packed[5:6, width:] = jnp.zeros((1, 1024 - width), F32)
        packed[6:7, :] = by_gain[:, :1024]
        packed[7:8, :512] = by_gain[:, 1024:]
        for r in range(3):
            packed[7:8, 512 + 128 * r : 640 + 128 * r] = heads_out[r : r + 1, :]
        packed[7:8, 896:] = jnp.zeros((1, 128), F32)


def scan_marks(segments):
    length = segments.shape[0]
    blocks = segments.reshape(-1, BLOCK)
    before = jnp.concatenate([jnp.full((1,), -1, jnp.int32), blocks[:-1, -1]], 0)

    def same(by):
        if by > 0:
            other = jnp.concatenate([jnp.full((by,), -1, jnp.int32), segments[:-by]], 0)
        else:
            other = jnp.concatenate([segments[-by:], jnp.full((-by,), -1, jnp.int32)], 0)
        return other == segments

    cols = [same(1), same(2), same(3), (blocks == before[:, None]).reshape(-1), (blocks == blocks[:, -1:]).reshape(-1)]
    cols += [same(-1), same(-2), same(-3), segments]
    marks = jnp.stack([c.astype(F32) for c in cols], 1)
    return jnp.pad(marks, ((0, 0), (0, 128 - len(cols)))), jnp.broadcast_to(segments.astype(F32), (8, length))


def scan_forward(tokens, grad_rows, weights, taps, heads, chan, gain, spread, marks, segrow):
    length, model = tokens.shape
    cols = 1152
    inner = cols - 384
    wide = cols - 128
    n = BLOCK
    blocks = length // n


    return pl.pallas_call(
        scan_forward_kernel,
        grid=(blocks,),
        in_specs=[
            pl.BlockSpec((n, model), lambda i: (i, 0)),
            pl.BlockSpec((n, model), lambda i: (i, 0)),
            column_block(model, inner, 0),
            *out_specs_of(model),
            *first_specs(model),
            whole((8, wide)),
            whole((8, 128)),
            whole((8, inner)),
            whole((8, inner)),
            whole((256, inner)),
            pl.BlockSpec((n, 128), lambda i: (i, 0)),
            pl.BlockSpec((8, n), lambda i: (0, i)),
        ],
        out_specs=[
            pl.BlockSpec((n, cols), lambda i: (i, 0)),
            pl.BlockSpec((n, inner), lambda i: (i, 0)),
            pl.BlockSpec((1, 128, inner), lambda i: (i, 0, 0)),
            pl.BlockSpec((n, inner), lambda i: (i, 0)),
            pl.BlockSpec((n, inner), lambda i: (i, 0)),
            pl.BlockSpec((8, n), lambda i: (0, i)),
        ],
        out_shape=[
            jax.ShapeDtypeStruct((length, cols), F32),
            jax.ShapeDtypeStruct((length, inner), F32),
            jax.ShapeDtypeStruct((blocks, 128, inner), BF16),
            jax.ShapeDtypeStruct((length, inner), F32),
            jax.ShapeDtypeStruct((length, inner), F32),
            jax.ShapeDtypeStruct((8, length), F32),
        ],
        scratch_shapes=[
            pltpu.VMEM((n + 8, wide), F32),
            pltpu.VMEM((n, wide), F32),
            pltpu.VMEM((128, inner), F32),
            pltpu.VMEM((n, inner), BF16),
        ],
        compiler_params=PARAMS,
        cost_estimate=cost(20),
        name="scan_forward",
    )(tokens, grad_rows, weights, weights, weights, weights, weights, weights, taps, heads, chan, gain, spread, marks, segrow)


def scan_backward(pre, taps, heads, chan, sums, spread, marks, segrow, grad, states, tokens, grad_gate, weights, norm_gain, gain_sums, me):
    length, cols = pre.shape
    model = tokens.shape[1]
    inner = cols - 384
    wide = cols - 128
    n = BLOCK
    blocks = length // n
    cut = 640
    shape_a, shape_b = (4, model // 16, cut), (4, model // 16, cols - cut)

    def rev(i):
        return blocks - 1 - i

    def rows(width):
        return pl.BlockSpec((n, width), lambda i, me: (rev(i), 0))

    return pl.pallas_call(
        scan_backward_kernel,
        grid_spec=pltpu.PrefetchScalarGridSpec(
            num_scalar_prefetch=1,
            grid=(blocks,),
            in_specs=[
                rows(cols),
                pl.BlockSpec((8, cols), lambda i, me: (jnp.maximum(rev(i) * (n // 8) - 1, 0), 0)),
                whole((8, wide)),
                whole((8, 128)),
                whole((8, inner)),
                whole((inner // 128, 256, 128)),
                whole((256, inner)),
                rows(128),
                pl.BlockSpec((8, n), lambda i, me: (0, rev(i))),
                rows(inner),
                pl.BlockSpec((1, 128, inner), lambda i, me: (rev(i), 0, 0)),
                rows(model),
                rows(inner),
                column_block(model, inner + cols, 0),
                whole(norm_gain.shape),
                whole(gain_sums.shape),
            ],
            out_specs=[whole((n, model))] * 4 + [whole(shape_a)] * 4 + [whole(shape_b)] * 4 + [whole((8, 1024))],
            scratch_shapes=[
                pltpu.VMEM((n + 8, wide), F32),
                pltpu.VMEM((n + 8, wide), F32),
                pltpu.VMEM((n, wide), F32),
                pltpu.VMEM((n, wide), F32),
                pltpu.VMEM((128, inner), F32),
                pltpu.VMEM((n, inner), BF16),
                pltpu.VMEM((n, inner), BF16),
                pltpu.VMEM((128, n), F32),
                pltpu.VMEM((n, inner + cols), BF16),
                pltpu.VMEM((8, wide), F32),
                pltpu.VMEM((8, 128), F32),
                pltpu.VMEM((8, model), F32),
                pltpu.VMEM((length, model), BF16),
                pltpu.VMEM((length, cols), BF16),
                pltpu.VMEM((model // 4, cols - cut), BF16),
            ],
        ),
        out_shape=[jax.ShapeDtypeStruct((n, model), BF16)] * 4
        + [jax.ShapeDtypeStruct(shape_a, BF16)] * 4
        + [jax.ShapeDtypeStruct(shape_b, BF16)] * 4
        + [jax.ShapeDtypeStruct((8, 1024), F32)],
        compiler_params=PARAMS,
        cost_estimate=cost(30),
        name="scan_backward",
    )(me, pre, pre, taps, heads, chan, sums, spread, marks, segrow, grad, states, tokens, grad_gate, weights, norm_gain, gain_sums)


def spread_table(inner):
    head = jnp.arange(inner) // 64
    return (jnp.arange(256)[:, None] % 128 == head[None, :]).astype(BF16)


def head_sum_table(inner):
    pairs = inner // 128
    lane = jnp.arange(256) % 128
    head = 2 * jnp.arange(pairs)[:, None] + (lane >= 64)[None, :]
    return (head[:, :, None] == jnp.arange(128)[None, None, :]).astype(BF16)


def store_block(value, outs):
    for k, out in enumerate(outs):

        @pl.when(pl.program_id(0) == k)
        def _():
            out[...] = value


def mix_second_kernel(channels, me, sums, gate, grad_mixed_in, scanned_in, out_a, out_b, gain, low_out, grad_scan, grad_gate, gain_out, *outs):
    n = gate.shape[0]

    @pl.when(pl.program_id(0) == 0)
    def _():
        gain_out[...] = jnp.zeros_like(gain_out)

    cols = jnp.concatenate([sums[...], jnp.zeros((120, n), F32)], 0).T
    scale = lax.rsqrt(cols[:, 0:1] / channels + EPS)
    pull = scale * scale * scale * (cols[:, 1:2] / channels)
    gate_pre = gate[...]
    grad_mixed = grad_mixed_in[...]
    scanned = scanned_in[...]
    sig = sigmoid(gate_pre)
    silu = gate_pre * sig
    gated = scanned * silu
    scaled = gated * scale
    mixed = (scaled * gain[0:1, :]).astype(BF16)
    low_out[...] = mixed
    gain_out[0:1, :] += jnp.sum(grad_mixed * scaled, axis=0, keepdims=True)
    grad_gated = scale * gain[0:1, :] * grad_mixed - gated * pull
    grad_scan[...] = grad_gated * silu
    grad_gate[...] = (grad_gated * scanned * (sig + silu * (1.0 - sig))).astype(BF16)
    projected = dot_nt(mixed[:, :384], out_a[...]) + dot_nt(mixed[:, 384:], out_b[...])
    store_block(projected.astype(BF16), outs)


def mix_second(sums, gate, grad_mixed, scanned, second, gain, channels, spot):
    length, width = gate.shape
    model = second.shape[0]
    n = 256

    def rows(cols):
        return pl.BlockSpec((n, cols), lambda i, me: (me[0] ^ (3 - i), 0))

    return pl.pallas_call(
        lambda *refs: mix_second_kernel(channels, *refs),
        grid_spec=pltpu.PrefetchScalarGridSpec(
            num_scalar_prefetch=1,
            grid=(4,),
            in_specs=[
                pl.BlockSpec((8, n), lambda i, me: (0, me[0] ^ (3 - i))),
                rows(width),
                rows(width),
                rows(width),
                *out_specs_of(model),
                whole((8, width)),
            ],
            out_specs=[rows(width), rows(width), rows(width), whole((8, width))] + [whole((n, model))] * 4,
        ),
        out_shape=[
            jax.ShapeDtypeStruct((length, width), BF16),
            jax.ShapeDtypeStruct((length, width), F32),
            jax.ShapeDtypeStruct((length, width), BF16),
            jax.ShapeDtypeStruct((8, width), F32),
        ]
        + [jax.ShapeDtypeStruct((n, model), BF16)] * 4,
        compiler_params=PARAMS,
        cost_estimate=cost(11),
        name="mix_second",
    )(spot, sums, gate, grad_mixed, scanned, second, second, gain)


def second_grads_kernel(tok, rows, grad_gate, mixed, out):
    width = grad_gate.shape[1]
    gate_part = lax.dot_general(tok[...], grad_gate[...], TN, preferred_element_type=F32)
    out_part = lax.dot_general(rows[...], mixed[...], TN, preferred_element_type=F32)
    out[:, :width] = gate_part.astype(BF16)
    out[:, width:] = out_part.astype(BF16)


def second_grads(tokens, grad_rows, grad_gate, mixed):
    length, model = tokens.shape
    width = grad_gate.shape[1]
    n = model // 4
    cols = pl.BlockSpec((length, n), lambda i: (0, i))
    return pl.pallas_call(
        second_grads_kernel,
        grid=(4,),
        in_specs=[cols, cols, whole((length, width)), whole((length, width))],
        out_specs=pl.BlockSpec((n, 2 * width), lambda i: (i, 0)),
        out_shape=jax.ShapeDtypeStruct((model, 2 * width), BF16),
        compiler_params=PARAMS,
        cost_estimate=cost(8),
        name="second_grads",
    )(tokens, grad_rows, grad_gate, mixed)


def four_sum(own, ahead, across, behind):
    return (own.astype(F32) + across.astype(F32)) + (ahead.astype(F32) + behind.astype(F32))


def add_split_kernel(me, *refs):
    ins, outs = refs[:8], refs[8:]
    for half in range(2):
        for d in range(4):
            e = (me[half] + d) % 4
            outs[4 * half + d][...] = four_sum(*[part[e] for part in ins[4 * half : 4 * half + 4]]).astype(BF16)


def add_split(parts_a, parts_b, me):
    shapes = [jax.ShapeDtypeStruct(parts[0].shape[1:], BF16) for parts in (parts_a, parts_b) for _ in range(4)]
    outs = pl.pallas_call(
        add_split_kernel,
        in_specs=[pl.BlockSpec(memory_space=pltpu.SMEM)] + [VMEM_SPEC] * 8,
        out_specs=[VMEM_SPEC] * 8,
        out_shape=shapes,
        compiler_params=PARAMS,
        name="add_split",
    )(me, *parts_a, *parts_b)
    return outs[:4], outs[4:]


def add_halve_kernel(me, *refs):
    ins, (keep, give, total) = refs[:8], refs[8:]
    cut = ins[0].shape[1]
    total[:, :cut] = four_sum(*[part[...] for part in ins[:4]])
    total[:, cut:] = four_sum(*[part[...] for part in ins[4:]])
    n = keep.shape[0]
    keep[...] = total[pl.ds(pl.multiple_of(me[0] * n, 16), n), :]
    give[...] = total[pl.ds(pl.multiple_of((1 - me[0]) * n, 16), n), :].astype(BF16)


def add_halve(parts_a, parts_b, me):
    rows = parts_a[0].shape[0]
    width = parts_a[0].shape[1] + parts_b[0].shape[1]
    return pl.pallas_call(
        add_halve_kernel,
        in_specs=[pl.BlockSpec(memory_space=pltpu.SMEM)] + [VMEM_SPEC] * 8,
        out_specs=[VMEM_SPEC] * 2,
        out_shape=[
            jax.ShapeDtypeStruct((rows // 2, width), F32),
            jax.ShapeDtypeStruct((rows // 2, width), BF16),
        ],
        scratch_shapes=[pltpu.VMEM((rows, width), F32)],
        compiler_params=PARAMS,
        name="add_halve",
    )(me, *parts_a, *parts_b)


def place_kernel(me, *refs):
    out = refs[-1]
    for k, part in enumerate(refs[:-1]):

        @pl.when(pl.program_id(0) == k)
        def _():
            out[...] = part[...].reshape(out.shape)


def place(parts, index, me, shape, block, name):
    return pl.pallas_call(
        place_kernel,
        grid_spec=pltpu.PrefetchScalarGridSpec(
            num_scalar_prefetch=1,
            grid=(len(parts),),
            in_specs=[whole(p.shape) for p in parts],
            out_specs=pl.BlockSpec(block, lambda i, me: index(i, me[0])),
        ),
        out_shape=jax.ShapeDtypeStruct(shape, parts[0].dtype),
        compiler_params=PARAMS,
        cost_estimate=cost(2),
        name=name,
    )(me, *parts)


def shift(value, axis, by):
    n = SIZES[axis]
    return lax.ppermute(value, axis, [(i, (i - by) % n) for i in range(n)])


def swap(value, axis):
    return shift(value, axis, 1)


def ring(value, axis):
    return [value, shift(value, axis, 1), shift(value, axis, 2), shift(value, axis, -1)]


def sends(blocks, axis):
    return [blocks[0], shift(blocks[1], axis, -1), shift(blocks[2], axis, 2), shift(blocks[3], axis, 1)]


def tensor_xor(value, by):
    return lax.ppermute(value, TENSOR, [(i, i ^ by) for i in range(4)])


def sum_ring(value, axis):
    own, ahead, across, behind = ring(value, axis)
    return (own + across) + (ahead + behind)


def sum_pair(value, axis):
    return value + swap(value, axis)


def after(value, *others):
    return lax.optimization_barrier((value,) + others)[0]


def index_of(axis):
    return lax.axis_index(axis).reshape(1).astype(jnp.int32)


def pair_kernel(me, main, other_main, side, other_side, out):
    cut, middle = 1536, side.shape[1]
    for k, (left, right) in enumerate(((main, side), (other_main, other_side))):

        @pl.when(pl.program_id(0) == k)
        def _():
            out[:, :cut] = left[:, :cut]
            out[:, cut : cut + middle] = right[...]
            out[:, cut + middle :] = left[:, cut:]


def pair_rows(main, side):
    rows = main.shape[0]
    width = main.shape[1] + side.shape[1]
    parts = [main, swap(main, "zl"), side, swap(side, "zl")]
    return pl.pallas_call(
        pair_kernel,
        grid_spec=pltpu.PrefetchScalarGridSpec(
            num_scalar_prefetch=1,
            grid=(2,),
            in_specs=[whole(p.shape) for p in parts],
            out_specs=pl.BlockSpec((rows, width), lambda i, me: ((me[0] + i) % 2, 0)),
        ),
        out_shape=jax.ShapeDtypeStruct((2 * rows, width), BF16),
        compiler_params=PARAMS,
        name="pair_rows",
    )(index_of("zl"), *parts)


def token_place(own, near, far, both, me):
    rows, width = own.shape
    return place([own, near, far, both], lambda i, me: (me ^ i, 0), me, (4 * rows, width), (rows, width), "place_tokens")


def per_device(
    hidden_in,
    norm_gain,
    proj_zx,
    proj_shared,
    proj_step,
    conv_inner,
    conv_shared,
    step_bias,
    decay_log,
    skip_gain,
    gated_gain,
    proj_out,
    out_grad,
    segments,
):
    model_width = hidden_in.shape[1]
    width = proj_zx.shape[2]
    heads = step_bias.shape[0]
    me = {axis: index_of(axis) for axis in DP + TENSOR}
    spot = 2 * me["zh"] + me["c"]

    shared_parts = [proj_shared] + [tensor_xor(proj_shared, by) for by in (1, 2, 3)]
    shared_rows = jnp.zeros((48, 256), BF16)
    for by, part in enumerate(shared_parts):
        shared_rows = lax.dynamic_update_slice(shared_rows, part, (((spot[0] ^ by) * 12), jnp.int32(0)))
    side_rows = jnp.concatenate([shared_rows, jnp.pad(proj_step, ((0, 0), (0, 128 - heads)))], 1)
    main_rows = jnp.concatenate([proj_zx[:, 0, :], proj_zx[:, 1, :], proj_out.T], 1)
    weights = lax.all_gather(pair_rows(main_rows, side_rows), ("y", "x"), axis=0, tiled=True)

    residual_in = hidden_in.astype(F32)
    scale_in = lax.rsqrt(jnp.mean(residual_in * residual_in, axis=-1, keepdims=True) + EPS)
    normed_low = (residual_in * scale_in * norm_gain).astype(BF16)
    normed_far = swap(normed_low, "zh")
    normed_near = swap(normed_low, "c")

    normed_both = swap(normed_far, "c")
    tokens = token_place(normed_low, normed_near, normed_far, normed_both, spot)
    grad_far = swap(after(out_grad, normed_far), "zh")
    grad_near = swap(after(out_grad, normed_far), "c")
    grad_both = swap(grad_far, "c")
    grad_rows = token_place(out_grad, grad_near, grad_far, grad_both, spot)

    pad = (0, 128 - heads)
    head_rows = jnp.stack([jnp.pad(step_bias, pad), jnp.pad(jnp.exp(decay_log), pad)], 0)
    head_rows = jnp.pad(head_rows, ((0, 6), (0, 0)))
    taps = jnp.pad(jnp.concatenate([conv_inner, conv_shared], 1), ((0, 3), (0, 0)))
    chan = jnp.broadcast_to(jnp.repeat(skip_gain, width // heads), (8, width))
    gain = jnp.broadcast_to(gated_gain, (8, width))
    norm_rows = jnp.broadcast_to(norm_gain, (8, model_width))
    marks, segrow = scan_marks(segments)
    spread = spread_table(width)
    sum_table = head_sum_table(width)
    tokens, grad_rows = lax.optimization_barrier((tokens, grad_rows))
    pre, scanned, states, gate_pre, grad_mixed, sums = scan_forward(
        tokens, grad_rows, weights, taps, head_rows, chan, gain, spread, marks, segrow
    )

    sums = lax.psum(sums, TENSOR)
    mixed_low, grad_scanned, gate_grad_low, gain_sums, *out_blocks = mix_second(
        sums, gate_pre, grad_mixed, scanned, weights, gain, 4 * width, spot
    )
    out_far = (out_blocks[1].astype(F32) + swap(out_blocks[0], "c").astype(F32)).astype(BF16)
    out_near = swap(out_blocks[2], "c")
    second_total = second_grads(tokens, grad_rows, gate_grad_low, mixed_low)
    second_sum = lax.psum_scatter(second_total, ("y", "x"), scatter_dimension=0, tiled=True)
    out_far_got = swap(out_far, "zh")

    grad_scanned = after(grad_scanned, out_far, second_total)
    *sent, small = scan_backward(
        pre,
        taps,
        head_rows,
        chan,
        sum_table,
        spread,
        marks,
        segrow,
        grad_scanned,
        states,
        tokens,
        gate_grad_low,
        weights,
        norm_rows,
        gain_sums,
        jnp.concatenate([spot, me["y"], me["x"]]),
    )
    row_blocks = [after(block, out_far_got, out_near) for block in sent[:4]]
    parts_a = sends(sent[4:8], "y")
    parts_b = sends(sent[8:], "x")
    far_got = swap(row_blocks[0], "c")
    row_far = (row_blocks[1].astype(F32) + far_got.astype(F32)).astype(BF16)
    row_far_got = swap(row_far, "zh")
    parts_a = [after(part, row_far) for part in parts_a]
    parts_b = [after(part, row_far) for part in parts_b]
    half_a, half_b = add_split(parts_a, parts_b, jnp.concatenate([me["x"], me["y"]]))
    near_got = swap(after(row_blocks[2], *half_a), "c")

    hidden_out = (
        residual_in + (out_blocks[3].astype(F32) + out_near.astype(F32) + out_far_got.astype(F32))
    ).astype(BF16)
    grad_normed = row_blocks[3].astype(F32) + near_got.astype(F32) + row_far_got.astype(F32)
    weighted = jnp.sum(grad_normed * norm_gain * residual_in, axis=-1, keepdims=True)
    grad_hidden = (
        out_grad.astype(F32)
        + scale_in * norm_gain * grad_normed
        - residual_in * scale_in**3 * weighted / model_width
    ).astype(BF16)
    parts_a = [after(part, row_far_got, second_sum) for part in sends(half_a, "x")]
    parts_b = [after(part, row_far_got, second_sum) for part in sends(half_b, "y")]
    first_keep, first_give = add_halve(parts_a, parts_b, me["zl"])
    first_mine = first_keep + swap(first_give, "zl").astype(F32)
    small = sum_ring(after(small, first_give), "y")
    small = sum_ring(small, "x")
    small = sum_pair(small, "zl")
    second_pairs = second_sum.reshape(2, 48, 2 * width)
    second_keep = lax.dynamic_index_in_dim(second_pairs, me["zl"][0], 0, keepdims=False)
    second_mine = second_keep.astype(F32) + swap(
        lax.dynamic_index_in_dim(second_pairs, 1 - me["zl"][0], 0, keepdims=False), "zl"
    ).astype(F32)
    grad_proj_out = second_mine[:, width:].T
    grad_proj_zx = jnp.stack([second_mine[:, :width], first_mine[:, :width]], 1)
    grad_proj_step = first_mine[:, width + 256 : width + 256 + heads]

    def quarter(by):
        return lax.dynamic_slice(first_mine, ((spot[0] ^ by) * 12, jnp.int32(width)), (12, 256))

    grad_proj_shared = (quarter(0) + tensor_xor(quarter(1), 1)) + (
        tensor_xor(quarter(2), 2) + tensor_xor(quarter(3), 3)
    )

    small = after(small, second_mine)
    summed = (small + tensor_xor(small, 1)) + (tensor_xor(small, 2) + tensor_xor(small, 3))
    grad_norm_gain = jnp.concatenate([summed[6], summed[7, :512]])
    return (
        hidden_out,
        grad_hidden,
        grad_norm_gain,
        grad_proj_zx,
        grad_proj_shared,
        grad_proj_step,
        small[:5, :width],
        summed[:5, width:],
        small[7, 512 : 512 + heads],
        small[7, 640 : 640 + heads],
        small[7, 768 : 768 + heads],
        small[5, :width],
        grad_proj_out,
    )


def solution(mesh):
    fine = Mesh(mesh.devices.reshape(4, 4, 2, 2, 2), DP + TENSOR)
    both = DP + TENSOR
    return jax.shard_map(
        per_device,
        mesh=fine,
        in_specs=(
            P(both, None),
            P(),
            P(DP, None, TENSOR),
            P(both, None),
            P(DP, TENSOR),
            P(None, TENSOR),
            P(),
            P(TENSOR),
            P(TENSOR),
            P(TENSOR),
            P(TENSOR),
            P(TENSOR, DP),
            P(both, None),
            P(DP),
        ),
        out_specs=(
            P(both, None),
            P(both, None),
            P(),
            P(DP, None, TENSOR),
            P(both, None),
            P(DP, TENSOR),
            P(None, TENSOR),
            P(),
            P(TENSOR),
            P(TENSOR),
            P(TENSOR),
            P(TENSOR),
            P(TENSOR, DP),
        ),
        check_vma=False,
    )
```

```python
import jax
import jax.numpy as jnp
from jax import lax
from jax.experimental import pallas as pl
from jax.experimental.pallas import tpu as pltpu
from jax.sharding import Mesh
from jax.sharding import PartitionSpec as P

EPS = 1e-05
DP = ("y", "x", "zl")
TENSOR = ("zh", "c")
SIZES = {"y": 4, "x": 4, "zl": 2, "zh": 2, "c": 2}

F32 = jnp.float32
BF16 = jnp.bfloat16
HIGH = lax.Precision.HIGHEST
BLOCK = 256
VMEM = 56 * 1024 * 1024
PARAMS = pltpu.CompilerParams(vmem_limit_bytes=VMEM)
NT = (((1,), (1,)), ((), ()))
TN = (((0,), (0,)), ((), ()))
VMEM_SPEC = pl.BlockSpec(memory_space=pltpu.VMEM)


def cost(us):
    return pl.CostEstimate(flops=int(us * 1e6), transcendentals=0, bytes_accessed=int(us * 3e3))


def whole(shape):
    return pl.BlockSpec(shape, lambda *i: (0,) * len(shape))


def column_block(rows, width, index):
    return pl.BlockSpec((rows, width), lambda *i: (0, index))


def first_specs(rows):
    return [column_block(rows, 384, index) for index in (2, 3, 4)]


def out_specs_of(rows):
    return [column_block(rows, 384, index) for index in (5, 6)]


def dot(a, b):
    return jnp.dot(a, b, preferred_element_type=F32)


def dot_nt(a, b):
    return lax.dot_general(a, b, NT, preferred_element_type=F32)


def sigmoid(a):
    return 0.5 * jnp.tanh(0.5 * a) + 0.5


def softplus(a):
    return jnp.maximum(a, 0.0) + jnp.log1p(jnp.exp(-jnp.abs(a)))


def conv_strip(ext, taps, aux, j):
    n = ext.shape[0] - 8
    lanes = slice(j * 128, (j + 1) * 128)
    total = taps[4:5, lanes] + taps[3:4, lanes] * ext[8 : 8 + n, lanes]
    for back in (1, 2, 3):
        total += taps[3 - back : 4 - back, lanes] * (
            aux[:, back - 1 : back] * ext[8 - back : 8 - back + n, lanes]
        )
    return total


def two_parts(value):
    high = value.astype(BF16)
    return jnp.concatenate([high, (value - high.astype(F32)).astype(BF16)], 1)


def spread_heads(cols, table):
    return dot(two_parts(cols), table)


def scan_forward_kernel(tok, rows, gate_w, out_a, out_b, weights_a, weights_b, weights_c, taps, heads, chan, gain, spread, aux, segrow, pre_out, scan_out, state_out, gate_out, mixed_out, sums_out, ext, act, carry, fed):
    n = tok.shape[0]
    pairs = carry.shape[1] // 128

    @pl.when(pl.program_id(0) == 0)
    def _():
        carry[...] = jnp.zeros_like(carry)
        ext[0:8, :] = jnp.zeros((8, ext.shape[1]), F32)

    pre = jnp.concatenate([dot(tok[...], w[...]) for w in (weights_a, weights_b, weights_c)], 1)
    pre_out[...] = pre
    wide = ext.shape[1]
    ext[8:, :] = pre[:, :wide]
    marks = aux[...]
    for j in range(wide // 128):
        total = conv_strip(ext, taps, marks, j)
        act[:, j * 128 : (j + 1) * 128] = total * sigmoid(total)
    ext[0:8, :] = ext[n : n + 8, :]

    step = softplus(pre[:, wide:] + heads[0:1, :])
    log_step = -step * heads[1:2, :]
    row = lax.broadcasted_iota(jnp.int32, (n, n), 0)
    col = lax.broadcasted_iota(jnp.int32, (n, n), 1)
    lower = (row >= col).astype(F32)
    cum = jnp.dot(lower, log_step, precision=HIGH, preferred_element_type=F32)
    cum_t = cum.T
    write = act[:, pairs * 128 : (pairs + 1) * 128]
    read = act[:, (pairs + 1) * 128 : (pairs + 2) * 128].astype(BF16)
    write_t = write.T.astype(BF16)
    allowed = (row >= col) & (marks[:, 8:9] == segrow[0:1, :])
    inner = jnp.where(allowed, dot(read, write_t), 0.0)
    last = cum[n - 1 : n, :]
    enters = jnp.exp(cum) * marks[:, 3:4]
    to_end = jnp.exp(last - cum) * marks[:, 4:5]
    keep = jnp.exp(last) * marks[n - 1 : n, 3:4]
    wide_cols = spread_heads(jnp.concatenate([step, enters, to_end, jnp.broadcast_to(keep, (8, 128))], 0), spread[...])
    held = carry[...]
    held_low = held.astype(BF16)
    state_out[0] = held_low
    from_state = dot(read, held_low)
    low_half = lax.broadcasted_iota(jnp.int32, (1, 128), 1) < 64
    for j in range(pairs):
        lanes = slice(j * 128, (j + 1) * 128)
        x = act[:, lanes]
        xdt = x * wide_cols[:n, lanes]
        parts = []
        for h in (2 * j, 2 * j + 1):
            decay = jnp.exp(jnp.minimum(cum[:, h : h + 1] - cum_t[h : h + 1, :], 0.0))
            parts.append((decay * inner).astype(BF16))
        xdt_low = xdt.astype(BF16)
        zero = jnp.zeros_like(xdt_low)
        pair = jnp.concatenate([jnp.where(low_half, xdt_low, zero), jnp.where(low_half, zero, xdt_low)], 0)
        y = dot(jnp.concatenate(parts, 1), pair)
        if j % 2 == 0:
            block = slice(128 * j, 128 * j + 256)
            gate_out[:, block] = dot(tok[...], gate_w[:, block])
        else:
            spot = 256 * (j // 2)
            out_w = (out_a[:, 0:256], jnp.concatenate([out_a[:, 256:], out_b[:, :128]], 1), out_b[:, 128:])[j // 2]
            mixed_out[:, spot : spot + 256] = dot(rows[...], out_w)
        y += wide_cols[n : 2 * n, lanes] * from_state[:, lanes] + chan[0:1, lanes] * x
        scan_out[:, lanes] = y
        fed[:, lanes] = (xdt * wide_cols[2 * n : 3 * n, lanes]).astype(BF16)
        carry[:, lanes] = held[:, lanes] * wide_cols[3 * n : 3 * n + 1, lanes]
    carry[...] += dot(write_t, fed[...])

    gate_pre = gate_out[...]
    grad_mixed = mixed_out[...]
    gated = scan_out[...] * (gate_pre * sigmoid(gate_pre))
    square = jnp.sum(gated * gated, axis=1, keepdims=True)
    inner = jnp.sum(grad_mixed * gain[0:1, :] * gated, axis=1, keepdims=True)
    lane = lax.broadcasted_iota(jnp.int32, (1, 128), 1)
    cols = jnp.where(lane == 0, square, jnp.where(lane == 1, inner, 0.0))
    sums_out[...] = cols.T[0:8, :]


def small_rows(value):
    high = value.astype(BF16)
    return jnp.concatenate([high, (value - high.astype(F32)).astype(BF16)], 0)


def read_small(rows):
    return rows[:16, :].astype(F32) + rows[16:, :].astype(F32)


def scan_backward_kernel(me, pre, pre_before, taps, heads, chan, sums, spread, aux, segrow, grad, state, tok, grad_gate, weights, norm_gain, gain_sums, *rest):
    row_outs, outs_a, outs_b = rest[:4], rest[4:8], rest[8:12]
    ext, gext, act, slope, carry, fed, back, rows, low_out, taps_out, heads_out, gains, all_tok, all_low, split, packed = rest[12:]
    n = pre.shape[0]
    pairs = carry.shape[1] // 128
    wide = ext.shape[1]
    gate_width = grad_gate.shape[1]

    @pl.when(pl.program_id(0) == 0)
    def _():
        carry[...] = jnp.zeros_like(carry)
        gext[n:, :] = jnp.zeros((8, wide), F32)
        taps_out[...] = jnp.zeros_like(taps_out)
        heads_out[...] = jnp.zeros_like(heads_out)
        rows[...] = jnp.zeros_like(rows)
        gains[...] = jnp.zeros_like(gains)

    marks = aux[...]
    ext[0:8, :] = pre_before[:, :wide]
    ext[8:, :] = pre[:, :wide]
    for j in range(wide // 128):
        lanes = slice(j * 128, (j + 1) * 128)
        total = conv_strip(ext, taps, marks, j)
        sig = sigmoid(total)
        value = total * sig
        act[:, lanes] = value
        slope[:, lanes] = sig + value * (1.0 - sig)

    step_arg = pre[:, wide:] + heads[0:1, :]
    step = softplus(step_arg)
    rate = heads[1:2, :]
    row = lax.broadcasted_iota(jnp.int32, (n, n), 0)
    col = lax.broadcasted_iota(jnp.int32, (n, n), 1)
    lower = (row >= col).astype(F32)
    cum = jnp.dot(lower, -step * rate, precision=HIGH, preferred_element_type=F32)
    cum_t = cum.T
    write = act[:, pairs * 128 : (pairs + 1) * 128]
    read = act[:, (pairs + 1) * 128 : (pairs + 2) * 128]
    read_t = read.T.astype(BF16)
    write_low = write.astype(BF16)
    read_low = read.astype(BF16)
    allowed = (row <= col) & (marks[:, 8:9] == segrow[0:1, :])
    inner_t = jnp.where(allowed, dot(write_low, read_t), 0.0)
    last = cum[n - 1 : n, :]
    enters = jnp.exp(cum) * marks[:, 3:4]
    to_end = jnp.exp(last - cum) * marks[:, 4:5]
    keep = jnp.exp(last) * marks[n - 1 : n, 3:4]
    wide_cols = spread_heads(jnp.concatenate([step, enters, to_end, jnp.broadcast_to(keep, (8, 128))], 0), spread[...])
    held = state[0]
    later = carry[...]
    later_low = later.astype(BF16)
    from_state = dot(read_low, held)
    from_later = dot(write_low, later_low)
    low_half = lax.broadcasted_iota(jnp.int32, (1, 128), 1) < 64
    head_lane = lax.broadcasted_iota(jnp.int32, (1, 128), 1)
    grad_inner = jnp.zeros((n, n), F32)
    col_sums = jnp.zeros((n, 128), F32)
    to_end_part = jnp.zeros((n, 128), F32)
    enter_part = jnp.zeros((n, 128), F32)
    step_part = jnp.zeros((n, 128), F32)
    skip_part = jnp.zeros((n, 128), F32)
    keep_part = jnp.zeros((8, 128), F32)

    def head_sums(value, j):
        return dot(two_parts(value), sums[j])

    for j in range(pairs):
        lanes = slice(j * 128, (j + 1) * 128)
        x = act[:, lanes]
        dy = grad[:, lanes].astype(F32)
        step_wide = wide_cols[:n, lanes]
        xdt = x * step_wide
        xdt_low = xdt.astype(BF16)
        dy_low = dy.astype(BF16)
        zero = jnp.zeros_like(xdt_low)
        products = dot_nt(
            jnp.concatenate([jnp.where(low_half, xdt_low, zero), jnp.where(low_half, zero, xdt_low)], 0),
            dy_low,
        )
        parts = []
        for k, h in enumerate((2 * j, 2 * j + 1)):
            product = products[k * n : (k + 1) * n, :]
            decay = jnp.exp(jnp.minimum(cum_t[h : h + 1, :] - cum[:, h : h + 1], 0.0))
            scaled = decay * product
            grad_inner += scaled
            weighted = scaled * inner_t
            rows[h : h + 1, :] = jnp.sum(weighted, axis=0, keepdims=True)
            col_sums += jnp.where(head_lane == h, jnp.sum(weighted, axis=1, keepdims=True), 0.0)
            parts.append((decay * inner_t).astype(BF16))
        grad_pair = jnp.concatenate([jnp.where(low_half, dy_low, zero), jnp.where(low_half, zero, dy_low)], 0)
        grad_xdt = dot(jnp.concatenate(parts, 1), grad_pair)
        end_wide = wide_cols[2 * n : 3 * n, lanes]
        enter_wide = wide_cols[n : 2 * n, lanes]
        later_part = end_wide * from_later[:, lanes]
        grad_xdt += later_part
        to_end_part += head_sums(later_part * xdt, j)
        fed[:, lanes] = (xdt * end_wide).astype(BF16)
        grad_enter = dy * enter_wide
        back[:, lanes] = grad_enter.astype(BF16)
        enter_part += head_sums(grad_enter * from_state[:, lanes], j)
        step_part += head_sums(grad_xdt * x, j)
        skip_part += head_sums(dy * x, j)
        kept = jnp.sum(held[:, lanes].astype(F32) * later[:, lanes], axis=0, keepdims=True)
        keep_part += head_sums(jnp.broadcast_to(kept, (8, 128)), j)
        act[:, lanes] = grad_xdt * step_wide + chan[0:1, lanes] * dy
        carry[:, lanes] = later[:, lanes] * wide_cols[3 * n : 3 * n + 1, lanes]

    grad_cum = rows[...].T - col_sums + enter_part - to_end_part
    grad_last = jnp.sum(to_end_part, axis=0, keepdims=True) + keep * keep_part[0:1, :]
    upper = (row <= col).astype(F32)
    grad_log = jnp.dot(upper, grad_cum, precision=HIGH, preferred_element_type=F32) + grad_last
    grad_step = (step_part - rate * grad_log) * sigmoid(step_arg)
    heads_out[0:1, :] += jnp.sum(grad_step, axis=0, keepdims=True)
    heads_out[1:2, :] += -rate * jnp.sum(step * grad_log, axis=0, keepdims=True)
    heads_out[2:3, :] += jnp.sum(skip_part, axis=0, keepdims=True)
    low_out[:, gate_width + wide :] = grad_step.astype(BF16)

    grad_inner = jnp.where(allowed, grad_inner, 0.0)
    act[:, pairs * 128 : (pairs + 1) * 128] = dot(grad_inner.astype(BF16), read_low) + dot_nt(fed[...], later_low)
    act[:, (pairs + 1) * 128 : (pairs + 2) * 128] = dot(grad_inner.T.astype(BF16), write_low) + dot_nt(back[...], held)
    carry[...] += dot(read_t, back[...])

    for j in range(wide // 128):
        lanes = slice(j * 128, (j + 1) * 128)
        grad_pre = act[:, lanes] * slope[:, lanes]
        gext[0:n, lanes] = grad_pre
        total = taps[3:4, lanes] * grad_pre
        taps_out[3:4, lanes] += jnp.sum(grad_pre * ext[8 : 8 + n, lanes], axis=0, keepdims=True)
        taps_out[4:5, lanes] += jnp.sum(grad_pre, axis=0, keepdims=True)
        for by in (1, 2, 3):
            total += taps[3 - by : 4 - by, lanes] * (marks[:, 4 + by : 5 + by] * gext[by : by + n, lanes])
            taps_out[3 - by : 4 - by, lanes] += jnp.sum(
                grad_pre * (marks[:, by - 1 : by] * ext[8 - by : 8 - by + n, lanes]), axis=0, keepdims=True
            )
        low_out[:, gate_width + j * 128 : gate_width + (j + 1) * 128] = total.astype(BF16)
    gext[n:, :] = gext[0:8, :]

    step_id = pl.program_id(0)
    low_out[:, : grad_gate.shape[1]] = grad_gate[...]
    token_grad = dot_nt(low_out[...], weights[...])
    gains[0:1, :] += jnp.sum(token_grad * tok[...].astype(F32), axis=0, keepdims=True)
    place = pl.ds(pl.multiple_of((3 - step_id) * n, n), n)
    all_tok[place, :] = tok[...]
    all_low[place, :] = low_out[:, grad_gate.shape[1] :]
    token_low = token_grad.astype(BF16)
    for k in range(4):

        @pl.when((me[0] ^ (3 - k)) == 3 - step_id)
        def _():
            row_outs[k][...] = token_low

    @pl.when(step_id == 3)
    def _():
        cut = outs_a[0].shape[2]
        deep = outs_a[0].shape[1]
        for k in range(4):
            first = pl.multiple_of(((me[1] + k) % 4) * (4 * deep), 128)
            grad_rows = lax.dot_general(
                all_tok[:, pl.ds(first, 4 * deep)], all_low[...], TN, preferred_element_type=F32
            ).astype(BF16)
            outs_a[k][...] = grad_rows[:, :cut].reshape(outs_a[k].shape)
            split[...] = grad_rows[:, cut:]
            y = (me[1] + k) % 4
            for d in range(4):
                start = pl.multiple_of(((me[2] + d) % 4) * deep, 16)
                outs_b[d][pl.ds(pl.multiple_of(y * deep, 16), deep), :] = split[pl.ds(start, deep), :]
        width = gain_sums.shape[1]
        by_gain = gains[0:1, :] / norm_gain[0:1, :]
        packed[0:5, :] = taps_out[0:5, :]
        packed[5:6, :width] = gain_sums[0:1, :]
        packed[5:6, width:] = jnp.zeros((1, 1024 - width), F32)
        packed[6:7, :] = by_gain[:, :1024]
        packed[7:8, :512] = by_gain[:, 1024:]
        for r in range(3):
            packed[7:8, 512 + 128 * r : 640 + 128 * r] = heads_out[r : r + 1, :]
        packed[7:8, 896:] = jnp.zeros((1, 128), F32)
        sums_low = small_rows(jnp.concatenate([packed[:, :512], packed[:, 512:]], 0))
        for k in range(4):
            outs_b[k][4 * deep :, :512] = sums_low
            outs_b[k][4 * deep :, 512:] = jnp.zeros((32, outs_b[k].shape[1] - 512), BF16)


def scan_marks(segments):
    length = segments.shape[0]
    blocks = segments.reshape(-1, BLOCK)
    before = jnp.concatenate([jnp.full((1,), -1, jnp.int32), blocks[:-1, -1]], 0)

    def same(by):
        if by > 0:
            other = jnp.concatenate([jnp.full((by,), -1, jnp.int32), segments[:-by]], 0)
        else:
            other = jnp.concatenate([segments[-by:], jnp.full((-by,), -1, jnp.int32)], 0)
        return other == segments

    cols = [same(1), same(2), same(3), (blocks == before[:, None]).reshape(-1), (blocks == blocks[:, -1:]).reshape(-1)]
    cols += [same(-1), same(-2), same(-3), segments]
    marks = jnp.stack([c.astype(F32) for c in cols], 1)
    return jnp.pad(marks, ((0, 0), (0, 128 - len(cols)))), jnp.broadcast_to(segments.astype(F32), (8, length))


def scan_forward(tokens, grad_rows, weights, taps, heads, chan, gain, spread, marks, segrow):
    length, model = tokens.shape
    cols = 1152
    inner = cols - 384
    wide = cols - 128
    n = BLOCK
    blocks = length // n


    return pl.pallas_call(
        scan_forward_kernel,
        grid=(blocks,),
        in_specs=[
            pl.BlockSpec((n, model), lambda i: (i, 0)),
            pl.BlockSpec((n, model), lambda i: (i, 0)),
            column_block(model, inner, 0),
            *out_specs_of(model),
            *first_specs(model),
            whole((8, wide)),
            whole((8, 128)),
            whole((8, inner)),
            whole((8, inner)),
            whole((256, inner)),
            pl.BlockSpec((n, 128), lambda i: (i, 0)),
            pl.BlockSpec((8, n), lambda i: (0, i)),
        ],
        out_specs=[
            pl.BlockSpec((n, cols), lambda i: (i, 0)),
            pl.BlockSpec((n, inner), lambda i: (i, 0)),
            pl.BlockSpec((1, 128, inner), lambda i: (i, 0, 0)),
            pl.BlockSpec((n, inner), lambda i: (i, 0)),
            pl.BlockSpec((n, inner), lambda i: (i, 0)),
            pl.BlockSpec((8, n), lambda i: (0, i)),
        ],
        out_shape=[
            jax.ShapeDtypeStruct((length, cols), F32),
            jax.ShapeDtypeStruct((length, inner), F32),
            jax.ShapeDtypeStruct((blocks, 128, inner), BF16),
            jax.ShapeDtypeStruct((length, inner), F32),
            jax.ShapeDtypeStruct((length, inner), F32),
            jax.ShapeDtypeStruct((8, length), F32),
        ],
        scratch_shapes=[
            pltpu.VMEM((n + 8, wide), F32),
            pltpu.VMEM((n, wide), F32),
            pltpu.VMEM((128, inner), F32),
            pltpu.VMEM((n, inner), BF16),
        ],
        compiler_params=PARAMS,
        cost_estimate=cost(20),
        name="scan_forward",
    )(tokens, grad_rows, weights, weights, weights, weights, weights, weights, taps, heads, chan, gain, spread, marks, segrow)


def scan_backward(pre, taps, heads, chan, sums, spread, marks, segrow, grad, states, tokens, grad_gate, weights, norm_gain, gain_sums, me):
    length, cols = pre.shape
    model = tokens.shape[1]
    inner = cols - 384
    wide = cols - 128
    n = BLOCK
    blocks = length // n
    cut = 512
    shape_a, shape_b = (4, model // 16, cut), (model // 4 + 32, cols - cut)

    def rev(i):
        return blocks - 1 - i

    def rows(width):
        return pl.BlockSpec((n, width), lambda i, me: (rev(i), 0))

    return pl.pallas_call(
        scan_backward_kernel,
        grid_spec=pltpu.PrefetchScalarGridSpec(
            num_scalar_prefetch=1,
            grid=(blocks,),
            in_specs=[
                rows(cols),
                pl.BlockSpec((8, cols), lambda i, me: (jnp.maximum(rev(i) * (n // 8) - 1, 0), 0)),
                whole((8, wide)),
                whole((8, 128)),
                whole((8, inner)),
                whole((inner // 128, 256, 128)),
                whole((256, inner)),
                rows(128),
                pl.BlockSpec((8, n), lambda i, me: (0, rev(i))),
                rows(inner),
                pl.BlockSpec((1, 128, inner), lambda i, me: (rev(i), 0, 0)),
                rows(model),
                rows(inner),
                column_block(model, inner + cols, 0),
                whole(norm_gain.shape),
                whole(gain_sums.shape),
            ],
            out_specs=[whole((n, model))] * 4 + [whole(shape_a)] * 4 + [whole(shape_b)] * 4,
            scratch_shapes=[
                pltpu.VMEM((n + 8, wide), F32),
                pltpu.VMEM((n + 8, wide), F32),
                pltpu.VMEM((n, wide), F32),
                pltpu.VMEM((n, wide), F32),
                pltpu.VMEM((128, inner), F32),
                pltpu.VMEM((n, inner), BF16),
                pltpu.VMEM((n, inner), BF16),
                pltpu.VMEM((128, n), F32),
                pltpu.VMEM((n, inner + cols), BF16),
                pltpu.VMEM((8, wide), F32),
                pltpu.VMEM((8, 128), F32),
                pltpu.VMEM((8, model), F32),
                pltpu.VMEM((length, model), BF16),
                pltpu.VMEM((length, cols), BF16),
                pltpu.VMEM((model // 4, cols - cut), BF16),
                pltpu.VMEM((8, 1024), F32),
            ],
        ),
        out_shape=[jax.ShapeDtypeStruct((n, model), BF16)] * 4
        + [jax.ShapeDtypeStruct(shape_a, BF16)] * 4
        + [jax.ShapeDtypeStruct(shape_b, BF16)] * 4,
        compiler_params=PARAMS,
        cost_estimate=cost(30),
        name="scan_backward",
    )(me, pre, pre, taps, heads, chan, sums, spread, marks, segrow, grad, states, tokens, grad_gate, weights, norm_gain, gain_sums)


def spread_table(inner):
    head = jnp.arange(inner) // 64
    return (jnp.arange(256)[:, None] % 128 == head[None, :]).astype(BF16)


def head_sum_table(inner):
    pairs = inner // 128
    lane = jnp.arange(256) % 128
    head = 2 * jnp.arange(pairs)[:, None] + (lane >= 64)[None, :]
    return (head[:, :, None] == jnp.arange(128)[None, None, :]).astype(BF16)


def store_block(value, outs):
    for k, out in enumerate(outs):

        @pl.when(pl.program_id(0) == k)
        def _():
            out[...] = value


def mix_second_kernel(channels, me, sums, gate, grad_mixed_in, scanned_in, out_a, out_b, gain, low_out, grad_scan, grad_gate, gain_out, *outs):
    n = gate.shape[0]

    @pl.when(pl.program_id(0) == 0)
    def _():
        gain_out[...] = jnp.zeros_like(gain_out)

    cols = jnp.concatenate([sums[...], jnp.zeros((120, n), F32)], 0).T
    scale = lax.rsqrt(cols[:, 0:1] / channels + EPS)
    pull = scale * scale * scale * (cols[:, 1:2] / channels)
    gate_pre = gate[...]
    grad_mixed = grad_mixed_in[...]
    scanned = scanned_in[...]
    sig = sigmoid(gate_pre)
    silu = gate_pre * sig
    gated = scanned * silu
    scaled = gated * scale
    mixed = (scaled * gain[0:1, :]).astype(BF16)
    low_out[...] = mixed
    gain_out[0:1, :] += jnp.sum(grad_mixed * scaled, axis=0, keepdims=True)
    grad_gated = scale * gain[0:1, :] * grad_mixed - gated * pull
    grad_scan[...] = grad_gated * silu
    grad_gate[...] = (grad_gated * scanned * (sig + silu * (1.0 - sig))).astype(BF16)
    projected = dot_nt(mixed[:, :384], out_a[...]) + dot_nt(mixed[:, 384:], out_b[...])
    store_block(projected.astype(BF16), outs)


def mix_second(sums, gate, grad_mixed, scanned, second, gain, channels, spot):
    length, width = gate.shape
    model = second.shape[0]
    n = 256

    def rows(cols):
        return pl.BlockSpec((n, cols), lambda i, me: (me[0] ^ (3 - i), 0))

    return pl.pallas_call(
        lambda *refs: mix_second_kernel(channels, *refs),
        grid_spec=pltpu.PrefetchScalarGridSpec(
            num_scalar_prefetch=1,
            grid=(4,),
            in_specs=[
                pl.BlockSpec((8, n), lambda i, me: (0, me[0] ^ (3 - i))),
                rows(width),
                rows(width),
                rows(width),
                *out_specs_of(model),
                whole((8, width)),
            ],
            out_specs=[rows(width), rows(width), rows(width), whole((8, width))] + [whole((n, model))] * 4,
        ),
        out_shape=[
            jax.ShapeDtypeStruct((length, width), BF16),
            jax.ShapeDtypeStruct((length, width), F32),
            jax.ShapeDtypeStruct((length, width), BF16),
            jax.ShapeDtypeStruct((8, width), F32),
        ]
        + [jax.ShapeDtypeStruct((n, model), BF16)] * 4,
        compiler_params=PARAMS,
        cost_estimate=cost(11),
        name="mix_second",
    )(spot, sums, gate, grad_mixed, scanned, second, second, gain)


def second_grads_kernel(tok, rows, grad_gate, mixed, out):
    width = grad_gate.shape[1]
    gate_part = lax.dot_general(tok[...], grad_gate[...], TN, preferred_element_type=F32)
    out_part = lax.dot_general(rows[...], mixed[...], TN, preferred_element_type=F32)
    out[:, :width] = gate_part.astype(BF16)
    out[:, width:] = out_part.astype(BF16)


def second_grads(tokens, grad_rows, grad_gate, mixed):
    length, model = tokens.shape
    width = grad_gate.shape[1]
    n = model // 4
    cols = pl.BlockSpec((length, n), lambda i: (0, i))
    return pl.pallas_call(
        second_grads_kernel,
        grid=(4,),
        in_specs=[cols, cols, whole((length, width)), whole((length, width))],
        out_specs=pl.BlockSpec((n, 2 * width), lambda i: (i, 0)),
        out_shape=jax.ShapeDtypeStruct((model, 2 * width), BF16),
        compiler_params=PARAMS,
        cost_estimate=cost(8),
        name="second_grads",
    )(tokens, grad_rows, grad_gate, mixed)


def four_sum(own, ahead, across, behind):
    return (own.astype(F32) + across.astype(F32)) + (ahead.astype(F32) + behind.astype(F32))


def add_split_kernel(me, *refs):
    parts_a, parts_b, outs_a, outs_b = refs[:4], refs[4:8], refs[8:12], refs[12:]
    deep = outs_a[0].shape[0]
    sums = small_rows(four_sum(*[read_small(part[4 * deep :, :512]) for part in parts_b]))
    for d in range(4):
        e = (me[0] + d) % 4
        outs_a[d][...] = four_sum(*[part[e] for part in parts_a]).astype(BF16)
        place = pl.ds(pl.multiple_of(((me[1] + d) % 4) * deep, 16), deep)
        outs_b[d][:deep, :] = four_sum(*[part[place, :] for part in parts_b]).astype(BF16)
        outs_b[d][deep:, :512] = sums
        outs_b[d][deep:, 512:] = jnp.zeros((32, outs_b[d].shape[1] - 512), BF16)


def add_split(parts_a, parts_b, me):
    deep, width_a = parts_a[0].shape[1:]
    width_b = parts_b[0].shape[1]
    outs = pl.pallas_call(
        add_split_kernel,
        in_specs=[pl.BlockSpec(memory_space=pltpu.SMEM)] + [VMEM_SPEC] * 8,
        out_specs=[VMEM_SPEC] * 8,
        out_shape=[jax.ShapeDtypeStruct((deep, width_a), BF16)] * 4 + [jax.ShapeDtypeStruct((deep + 32, width_b), BF16)] * 4,
        compiler_params=PARAMS,
        name="add_split",
    )(me, *parts_a, *parts_b)
    return outs[:4], outs[4:]


def add_halve_kernel(me, *refs):
    ins, (keep, sums, give, total) = refs[:8], refs[8:]
    rows, cut = ins[0].shape
    total[:, :cut] = four_sum(*[part[...] for part in ins[:4]])
    total[:, cut:] = four_sum(*[part[:rows, :] for part in ins[4:]])
    n = keep.shape[0]
    keep[...] = total[pl.ds(pl.multiple_of(me[0] * n, 16), n), :]
    give[:n, :] = total[pl.ds(pl.multiple_of((1 - me[0]) * n, 16), n), :].astype(BF16)
    low = small_rows(four_sum(*[read_small(part[rows:, :512]) for part in ins[4:]]))
    give[n:, :512] = low
    give[n:, 512:] = jnp.zeros((32, give.shape[1] - 512), BF16)
    sums[...] = read_small(low)


def add_halve(parts_a, parts_b, me):
    rows = parts_a[0].shape[0]
    width = parts_a[0].shape[1] + parts_b[0].shape[1]
    return pl.pallas_call(
        add_halve_kernel,
        in_specs=[pl.BlockSpec(memory_space=pltpu.SMEM)] + [VMEM_SPEC] * 8,
        out_specs=[VMEM_SPEC] * 3,
        out_shape=[
            jax.ShapeDtypeStruct((rows // 2, width), F32),
            jax.ShapeDtypeStruct((16, 512), F32),
            jax.ShapeDtypeStruct((rows // 2 + 32, width), BF16),
        ],
        scratch_shapes=[pltpu.VMEM((rows, width), F32)],
        compiler_params=PARAMS,
        name="add_halve",
    )(me, *parts_a, *parts_b)


def place_kernel(me, *refs):
    out = refs[-1]
    for k, part in enumerate(refs[:-1]):

        @pl.when(pl.program_id(0) == k)
        def _():
            out[...] = part[...].reshape(out.shape)


def place(parts, index, me, shape, block, name):
    return pl.pallas_call(
        place_kernel,
        grid_spec=pltpu.PrefetchScalarGridSpec(
            num_scalar_prefetch=1,
            grid=(len(parts),),
            in_specs=[whole(p.shape) for p in parts],
            out_specs=pl.BlockSpec(block, lambda i, me: index(i, me[0])),
        ),
        out_shape=jax.ShapeDtypeStruct(shape, parts[0].dtype),
        compiler_params=PARAMS,
        cost_estimate=cost(2),
        name=name,
    )(me, *parts)


def shift(value, axis, by):
    n = SIZES[axis]
    return lax.ppermute(value, axis, [(i, (i - by) % n) for i in range(n)])


def swap(value, axis):
    return shift(value, axis, 1)


def ring(value, axis):
    return [value, shift(value, axis, 1), shift(value, axis, 2), shift(value, axis, -1)]


def sends(blocks, axis):
    return [blocks[0], shift(blocks[1], axis, -1), shift(blocks[2], axis, 2), shift(blocks[3], axis, 1)]


def tensor_xor(value, by):
    return lax.ppermute(value, TENSOR, [(i, i ^ by) for i in range(4)])


def sum_ring(value, axis):
    own, ahead, across, behind = ring(value, axis)
    return (own + across) + (ahead + behind)


def sum_pair(value, axis):
    return value + swap(value, axis)


def after(value, *others):
    return lax.optimization_barrier((value,) + others)[0]


def index_of(axis):
    return lax.axis_index(axis).reshape(1).astype(jnp.int32)


def pair_kernel(me, main, other_main, side, other_side, out):
    cut, middle = 1536, side.shape[1]
    for k, (left, right) in enumerate(((main, side), (other_main, other_side))):

        @pl.when(pl.program_id(0) == k)
        def _():
            out[:, :cut] = left[:, :cut]
            out[:, cut : cut + middle] = right[...]
            out[:, cut + middle :] = left[:, cut:]


def pair_rows(main, side):
    rows = main.shape[0]
    width = main.shape[1] + side.shape[1]
    parts = [main, swap(main, "zl"), side, swap(side, "zl")]
    return pl.pallas_call(
        pair_kernel,
        grid_spec=pltpu.PrefetchScalarGridSpec(
            num_scalar_prefetch=1,
            grid=(2,),
            in_specs=[whole(p.shape) for p in parts],
            out_specs=pl.BlockSpec((rows, width), lambda i, me: ((me[0] + i) % 2, 0)),
        ),
        out_shape=jax.ShapeDtypeStruct((2 * rows, width), BF16),
        compiler_params=PARAMS,
        name="pair_rows",
    )(index_of("zl"), *parts)


def token_place(own, near, far, both, me):
    rows, width = own.shape
    return place([own, near, far, both], lambda i, me: (me ^ i, 0), me, (4 * rows, width), (rows, width), "place_tokens")


def per_device(
    hidden_in,
    norm_gain,
    proj_zx,
    proj_shared,
    proj_step,
    conv_inner,
    conv_shared,
    step_bias,
    decay_log,
    skip_gain,
    gated_gain,
    proj_out,
    out_grad,
    segments,
):
    model_width = hidden_in.shape[1]
    width = proj_zx.shape[2]
    heads = step_bias.shape[0]
    me = {axis: index_of(axis) for axis in DP + TENSOR}
    spot = 2 * me["zh"] + me["c"]

    shared_parts = [proj_shared] + [tensor_xor(proj_shared, by) for by in (1, 2, 3)]
    shared_rows = jnp.zeros((48, 256), BF16)
    for by, part in enumerate(shared_parts):
        shared_rows = lax.dynamic_update_slice(shared_rows, part, (((spot[0] ^ by) * 12), jnp.int32(0)))
    side_rows = jnp.concatenate([shared_rows, jnp.pad(proj_step, ((0, 0), (0, 128 - heads)))], 1)
    main_rows = jnp.concatenate([proj_zx[:, 0, :], proj_zx[:, 1, :], proj_out.T], 1)
    weights = lax.all_gather(pair_rows(main_rows, side_rows), ("y", "x"), axis=0, tiled=True)

    residual_in = hidden_in.astype(F32)
    scale_in = lax.rsqrt(jnp.mean(residual_in * residual_in, axis=-1, keepdims=True) + EPS)
    normed_low = (residual_in * scale_in * norm_gain).astype(BF16)
    normed_far = swap(normed_low, "zh")
    normed_near = swap(normed_low, "c")

    normed_both = swap(normed_far, "c")
    tokens = token_place(normed_low, normed_near, normed_far, normed_both, spot)
    grad_far = swap(after(out_grad, normed_far), "zh")
    grad_near = swap(after(out_grad, normed_far), "c")
    grad_both = swap(grad_far, "c")
    grad_rows = token_place(out_grad, grad_near, grad_far, grad_both, spot)

    pad = (0, 128 - heads)
    head_rows = jnp.stack([jnp.pad(step_bias, pad), jnp.pad(jnp.exp(decay_log), pad)], 0)
    head_rows = jnp.pad(head_rows, ((0, 6), (0, 0)))
    taps = jnp.pad(jnp.concatenate([conv_inner, conv_shared], 1), ((0, 3), (0, 0)))
    chan = jnp.broadcast_to(jnp.repeat(skip_gain, width // heads), (8, width))
    gain = jnp.broadcast_to(gated_gain, (8, width))
    norm_rows = jnp.broadcast_to(norm_gain, (8, model_width))
    marks, segrow = scan_marks(segments)
    spread = spread_table(width)
    sum_table = head_sum_table(width)
    tokens, grad_rows = lax.optimization_barrier((tokens, grad_rows))
    pre, scanned, states, gate_pre, grad_mixed, sums = scan_forward(
        tokens, grad_rows, weights, taps, head_rows, chan, gain, spread, marks, segrow
    )

    sums = (sums + tensor_xor(sums, 1)) + (tensor_xor(sums, 2) + tensor_xor(sums, 3))
    mixed_low, grad_scanned, gate_grad_low, gain_sums, *out_blocks = mix_second(
        sums, gate_pre, grad_mixed, scanned, weights, gain, 4 * width, spot
    )
    out_far = (out_blocks[1].astype(F32) + swap(out_blocks[0], "c").astype(F32)).astype(BF16)
    out_near = swap(out_blocks[2], "c")
    second_total = second_grads(tokens, grad_rows, gate_grad_low, mixed_low)
    second_sum = lax.psum_scatter(second_total, ("y", "x"), scatter_dimension=0, tiled=True)
    out_far_got = swap(out_far, "zh")

    grad_scanned = after(grad_scanned, out_far, second_total)
    sent = scan_backward(
        pre,
        taps,
        head_rows,
        chan,
        sum_table,
        spread,
        marks,
        segrow,
        grad_scanned,
        states,
        tokens,
        gate_grad_low,
        weights,
        norm_rows,
        gain_sums,
        jnp.concatenate([spot, me["y"], me["x"]]),
    )
    row_blocks = [after(block, out_far_got, out_near) for block in sent[:4]]
    far_got = swap(row_blocks[0], "c")
    row_far = (row_blocks[1].astype(F32) + far_got.astype(F32)).astype(BF16)
    row_far_got = swap(row_far, "zh")
    parts_b = sends([after(block, row_far) for block in sent[8:]], "x")
    parts_a = sends([after(block, row_far) for block in sent[4:8]], "y")
    half_a, half_b = add_split(parts_a, parts_b, jnp.concatenate([me["x"], me["y"]]))
    near_got = swap(after(row_blocks[2], *half_a), "c")

    hidden_out = (
        residual_in + (out_blocks[3].astype(F32) + out_near.astype(F32) + out_far_got.astype(F32))
    ).astype(BF16)
    grad_normed = row_blocks[3].astype(F32) + near_got.astype(F32) + row_far_got.astype(F32)
    weighted = jnp.sum(grad_normed * norm_gain * residual_in, axis=-1, keepdims=True)
    grad_hidden = (
        out_grad.astype(F32)
        + scale_in * norm_gain * grad_normed
        - residual_in * scale_in**3 * weighted / model_width
    ).astype(BF16)
    parts_a = [after(part, row_far_got, second_sum) for part in sends(half_a, "x")]
    parts_b = [after(part, row_far_got, second_sum) for part in sends(half_b, "y")]
    first_keep, small, first_give = add_halve(parts_a, parts_b, me["zl"])
    first_got = swap(first_give, "zl")
    first_mine = first_keep + first_got[:48].astype(F32)
    small = small + read_small(first_got[48:, :512])
    second_pairs = second_sum.reshape(2, 48, 2 * width)
    second_keep = lax.dynamic_index_in_dim(second_pairs, me["zl"][0], 0, keepdims=False)
    second_mine = second_keep.astype(F32) + swap(
        lax.dynamic_index_in_dim(second_pairs, 1 - me["zl"][0], 0, keepdims=False), "zl"
    ).astype(F32)
    grad_proj_out = second_mine[:, width:].T
    grad_proj_zx = jnp.stack([second_mine[:, :width], first_mine[:, :width]], 1)
    grad_proj_step = first_mine[:, width + 256 : width + 256 + heads]

    def quarter(by):
        part = lax.dynamic_slice(first_mine, ((spot[0] ^ by) * 12, jnp.int32(width)), (12, 256))
        return jnp.concatenate([small, jnp.pad(part, ((0, 0), (0, 256)))], 0)

    summed = (quarter(0) + tensor_xor(quarter(1), 1)) + (tensor_xor(quarter(2), 2) + tensor_xor(quarter(3), 3))
    rest = width - 512
    return (
        hidden_out,
        grad_hidden,
        jnp.concatenate([summed[6], summed[14], summed[7]]),
        grad_proj_zx,
        summed[16:, :256],
        grad_proj_step,
        jnp.concatenate([small[:5], small[8:13, :rest]], 1),
        summed[8:13, rest:],
        small[15, :heads],
        small[15, 128 : 128 + heads],
        small[15, 256 : 256 + heads],
        jnp.concatenate([small[5], small[13, :rest]]),
        grad_proj_out,
    )


def solution(mesh):
    fine = Mesh(mesh.devices.reshape(4, 4, 2, 2, 2), DP + TENSOR)
    both = DP + TENSOR
    return jax.shard_map(
        per_device,
        mesh=fine,
        in_specs=(
            P(both, None),
            P(),
            P(DP, None, TENSOR),
            P(both, None),
            P(DP, TENSOR),
            P(None, TENSOR),
            P(),
            P(TENSOR),
            P(TENSOR),
            P(TENSOR),
            P(TENSOR),
            P(TENSOR, DP),
            P(both, None),
            P(DP),
        ),
        out_specs=(
            P(both, None),
            P(both, None),
            P(),
            P(DP, None, TENSOR),
            P(both, None),
            P(DP, TENSOR),
            P(None, TENSOR),
            P(),
            P(TENSOR),
            P(TENSOR),
            P(TENSOR),
            P(TENSOR),
            P(TENSOR, DP),
        ),
        check_vma=False,
    )
```

```python
import jax
import jax.numpy as jnp
from jax import lax
from jax.experimental import pallas as pl
from jax.experimental.pallas import tpu as pltpu
from jax.sharding import Mesh
from jax.sharding import PartitionSpec as P

EPS = 1e-05
DP = ("y", "x", "zl")
TENSOR = ("zh", "c")
SIZES = {"y": 4, "x": 4, "zl": 2, "zh": 2, "c": 2}

F32 = jnp.float32
BF16 = jnp.bfloat16
HIGH = lax.Precision.HIGHEST
BLOCK = 256
VMEM = 56 * 1024 * 1024
PARAMS = pltpu.CompilerParams(vmem_limit_bytes=VMEM)
NT = (((1,), (1,)), ((), ()))
TN = (((0,), (0,)), ((), ()))
VMEM_SPEC = pl.BlockSpec(memory_space=pltpu.VMEM)


def cost(us):
    return pl.CostEstimate(flops=int(us * 1e6), transcendentals=0, bytes_accessed=int(us * 3e3))


def whole(shape):
    return pl.BlockSpec(shape, lambda *i: (0,) * len(shape))


def column_block(rows, width, index):
    return pl.BlockSpec((rows, width), lambda *i: (0, index))


def first_specs(rows):
    return [column_block(rows, 384, index) for index in (2, 3, 4)]


def out_specs_of(rows):
    return [column_block(rows, 384, index) for index in (5, 6)]


def dot(a, b):
    return jnp.dot(a, b, preferred_element_type=F32)


def dot_nt(a, b):
    return lax.dot_general(a, b, NT, preferred_element_type=F32)


def sigmoid(a):
    return 0.5 * jnp.tanh(0.5 * a) + 0.5


def softplus(a):
    return jnp.maximum(a, 0.0) + jnp.log1p(jnp.exp(-jnp.abs(a)))


def conv_strip(ext, taps, aux, j):
    n = ext.shape[0] - 8
    lanes = slice(j * 128, (j + 1) * 128)
    total = taps[4:5, lanes] + taps[3:4, lanes] * ext[8 : 8 + n, lanes]
    for back in (1, 2, 3):
        total += taps[3 - back : 4 - back, lanes] * (
            aux[:, back - 1 : back] * ext[8 - back : 8 - back + n, lanes]
        )
    return total


def two_parts(value):
    high = value.astype(BF16)
    return jnp.concatenate([high, (value - high.astype(F32)).astype(BF16)], 1)


def spread_heads(cols, table):
    return dot(two_parts(cols), table)


def scan_forward_kernel(tok, rows, gate_w, out_a, out_b, weights_a, weights_b, weights_c, taps, heads, chan, gain, spread, aux, segrow, pre_out, scan_low, state_out, gate_low, mixed_low, sums_out, ext, act, carry, fed, scan_out, gate_out, mixed_out):
    n = tok.shape[0]
    pairs = carry.shape[1] // 128

    @pl.when(pl.program_id(0) == 0)
    def _():
        carry[...] = jnp.zeros_like(carry)
        ext[0:8, :] = jnp.zeros((8, ext.shape[1]), F32)

    pre = jnp.concatenate([dot(tok[...], w[...]) for w in (weights_a, weights_b, weights_c)], 1)
    pre_out[...] = pre
    wide = ext.shape[1]
    ext[8:, :] = pre[:, :wide]
    marks = aux[...]
    for j in range(wide // 128):
        total = conv_strip(ext, taps, marks, j)
        act[:, j * 128 : (j + 1) * 128] = total * sigmoid(total)
    ext[0:8, :] = ext[n : n + 8, :]

    step = softplus(pre[:, wide:] + heads[0:1, :])
    log_step = -step * heads[1:2, :]
    row = lax.broadcasted_iota(jnp.int32, (n, n), 0)
    col = lax.broadcasted_iota(jnp.int32, (n, n), 1)
    lower = (row >= col).astype(F32)
    cum = jnp.dot(lower, log_step, precision=HIGH, preferred_element_type=F32)
    cum_t = cum.T
    write = act[:, pairs * 128 : (pairs + 1) * 128]
    read = act[:, (pairs + 1) * 128 : (pairs + 2) * 128].astype(BF16)
    write_t = write.T.astype(BF16)
    allowed = (row >= col) & (marks[:, 8:9] == segrow[0:1, :])
    inner = jnp.where(allowed, dot(read, write_t), 0.0)
    last = cum[n - 1 : n, :]
    enters = jnp.exp(cum) * marks[:, 3:4]
    to_end = jnp.exp(last - cum) * marks[:, 4:5]
    keep = jnp.exp(last) * marks[n - 1 : n, 3:4]
    wide_cols = spread_heads(jnp.concatenate([step, enters, to_end, jnp.broadcast_to(keep, (8, 128))], 0), spread[...])
    held = carry[...]
    held_low = held.astype(BF16)
    state_out[0] = held_low
    from_state = dot(read, held_low)
    low_half = lax.broadcasted_iota(jnp.int32, (1, 128), 1) < 64
    for j in range(pairs):
        lanes = slice(j * 128, (j + 1) * 128)
        x = act[:, lanes]
        xdt = x * wide_cols[:n, lanes]
        parts = []
        for h in (2 * j, 2 * j + 1):
            decay = jnp.exp(jnp.minimum(cum[:, h : h + 1] - cum_t[h : h + 1, :], 0.0))
            parts.append((decay * inner).astype(BF16))
        xdt_low = xdt.astype(BF16)
        zero = jnp.zeros_like(xdt_low)
        pair = jnp.concatenate([jnp.where(low_half, xdt_low, zero), jnp.where(low_half, zero, xdt_low)], 0)
        y = dot(jnp.concatenate(parts, 1), pair)
        if j % 2 == 0:
            block = slice(128 * j, 128 * j + 256)
            gate_out[:, block] = dot(tok[...], gate_w[:, block])
        else:
            spot = 256 * (j // 2)
            out_w = (out_a[:, 0:256], jnp.concatenate([out_a[:, 256:], out_b[:, :128]], 1), out_b[:, 128:])[j // 2]
            mixed_out[:, spot : spot + 256] = dot(rows[...], out_w)
        y += wide_cols[n : 2 * n, lanes] * from_state[:, lanes] + chan[0:1, lanes] * x
        scan_out[:, lanes] = y
        fed[:, lanes] = (xdt * wide_cols[2 * n : 3 * n, lanes]).astype(BF16)
        carry[:, lanes] = held[:, lanes] * wide_cols[3 * n : 3 * n + 1, lanes]
    carry[...] += dot(write_t, fed[...])

    gate_pre = gate_out[...]
    grad_mixed = mixed_out[...]
    scanned = scan_out[...]
    gate_low[...] = gate_pre.astype(BF16)
    mixed_low[...] = grad_mixed.astype(BF16)
    scan_low[...] = scanned.astype(BF16)
    gated = scanned * (gate_pre * sigmoid(gate_pre))
    square = jnp.sum(gated * gated, axis=1, keepdims=True)
    inner = jnp.sum(grad_mixed * gain[0:1, :] * gated, axis=1, keepdims=True)
    lane = lax.broadcasted_iota(jnp.int32, (1, 128), 1)
    cols = jnp.where(lane == 0, square, jnp.where(lane == 1, inner, 0.0))
    sums_out[...] = cols.T[0:8, :]


def small_rows(value):
    high = value.astype(BF16)
    return jnp.concatenate([high, (value - high.astype(F32)).astype(BF16)], 0)


def read_small(rows):
    return rows[:16, :].astype(F32) + rows[16:, :].astype(F32)


def scan_backward_kernel(me, pre, pre_before, taps, heads, chan, sums, spread, aux, segrow, grad, state, tok, grad_gate, weights, norm_gain, gain_sums, *rest):
    row_outs, outs_a, outs_b = rest[:4], rest[4:8], rest[8:12]
    ext, gext, act, slope, carry, fed, back, rows, low_out, taps_out, heads_out, gains, all_tok, all_low, split, packed = rest[12:]
    n = pre.shape[0]
    pairs = carry.shape[1] // 128
    wide = ext.shape[1]
    gate_width = grad_gate.shape[1]

    @pl.when(pl.program_id(0) == 0)
    def _():
        carry[...] = jnp.zeros_like(carry)
        gext[n:, :] = jnp.zeros((8, wide), F32)
        taps_out[...] = jnp.zeros_like(taps_out)
        heads_out[...] = jnp.zeros_like(heads_out)
        rows[...] = jnp.zeros_like(rows)
        gains[...] = jnp.zeros_like(gains)

    marks = aux[...]
    ext[0:8, :] = pre_before[:, :wide]
    ext[8:, :] = pre[:, :wide]
    for j in range(wide // 128):
        lanes = slice(j * 128, (j + 1) * 128)
        total = conv_strip(ext, taps, marks, j)
        sig = sigmoid(total)
        value = total * sig
        act[:, lanes] = value
        slope[:, lanes] = sig + value * (1.0 - sig)

    step_arg = pre[:, wide:] + heads[0:1, :]
    step = softplus(step_arg)
    rate = heads[1:2, :]
    row = lax.broadcasted_iota(jnp.int32, (n, n), 0)
    col = lax.broadcasted_iota(jnp.int32, (n, n), 1)
    lower = (row >= col).astype(F32)
    cum = jnp.dot(lower, -step * rate, precision=HIGH, preferred_element_type=F32)
    cum_t = cum.T
    write = act[:, pairs * 128 : (pairs + 1) * 128]
    read = act[:, (pairs + 1) * 128 : (pairs + 2) * 128]
    read_t = read.T.astype(BF16)
    write_low = write.astype(BF16)
    read_low = read.astype(BF16)
    allowed = (row <= col) & (marks[:, 8:9] == segrow[0:1, :])
    inner_t = jnp.where(allowed, dot(write_low, read_t), 0.0)
    last = cum[n - 1 : n, :]
    enters = jnp.exp(cum) * marks[:, 3:4]
    to_end = jnp.exp(last - cum) * marks[:, 4:5]
    keep = jnp.exp(last) * marks[n - 1 : n, 3:4]
    wide_cols = spread_heads(jnp.concatenate([step, enters, to_end, jnp.broadcast_to(keep, (8, 128))], 0), spread[...])
    held = state[0]
    later = carry[...]
    later_low = later.astype(BF16)
    from_state = dot(read_low, held)
    from_later = dot(write_low, later_low)
    low_half = lax.broadcasted_iota(jnp.int32, (1, 128), 1) < 64
    head_lane = lax.broadcasted_iota(jnp.int32, (1, 128), 1)
    grad_inner = jnp.zeros((n, n), F32)
    col_sums = jnp.zeros((n, 128), F32)
    to_end_part = jnp.zeros((n, 128), F32)
    enter_part = jnp.zeros((n, 128), F32)
    step_part = jnp.zeros((n, 128), F32)
    skip_part = jnp.zeros((n, 128), F32)
    keep_part = jnp.zeros((8, 128), F32)

    def head_sums(value, j):
        return dot(two_parts(value), sums[j])

    for j in range(pairs):
        lanes = slice(j * 128, (j + 1) * 128)
        x = act[:, lanes]
        dy = grad[:, lanes].astype(F32)
        step_wide = wide_cols[:n, lanes]
        xdt = x * step_wide
        xdt_low = xdt.astype(BF16)
        dy_low = dy.astype(BF16)
        zero = jnp.zeros_like(xdt_low)
        products = dot_nt(
            jnp.concatenate([jnp.where(low_half, xdt_low, zero), jnp.where(low_half, zero, xdt_low)], 0),
            dy_low,
        )
        parts = []
        for k, h in enumerate((2 * j, 2 * j + 1)):
            product = products[k * n : (k + 1) * n, :]
            decay = jnp.exp(jnp.minimum(cum_t[h : h + 1, :] - cum[:, h : h + 1], 0.0))
            scaled = decay * product
            grad_inner += scaled
            weighted = scaled * inner_t
            rows[h : h + 1, :] = jnp.sum(weighted, axis=0, keepdims=True)
            col_sums += jnp.where(head_lane == h, jnp.sum(weighted, axis=1, keepdims=True), 0.0)
            parts.append((decay * inner_t).astype(BF16))
        grad_pair = jnp.concatenate([jnp.where(low_half, dy_low, zero), jnp.where(low_half, zero, dy_low)], 0)
        grad_xdt = dot(jnp.concatenate(parts, 1), grad_pair)
        end_wide = wide_cols[2 * n : 3 * n, lanes]
        enter_wide = wide_cols[n : 2 * n, lanes]
        later_part = end_wide * from_later[:, lanes]
        grad_xdt += later_part
        to_end_part += head_sums(later_part * xdt, j)
        fed[:, lanes] = (xdt * end_wide).astype(BF16)
        grad_enter = dy * enter_wide
        back[:, lanes] = grad_enter.astype(BF16)
        enter_part += head_sums(grad_enter * from_state[:, lanes], j)
        step_part += head_sums(grad_xdt * x, j)
        skip_part += head_sums(dy * x, j)
        kept = jnp.sum(held[:, lanes].astype(F32) * later[:, lanes], axis=0, keepdims=True)
        keep_part += head_sums(jnp.broadcast_to(kept, (8, 128)), j)
        act[:, lanes] = grad_xdt * step_wide + chan[0:1, lanes] * dy
        carry[:, lanes] = later[:, lanes] * wide_cols[3 * n : 3 * n + 1, lanes]

    grad_cum = rows[...].T - col_sums + enter_part - to_end_part
    grad_last = jnp.sum(to_end_part, axis=0, keepdims=True) + keep * keep_part[0:1, :]
    upper = (row <= col).astype(F32)
    grad_log = jnp.dot(upper, grad_cum, precision=HIGH, preferred_element_type=F32) + grad_last
    grad_step = (step_part - rate * grad_log) * sigmoid(step_arg)
    heads_out[0:1, :] += jnp.sum(grad_step, axis=0, keepdims=True)
    heads_out[1:2, :] += -rate * jnp.sum(step * grad_log, axis=0, keepdims=True)
    heads_out[2:3, :] += jnp.sum(skip_part, axis=0, keepdims=True)
    low_out[:, gate_width + wide :] = grad_step.astype(BF16)

    grad_inner = jnp.where(allowed, grad_inner, 0.0)
    act[:, pairs * 128 : (pairs + 1) * 128] = dot(grad_inner.astype(BF16), read_low) + dot_nt(fed[...], later_low)
    act[:, (pairs + 1) * 128 : (pairs + 2) * 128] = dot(grad_inner.T.astype(BF16), write_low) + dot_nt(back[...], held)
    carry[...] += dot(read_t, back[...])

    for j in range(wide // 128):
        lanes = slice(j * 128, (j + 1) * 128)
        grad_pre = act[:, lanes] * slope[:, lanes]
        gext[0:n, lanes] = grad_pre
        total = taps[3:4, lanes] * grad_pre
        taps_out[3:4, lanes] += jnp.sum(grad_pre * ext[8 : 8 + n, lanes], axis=0, keepdims=True)
        taps_out[4:5, lanes] += jnp.sum(grad_pre, axis=0, keepdims=True)
        for by in (1, 2, 3):
            total += taps[3 - by : 4 - by, lanes] * (marks[:, 4 + by : 5 + by] * gext[by : by + n, lanes])
            taps_out[3 - by : 4 - by, lanes] += jnp.sum(
                grad_pre * (marks[:, by - 1 : by] * ext[8 - by : 8 - by + n, lanes]), axis=0, keepdims=True
            )
        low_out[:, gate_width + j * 128 : gate_width + (j + 1) * 128] = total.astype(BF16)
    gext[n:, :] = gext[0:8, :]

    step_id = pl.program_id(0)
    low_out[:, : grad_gate.shape[1]] = grad_gate[...]
    token_grad = dot_nt(low_out[...], weights[...])
    gains[0:1, :] += jnp.sum(token_grad * tok[...].astype(F32), axis=0, keepdims=True)
    place = pl.ds(pl.multiple_of((3 - step_id) * n, n), n)
    all_tok[place, :] = tok[...]
    all_low[place, :] = low_out[:, grad_gate.shape[1] :]
    token_low = token_grad.astype(BF16)
    for k in range(4):

        @pl.when((me[0] ^ (3 - k)) == 3 - step_id)
        def _():
            row_outs[k][...] = token_low

    @pl.when(step_id == 3)
    def _():
        cut = outs_a[0].shape[2]
        deep = outs_a[0].shape[1]
        for k in range(4):
            first = pl.multiple_of(((me[1] + k) % 4) * (4 * deep), 128)
            grad_rows = lax.dot_general(
                all_tok[:, pl.ds(first, 4 * deep)], all_low[...], TN, preferred_element_type=F32
            ).astype(BF16)
            outs_a[k][...] = grad_rows[:, :cut].reshape(outs_a[k].shape)
            split[...] = grad_rows[:, cut:]
            y = (me[1] + k) % 4
            for d in range(4):
                start = pl.multiple_of(((me[2] + d) % 4) * deep, 16)
                outs_b[d][pl.ds(pl.multiple_of(y * deep, 16), deep), :] = split[pl.ds(start, deep), :]
        width = gain_sums.shape[1]
        by_gain = gains[0:1, :] / norm_gain[0:1, :]
        packed[0:5, :] = taps_out[0:5, :]
        packed[5:6, :width] = gain_sums[0:1, :]
        packed[5:6, width:] = jnp.zeros((1, 1024 - width), F32)
        packed[6:7, :] = by_gain[:, :1024]
        packed[7:8, :512] = by_gain[:, 1024:]
        for r in range(3):
            packed[7:8, 512 + 128 * r : 640 + 128 * r] = heads_out[r : r + 1, :]
        packed[7:8, 896:] = jnp.zeros((1, 128), F32)
        sums_low = small_rows(jnp.concatenate([packed[:, :512], packed[:, 512:]], 0))
        for k in range(4):
            outs_b[k][4 * deep :, :512] = sums_low
            outs_b[k][4 * deep :, 512:] = jnp.zeros((32, outs_b[k].shape[1] - 512), BF16)


def scan_marks(segments):
    length = segments.shape[0]
    blocks = segments.reshape(-1, BLOCK)
    before = jnp.concatenate([jnp.full((1,), -1, jnp.int32), blocks[:-1, -1]], 0)

    def same(by):
        if by > 0:
            other = jnp.concatenate([jnp.full((by,), -1, jnp.int32), segments[:-by]], 0)
        else:
            other = jnp.concatenate([segments[-by:], jnp.full((-by,), -1, jnp.int32)], 0)
        return other == segments

    cols = [same(1), same(2), same(3), (blocks == before[:, None]).reshape(-1), (blocks == blocks[:, -1:]).reshape(-1)]
    cols += [same(-1), same(-2), same(-3), segments]
    marks = jnp.stack([c.astype(F32) for c in cols], 1)
    return jnp.pad(marks, ((0, 0), (0, 128 - len(cols)))), jnp.broadcast_to(segments.astype(F32), (8, length))


def scan_forward(tokens, grad_rows, weights, taps, heads, chan, gain, spread, marks, segrow):
    length, model = tokens.shape
    cols = 1152
    inner = cols - 384
    wide = cols - 128
    n = BLOCK
    blocks = length // n


    return pl.pallas_call(
        scan_forward_kernel,
        grid=(blocks,),
        in_specs=[
            pl.BlockSpec((n, model), lambda i: (i, 0)),
            pl.BlockSpec((n, model), lambda i: (i, 0)),
            column_block(model, inner, 0),
            *out_specs_of(model),
            *first_specs(model),
            whole((8, wide)),
            whole((8, 128)),
            whole((8, inner)),
            whole((8, inner)),
            whole((256, inner)),
            pl.BlockSpec((n, 128), lambda i: (i, 0)),
            pl.BlockSpec((8, n), lambda i: (0, i)),
        ],
        out_specs=[
            pl.BlockSpec((n, cols), lambda i: (i, 0)),
            pl.BlockSpec((n, inner), lambda i: (i, 0)),
            pl.BlockSpec((1, 128, inner), lambda i: (i, 0, 0)),
            pl.BlockSpec((n, inner), lambda i: (i, 0)),
            pl.BlockSpec((n, inner), lambda i: (i, 0)),
            pl.BlockSpec((8, n), lambda i: (0, i)),
        ],
        out_shape=[
            jax.ShapeDtypeStruct((length, cols), F32),
            jax.ShapeDtypeStruct((length, inner), BF16),
            jax.ShapeDtypeStruct((blocks, 128, inner), BF16),
            jax.ShapeDtypeStruct((length, inner), BF16),
            jax.ShapeDtypeStruct((length, inner), BF16),
            jax.ShapeDtypeStruct((8, length), F32),
        ],
        scratch_shapes=[
            pltpu.VMEM((n + 8, wide), F32),
            pltpu.VMEM((n, wide), F32),
            pltpu.VMEM((128, inner), F32),
            pltpu.VMEM((n, inner), BF16),
            pltpu.VMEM((n, inner), F32),
            pltpu.VMEM((n, inner), F32),
            pltpu.VMEM((n, inner), F32),
        ],
        compiler_params=PARAMS,
        cost_estimate=cost(20),
        name="scan_forward",
    )(tokens, grad_rows, weights, weights, weights, weights, weights, weights, taps, heads, chan, gain, spread, marks, segrow)


def scan_backward(pre, taps, heads, chan, sums, spread, marks, segrow, grad, states, tokens, grad_gate, weights, norm_gain, gain_sums, me):
    length, cols = pre.shape
    model = tokens.shape[1]
    inner = cols - 384
    wide = cols - 128
    n = BLOCK
    blocks = length // n
    cut = 512
    shape_a, shape_b = (4, model // 16, cut), (model // 4 + 32, cols - cut)

    def rev(i):
        return blocks - 1 - i

    def rows(width):
        return pl.BlockSpec((n, width), lambda i, me: (rev(i), 0))

    return pl.pallas_call(
        scan_backward_kernel,
        grid_spec=pltpu.PrefetchScalarGridSpec(
            num_scalar_prefetch=1,
            grid=(blocks,),
            in_specs=[
                rows(cols),
                pl.BlockSpec((8, cols), lambda i, me: (jnp.maximum(rev(i) * (n // 8) - 1, 0), 0)),
                whole((8, wide)),
                whole((8, 128)),
                whole((8, inner)),
                whole((inner // 128, 256, 128)),
                whole((256, inner)),
                rows(128),
                pl.BlockSpec((8, n), lambda i, me: (0, rev(i))),
                rows(inner),
                pl.BlockSpec((1, 128, inner), lambda i, me: (rev(i), 0, 0)),
                rows(model),
                rows(inner),
                column_block(model, inner + cols, 0),
                whole(norm_gain.shape),
                whole(gain_sums.shape),
            ],
            out_specs=[whole((n, model))] * 4 + [whole(shape_a)] * 4 + [whole(shape_b)] * 4,
            scratch_shapes=[
                pltpu.VMEM((n + 8, wide), F32),
                pltpu.VMEM((n + 8, wide), F32),
                pltpu.VMEM((n, wide), F32),
                pltpu.VMEM((n, wide), F32),
                pltpu.VMEM((128, inner), F32),
                pltpu.VMEM((n, inner), BF16),
                pltpu.VMEM((n, inner), BF16),
                pltpu.VMEM((128, n), F32),
                pltpu.VMEM((n, inner + cols), BF16),
                pltpu.VMEM((8, wide), F32),
                pltpu.VMEM((8, 128), F32),
                pltpu.VMEM((8, model), F32),
                pltpu.VMEM((length, model), BF16),
                pltpu.VMEM((length, cols), BF16),
                pltpu.VMEM((model // 4, cols - cut), BF16),
                pltpu.VMEM((8, 1024), F32),
            ],
        ),
        out_shape=[jax.ShapeDtypeStruct((n, model), BF16)] * 4
        + [jax.ShapeDtypeStruct(shape_a, BF16)] * 4
        + [jax.ShapeDtypeStruct(shape_b, BF16)] * 4,
        compiler_params=PARAMS,
        cost_estimate=cost(30),
        name="scan_backward",
    )(me, pre, pre, taps, heads, chan, sums, spread, marks, segrow, grad, states, tokens, grad_gate, weights, norm_gain, gain_sums)


def spread_table(inner):
    head = jnp.arange(inner) // 64
    return (jnp.arange(256)[:, None] % 128 == head[None, :]).astype(BF16)


def head_sum_table(inner):
    pairs = inner // 128
    lane = jnp.arange(256) % 128
    head = 2 * jnp.arange(pairs)[:, None] + (lane >= 64)[None, :]
    return (head[:, :, None] == jnp.arange(128)[None, None, :]).astype(BF16)


def store_block(value, outs):
    for k, out in enumerate(outs):

        @pl.when(pl.program_id(0) == k)
        def _():
            out[...] = value


def mix_second_kernel(channels, me, sums, gate, grad_mixed_in, scanned_in, out_a, out_b, gain, tok, rows, grad_scan, grad_gate, gain_out, grads_out, *rest):
    outs, all_gate, all_mixed = rest[:4], rest[4], rest[5]
    step = pl.program_id(0)
    n, width = gate.shape

    @pl.when(step == 0)
    def _():
        gain_out[...] = jnp.zeros_like(gain_out)

    @pl.when(step < 4)
    def _():
        cols = jnp.concatenate([sums[...], jnp.zeros((120, n), F32)], 0).T
        scale = lax.rsqrt(cols[:, 0:1] / channels + EPS)
        pull = scale * scale * scale * (cols[:, 1:2] / channels)
        gate_pre = gate[...].astype(F32)
        grad_mixed = grad_mixed_in[...].astype(F32)
        scanned = scanned_in[...].astype(F32)
        sig = sigmoid(gate_pre)
        silu = gate_pre * sig
        gated = scanned * silu
        scaled = gated * scale
        mixed = (scaled * gain[0:1, :]).astype(BF16)
        place = pl.ds(pl.multiple_of((me[0] ^ (3 - step)) * n, n), n)
        all_mixed[place, :] = mixed
        gain_out[0:1, :] += jnp.sum(grad_mixed * scaled, axis=0, keepdims=True)
        grad_gated = scale * gain[0:1, :] * grad_mixed - gated * pull
        grad_scan[...] = (grad_gated * silu).astype(BF16)
        grad_gate_low = (grad_gated * scanned * (sig + silu * (1.0 - sig))).astype(BF16)
        grad_gate[...] = grad_gate_low
        all_gate[place, :] = grad_gate_low
        projected = dot_nt(mixed[:, :384], out_a[...]) + dot_nt(mixed[:, 384:], out_b[...])
        store_block(projected.astype(BF16), outs)

    @pl.when(step >= 4)
    def _():
        gate_part = lax.dot_general(tok[...], all_gate[...], TN, preferred_element_type=F32)
        out_part = lax.dot_general(rows[...], all_mixed[...], TN, preferred_element_type=F32)
        grads_out[:, :width] = gate_part.astype(BF16)
        grads_out[:, width:] = out_part.astype(BF16)


def mix_second(sums, gate, grad_mixed, scanned, second, gain, tokens, grad_rows, channels, spot):
    length, width = gate.shape
    model = second.shape[0]
    n = 256
    m = model // 4

    def token_block(i, me):
        return me[0] ^ (3 - jnp.minimum(i, 3))

    def rows(cols):
        return pl.BlockSpec((n, cols), lambda i, me: (token_block(i, me), 0))

    def cols():
        return pl.BlockSpec((length, m), lambda i, me: (0, jnp.maximum(i - 4, 0)))

    return pl.pallas_call(
        lambda *refs: mix_second_kernel(channels, *refs),
        grid_spec=pltpu.PrefetchScalarGridSpec(
            num_scalar_prefetch=1,
            grid=(8,),
            in_specs=[
                pl.BlockSpec((8, n), lambda i, me: (0, token_block(i, me))),
                rows(width),
                rows(width),
                rows(width),
                *out_specs_of(model),
                whole((8, width)),
                cols(),
                cols(),
            ],
            out_specs=[
                rows(width),
                rows(width),
                whole((8, width)),
                pl.BlockSpec((m, 2 * width), lambda i, me: (jnp.maximum(i - 4, 0), 0)),
            ]
            + [whole((n, model))] * 4,
            scratch_shapes=[pltpu.VMEM((length, width), BF16), pltpu.VMEM((length, width), BF16)],
        ),
        out_shape=[
            jax.ShapeDtypeStruct((length, width), BF16),
            jax.ShapeDtypeStruct((length, width), BF16),
            jax.ShapeDtypeStruct((8, width), F32),
            jax.ShapeDtypeStruct((model, 2 * width), BF16),
        ]
        + [jax.ShapeDtypeStruct((n, model), BF16)] * 4,
        compiler_params=PARAMS,
        cost_estimate=cost(11),
        name="mix_second",
    )(spot, sums, gate, grad_mixed, scanned, second, second, gain, tokens, grad_rows)


def four_sum(own, ahead, across, behind):
    return (own.astype(F32) + across.astype(F32)) + (ahead.astype(F32) + behind.astype(F32))


def add_split_kernel(me, *refs):
    parts_a, parts_b, outs_a, outs_b = refs[:4], refs[4:8], refs[8:12], refs[12:]
    deep = outs_a[0].shape[0]
    sums = small_rows(four_sum(*[read_small(part[4 * deep :, :512]) for part in parts_b]))
    for d in range(4):
        e = (me[0] + d) % 4
        outs_a[d][...] = four_sum(*[part[e] for part in parts_a]).astype(BF16)
        place = pl.ds(pl.multiple_of(((me[1] + d) % 4) * deep, 16), deep)
        outs_b[d][:deep, :] = four_sum(*[part[place, :] for part in parts_b]).astype(BF16)
        outs_b[d][deep:, :512] = sums
        outs_b[d][deep:, 512:] = jnp.zeros((32, outs_b[d].shape[1] - 512), BF16)


def add_split(parts_a, parts_b, me):
    deep, width_a = parts_a[0].shape[1:]
    width_b = parts_b[0].shape[1]
    outs = pl.pallas_call(
        add_split_kernel,
        in_specs=[pl.BlockSpec(memory_space=pltpu.SMEM)] + [VMEM_SPEC] * 8,
        out_specs=[VMEM_SPEC] * 8,
        out_shape=[jax.ShapeDtypeStruct((deep, width_a), BF16)] * 4 + [jax.ShapeDtypeStruct((deep + 32, width_b), BF16)] * 4,
        compiler_params=PARAMS,
        name="add_split",
    )(me, *parts_a, *parts_b)
    return outs[:4], outs[4:]


def add_halve_kernel(me, *refs):
    ins, (keep, sums, give, total) = refs[:8], refs[8:]
    rows, cut = ins[0].shape
    total[:, :cut] = four_sum(*[part[...] for part in ins[:4]])
    total[:, cut:] = four_sum(*[part[:rows, :] for part in ins[4:]])
    n = keep.shape[0]
    keep[...] = total[pl.ds(pl.multiple_of(me[0] * n, 16), n), :]
    give[:n, :] = total[pl.ds(pl.multiple_of((1 - me[0]) * n, 16), n), :].astype(BF16)
    low = small_rows(four_sum(*[read_small(part[rows:, :512]) for part in ins[4:]]))
    give[n:, :512] = low
    give[n:, 512:] = jnp.zeros((32, give.shape[1] - 512), BF16)
    sums[...] = read_small(low)


def add_halve(parts_a, parts_b, me):
    rows = parts_a[0].shape[0]
    width = parts_a[0].shape[1] + parts_b[0].shape[1]
    return pl.pallas_call(
        add_halve_kernel,
        in_specs=[pl.BlockSpec(memory_space=pltpu.SMEM)] + [VMEM_SPEC] * 8,
        out_specs=[VMEM_SPEC] * 3,
        out_shape=[
            jax.ShapeDtypeStruct((rows // 2, width), F32),
            jax.ShapeDtypeStruct((16, 512), F32),
            jax.ShapeDtypeStruct((rows // 2 + 32, width), BF16),
        ],
        scratch_shapes=[pltpu.VMEM((rows, width), F32)],
        compiler_params=PARAMS,
        name="add_halve",
    )(me, *parts_a, *parts_b)


def place_kernel(me, *refs):
    out = refs[-1]
    for k, part in enumerate(refs[:-1]):

        @pl.when(pl.program_id(0) == k)
        def _():
            out[...] = part[...].reshape(out.shape)


def place(parts, index, me, shape, block, name):
    return pl.pallas_call(
        place_kernel,
        grid_spec=pltpu.PrefetchScalarGridSpec(
            num_scalar_prefetch=1,
            grid=(len(parts),),
            in_specs=[whole(p.shape) for p in parts],
            out_specs=pl.BlockSpec(block, lambda i, me: index(i, me[0])),
        ),
        out_shape=jax.ShapeDtypeStruct(shape, parts[0].dtype),
        compiler_params=PARAMS,
        cost_estimate=cost(2),
        name=name,
    )(me, *parts)


def shift(value, axis, by):
    n = SIZES[axis]
    return lax.ppermute(value, axis, [(i, (i - by) % n) for i in range(n)])


def swap(value, axis):
    return shift(value, axis, 1)


def ring(value, axis):
    return [value, shift(value, axis, 1), shift(value, axis, 2), shift(value, axis, -1)]


def sends(blocks, axis):
    return [blocks[0], shift(blocks[1], axis, -1), shift(blocks[2], axis, 2), shift(blocks[3], axis, 1)]


def tensor_xor(value, by):
    return lax.ppermute(value, TENSOR, [(i, i ^ by) for i in range(4)])


def sum_ring(value, axis):
    own, ahead, across, behind = ring(value, axis)
    return (own + across) + (ahead + behind)


def sum_pair(value, axis):
    return value + swap(value, axis)


def after(value, *others):
    return lax.optimization_barrier((value,) + others)[0]


def index_of(axis):
    return lax.axis_index(axis).reshape(1).astype(jnp.int32)


def pair_kernel(me, main, other_main, side, other_side, out):
    cut, middle = 1536, side.shape[1]
    for k, (left, right) in enumerate(((main, side), (other_main, other_side))):

        @pl.when(pl.program_id(0) == k)
        def _():
            out[:, :cut] = left[:, :cut]
            out[:, cut : cut + middle] = right[...]
            out[:, cut + middle :] = left[:, cut:]


def pair_rows(main, side):
    rows = main.shape[0]
    width = main.shape[1] + side.shape[1]
    parts = [main, swap(main, "zl"), side, swap(side, "zl")]
    return pl.pallas_call(
        pair_kernel,
        grid_spec=pltpu.PrefetchScalarGridSpec(
            num_scalar_prefetch=1,
            grid=(2,),
            in_specs=[whole(p.shape) for p in parts],
            out_specs=pl.BlockSpec((rows, width), lambda i, me: ((me[0] + i) % 2, 0)),
        ),
        out_shape=jax.ShapeDtypeStruct((2 * rows, width), BF16),
        compiler_params=PARAMS,
        name="pair_rows",
    )(index_of("zl"), *parts)


def token_place(own, near, far, both, me):
    rows, width = own.shape
    return place([own, near, far, both], lambda i, me: (me ^ i, 0), me, (4 * rows, width), (rows, width), "place_tokens")


def per_device(
    hidden_in,
    norm_gain,
    proj_zx,
    proj_shared,
    proj_step,
    conv_inner,
    conv_shared,
    step_bias,
    decay_log,
    skip_gain,
    gated_gain,
    proj_out,
    out_grad,
    segments,
):
    model_width = hidden_in.shape[1]
    width = proj_zx.shape[2]
    heads = step_bias.shape[0]
    me = {axis: index_of(axis) for axis in DP + TENSOR}
    spot = 2 * me["zh"] + me["c"]

    shared_parts = [proj_shared] + [tensor_xor(proj_shared, by) for by in (1, 2, 3)]
    shared_rows = jnp.zeros((48, 256), BF16)
    for by, part in enumerate(shared_parts):
        shared_rows = lax.dynamic_update_slice(shared_rows, part, (((spot[0] ^ by) * 12), jnp.int32(0)))
    side_rows = jnp.concatenate([shared_rows, jnp.pad(proj_step, ((0, 0), (0, 128 - heads)))], 1)
    main_rows = jnp.concatenate([proj_zx[:, 0, :], proj_zx[:, 1, :], proj_out.T], 1)
    weights = lax.all_gather(pair_rows(main_rows, side_rows), ("y", "x"), axis=0, tiled=True)

    residual_in = hidden_in.astype(F32)
    scale_in = lax.rsqrt(jnp.mean(residual_in * residual_in, axis=-1, keepdims=True) + EPS)
    normed_low = (residual_in * scale_in * norm_gain).astype(BF16)
    normed_far = swap(normed_low, "zh")
    normed_near = swap(normed_low, "c")

    normed_both = swap(normed_far, "c")
    tokens = token_place(normed_low, normed_near, normed_far, normed_both, spot)
    grad_far = swap(after(out_grad, normed_far), "zh")
    grad_near = swap(after(out_grad, normed_far), "c")
    grad_both = swap(grad_far, "c")
    grad_rows = token_place(out_grad, grad_near, grad_far, grad_both, spot)

    pad = (0, 128 - heads)
    head_rows = jnp.stack([jnp.pad(step_bias, pad), jnp.pad(jnp.exp(decay_log), pad)], 0)
    head_rows = jnp.pad(head_rows, ((0, 6), (0, 0)))
    taps = jnp.pad(jnp.concatenate([conv_inner, conv_shared], 1), ((0, 3), (0, 0)))
    chan = jnp.broadcast_to(jnp.repeat(skip_gain, width // heads), (8, width))
    gain = jnp.broadcast_to(gated_gain, (8, width))
    norm_rows = jnp.broadcast_to(norm_gain, (8, model_width))
    marks, segrow = scan_marks(segments)
    spread = spread_table(width)
    sum_table = head_sum_table(width)
    tokens, grad_rows = lax.optimization_barrier((tokens, grad_rows))
    pre, scanned, states, gate_pre, grad_mixed, sums = scan_forward(
        tokens, grad_rows, weights, taps, head_rows, chan, gain, spread, marks, segrow
    )

    sums = sum_pair(sum_pair(sums, "c"), "zh")
    grad_scanned, gate_grad_low, gain_sums, second_total, *out_blocks = mix_second(
        sums, gate_pre, grad_mixed, scanned, weights, gain, tokens, grad_rows, 4 * width, spot
    )
    out_far = (out_blocks[1].astype(F32) + swap(out_blocks[0], "c").astype(F32)).astype(BF16)
    out_near = swap(out_blocks[2], "c")
    second_sum = lax.psum_scatter(second_total, ("y", "x"), scatter_dimension=0, tiled=True)
    out_far_got = swap(out_far, "zh")

    grad_scanned = after(grad_scanned, out_far, second_total)
    sent = scan_backward(
        pre,
        taps,
        head_rows,
        chan,
        sum_table,
        spread,
        marks,
        segrow,
        grad_scanned,
        states,
        tokens,
        gate_grad_low,
        weights,
        norm_rows,
        gain_sums,
        jnp.concatenate([spot, me["y"], me["x"]]),
    )
    row_blocks = [after(block, out_far_got, out_near) for block in sent[:4]]
    far_got = swap(row_blocks[0], "c")
    row_far = (row_blocks[1].astype(F32) + far_got.astype(F32)).astype(BF16)
    row_far_got = swap(row_far, "zh")
    parts_b = sends([after(block, row_far) for block in sent[8:]], "x")
    parts_a = sends([after(block, row_far) for block in sent[4:8]], "y")
    half_a, half_b = add_split(parts_a, parts_b, jnp.concatenate([me["x"], me["y"]]))
    near_got = swap(after(row_blocks[2], *half_a), "c")

    hidden_out = (
        residual_in + (out_blocks[3].astype(F32) + out_near.astype(F32) + out_far_got.astype(F32))
    ).astype(BF16)
    grad_normed = row_blocks[3].astype(F32) + near_got.astype(F32) + row_far_got.astype(F32)
    weighted = jnp.sum(grad_normed * norm_gain * residual_in, axis=-1, keepdims=True)
    grad_hidden = (
        out_grad.astype(F32)
        + scale_in * norm_gain * grad_normed
        - residual_in * scale_in**3 * weighted / model_width
    ).astype(BF16)
    parts_a = [after(part, row_far_got, second_sum) for part in sends(half_a, "x")]
    parts_b = [after(part, row_far_got, second_sum) for part in sends(half_b, "y")]
    first_keep, small, first_give = add_halve(parts_a, parts_b, me["zl"])
    first_got = swap(first_give, "zl")
    first_mine = first_keep + first_got[:48].astype(F32)
    small = small + read_small(first_got[48:, :512])
    second_pairs = second_sum.reshape(2, 48, 2 * width)
    second_keep = lax.dynamic_index_in_dim(second_pairs, me["zl"][0], 0, keepdims=False)
    second_mine = second_keep.astype(F32) + swap(
        lax.dynamic_index_in_dim(second_pairs, 1 - me["zl"][0], 0, keepdims=False), "zl"
    ).astype(F32)
    grad_proj_out = second_mine[:, width:].T
    grad_proj_zx = jnp.stack([second_mine[:, :width], first_mine[:, :width]], 1)
    grad_proj_step = first_mine[:, width + 256 : width + 256 + heads]

    def quarter(by):
        part = lax.dynamic_slice(first_mine, ((spot[0] ^ by) * 12, jnp.int32(width)), (12, 256))
        return jnp.concatenate([small, jnp.pad(part, ((0, 0), (0, 256)))], 0)

    summed = (quarter(0) + tensor_xor(quarter(1), 1)) + (tensor_xor(quarter(2), 2) + tensor_xor(quarter(3), 3))
    rest = width - 512
    return (
        hidden_out,
        grad_hidden,
        jnp.concatenate([summed[6], summed[14], summed[7]]),
        grad_proj_zx,
        summed[16:, :256],
        grad_proj_step,
        jnp.concatenate([small[:5], small[8:13, :rest]], 1),
        summed[8:13, rest:],
        small[15, :heads],
        small[15, 128 : 128 + heads],
        small[15, 256 : 256 + heads],
        jnp.concatenate([small[5], small[13, :rest]]),
        grad_proj_out,
    )


def solution(mesh):
    fine = Mesh(mesh.devices.reshape(4, 4, 2, 2, 2), DP + TENSOR)
    both = DP + TENSOR
    return jax.shard_map(
        per_device,
        mesh=fine,
        in_specs=(
            P(both, None),
            P(),
            P(DP, None, TENSOR),
            P(both, None),
            P(DP, TENSOR),
            P(None, TENSOR),
            P(),
            P(TENSOR),
            P(TENSOR),
            P(TENSOR),
            P(TENSOR),
            P(TENSOR, DP),
            P(both, None),
            P(DP),
        ),
        out_specs=(
            P(both, None),
            P(both, None),
            P(),
            P(DP, None, TENSOR),
            P(both, None),
            P(DP, TENSOR),
            P(None, TENSOR),
            P(),
            P(TENSOR),
            P(TENSOR),
            P(TENSOR),
            P(TENSOR),
            P(TENSOR, DP),
        ),
        check_vma=False,
    )
```

```python
import jax
import jax.numpy as jnp
from jax import lax
from jax.experimental import pallas as pl
from jax.experimental.pallas import tpu as pltpu
from jax.sharding import Mesh
from jax.sharding import PartitionSpec as P

EPS = 1e-05
DP = ("y", "x", "zl")
TENSOR = ("zh", "c")
SIZES = {"y": 4, "x": 4, "zl": 2, "zh": 2, "c": 2}

F32 = jnp.float32
BF16 = jnp.bfloat16
HIGH = lax.Precision.HIGHEST
BLOCK = 256
VMEM = 56 * 1024 * 1024
PARAMS = pltpu.CompilerParams(vmem_limit_bytes=VMEM)
NT = (((1,), (1,)), ((), ()))
TN = (((0,), (0,)), ((), ()))
VMEM_SPEC = pl.BlockSpec(memory_space=pltpu.VMEM)


def cost(us):
    return pl.CostEstimate(flops=int(us * 1e6), transcendentals=0, bytes_accessed=int(us * 3e3))


def whole(shape):
    return pl.BlockSpec(shape, lambda *i: (0,) * len(shape))


def column_block(rows, width, index):
    return pl.BlockSpec((rows, width), lambda *i: (0, index))


def first_specs(rows):
    return [column_block(rows, 384, index) for index in (2, 3, 4)]


def out_specs_of(rows):
    return [column_block(rows, 384, index) for index in (5, 6)]


def dot(a, b):
    return jnp.dot(a, b, preferred_element_type=F32)


def dot_nt(a, b):
    return lax.dot_general(a, b, NT, preferred_element_type=F32)


def sigmoid(a):
    return 0.5 * jnp.tanh(0.5 * a) + 0.5


def softplus(a):
    return jnp.maximum(a, 0.0) + jnp.log1p(jnp.exp(-jnp.abs(a)))


def conv_strip(ext, taps, aux, j):
    n = ext.shape[0] - 8
    lanes = slice(j * 128, (j + 1) * 128)
    total = taps[4:5, lanes] + taps[3:4, lanes] * ext[8 : 8 + n, lanes]
    for back in (1, 2, 3):
        total += taps[3 - back : 4 - back, lanes] * (
            aux[:, back - 1 : back] * ext[8 - back : 8 - back + n, lanes]
        )
    return total


def two_parts(value):
    high = value.astype(BF16)
    return jnp.concatenate([high, (value - high.astype(F32)).astype(BF16)], 1)


def spread_heads(cols, table):
    return dot(two_parts(cols), table)


def scan_forward_kernel(tok, weights_a, weights_b, weights_c, taps, heads, chan, spread, aux, segrow, pre_out, scan_out, state_out, ext, act, carry, fed):
    n = tok.shape[0]
    pairs = carry.shape[1] // 128

    @pl.when(pl.program_id(0) == 0)
    def _():
        carry[...] = jnp.zeros_like(carry)
        ext[0:8, :] = jnp.zeros((8, ext.shape[1]), F32)

    pre = jnp.concatenate([dot(tok[...], w[...]) for w in (weights_a, weights_b, weights_c)], 1)
    pre_out[...] = pre
    wide = ext.shape[1]
    ext[8:, :] = pre[:, :wide]
    marks = aux[...]
    for j in range(wide // 128):
        total = conv_strip(ext, taps, marks, j)
        act[:, j * 128 : (j + 1) * 128] = total * sigmoid(total)
    ext[0:8, :] = ext[n : n + 8, :]

    step = softplus(pre[:, wide:] + heads[0:1, :])
    log_step = -step * heads[1:2, :]
    row = lax.broadcasted_iota(jnp.int32, (n, n), 0)
    col = lax.broadcasted_iota(jnp.int32, (n, n), 1)
    lower = (row >= col).astype(F32)
    cum = jnp.dot(lower, log_step, precision=HIGH, preferred_element_type=F32)
    cum_t = cum.T
    write = act[:, pairs * 128 : (pairs + 1) * 128]
    read = act[:, (pairs + 1) * 128 : (pairs + 2) * 128].astype(BF16)
    write_t = write.T.astype(BF16)
    allowed = (row >= col) & (marks[:, 8:9] == segrow[0:1, :])
    inner = jnp.where(allowed, dot(read, write_t), 0.0)
    last = cum[n - 1 : n, :]
    enters = jnp.exp(cum) * marks[:, 3:4]
    to_end = jnp.exp(last - cum) * marks[:, 4:5]
    keep = jnp.exp(last) * marks[n - 1 : n, 3:4]
    wide_cols = spread_heads(jnp.concatenate([step, enters, to_end, jnp.broadcast_to(keep, (8, 128))], 0), spread[...])
    held = carry[...]
    held_low = held.astype(BF16)
    state_out[0] = held_low
    from_state = dot(read, held_low)
    low_half = lax.broadcasted_iota(jnp.int32, (1, 128), 1) < 64
    for j in range(pairs):
        lanes = slice(j * 128, (j + 1) * 128)
        x = act[:, lanes]
        xdt = x * wide_cols[:n, lanes]
        parts = []
        for h in (2 * j, 2 * j + 1):
            decay = jnp.exp(jnp.minimum(cum[:, h : h + 1] - cum_t[h : h + 1, :], 0.0))
            parts.append((decay * inner).astype(BF16))
        xdt_low = xdt.astype(BF16)
        zero = jnp.zeros_like(xdt_low)
        pair = jnp.concatenate([jnp.where(low_half, xdt_low, zero), jnp.where(low_half, zero, xdt_low)], 0)
        y = dot(jnp.concatenate(parts, 1), pair)
        y += wide_cols[n : 2 * n, lanes] * from_state[:, lanes] + chan[0:1, lanes] * x
        scan_out[:, lanes] = y.astype(BF16)
        fed[:, lanes] = (xdt * wide_cols[2 * n : 3 * n, lanes]).astype(BF16)
        carry[:, lanes] = held[:, lanes] * wide_cols[3 * n : 3 * n + 1, lanes]
    carry[...] += dot(write_t, fed[...])


def mix_first_kernel(tok, rows, gate_w, out_a, out_b, scanned, gain, gate_out, mixed_out, sums_out):
    gate_pre = dot(tok[...], gate_w[...])
    grad_mixed = jnp.concatenate([dot(rows[...], w[...]) for w in (out_a, out_b)], 1)
    gate_out[...] = gate_pre.astype(BF16)
    mixed_out[...] = grad_mixed.astype(BF16)
    gated = scanned[...].astype(F32) * (gate_pre * sigmoid(gate_pre))
    square = jnp.sum(gated * gated, axis=1, keepdims=True)
    inner = jnp.sum(grad_mixed * gain[0:1, :] * gated, axis=1, keepdims=True)
    lane = lax.broadcasted_iota(jnp.int32, (1, 128), 1)
    cols = jnp.where(lane == 0, square, jnp.where(lane == 1, inner, 0.0))
    sums_out[...] = cols.T[0:8, :]


def mix_first(tokens, grad_rows, weights, scanned, gain):
    length, model = tokens.shape
    width = scanned.shape[1]
    n = 256

    def rows(cols):
        return pl.BlockSpec((n, cols), lambda i: (i, 0))

    return pl.pallas_call(
        mix_first_kernel,
        grid=(length // n,),
        in_specs=[
            rows(model),
            rows(model),
            column_block(model, width, 0),
            *out_specs_of(model),
            rows(width),
            whole((8, width)),
        ],
        out_specs=[rows(width), rows(width), pl.BlockSpec((8, n), lambda i: (0, i))],
        out_shape=[
            jax.ShapeDtypeStruct((length, width), BF16),
            jax.ShapeDtypeStruct((length, width), BF16),
            jax.ShapeDtypeStruct((8, length), F32),
        ],
        compiler_params=PARAMS,
        cost_estimate=cost(10),
        name="mix_first",
    )(tokens, grad_rows, weights, weights, weights, scanned, gain)


def small_rows(value):
    high = value.astype(BF16)
    return jnp.concatenate([high, (value - high.astype(F32)).astype(BF16)], 0)


def read_small(rows):
    return rows[:16, :].astype(F32) + rows[16:, :].astype(F32)


def scan_backward_kernel(me, pre, pre_before, taps, heads, chan, sums, spread, aux, segrow, grad, state, tok, grad_gate, weights, norm_gain, gain_sums, *rest):
    row_outs, (own_a, plus_a, minus_a), (own_b, plus_b, minus_b) = rest[:4], rest[4:7], rest[7:10]
    ext, gext, act, slope, carry, fed, back, rows, low_out, taps_out, heads_out, gains, all_tok, all_low, split, packed = rest[10:]
    n = pre.shape[0]
    pairs = carry.shape[1] // 128
    wide = ext.shape[1]
    gate_width = grad_gate.shape[1]

    @pl.when(pl.program_id(0) == 0)
    def _():
        carry[...] = jnp.zeros_like(carry)
        gext[n:, :] = jnp.zeros((8, wide), F32)
        taps_out[...] = jnp.zeros_like(taps_out)
        heads_out[...] = jnp.zeros_like(heads_out)
        rows[...] = jnp.zeros_like(rows)
        gains[...] = jnp.zeros_like(gains)

    marks = aux[...]
    ext[0:8, :] = pre_before[:, :wide]
    ext[8:, :] = pre[:, :wide]
    for j in range(wide // 128):
        lanes = slice(j * 128, (j + 1) * 128)
        total = conv_strip(ext, taps, marks, j)
        sig = sigmoid(total)
        value = total * sig
        act[:, lanes] = value
        slope[:, lanes] = sig + value * (1.0 - sig)

    step_arg = pre[:, wide:] + heads[0:1, :]
    step = softplus(step_arg)
    rate = heads[1:2, :]
    row = lax.broadcasted_iota(jnp.int32, (n, n), 0)
    col = lax.broadcasted_iota(jnp.int32, (n, n), 1)
    lower = (row >= col).astype(F32)
    cum = jnp.dot(lower, -step * rate, precision=HIGH, preferred_element_type=F32)
    cum_t = cum.T
    write = act[:, pairs * 128 : (pairs + 1) * 128]
    read = act[:, (pairs + 1) * 128 : (pairs + 2) * 128]
    read_t = read.T.astype(BF16)
    write_low = write.astype(BF16)
    read_low = read.astype(BF16)
    allowed = (row <= col) & (marks[:, 8:9] == segrow[0:1, :])
    inner_t = jnp.where(allowed, dot(write_low, read_t), 0.0)
    last = cum[n - 1 : n, :]
    enters = jnp.exp(cum) * marks[:, 3:4]
    to_end = jnp.exp(last - cum) * marks[:, 4:5]
    keep = jnp.exp(last) * marks[n - 1 : n, 3:4]
    wide_cols = spread_heads(jnp.concatenate([step, enters, to_end, jnp.broadcast_to(keep, (8, 128))], 0), spread[...])
    held = state[0]
    later = carry[...]
    later_low = later.astype(BF16)
    from_state = dot(read_low, held)
    from_later = dot(write_low, later_low)
    low_half = lax.broadcasted_iota(jnp.int32, (1, 128), 1) < 64
    head_lane = lax.broadcasted_iota(jnp.int32, (1, 128), 1)
    grad_inner = jnp.zeros((n, n), F32)
    col_sums = jnp.zeros((n, 128), F32)
    to_end_part = jnp.zeros((n, 128), F32)
    enter_part = jnp.zeros((n, 128), F32)
    step_part = jnp.zeros((n, 128), F32)
    skip_part = jnp.zeros((n, 128), F32)
    keep_part = jnp.zeros((8, 128), F32)

    def head_sums(value, j):
        return dot(two_parts(value), sums[j])

    for j in range(pairs):
        lanes = slice(j * 128, (j + 1) * 128)
        x = act[:, lanes]
        dy = grad[:, lanes].astype(F32)
        step_wide = wide_cols[:n, lanes]
        xdt = x * step_wide
        xdt_low = xdt.astype(BF16)
        dy_low = dy.astype(BF16)
        zero = jnp.zeros_like(xdt_low)
        products = dot_nt(
            jnp.concatenate([jnp.where(low_half, xdt_low, zero), jnp.where(low_half, zero, xdt_low)], 0),
            dy_low,
        )
        parts = []
        for k, h in enumerate((2 * j, 2 * j + 1)):
            product = products[k * n : (k + 1) * n, :]
            decay = jnp.exp(jnp.minimum(cum_t[h : h + 1, :] - cum[:, h : h + 1], 0.0))
            scaled = decay * product
            grad_inner += scaled
            weighted = scaled * inner_t
            rows[h : h + 1, :] = jnp.sum(weighted, axis=0, keepdims=True)
            col_sums += jnp.where(head_lane == h, jnp.sum(weighted, axis=1, keepdims=True), 0.0)
            parts.append((decay * inner_t).astype(BF16))
        grad_pair = jnp.concatenate([jnp.where(low_half, dy_low, zero), jnp.where(low_half, zero, dy_low)], 0)
        grad_xdt = dot(jnp.concatenate(parts, 1), grad_pair)
        end_wide = wide_cols[2 * n : 3 * n, lanes]
        enter_wide = wide_cols[n : 2 * n, lanes]
        later_part = end_wide * from_later[:, lanes]
        grad_xdt += later_part
        to_end_part += head_sums(later_part * xdt, j)
        fed[:, lanes] = (xdt * end_wide).astype(BF16)
        grad_enter = dy * enter_wide
        back[:, lanes] = grad_enter.astype(BF16)
        enter_part += head_sums(grad_enter * from_state[:, lanes], j)
        step_part += head_sums(grad_xdt * x, j)
        skip_part += head_sums(dy * x, j)
        kept = jnp.sum(held[:, lanes].astype(F32) * later[:, lanes], axis=0, keepdims=True)
        keep_part += head_sums(jnp.broadcast_to(kept, (8, 128)), j)
        act[:, lanes] = grad_xdt * step_wide + chan[0:1, lanes] * dy
        carry[:, lanes] = later[:, lanes] * wide_cols[3 * n : 3 * n + 1, lanes]

    grad_cum = rows[...].T - col_sums + enter_part - to_end_part
    grad_last = jnp.sum(to_end_part, axis=0, keepdims=True) + keep * keep_part[0:1, :]
    upper = (row <= col).astype(F32)
    grad_log = jnp.dot(upper, grad_cum, precision=HIGH, preferred_element_type=F32) + grad_last
    grad_step = (step_part - rate * grad_log) * sigmoid(step_arg)
    heads_out[0:1, :] += jnp.sum(grad_step, axis=0, keepdims=True)
    heads_out[1:2, :] += -rate * jnp.sum(step * grad_log, axis=0, keepdims=True)
    heads_out[2:3, :] += jnp.sum(skip_part, axis=0, keepdims=True)
    low_out[:, gate_width + wide :] = grad_step.astype(BF16)

    grad_inner = jnp.where(allowed, grad_inner, 0.0)
    act[:, pairs * 128 : (pairs + 1) * 128] = dot(grad_inner.astype(BF16), read_low) + dot_nt(fed[...], later_low)
    act[:, (pairs + 1) * 128 : (pairs + 2) * 128] = dot(grad_inner.T.astype(BF16), write_low) + dot_nt(back[...], held)
    carry[...] += dot(read_t, back[...])

    for j in range(wide // 128):
        lanes = slice(j * 128, (j + 1) * 128)
        grad_pre = act[:, lanes] * slope[:, lanes]
        gext[0:n, lanes] = grad_pre
        total = taps[3:4, lanes] * grad_pre
        taps_out[3:4, lanes] += jnp.sum(grad_pre * ext[8 : 8 + n, lanes], axis=0, keepdims=True)
        taps_out[4:5, lanes] += jnp.sum(grad_pre, axis=0, keepdims=True)
        for by in (1, 2, 3):
            total += taps[3 - by : 4 - by, lanes] * (marks[:, 4 + by : 5 + by] * gext[by : by + n, lanes])
            taps_out[3 - by : 4 - by, lanes] += jnp.sum(
                grad_pre * (marks[:, by - 1 : by] * ext[8 - by : 8 - by + n, lanes]), axis=0, keepdims=True
            )
        low_out[:, gate_width + j * 128 : gate_width + (j + 1) * 128] = total.astype(BF16)
    gext[n:, :] = gext[0:8, :]

    step_id = pl.program_id(0)
    low_out[:, : grad_gate.shape[1]] = grad_gate[...]
    token_grad = dot_nt(low_out[...], weights[...])
    gains[0:1, :] += jnp.sum(token_grad * tok[...].astype(F32), axis=0, keepdims=True)
    place = pl.ds(pl.multiple_of((3 - step_id) * n, n), n)
    all_tok[place, :] = tok[...]
    all_low[place, :] = low_out[:, grad_gate.shape[1] :]
    token_low = token_grad.astype(BF16)
    for k in range(4):

        @pl.when((me[0] ^ (3 - k)) == 3 - step_id)
        def _():
            row_outs[k][...] = token_low

    @pl.when(step_id == 3)
    def _():
        deep, cut = own_a.shape[1:]
        for k in range(4):
            y = (me[1] + k) % 4
            first = pl.multiple_of(y * (4 * deep), 128)
            grad_rows = lax.dot_general(
                all_tok[:, pl.ds(first, 4 * deep)], all_low[...], TN, preferred_element_type=F32
            ).astype(BF16)
            part_a = grad_rows[:, :cut].reshape(4, deep, cut)
            if k == 0:
                own_a[...] = part_a
            elif k == 1:
                plus_a[0:4] = part_a
            elif k == 2:
                plus_a[4:6] = part_a[0:2]
                minus_a[4:6] = part_a[2:4]
            else:
                minus_a[0:4] = part_a
            split[...] = grad_rows[:, cut:]
            for d, out in ((0, own_b), (1, plus_b), (3, minus_b)):
                start = pl.multiple_of(((me[2] + d) % 4) * deep, 16)
                out[pl.ds(pl.multiple_of(y * deep, 16), deep), :] = split[pl.ds(start, deep), :]
            start = pl.multiple_of(((me[2] + 2) % 4) * deep, 16)
            place = pl.ds(pl.multiple_of(4 * deep + 32 + (y % 2) * deep, 16), deep)

            @pl.when(y < 2)
            def _():
                plus_b[place, :] = split[pl.ds(start, deep), :]

            @pl.when(y >= 2)
            def _():
                minus_b[place, :] = split[pl.ds(start, deep), :]

        width = gain_sums.shape[1]
        by_gain = gains[0:1, :] / norm_gain[0:1, :]
        packed[0:5, :] = taps_out[0:5, :]
        packed[5:6, :width] = gain_sums[0:1, :]
        packed[5:6, width:] = jnp.zeros((1, 1024 - width), F32)
        packed[6:7, :] = by_gain[:, :1024]
        packed[7:8, :512] = by_gain[:, 1024:]
        for r in range(3):
            packed[7:8, 512 + 128 * r : 640 + 128 * r] = heads_out[r : r + 1, :]
        packed[7:8, 896:] = jnp.zeros((1, 128), F32)
        sums_low = small_rows(jnp.concatenate([packed[:, :512], packed[:, 512:]], 0))
        for out in (own_b, plus_b, minus_b):
            out[4 * deep : 4 * deep + 32, :512] = sums_low
            out[4 * deep : 4 * deep + 32, 512:] = jnp.zeros((32, out.shape[1] - 512), BF16)


def scan_marks(segments):
    length = segments.shape[0]
    blocks = segments.reshape(-1, BLOCK)
    before = jnp.concatenate([jnp.full((1,), -1, jnp.int32), blocks[:-1, -1]], 0)

    def same(by):
        if by > 0:
            other = jnp.concatenate([jnp.full((by,), -1, jnp.int32), segments[:-by]], 0)
        else:
            other = jnp.concatenate([segments[-by:], jnp.full((-by,), -1, jnp.int32)], 0)
        return other == segments

    cols = [same(1), same(2), same(3), (blocks == before[:, None]).reshape(-1), (blocks == blocks[:, -1:]).reshape(-1)]
    cols += [same(-1), same(-2), same(-3), segments]
    marks = jnp.stack([c.astype(F32) for c in cols], 1)
    return jnp.pad(marks, ((0, 0), (0, 128 - len(cols)))), jnp.broadcast_to(segments.astype(F32), (8, length))


def scan_forward(tokens, weights, taps, heads, chan, spread, marks, segrow):
    length, model = tokens.shape
    cols = 1152
    inner = cols - 384
    wide = cols - 128
    n = BLOCK
    blocks = length // n


    return pl.pallas_call(
        scan_forward_kernel,
        grid=(blocks,),
        in_specs=[
            pl.BlockSpec((n, model), lambda i: (i, 0)),
            *first_specs(model),
            whole((8, wide)),
            whole((8, 128)),
            whole((8, inner)),
            whole((256, inner)),
            pl.BlockSpec((n, 128), lambda i: (i, 0)),
            pl.BlockSpec((8, n), lambda i: (0, i)),
        ],
        out_specs=[
            pl.BlockSpec((n, cols), lambda i: (i, 0)),
            pl.BlockSpec((n, inner), lambda i: (i, 0)),
            pl.BlockSpec((1, 128, inner), lambda i: (i, 0, 0)),
        ],
        out_shape=[
            jax.ShapeDtypeStruct((length, cols), F32),
            jax.ShapeDtypeStruct((length, inner), BF16),
            jax.ShapeDtypeStruct((blocks, 128, inner), BF16),
        ],
        scratch_shapes=[
            pltpu.VMEM((n + 8, wide), F32),
            pltpu.VMEM((n, wide), F32),
            pltpu.VMEM((128, inner), F32),
            pltpu.VMEM((n, inner), BF16),
        ],
        compiler_params=PARAMS,
        cost_estimate=cost(20),
        name="scan_forward",
    )(tokens, weights, weights, weights, taps, heads, chan, spread, marks, segrow)


def scan_backward(pre, taps, heads, chan, sums, spread, marks, segrow, grad, states, tokens, grad_gate, weights, norm_gain, gain_sums, me):
    length, cols = pre.shape
    model = tokens.shape[1]
    inner = cols - 384
    wide = cols - 128
    n = BLOCK
    blocks = length // n
    cut = 512
    deep = model // 16
    shapes = [(4, deep, cut), (6, deep, cut), (6, deep, cut)]
    shapes += [(4 * deep + 32, cols - cut), (6 * deep + 32, cols - cut), (6 * deep + 32, cols - cut)]

    def rev(i):
        return blocks - 1 - i

    def rows(width):
        return pl.BlockSpec((n, width), lambda i, me: (rev(i), 0))

    return pl.pallas_call(
        scan_backward_kernel,
        grid_spec=pltpu.PrefetchScalarGridSpec(
            num_scalar_prefetch=1,
            grid=(blocks,),
            in_specs=[
                rows(cols),
                pl.BlockSpec((8, cols), lambda i, me: (jnp.maximum(rev(i) * (n // 8) - 1, 0), 0)),
                whole((8, wide)),
                whole((8, 128)),
                whole((8, inner)),
                whole((inner // 128, 256, 128)),
                whole((256, inner)),
                rows(128),
                pl.BlockSpec((8, n), lambda i, me: (0, rev(i))),
                rows(inner),
                pl.BlockSpec((1, 128, inner), lambda i, me: (rev(i), 0, 0)),
                rows(model),
                rows(inner),
                column_block(model, inner + cols, 0),
                whole(norm_gain.shape),
                whole(gain_sums.shape),
            ],
            out_specs=[whole((n, model))] * 4 + [whole(shape) for shape in shapes],
            scratch_shapes=[
                pltpu.VMEM((n + 8, wide), F32),
                pltpu.VMEM((n + 8, wide), F32),
                pltpu.VMEM((n, wide), F32),
                pltpu.VMEM((n, wide), F32),
                pltpu.VMEM((128, inner), F32),
                pltpu.VMEM((n, inner), BF16),
                pltpu.VMEM((n, inner), BF16),
                pltpu.VMEM((128, n), F32),
                pltpu.VMEM((n, inner + cols), BF16),
                pltpu.VMEM((8, wide), F32),
                pltpu.VMEM((8, 128), F32),
                pltpu.VMEM((8, model), F32),
                pltpu.VMEM((length, model), BF16),
                pltpu.VMEM((length, cols), BF16),
                pltpu.VMEM((model // 4, cols - cut), BF16),
                pltpu.VMEM((8, 1024), F32),
            ],
        ),
        out_shape=[jax.ShapeDtypeStruct((n, model), BF16)] * 4
        + [jax.ShapeDtypeStruct(shape, BF16) for shape in shapes],
        compiler_params=PARAMS,
        cost_estimate=cost(30),
        name="scan_backward",
    )(me, pre, pre, taps, heads, chan, sums, spread, marks, segrow, grad, states, tokens, grad_gate, weights, norm_gain, gain_sums)


def spread_table(inner):
    head = jnp.arange(inner) // 64
    return (jnp.arange(256)[:, None] % 128 == head[None, :]).astype(BF16)


def head_sum_table(inner):
    pairs = inner // 128
    lane = jnp.arange(256) % 128
    head = 2 * jnp.arange(pairs)[:, None] + (lane >= 64)[None, :]
    return (head[:, :, None] == jnp.arange(128)[None, None, :]).astype(BF16)


def store_block(value, outs):
    for k, out in enumerate(outs):

        @pl.when(pl.program_id(0) == k)
        def _():
            out[...] = value


def mix_second_kernel(channels, me, sums, gate, grad_mixed_in, scanned_in, out_a, out_b, gain, tok, rows, grad_scan, grad_gate, gain_out, grads_out, *rest):
    outs, all_gate, all_mixed = rest[:4], rest[4], rest[5]
    step = pl.program_id(0)
    n, width = gate.shape

    @pl.when(step == 0)
    def _():
        gain_out[...] = jnp.zeros_like(gain_out)

    @pl.when(step < 4)
    def _():
        cols = jnp.concatenate([sums[...], jnp.zeros((120, n), F32)], 0).T
        scale = lax.rsqrt(cols[:, 0:1] / channels + EPS)
        pull = scale * scale * scale * (cols[:, 1:2] / channels)
        gate_pre = gate[...].astype(F32)
        grad_mixed = grad_mixed_in[...].astype(F32)
        scanned = scanned_in[...].astype(F32)
        sig = sigmoid(gate_pre)
        silu = gate_pre * sig
        gated = scanned * silu
        scaled = gated * scale
        mixed = (scaled * gain[0:1, :]).astype(BF16)
        place = pl.ds(pl.multiple_of((me[0] ^ (3 - step)) * n, n), n)
        all_mixed[place, :] = mixed
        gain_out[0:1, :] += jnp.sum(grad_mixed * scaled, axis=0, keepdims=True)
        grad_gated = scale * gain[0:1, :] * grad_mixed - gated * pull
        grad_scan[...] = (grad_gated * silu).astype(BF16)
        grad_gate_low = (grad_gated * scanned * (sig + silu * (1.0 - sig))).astype(BF16)
        grad_gate[...] = grad_gate_low
        all_gate[place, :] = grad_gate_low
        projected = dot_nt(mixed[:, :384], out_a[...]) + dot_nt(mixed[:, 384:], out_b[...])
        store_block(projected.astype(BF16), outs)

    @pl.when(step >= 4)
    def _():
        gate_part = lax.dot_general(tok[...], all_gate[...], TN, preferred_element_type=F32)
        out_part = lax.dot_general(rows[...], all_mixed[...], TN, preferred_element_type=F32)
        grads_out[:, :width] = gate_part.astype(BF16)
        grads_out[:, width:] = out_part.astype(BF16)


def mix_second(sums, gate, grad_mixed, scanned, second, gain, tokens, grad_rows, channels, spot):
    length, width = gate.shape
    model = second.shape[0]
    n = 256
    m = model // 4

    def token_block(i, me):
        return me[0] ^ (3 - jnp.minimum(i, 3))

    def rows(cols):
        return pl.BlockSpec((n, cols), lambda i, me: (token_block(i, me), 0))

    def cols():
        return pl.BlockSpec((length, m), lambda i, me: (0, jnp.maximum(i - 4, 0)))

    return pl.pallas_call(
        lambda *refs: mix_second_kernel(channels, *refs),
        grid_spec=pltpu.PrefetchScalarGridSpec(
            num_scalar_prefetch=1,
            grid=(8,),
            in_specs=[
                pl.BlockSpec((8, n), lambda i, me: (0, token_block(i, me))),
                rows(width),
                rows(width),
                rows(width),
                *out_specs_of(model),
                whole((8, width)),
                cols(),
                cols(),
            ],
            out_specs=[
                rows(width),
                rows(width),
                whole((8, width)),
                pl.BlockSpec((m, 2 * width), lambda i, me: (jnp.maximum(i - 4, 0), 0)),
            ]
            + [whole((n, model))] * 4,
            scratch_shapes=[pltpu.VMEM((length, width), BF16), pltpu.VMEM((length, width), BF16)],
        ),
        out_shape=[
            jax.ShapeDtypeStruct((length, width), BF16),
            jax.ShapeDtypeStruct((length, width), BF16),
            jax.ShapeDtypeStruct((8, width), F32),
            jax.ShapeDtypeStruct((model, 2 * width), BF16),
        ]
        + [jax.ShapeDtypeStruct((n, model), BF16)] * 4,
        compiler_params=PARAMS,
        cost_estimate=cost(11),
        name="mix_second",
    )(spot, sums, gate, grad_mixed, scanned, second, second, gain, tokens, grad_rows)


def four_sum(own, ahead, across, behind):
    return (own.astype(F32) + across.astype(F32)) + (ahead.astype(F32) + behind.astype(F32))


def add_split_kernel(me, *refs):
    own_a, back_a, next_a, low_a, high_a = refs[:5]
    own_b, back_b, next_b, low_b, high_b = refs[5:10]
    outs_a, outs_b = refs[10:14], refs[14:]
    deep = outs_a[0].shape[0]
    here = slice(4 * deep, 4 * deep + 32)
    sums = four_sum(*[read_small(rows) for rows in (own_b[here, :512], next_b[here, :512], low_b[:32, :512], back_b[here, :512])])
    sums = small_rows(sums)
    for d in range(4):
        e = (me[0] + d) % 4
        across = jnp.where(e < 2, low_a[e % 2], high_a[e % 2])
        outs_a[d][...] = four_sum(own_a[e], next_a[e], across, back_a[e]).astype(BF16)
        e = (me[1] + d) % 4
        place = pl.ds(pl.multiple_of(e * deep, 16), deep)
        half = pl.ds(pl.multiple_of((e % 2) * deep + 32, 16), deep)
        across = jnp.where(e < 2, low_b[half, :], high_b[half, :])
        outs_b[d][:deep, :] = four_sum(own_b[place, :], next_b[place, :], across, back_b[place, :]).astype(BF16)
        outs_b[d][deep:, :512] = sums
        outs_b[d][deep:, 512:] = jnp.zeros((32, outs_b[d].shape[1] - 512), BF16)


def add_split(parts_a, parts_b, me):
    deep, width_a = parts_a[0].shape[1:]
    width_b = parts_b[0].shape[1]
    outs = pl.pallas_call(
        add_split_kernel,
        in_specs=[pl.BlockSpec(memory_space=pltpu.SMEM)] + [VMEM_SPEC] * 10,
        out_specs=[VMEM_SPEC] * 8,
        out_shape=[jax.ShapeDtypeStruct((deep, width_a), BF16)] * 4 + [jax.ShapeDtypeStruct((deep + 32, width_b), BF16)] * 4,
        compiler_params=PARAMS,
        name="add_split",
    )(me, *parts_a, *parts_b)
    return outs[:4], outs[4:]


def add_halve_kernel(me, *refs):
    ins, (keep, sums, give, total) = refs[:8], refs[8:]
    rows, cut = ins[0].shape
    total[:, :cut] = four_sum(*[part[...] for part in ins[:4]])
    total[:, cut:] = four_sum(*[part[:rows, :] for part in ins[4:]])
    n = keep.shape[0]
    keep[...] = total[pl.ds(pl.multiple_of(me[0] * n, 16), n), :]
    give[:n, :] = total[pl.ds(pl.multiple_of((1 - me[0]) * n, 16), n), :].astype(BF16)
    low = small_rows(four_sum(*[read_small(part[rows:, :512]) for part in ins[4:]]))
    give[n:, :512] = low
    give[n:, 512:] = jnp.zeros((32, give.shape[1] - 512), BF16)
    sums[...] = read_small(low)


def add_halve(parts_a, parts_b, me):
    rows = parts_a[0].shape[0]
    width = parts_a[0].shape[1] + parts_b[0].shape[1]
    return pl.pallas_call(
        add_halve_kernel,
        in_specs=[pl.BlockSpec(memory_space=pltpu.SMEM)] + [VMEM_SPEC] * 8,
        out_specs=[VMEM_SPEC] * 3,
        out_shape=[
            jax.ShapeDtypeStruct((rows // 2, width), F32),
            jax.ShapeDtypeStruct((16, 512), F32),
            jax.ShapeDtypeStruct((rows // 2 + 32, width), BF16),
        ],
        scratch_shapes=[pltpu.VMEM((rows, width), F32)],
        compiler_params=PARAMS,
        name="add_halve",
    )(me, *parts_a, *parts_b)


def place_kernel(me, *refs):
    out = refs[-1]
    for k, part in enumerate(refs[:-1]):

        @pl.when(pl.program_id(0) == k)
        def _():
            out[...] = part[...].reshape(out.shape)


def place(parts, index, me, shape, block, name):
    return pl.pallas_call(
        place_kernel,
        grid_spec=pltpu.PrefetchScalarGridSpec(
            num_scalar_prefetch=1,
            grid=(len(parts),),
            in_specs=[whole(p.shape) for p in parts],
            out_specs=pl.BlockSpec(block, lambda i, me: index(i, me[0])),
        ),
        out_shape=jax.ShapeDtypeStruct(shape, parts[0].dtype),
        compiler_params=PARAMS,
        cost_estimate=cost(2),
        name=name,
    )(me, *parts)


def shift(value, axis, by):
    n = SIZES[axis]
    return lax.ppermute(value, axis, [(i, (i - by) % n) for i in range(n)])


def swap(value, axis):
    return shift(value, axis, 1)


def ring(value, axis):
    return [value, shift(value, axis, 1), shift(value, axis, 2), shift(value, axis, -1)]


def sends(blocks, axis):
    return [blocks[0], shift(blocks[1], axis, -1), shift(blocks[2], axis, 2), shift(blocks[3], axis, 1)]


def relay(messages, axis, cut):
    own, plus, minus = messages
    back, ahead = shift(plus, axis, -1), shift(minus, axis, 1)
    return [own, back, ahead, shift(back[cut:], axis, -1), shift(ahead[cut:], axis, 1)]


def tensor_xor(value, by):
    return lax.ppermute(value, TENSOR, [(i, i ^ by) for i in range(4)])


def sum_ring(value, axis):
    own, ahead, across, behind = ring(value, axis)
    return (own + across) + (ahead + behind)


def sum_pair(value, axis):
    return value + swap(value, axis)


def after(value, *others):
    return lax.optimization_barrier((value,) + others)[0]


def index_of(axis):
    return lax.axis_index(axis).reshape(1).astype(jnp.int32)


def pair_kernel(me, main, other_main, side, other_side, out):
    cut, middle = 1536, side.shape[1]
    for k, (left, right) in enumerate(((main, side), (other_main, other_side))):

        @pl.when(pl.program_id(0) == k)
        def _():
            out[:, :cut] = left[:, :cut]
            out[:, cut : cut + middle] = right[...]
            out[:, cut + middle :] = left[:, cut:]


def pair_rows(main, side):
    rows = main.shape[0]
    width = main.shape[1] + side.shape[1]
    parts = [main, swap(main, "zl"), side, swap(side, "zl")]
    return pl.pallas_call(
        pair_kernel,
        grid_spec=pltpu.PrefetchScalarGridSpec(
            num_scalar_prefetch=1,
            grid=(2,),
            in_specs=[whole(p.shape) for p in parts],
            out_specs=pl.BlockSpec((rows, width), lambda i, me: ((me[0] + i) % 2, 0)),
        ),
        out_shape=jax.ShapeDtypeStruct((2 * rows, width), BF16),
        compiler_params=PARAMS,
        name="pair_rows",
    )(index_of("zl"), *parts)


def token_place(own, near, far, both, me):
    rows, width = own.shape
    return place([own, near, far, both], lambda i, me: (me ^ i, 0), me, (4 * rows, width), (rows, width), "place_tokens")


def per_device(
    hidden_in,
    norm_gain,
    proj_zx,
    proj_shared,
    proj_step,
    conv_inner,
    conv_shared,
    step_bias,
    decay_log,
    skip_gain,
    gated_gain,
    proj_out,
    out_grad,
    segments,
):
    model_width = hidden_in.shape[1]
    width = proj_zx.shape[2]
    heads = step_bias.shape[0]
    me = {axis: index_of(axis) for axis in DP + TENSOR}
    spot = 2 * me["zh"] + me["c"]

    shared_parts = [proj_shared] + [tensor_xor(proj_shared, by) for by in (1, 2, 3)]
    shared_rows = jnp.zeros((48, 256), BF16)
    for by, part in enumerate(shared_parts):
        shared_rows = lax.dynamic_update_slice(shared_rows, part, (((spot[0] ^ by) * 12), jnp.int32(0)))
    side_rows = jnp.concatenate([shared_rows, jnp.pad(proj_step, ((0, 0), (0, 128 - heads)))], 1)
    main_rows = jnp.concatenate([proj_zx[:, 0, :], proj_zx[:, 1, :], proj_out.T], 1)
    weights = lax.all_gather(pair_rows(main_rows, side_rows), ("y", "x"), axis=0, tiled=True)

    residual_in = hidden_in.astype(F32)
    scale_in = lax.rsqrt(jnp.mean(residual_in * residual_in, axis=-1, keepdims=True) + EPS)
    normed_low = (residual_in * scale_in * norm_gain).astype(BF16)
    normed_far = swap(normed_low, "zh")
    normed_near = swap(normed_low, "c")

    normed_both = swap(normed_far, "c")
    tokens = token_place(normed_low, normed_near, normed_far, normed_both, spot)
    grad_far = swap(after(out_grad, normed_far), "zh")
    grad_near = swap(after(out_grad, normed_far), "c")
    grad_both = swap(grad_far, "c")
    grad_rows = token_place(out_grad, grad_near, grad_far, grad_both, spot)

    pad = (0, 128 - heads)
    head_rows = jnp.stack([jnp.pad(step_bias, pad), jnp.pad(jnp.exp(decay_log), pad)], 0)
    head_rows = jnp.pad(head_rows, ((0, 6), (0, 0)))
    taps = jnp.pad(jnp.concatenate([conv_inner, conv_shared], 1), ((0, 3), (0, 0)))
    chan = jnp.broadcast_to(jnp.repeat(skip_gain, width // heads), (8, width))
    gain = jnp.broadcast_to(gated_gain, (8, width))
    norm_rows = jnp.broadcast_to(norm_gain, (8, model_width))
    marks, segrow = scan_marks(segments)
    spread = spread_table(width)
    sum_table = head_sum_table(width)
    tokens, grad_rows = lax.optimization_barrier((tokens, grad_rows))
    pre, scanned, states = scan_forward(tokens, weights, taps, head_rows, chan, spread, marks, segrow)
    gate_pre, grad_mixed, sums = mix_first(tokens, grad_rows, weights, scanned, gain)

    sums = sum_pair(sum_pair(sums, "c"), "zh")
    grad_scanned, gate_grad_low, gain_sums, second_total, *out_blocks = mix_second(
        sums, gate_pre, grad_mixed, scanned, weights, gain, tokens, grad_rows, 4 * width, spot
    )
    out_far = (out_blocks[1].astype(F32) + swap(out_blocks[0], "c").astype(F32)).astype(BF16)
    out_near = swap(out_blocks[2], "c")
    second_sum = lax.psum_scatter(second_total, ("y", "x"), scatter_dimension=0, tiled=True)
    out_far_got = swap(out_far, "zh")

    grad_scanned = after(grad_scanned, out_far, second_total)
    sent = scan_backward(
        pre,
        taps,
        head_rows,
        chan,
        sum_table,
        spread,
        marks,
        segrow,
        grad_scanned,
        states,
        tokens,
        gate_grad_low,
        weights,
        norm_rows,
        gain_sums,
        jnp.concatenate([spot, me["y"], me["x"]]),
    )
    row_blocks = [after(block, out_far_got, out_near) for block in sent[:4]]
    far_got = swap(row_blocks[0], "c")
    row_far = (row_blocks[1].astype(F32) + far_got.astype(F32)).astype(BF16)
    row_far_got = swap(row_far, "zh")
    ready = [after(block, row_far) for block in sent[4:]]
    parts_a = relay(ready[:3], "y", 4)
    parts_b = relay(ready[3:], "x", 384)
    half_a, half_b = add_split(parts_a, parts_b, jnp.concatenate([me["x"], me["y"]]))
    near_got = swap(after(row_blocks[2], *half_a), "c")

    hidden_out = (
        residual_in + (out_blocks[3].astype(F32) + out_near.astype(F32) + out_far_got.astype(F32))
    ).astype(BF16)
    grad_normed = row_blocks[3].astype(F32) + near_got.astype(F32) + row_far_got.astype(F32)
    weighted = jnp.sum(grad_normed * norm_gain * residual_in, axis=-1, keepdims=True)
    grad_hidden = (
        out_grad.astype(F32)
        + scale_in * norm_gain * grad_normed
        - residual_in * scale_in**3 * weighted / model_width
    ).astype(BF16)
    parts_a = [after(part, row_far_got, second_sum) for part in sends(half_a, "x")]
    parts_b = [after(part, row_far_got, second_sum) for part in sends(half_b, "y")]
    first_keep, small, first_give = add_halve(parts_a, parts_b, me["zl"])
    first_got = swap(first_give, "zl")
    first_mine = first_keep + first_got[:48].astype(F32)
    small = small + read_small(first_got[48:, :512])
    second_pairs = second_sum.reshape(2, 48, 2 * width)
    second_keep = lax.dynamic_index_in_dim(second_pairs, me["zl"][0], 0, keepdims=False)
    second_mine = second_keep.astype(F32) + swap(
        lax.dynamic_index_in_dim(second_pairs, 1 - me["zl"][0], 0, keepdims=False), "zl"
    ).astype(F32)
    grad_proj_out = second_mine[:, width:].T
    grad_proj_zx = jnp.stack([second_mine[:, :width], first_mine[:, :width]], 1)
    grad_proj_step = first_mine[:, width + 256 : width + 256 + heads]

    def quarter(by):
        part = lax.dynamic_slice(first_mine, ((spot[0] ^ by) * 12, jnp.int32(width)), (12, 256))
        return jnp.concatenate([small, jnp.pad(part, ((0, 0), (0, 256)))], 0)

    summed = (quarter(0) + tensor_xor(quarter(1), 1)) + (tensor_xor(quarter(2), 2) + tensor_xor(quarter(3), 3))
    rest = width - 512
    return (
        hidden_out,
        grad_hidden,
        jnp.concatenate([summed[6], summed[14], summed[7]]),
        grad_proj_zx,
        summed[16:, :256],
        grad_proj_step,
        jnp.concatenate([small[:5], small[8:13, :rest]], 1),
        summed[8:13, rest:],
        small[15, :heads],
        small[15, 128 : 128 + heads],
        small[15, 256 : 256 + heads],
        jnp.concatenate([small[5], small[13, :rest]]),
        grad_proj_out,
    )


def solution(mesh):
    fine = Mesh(mesh.devices.reshape(4, 4, 2, 2, 2), DP + TENSOR)
    both = DP + TENSOR
    return jax.shard_map(
        per_device,
        mesh=fine,
        in_specs=(
            P(both, None),
            P(),
            P(DP, None, TENSOR),
            P(both, None),
            P(DP, TENSOR),
            P(None, TENSOR),
            P(),
            P(TENSOR),
            P(TENSOR),
            P(TENSOR),
            P(TENSOR),
            P(TENSOR, DP),
            P(both, None),
            P(DP),
        ),
        out_specs=(
            P(both, None),
            P(both, None),
            P(),
            P(DP, None, TENSOR),
            P(both, None),
            P(DP, TENSOR),
            P(None, TENSOR),
            P(),
            P(TENSOR),
            P(TENSOR),
            P(TENSOR),
            P(TENSOR),
            P(TENSOR, DP),
        ),
        check_vma=False,
    )
```

```python
import jax
import jax.numpy as jnp
from jax import lax
from jax.experimental import pallas as pl
from jax.experimental.pallas import tpu as pltpu
from jax.sharding import Mesh
from jax.sharding import PartitionSpec as P

EPS = 1e-05
DP = ("y", "x", "zl")
TENSOR = ("zh", "c")
SIZES = {"y": 4, "x": 4, "zl": 2, "zh": 2, "c": 2}

F32 = jnp.float32
BF16 = jnp.bfloat16
HIGH = lax.Precision.HIGHEST
FORWARD_BLOCK = 128
BACKWARD_BLOCK = 256
VMEM = 56 * 1024 * 1024
PARAMS = pltpu.CompilerParams(vmem_limit_bytes=VMEM)
NT = (((1,), (1,)), ((), ()))
TN = (((0,), (0,)), ((), ()))
VMEM_SPEC = pl.BlockSpec(memory_space=pltpu.VMEM)


def cost(us):
    return pl.CostEstimate(flops=int(us * 1e6), transcendentals=0, bytes_accessed=int(us * 3e3))


def whole(shape):
    return pl.BlockSpec(shape, lambda *i: (0,) * len(shape))


def column_block(rows, width, index):
    return pl.BlockSpec((rows, width), lambda *i: (0, index))


def first_specs(rows):
    return [column_block(rows, 384, index) for index in (2, 3, 4)]


def out_specs_of(rows):
    return [column_block(rows, 384, index) for index in (5, 6)]


def dot(a, b):
    return jnp.dot(a, b, preferred_element_type=F32)


def dot_nt(a, b):
    return lax.dot_general(a, b, NT, preferred_element_type=F32)


def sigmoid(a):
    return 0.5 * jnp.tanh(0.5 * a) + 0.5


def softplus(a):
    return jnp.maximum(a, 0.0) + jnp.log1p(jnp.exp(-jnp.abs(a)))


def conv_strip(ext, taps, aux, j):
    n = ext.shape[0] - 8
    lanes = slice(j * 128, (j + 1) * 128)
    total = taps[4:5, lanes] + taps[3:4, lanes] * ext[8 : 8 + n, lanes]
    for back in (1, 2, 3):
        total += taps[3 - back : 4 - back, lanes] * (
            aux[:, back - 1 : back] * ext[8 - back : 8 - back + n, lanes]
        )
    return total


def two_parts(value):
    high = value.astype(BF16)
    return jnp.concatenate([high, (value - high.astype(F32)).astype(BF16)], 1)


def spread_heads(cols, table):
    return dot(two_parts(cols), table)


def scan_forward_kernel(tok, rows, gate_w, out_a, out_b, weights_a, weights_b, weights_c, taps, heads, chan, gain, spread, aux, segrow, pre_out, scan_low, state_out, gate_low, mixed_low, sums_out, ext, act, carry, fed, scan_out, gate_out, mixed_out):
    n = tok.shape[0]
    pairs = carry.shape[1] // 128

    @pl.when(pl.program_id(0) == 0)
    def _():
        carry[...] = jnp.zeros_like(carry)
        ext[0:8, :] = jnp.zeros((8, ext.shape[1]), F32)

    pre = jnp.concatenate([dot(tok[...], w[...]) for w in (weights_a, weights_b, weights_c)], 1)
    pre_out[...] = pre
    wide = ext.shape[1]
    ext[8:, :] = pre[:, :wide]
    marks = aux[...]
    for j in range(wide // 128):
        total = conv_strip(ext, taps, marks, j)
        act[:, j * 128 : (j + 1) * 128] = total * sigmoid(total)
    ext[0:8, :] = ext[n : n + 8, :]

    step = softplus(pre[:, wide:] + heads[0:1, :])
    log_step = -step * heads[1:2, :]
    row = lax.broadcasted_iota(jnp.int32, (n, n), 0)
    col = lax.broadcasted_iota(jnp.int32, (n, n), 1)
    lower = (row >= col).astype(F32)
    cum = jnp.dot(lower, log_step, precision=HIGH, preferred_element_type=F32)
    cum_t = cum.T
    write = act[:, pairs * 128 : (pairs + 1) * 128]
    read = act[:, (pairs + 1) * 128 : (pairs + 2) * 128].astype(BF16)
    write_t = write.T.astype(BF16)
    allowed = (row >= col) & (marks[:, 8:9] == segrow[0:1, :])
    inner = jnp.where(allowed, dot(read, write_t), 0.0)
    last = cum[n - 1 : n, :]
    enters = jnp.exp(cum) * marks[:, 3:4]
    to_end = jnp.exp(last - cum) * marks[:, 4:5]
    keep = jnp.exp(last) * marks[n - 1 : n, 3:4]
    wide_cols = spread_heads(jnp.concatenate([step, enters, to_end, jnp.broadcast_to(keep, (8, 128))], 0), spread[...])
    held = carry[...]
    held_low = held.astype(BF16)
    state_out[0] = held_low
    from_state = dot(read, held_low)
    low_half = lax.broadcasted_iota(jnp.int32, (1, 128), 1) < 64
    for j in range(pairs):
        lanes = slice(j * 128, (j + 1) * 128)
        x = act[:, lanes]
        xdt = x * wide_cols[:n, lanes]
        parts = []
        for h in (2 * j, 2 * j + 1):
            decay = jnp.exp(jnp.minimum(cum[:, h : h + 1] - cum_t[h : h + 1, :], 0.0))
            parts.append((decay * inner).astype(BF16))
        xdt_low = xdt.astype(BF16)
        zero = jnp.zeros_like(xdt_low)
        pair = jnp.concatenate([jnp.where(low_half, xdt_low, zero), jnp.where(low_half, zero, xdt_low)], 0)
        y = dot(jnp.concatenate(parts, 1), pair)
        if j % 2 == 0:
            block = slice(128 * j, 128 * j + 256)
            gate_out[:, block] = dot(tok[...], gate_w[:, block])
        else:
            spot = 256 * (j // 2)
            out_w = (out_a[:, 0:256], jnp.concatenate([out_a[:, 256:], out_b[:, :128]], 1), out_b[:, 128:])[j // 2]
            mixed_out[:, spot : spot + 256] = dot(rows[...], out_w)
        y += wide_cols[n : 2 * n, lanes] * from_state[:, lanes] + chan[0:1, lanes] * x
        scan_out[:, lanes] = y
        fed[:, lanes] = (xdt * wide_cols[2 * n : 3 * n, lanes]).astype(BF16)
        carry[:, lanes] = held[:, lanes] * wide_cols[3 * n : 3 * n + 1, lanes]
    carry[...] += dot(write_t, fed[...])

    gate_pre = gate_out[...]
    grad_mixed = mixed_out[...]
    scanned = scan_out[...]
    gate_low[...] = gate_pre.astype(BF16)
    mixed_low[...] = grad_mixed.astype(BF16)
    scan_low[...] = scanned.astype(BF16)
    gated = scanned * (gate_pre * sigmoid(gate_pre))
    square = jnp.sum(gated * gated, axis=1, keepdims=True)
    inner = jnp.sum(grad_mixed * gain[0:1, :] * gated, axis=1, keepdims=True)
    lane = lax.broadcasted_iota(jnp.int32, (1, 128), 1)
    cols = jnp.where(lane == 0, square, jnp.where(lane == 1, inner, 0.0))
    sums_out[...] = cols.T[0:8, :]


def small_rows(value):
    high = value.astype(BF16)
    return jnp.concatenate([high, (value - high.astype(F32)).astype(BF16)], 0)


def read_small(rows):
    return rows[:16, :].astype(F32) + rows[16:, :].astype(F32)


def scan_backward_kernel(me, pre, pre_before, taps, heads, chan, sums, spread, aux, segrow, grad, state, tok, grad_gate, weights, norm_gain, gain_sums, *rest):
    row_outs, outs_a, outs_b = rest[:4], rest[4:8], rest[8:12]
    ext, gext, act, slope, carry, fed, back, rows, low_out, taps_out, heads_out, gains, all_tok, all_low, split, packed = rest[12:]
    n = pre.shape[0]
    pairs = carry.shape[1] // 128
    wide = ext.shape[1]
    gate_width = grad_gate.shape[1]

    @pl.when(pl.program_id(0) == 0)
    def _():
        carry[...] = jnp.zeros_like(carry)
        gext[n:, :] = jnp.zeros((8, wide), F32)
        taps_out[...] = jnp.zeros_like(taps_out)
        heads_out[...] = jnp.zeros_like(heads_out)
        rows[...] = jnp.zeros_like(rows)
        gains[...] = jnp.zeros_like(gains)

    marks = aux[...]
    ext[0:8, :] = pre_before[:, :wide]
    ext[8:, :] = pre[:, :wide]
    for j in range(wide // 128):
        lanes = slice(j * 128, (j + 1) * 128)
        total = conv_strip(ext, taps, marks, j)
        sig = sigmoid(total)
        value = total * sig
        act[:, lanes] = value
        slope[:, lanes] = sig + value * (1.0 - sig)

    step_arg = pre[:, wide:] + heads[0:1, :]
    step = softplus(step_arg)
    rate = heads[1:2, :]
    row = lax.broadcasted_iota(jnp.int32, (n, n), 0)
    col = lax.broadcasted_iota(jnp.int32, (n, n), 1)
    lower = (row >= col).astype(F32)
    cum = jnp.dot(lower, -step * rate, precision=HIGH, preferred_element_type=F32)
    cum_t = cum.T
    write = act[:, pairs * 128 : (pairs + 1) * 128]
    read = act[:, (pairs + 1) * 128 : (pairs + 2) * 128]
    read_t = read.T.astype(BF16)
    write_low = write.astype(BF16)
    read_low = read.astype(BF16)
    allowed = (row <= col) & (marks[:, 8:9] == segrow[0:1, :])
    inner_t = jnp.where(allowed, dot(write_low, read_t), 0.0)
    last = cum[n - 1 : n, :]
    enters = jnp.exp(cum) * marks[:, 9:10]
    to_end = jnp.exp(last - cum) * marks[:, 10:11]
    keep = jnp.exp(last) * marks[n - 1 : n, 9:10]
    wide_cols = spread_heads(jnp.concatenate([step, enters, to_end, jnp.broadcast_to(keep, (8, 128))], 0), spread[...])
    held = state[0]
    later = carry[...]
    later_low = later.astype(BF16)
    from_state = dot(read_low, held)
    from_later = dot(write_low, later_low)
    low_half = lax.broadcasted_iota(jnp.int32, (1, 128), 1) < 64
    head_lane = lax.broadcasted_iota(jnp.int32, (1, 128), 1)
    grad_inner = jnp.zeros((n, n), F32)
    col_sums = jnp.zeros((n, 128), F32)
    to_end_part = jnp.zeros((n, 128), F32)
    enter_part = jnp.zeros((n, 128), F32)
    step_part = jnp.zeros((n, 128), F32)
    skip_part = jnp.zeros((n, 128), F32)
    keep_part = jnp.zeros((8, 128), F32)

    def head_sums(value, j):
        return dot(two_parts(value), sums[j])

    for j in range(pairs):
        lanes = slice(j * 128, (j + 1) * 128)
        x = act[:, lanes]
        dy = grad[:, lanes].astype(F32)
        step_wide = wide_cols[:n, lanes]
        xdt = x * step_wide
        xdt_low = xdt.astype(BF16)
        dy_low = dy.astype(BF16)
        zero = jnp.zeros_like(xdt_low)
        products = dot_nt(
            jnp.concatenate([jnp.where(low_half, xdt_low, zero), jnp.where(low_half, zero, xdt_low)], 0),
            dy_low,
        )
        parts = []
        for k, h in enumerate((2 * j, 2 * j + 1)):
            product = products[k * n : (k + 1) * n, :]
            decay = jnp.exp(jnp.minimum(cum_t[h : h + 1, :] - cum[:, h : h + 1], 0.0))
            scaled = decay * product
            grad_inner += scaled
            weighted = scaled * inner_t
            rows[h : h + 1, :] = jnp.sum(weighted, axis=0, keepdims=True)
            col_sums += jnp.where(head_lane == h, jnp.sum(weighted, axis=1, keepdims=True), 0.0)
            parts.append((decay * inner_t).astype(BF16))
        grad_pair = jnp.concatenate([jnp.where(low_half, dy_low, zero), jnp.where(low_half, zero, dy_low)], 0)
        grad_xdt = dot(jnp.concatenate(parts, 1), grad_pair)
        end_wide = wide_cols[2 * n : 3 * n, lanes]
        enter_wide = wide_cols[n : 2 * n, lanes]
        later_part = end_wide * from_later[:, lanes]
        grad_xdt += later_part
        to_end_part += head_sums(later_part * xdt, j)
        fed[:, lanes] = (xdt * end_wide).astype(BF16)
        grad_enter = dy * enter_wide
        back[:, lanes] = grad_enter.astype(BF16)
        enter_part += head_sums(grad_enter * from_state[:, lanes], j)
        step_part += head_sums(grad_xdt * x, j)
        skip_part += head_sums(dy * x, j)
        kept = jnp.sum(held[:, lanes].astype(F32) * later[:, lanes], axis=0, keepdims=True)
        keep_part += head_sums(jnp.broadcast_to(kept, (8, 128)), j)
        act[:, lanes] = grad_xdt * step_wide + chan[0:1, lanes] * dy
        carry[:, lanes] = later[:, lanes] * wide_cols[3 * n : 3 * n + 1, lanes]

    grad_cum = rows[...].T - col_sums + enter_part - to_end_part
    grad_last = jnp.sum(to_end_part, axis=0, keepdims=True) + keep * keep_part[0:1, :]
    upper = (row <= col).astype(F32)
    grad_log = jnp.dot(upper, grad_cum, precision=HIGH, preferred_element_type=F32) + grad_last
    grad_step = (step_part - rate * grad_log) * sigmoid(step_arg)
    heads_out[0:1, :] += jnp.sum(grad_step, axis=0, keepdims=True)
    heads_out[1:2, :] += -rate * jnp.sum(step * grad_log, axis=0, keepdims=True)
    heads_out[2:3, :] += jnp.sum(skip_part, axis=0, keepdims=True)
    low_out[:, gate_width + wide :] = grad_step.astype(BF16)

    grad_inner = jnp.where(allowed, grad_inner, 0.0)
    act[:, pairs * 128 : (pairs + 1) * 128] = dot(grad_inner.astype(BF16), read_low) + dot_nt(fed[...], later_low)
    act[:, (pairs + 1) * 128 : (pairs + 2) * 128] = dot(grad_inner.T.astype(BF16), write_low) + dot_nt(back[...], held)
    carry[...] += dot(read_t, back[...])

    for j in range(wide // 128):
        lanes = slice(j * 128, (j + 1) * 128)
        grad_pre = act[:, lanes] * slope[:, lanes]
        gext[0:n, lanes] = grad_pre
        total = taps[3:4, lanes] * grad_pre
        taps_out[3:4, lanes] += jnp.sum(grad_pre * ext[8 : 8 + n, lanes], axis=0, keepdims=True)
        taps_out[4:5, lanes] += jnp.sum(grad_pre, axis=0, keepdims=True)
        for by in (1, 2, 3):
            total += taps[3 - by : 4 - by, lanes] * (marks[:, 4 + by : 5 + by] * gext[by : by + n, lanes])
            taps_out[3 - by : 4 - by, lanes] += jnp.sum(
                grad_pre * (marks[:, by - 1 : by] * ext[8 - by : 8 - by + n, lanes]), axis=0, keepdims=True
            )
        low_out[:, gate_width + j * 128 : gate_width + (j + 1) * 128] = total.astype(BF16)
    gext[n:, :] = gext[0:8, :]

    step_id = pl.program_id(0)
    low_out[:, : grad_gate.shape[1]] = grad_gate[...]
    token_grad = dot_nt(low_out[...], weights[...])
    gains[0:1, :] += jnp.sum(token_grad * tok[...].astype(F32), axis=0, keepdims=True)
    place = pl.ds(pl.multiple_of((3 - step_id) * n, n), n)
    all_tok[place, :] = tok[...]
    all_low[place, :] = low_out[:, grad_gate.shape[1] :]
    token_low = token_grad.astype(BF16)
    for k in range(4):

        @pl.when((me[0] ^ (3 - k)) == 3 - step_id)
        def _():
            row_outs[k][...] = token_low

    @pl.when(step_id == 3)
    def _():
        cut = outs_a[0].shape[2]
        deep = outs_a[0].shape[1]
        for k in range(4):
            first = pl.multiple_of(((me[1] + k) % 4) * (4 * deep), 128)
            grad_rows = lax.dot_general(
                all_tok[:, pl.ds(first, 4 * deep)], all_low[...], TN, preferred_element_type=F32
            ).astype(BF16)
            outs_a[k][...] = grad_rows[:, :cut].reshape(outs_a[k].shape)
            split[...] = grad_rows[:, cut:]
            y = (me[1] + k) % 4
            for d in range(4):
                start = pl.multiple_of(((me[2] + d) % 4) * deep, 16)
                outs_b[d][pl.ds(pl.multiple_of(y * deep, 16), deep), :] = split[pl.ds(start, deep), :]
        width = gain_sums.shape[1]
        by_gain = gains[0:1, :] / norm_gain[0:1, :]
        packed[0:5, :] = taps_out[0:5, :]
        packed[5:6, :width] = gain_sums[0:1, :]
        packed[5:6, width:] = jnp.zeros((1, 1024 - width), F32)
        packed[6:7, :] = by_gain[:, :1024]
        packed[7:8, :512] = by_gain[:, 1024:]
        for r in range(3):
            packed[7:8, 512 + 128 * r : 640 + 128 * r] = heads_out[r : r + 1, :]
        packed[7:8, 896:] = jnp.zeros((1, 128), F32)
        sums_low = small_rows(jnp.concatenate([packed[:, :512], packed[:, 512:]], 0))
        for k in range(4):
            outs_b[k][4 * deep :, :512] = sums_low
            outs_b[k][4 * deep :, 512:] = jnp.zeros((32, outs_b[k].shape[1] - 512), BF16)


def scan_marks(segments):
    length = segments.shape[0]

    def same(by):
        if by > 0:
            other = jnp.concatenate([jnp.full((by,), -1, jnp.int32), segments[:-by]], 0)
        else:
            other = jnp.concatenate([segments[-by:], jnp.full((-by,), -1, jnp.int32)], 0)
        return other == segments

    def ends(size):
        blocks = segments.reshape(-1, size)
        before = jnp.concatenate([jnp.full((1,), -1, jnp.int32), blocks[:-1, -1]], 0)
        return [(blocks == before[:, None]).reshape(-1), (blocks == blocks[:, -1:]).reshape(-1)]

    cols = [same(1), same(2), same(3), *ends(FORWARD_BLOCK)]
    cols += [same(-1), same(-2), same(-3), segments, *ends(BACKWARD_BLOCK)]
    marks = jnp.stack([c.astype(F32) for c in cols], 1)
    return jnp.pad(marks, ((0, 0), (0, 128 - len(cols)))), jnp.broadcast_to(segments.astype(F32), (8, length))


def scan_forward(tokens, grad_rows, weights, taps, heads, chan, gain, spread, marks, segrow):
    length, model = tokens.shape
    cols = 1152
    inner = cols - 384
    wide = cols - 128
    n = FORWARD_BLOCK
    blocks = length // n


    return pl.pallas_call(
        scan_forward_kernel,
        grid=(blocks,),
        in_specs=[
            pl.BlockSpec((n, model), lambda i: (i, 0)),
            pl.BlockSpec((n, model), lambda i: (i, 0)),
            column_block(model, inner, 0),
            *out_specs_of(model),
            *first_specs(model),
            whole((8, wide)),
            whole((8, 128)),
            whole((8, inner)),
            whole((8, inner)),
            whole((256, inner)),
            pl.BlockSpec((n, 128), lambda i: (i, 0)),
            pl.BlockSpec((8, n), lambda i: (0, i)),
        ],
        out_specs=[
            pl.BlockSpec((n, cols), lambda i: (i, 0)),
            pl.BlockSpec((n, inner), lambda i: (i, 0)),
            pl.BlockSpec((1, 128, inner), lambda i: (i, 0, 0)),
            pl.BlockSpec((n, inner), lambda i: (i, 0)),
            pl.BlockSpec((n, inner), lambda i: (i, 0)),
            pl.BlockSpec((8, n), lambda i: (0, i)),
        ],
        out_shape=[
            jax.ShapeDtypeStruct((length, cols), F32),
            jax.ShapeDtypeStruct((length, inner), BF16),
            jax.ShapeDtypeStruct((blocks, 128, inner), BF16),
            jax.ShapeDtypeStruct((length, inner), BF16),
            jax.ShapeDtypeStruct((length, inner), BF16),
            jax.ShapeDtypeStruct((8, length), F32),
        ],
        scratch_shapes=[
            pltpu.VMEM((n + 8, wide), F32),
            pltpu.VMEM((n, wide), F32),
            pltpu.VMEM((128, inner), F32),
            pltpu.VMEM((n, inner), BF16),
            pltpu.VMEM((n, inner), F32),
            pltpu.VMEM((n, inner), F32),
            pltpu.VMEM((n, inner), F32),
        ],
        compiler_params=PARAMS,
        cost_estimate=cost(20),
        name="scan_forward",
    )(tokens, grad_rows, weights, weights, weights, weights, weights, weights, taps, heads, chan, gain, spread, marks, segrow)


def scan_backward(pre, taps, heads, chan, sums, spread, marks, segrow, grad, states, tokens, grad_gate, weights, norm_gain, gain_sums, me):
    length, cols = pre.shape
    model = tokens.shape[1]
    inner = cols - 384
    wide = cols - 128
    n = BACKWARD_BLOCK
    blocks = length // n
    cut = 512
    shape_a, shape_b = (4, model // 16, cut), (model // 4 + 32, cols - cut)

    def rev(i):
        return blocks - 1 - i

    def rows(width):
        return pl.BlockSpec((n, width), lambda i, me: (rev(i), 0))

    return pl.pallas_call(
        scan_backward_kernel,
        grid_spec=pltpu.PrefetchScalarGridSpec(
            num_scalar_prefetch=1,
            grid=(blocks,),
            in_specs=[
                rows(cols),
                pl.BlockSpec((8, cols), lambda i, me: (jnp.maximum(rev(i) * (n // 8) - 1, 0), 0)),
                whole((8, wide)),
                whole((8, 128)),
                whole((8, inner)),
                whole((inner // 128, 256, 128)),
                whole((256, inner)),
                rows(128),
                pl.BlockSpec((8, n), lambda i, me: (0, rev(i))),
                rows(inner),
                pl.BlockSpec((1, 128, inner), lambda i, me: (rev(i) * (n // FORWARD_BLOCK), 0, 0)),
                rows(model),
                rows(inner),
                column_block(model, inner + cols, 0),
                whole(norm_gain.shape),
                whole(gain_sums.shape),
            ],
            out_specs=[whole((n, model))] * 4 + [whole(shape_a)] * 4 + [whole(shape_b)] * 4,
            scratch_shapes=[
                pltpu.VMEM((n + 8, wide), F32),
                pltpu.VMEM((n + 8, wide), F32),
                pltpu.VMEM((n, wide), F32),
                pltpu.VMEM((n, wide), F32),
                pltpu.VMEM((128, inner), F32),
                pltpu.VMEM((n, inner), BF16),
                pltpu.VMEM((n, inner), BF16),
                pltpu.VMEM((128, n), F32),
                pltpu.VMEM((n, inner + cols), BF16),
                pltpu.VMEM((8, wide), F32),
                pltpu.VMEM((8, 128), F32),
                pltpu.VMEM((8, model), F32),
                pltpu.VMEM((length, model), BF16),
                pltpu.VMEM((length, cols), BF16),
                pltpu.VMEM((model // 4, cols - cut), BF16),
                pltpu.VMEM((8, 1024), F32),
            ],
        ),
        out_shape=[jax.ShapeDtypeStruct((n, model), BF16)] * 4
        + [jax.ShapeDtypeStruct(shape_a, BF16)] * 4
        + [jax.ShapeDtypeStruct(shape_b, BF16)] * 4,
        compiler_params=PARAMS,
        cost_estimate=cost(30),
        name="scan_backward",
    )(me, pre, pre, taps, heads, chan, sums, spread, marks, segrow, grad, states, tokens, grad_gate, weights, norm_gain, gain_sums)


def spread_table(inner):
    head = jnp.arange(inner) // 64
    return (jnp.arange(256)[:, None] % 128 == head[None, :]).astype(BF16)


def head_sum_table(inner):
    pairs = inner // 128
    lane = jnp.arange(256) % 128
    head = 2 * jnp.arange(pairs)[:, None] + (lane >= 64)[None, :]
    return (head[:, :, None] == jnp.arange(128)[None, None, :]).astype(BF16)


def store_block(value, outs):
    for k, out in enumerate(outs):

        @pl.when(pl.program_id(0) == k)
        def _():
            out[...] = value


def mix_second_kernel(channels, me, sums, gate, grad_mixed_in, scanned_in, out_a, out_b, gain, tok, rows, grad_scan, grad_gate, gain_out, grads_out, *rest):
    outs, all_gate, all_mixed = rest[:4], rest[4], rest[5]
    step = pl.program_id(0)
    n, width = gate.shape

    @pl.when(step == 0)
    def _():
        gain_out[...] = jnp.zeros_like(gain_out)

    @pl.when(step < 4)
    def _():
        cols = jnp.concatenate([sums[...], jnp.zeros((120, n), F32)], 0).T
        scale = lax.rsqrt(cols[:, 0:1] / channels + EPS)
        pull = scale * scale * scale * (cols[:, 1:2] / channels)
        gate_pre = gate[...].astype(F32)
        grad_mixed = grad_mixed_in[...].astype(F32)
        scanned = scanned_in[...].astype(F32)
        sig = sigmoid(gate_pre)
        silu = gate_pre * sig
        gated = scanned * silu
        scaled = gated * scale
        mixed = (scaled * gain[0:1, :]).astype(BF16)
        place = pl.ds(pl.multiple_of((me[0] ^ (3 - step)) * n, n), n)
        all_mixed[place, :] = mixed
        gain_out[0:1, :] += jnp.sum(grad_mixed * scaled, axis=0, keepdims=True)
        grad_gated = scale * gain[0:1, :] * grad_mixed - gated * pull
        grad_scan[...] = (grad_gated * silu).astype(BF16)
        grad_gate_low = (grad_gated * scanned * (sig + silu * (1.0 - sig))).astype(BF16)
        grad_gate[...] = grad_gate_low
        all_gate[place, :] = grad_gate_low
        projected = dot_nt(mixed[:, :384], out_a[...]) + dot_nt(mixed[:, 384:], out_b[...])
        store_block(projected.astype(BF16), outs)

    @pl.when(step >= 4)
    def _():
        gate_part = lax.dot_general(tok[...], all_gate[...], TN, preferred_element_type=F32)
        out_part = lax.dot_general(rows[...], all_mixed[...], TN, preferred_element_type=F32)
        grads_out[:, :width] = gate_part.astype(BF16)
        grads_out[:, width:] = out_part.astype(BF16)


def mix_second(sums, gate, grad_mixed, scanned, second, gain, tokens, grad_rows, channels, spot):
    length, width = gate.shape
    model = second.shape[0]
    n = 256
    m = model // 4

    def token_block(i, me):
        return me[0] ^ (3 - jnp.minimum(i, 3))

    def rows(cols):
        return pl.BlockSpec((n, cols), lambda i, me: (token_block(i, me), 0))

    def cols():
        return pl.BlockSpec((length, m), lambda i, me: (0, jnp.maximum(i - 4, 0)))

    return pl.pallas_call(
        lambda *refs: mix_second_kernel(channels, *refs),
        grid_spec=pltpu.PrefetchScalarGridSpec(
            num_scalar_prefetch=1,
            grid=(8,),
            in_specs=[
                pl.BlockSpec((8, n), lambda i, me: (0, token_block(i, me))),
                rows(width),
                rows(width),
                rows(width),
                *out_specs_of(model),
                whole((8, width)),
                cols(),
                cols(),
            ],
            out_specs=[
                rows(width),
                rows(width),
                whole((8, width)),
                pl.BlockSpec((m, 2 * width), lambda i, me: (jnp.maximum(i - 4, 0), 0)),
            ]
            + [whole((n, model))] * 4,
            scratch_shapes=[pltpu.VMEM((length, width), BF16), pltpu.VMEM((length, width), BF16)],
        ),
        out_shape=[
            jax.ShapeDtypeStruct((length, width), BF16),
            jax.ShapeDtypeStruct((length, width), BF16),
            jax.ShapeDtypeStruct((8, width), F32),
            jax.ShapeDtypeStruct((model, 2 * width), BF16),
        ]
        + [jax.ShapeDtypeStruct((n, model), BF16)] * 4,
        compiler_params=PARAMS,
        cost_estimate=cost(11),
        name="mix_second",
    )(spot, sums, gate, grad_mixed, scanned, second, second, gain, tokens, grad_rows)


def four_sum(own, ahead, across, behind):
    return (own.astype(F32) + across.astype(F32)) + (ahead.astype(F32) + behind.astype(F32))


def add_split_kernel(me, *refs):
    parts_a, parts_b, outs_a, outs_b = refs[:4], refs[4:8], refs[8:12], refs[12:]
    deep = outs_a[0].shape[0]
    sums = small_rows(four_sum(*[read_small(part[4 * deep :, :512]) for part in parts_b]))
    for d in range(4):
        e = (me[0] + d) % 4
        outs_a[d][...] = four_sum(*[part[e] for part in parts_a]).astype(BF16)
        place = pl.ds(pl.multiple_of(((me[1] + d) % 4) * deep, 16), deep)
        outs_b[d][:deep, :] = four_sum(*[part[place, :] for part in parts_b]).astype(BF16)
        outs_b[d][deep:, :512] = sums
        outs_b[d][deep:, 512:] = jnp.zeros((32, outs_b[d].shape[1] - 512), BF16)


def add_split(parts_a, parts_b, me):
    deep, width_a = parts_a[0].shape[1:]
    width_b = parts_b[0].shape[1]
    outs = pl.pallas_call(
        add_split_kernel,
        in_specs=[pl.BlockSpec(memory_space=pltpu.SMEM)] + [VMEM_SPEC] * 8,
        out_specs=[VMEM_SPEC] * 8,
        out_shape=[jax.ShapeDtypeStruct((deep, width_a), BF16)] * 4 + [jax.ShapeDtypeStruct((deep + 32, width_b), BF16)] * 4,
        compiler_params=PARAMS,
        name="add_split",
    )(me, *parts_a, *parts_b)
    return outs[:4], outs[4:]


def add_halve_kernel(me, *refs):
    ins, (keep, sums, give, total) = refs[:8], refs[8:]
    rows, cut = ins[0].shape
    total[:, :cut] = four_sum(*[part[...] for part in ins[:4]])
    total[:, cut:] = four_sum(*[part[:rows, :] for part in ins[4:]])
    n = keep.shape[0]
    keep[...] = total[pl.ds(pl.multiple_of(me[0] * n, 16), n), :]
    give[:n, :] = total[pl.ds(pl.multiple_of((1 - me[0]) * n, 16), n), :].astype(BF16)
    low = small_rows(four_sum(*[read_small(part[rows:, :512]) for part in ins[4:]]))
    give[n:, :512] = low
    give[n:, 512:] = jnp.zeros((32, give.shape[1] - 512), BF16)
    sums[...] = read_small(low)


def add_halve(parts_a, parts_b, me):
    rows = parts_a[0].shape[0]
    width = parts_a[0].shape[1] + parts_b[0].shape[1]
    return pl.pallas_call(
        add_halve_kernel,
        in_specs=[pl.BlockSpec(memory_space=pltpu.SMEM)] + [VMEM_SPEC] * 8,
        out_specs=[VMEM_SPEC] * 3,
        out_shape=[
            jax.ShapeDtypeStruct((rows // 2, width), F32),
            jax.ShapeDtypeStruct((16, 512), F32),
            jax.ShapeDtypeStruct((rows // 2 + 32, width), BF16),
        ],
        scratch_shapes=[pltpu.VMEM((rows, width), F32)],
        compiler_params=PARAMS,
        name="add_halve",
    )(me, *parts_a, *parts_b)


def place_kernel(me, *refs):
    out = refs[-1]
    for k, part in enumerate(refs[:-1]):

        @pl.when(pl.program_id(0) == k)
        def _():
            out[...] = part[...].reshape(out.shape)


def place(parts, index, me, shape, block, name):
    return pl.pallas_call(
        place_kernel,
        grid_spec=pltpu.PrefetchScalarGridSpec(
            num_scalar_prefetch=1,
            grid=(len(parts),),
            in_specs=[whole(p.shape) for p in parts],
            out_specs=pl.BlockSpec(block, lambda i, me: index(i, me[0])),
        ),
        out_shape=jax.ShapeDtypeStruct(shape, parts[0].dtype),
        compiler_params=PARAMS,
        cost_estimate=cost(2),
        name=name,
    )(me, *parts)


def shift(value, axis, by):
    n = SIZES[axis]
    return lax.ppermute(value, axis, [(i, (i - by) % n) for i in range(n)])


def swap(value, axis):
    return shift(value, axis, 1)


def ring(value, axis):
    return [value, shift(value, axis, 1), shift(value, axis, 2), shift(value, axis, -1)]


def sends(blocks, axis):
    return [blocks[0], shift(blocks[1], axis, -1), shift(blocks[2], axis, 2), shift(blocks[3], axis, 1)]


def tensor_xor(value, by):
    return lax.ppermute(value, TENSOR, [(i, i ^ by) for i in range(4)])


def sum_ring(value, axis):
    own, ahead, across, behind = ring(value, axis)
    return (own + across) + (ahead + behind)


def sum_pair(value, axis):
    return value + swap(value, axis)


def after(value, *others):
    return lax.optimization_barrier((value,) + others)[0]


def index_of(axis):
    return lax.axis_index(axis).reshape(1).astype(jnp.int32)


def pair_kernel(me, main, other_main, side, other_side, out):
    cut, middle = 1536, side.shape[1]
    for k, (left, right) in enumerate(((main, side), (other_main, other_side))):

        @pl.when(pl.program_id(0) == k)
        def _():
            out[:, :cut] = left[:, :cut]
            out[:, cut : cut + middle] = right[...]
            out[:, cut + middle :] = left[:, cut:]


def pair_rows(main, side):
    rows = main.shape[0]
    width = main.shape[1] + side.shape[1]
    parts = [main, swap(main, "zl"), side, swap(side, "zl")]
    return pl.pallas_call(
        pair_kernel,
        grid_spec=pltpu.PrefetchScalarGridSpec(
            num_scalar_prefetch=1,
            grid=(2,),
            in_specs=[whole(p.shape) for p in parts],
            out_specs=pl.BlockSpec((rows, width), lambda i, me: ((me[0] + i) % 2, 0)),
        ),
        out_shape=jax.ShapeDtypeStruct((2 * rows, width), BF16),
        compiler_params=PARAMS,
        name="pair_rows",
    )(index_of("zl"), *parts)


def token_place(own, near, far, both, me):
    rows, width = own.shape
    return place([own, near, far, both], lambda i, me: (me ^ i, 0), me, (4 * rows, width), (rows, width), "place_tokens")


def per_device(
    hidden_in,
    norm_gain,
    proj_zx,
    proj_shared,
    proj_step,
    conv_inner,
    conv_shared,
    step_bias,
    decay_log,
    skip_gain,
    gated_gain,
    proj_out,
    out_grad,
    segments,
):
    model_width = hidden_in.shape[1]
    width = proj_zx.shape[2]
    heads = step_bias.shape[0]
    me = {axis: index_of(axis) for axis in DP + TENSOR}
    spot = 2 * me["zh"] + me["c"]

    shared_parts = [proj_shared] + [tensor_xor(proj_shared, by) for by in (1, 2, 3)]
    shared_rows = jnp.zeros((48, 256), BF16)
    for by, part in enumerate(shared_parts):
        shared_rows = lax.dynamic_update_slice(shared_rows, part, (((spot[0] ^ by) * 12), jnp.int32(0)))
    side_rows = jnp.concatenate([shared_rows, jnp.pad(proj_step, ((0, 0), (0, 128 - heads)))], 1)
    main_rows = jnp.concatenate([proj_zx[:, 0, :], proj_zx[:, 1, :], proj_out.T], 1)
    weights = lax.all_gather(pair_rows(main_rows, side_rows), ("y", "x"), axis=0, tiled=True)

    residual_in = hidden_in.astype(F32)
    scale_in = lax.rsqrt(jnp.mean(residual_in * residual_in, axis=-1, keepdims=True) + EPS)
    normed_low = (residual_in * scale_in * norm_gain).astype(BF16)
    normed_far = swap(normed_low, "zh")
    normed_near = swap(normed_low, "c")

    normed_both = swap(normed_far, "c")
    tokens = token_place(normed_low, normed_near, normed_far, normed_both, spot)
    grad_far = swap(after(out_grad, normed_far), "zh")
    grad_near = swap(after(out_grad, normed_far), "c")
    grad_both = swap(grad_far, "c")
    grad_rows = token_place(out_grad, grad_near, grad_far, grad_both, spot)

    pad = (0, 128 - heads)
    head_rows = jnp.stack([jnp.pad(step_bias, pad), jnp.pad(jnp.exp(decay_log), pad)], 0)
    head_rows = jnp.pad(head_rows, ((0, 6), (0, 0)))
    taps = jnp.pad(jnp.concatenate([conv_inner, conv_shared], 1), ((0, 3), (0, 0)))
    chan = jnp.broadcast_to(jnp.repeat(skip_gain, width // heads), (8, width))
    gain = jnp.broadcast_to(gated_gain, (8, width))
    norm_rows = jnp.broadcast_to(norm_gain, (8, model_width))
    marks, segrow = scan_marks(segments)
    spread = spread_table(width)
    sum_table = head_sum_table(width)
    tokens, grad_rows = lax.optimization_barrier((tokens, grad_rows))
    pre, scanned, states, gate_pre, grad_mixed, sums = scan_forward(
        tokens, grad_rows, weights, taps, head_rows, chan, gain, spread, marks, segrow
    )

    sums = sum_pair(sum_pair(sums, "c"), "zh")
    grad_scanned, gate_grad_low, gain_sums, second_total, *out_blocks = mix_second(
        sums, gate_pre, grad_mixed, scanned, weights, gain, tokens, grad_rows, 4 * width, spot
    )
    out_far = (out_blocks[1].astype(F32) + swap(out_blocks[0], "c").astype(F32)).astype(BF16)
    out_near = swap(out_blocks[2], "c")
    second_sum = lax.psum_scatter(second_total, ("y", "x"), scatter_dimension=0, tiled=True)
    out_far_got = swap(out_far, "zh")

    grad_scanned = after(grad_scanned, out_far, second_total)
    sent = scan_backward(
        pre,
        taps,
        head_rows,
        chan,
        sum_table,
        spread,
        marks,
        segrow,
        grad_scanned,
        states,
        tokens,
        gate_grad_low,
        weights,
        norm_rows,
        gain_sums,
        jnp.concatenate([spot, me["y"], me["x"]]),
    )
    row_blocks = [after(block, out_far_got, out_near) for block in sent[:4]]
    far_got = swap(row_blocks[0], "c")
    row_far = (row_blocks[1].astype(F32) + far_got.astype(F32)).astype(BF16)
    row_far_got = swap(row_far, "zh")
    parts_b = sends([after(block, row_far) for block in sent[8:]], "x")
    parts_a = sends([after(block, row_far) for block in sent[4:8]], "y")
    half_a, half_b = add_split(parts_a, parts_b, jnp.concatenate([me["x"], me["y"]]))
    near_got = swap(after(row_blocks[2], *half_a), "c")

    hidden_out = (
        residual_in + (out_blocks[3].astype(F32) + out_near.astype(F32) + out_far_got.astype(F32))
    ).astype(BF16)
    grad_normed = row_blocks[3].astype(F32) + near_got.astype(F32) + row_far_got.astype(F32)
    weighted = jnp.sum(grad_normed * norm_gain * residual_in, axis=-1, keepdims=True)
    grad_hidden = (
        out_grad.astype(F32)
        + scale_in * norm_gain * grad_normed
        - residual_in * scale_in**3 * weighted / model_width
    ).astype(BF16)
    parts_a = [after(part, row_far_got, second_sum) for part in sends(half_a, "x")]
    parts_b = [after(part, row_far_got, second_sum) for part in sends(half_b, "y")]
    first_keep, small, first_give = add_halve(parts_a, parts_b, me["zl"])
    first_got = swap(first_give, "zl")
    first_mine = first_keep + first_got[:48].astype(F32)
    small = small + read_small(first_got[48:, :512])
    second_pairs = second_sum.reshape(2, 48, 2 * width)
    second_keep = lax.dynamic_index_in_dim(second_pairs, me["zl"][0], 0, keepdims=False)
    second_mine = second_keep.astype(F32) + swap(
        lax.dynamic_index_in_dim(second_pairs, 1 - me["zl"][0], 0, keepdims=False), "zl"
    ).astype(F32)
    grad_proj_out = second_mine[:, width:].T
    grad_proj_zx = jnp.stack([second_mine[:, :width], first_mine[:, :width]], 1)
    grad_proj_step = first_mine[:, width + 256 : width + 256 + heads]

    def quarter(by):
        part = lax.dynamic_slice(first_mine, ((spot[0] ^ by) * 12, jnp.int32(width)), (12, 256))
        return jnp.concatenate([small, jnp.pad(part, ((0, 0), (0, 256)))], 0)

    summed = (quarter(0) + tensor_xor(quarter(1), 1)) + (tensor_xor(quarter(2), 2) + tensor_xor(quarter(3), 3))
    rest = width - 512
    return (
        hidden_out,
        grad_hidden,
        jnp.concatenate([summed[6], summed[14], summed[7]]),
        grad_proj_zx,
        summed[16:, :256],
        grad_proj_step,
        jnp.concatenate([small[:5], small[8:13, :rest]], 1),
        summed[8:13, rest:],
        small[15, :heads],
        small[15, 128 : 128 + heads],
        small[15, 256 : 256 + heads],
        jnp.concatenate([small[5], small[13, :rest]]),
        grad_proj_out,
    )


def solution(mesh):
    fine = Mesh(mesh.devices.reshape(4, 4, 2, 2, 2), DP + TENSOR)
    both = DP + TENSOR
    return jax.shard_map(
        per_device,
        mesh=fine,
        in_specs=(
            P(both, None),
            P(),
            P(DP, None, TENSOR),
            P(both, None),
            P(DP, TENSOR),
            P(None, TENSOR),
            P(),
            P(TENSOR),
            P(TENSOR),
            P(TENSOR),
            P(TENSOR),
            P(TENSOR, DP),
            P(both, None),
            P(DP),
        ),
        out_specs=(
            P(both, None),
            P(both, None),
            P(),
            P(DP, None, TENSOR),
            P(both, None),
            P(DP, TENSOR),
            P(None, TENSOR),
            P(),
            P(TENSOR),
            P(TENSOR),
            P(TENSOR),
            P(TENSOR),
            P(TENSOR, DP),
        ),
        check_vma=False,
    )
```

```python
import jax
import jax.numpy as jnp
from jax import lax
from jax.experimental import pallas as pl
from jax.experimental.pallas import tpu as pltpu
from jax.sharding import Mesh
from jax.sharding import PartitionSpec as P

EPS = 1e-05
DP = ("y", "x", "zl")
TENSOR = ("zh", "c")
SIZES = {"y": 4, "x": 4, "zl": 2, "zh": 2, "c": 2}

F32 = jnp.float32
BF16 = jnp.bfloat16
HIGH = lax.Precision.HIGHEST
FORWARD_BLOCK = 128
BACKWARD_BLOCK = 256
VMEM = 56 * 1024 * 1024
PARAMS = pltpu.CompilerParams(vmem_limit_bytes=VMEM)
NT = (((1,), (1,)), ((), ()))
TN = (((0,), (0,)), ((), ()))
VMEM_SPEC = pl.BlockSpec(memory_space=pltpu.VMEM)


def cost(us):
    return pl.CostEstimate(flops=int(us * 1e6), transcendentals=0, bytes_accessed=int(us * 3e3))


def whole(shape):
    return pl.BlockSpec(shape, lambda *i: (0,) * len(shape))


def column_block(rows, width, index):
    return pl.BlockSpec((rows, width), lambda *i: (0, index))


def first_specs(rows):
    return [column_block(rows, 384, index) for index in (2, 3, 4)]


def out_specs_of(rows):
    return [column_block(rows, 384, index) for index in (5, 6)]


def dot(a, b):
    return jnp.dot(a, b, preferred_element_type=F32)


def dot_nt(a, b):
    return lax.dot_general(a, b, NT, preferred_element_type=F32)


def sigmoid(a):
    return 0.5 * jnp.tanh(0.5 * a) + 0.5


def softplus(a):
    return jnp.maximum(a, 0.0) + jnp.log1p(jnp.exp(-jnp.abs(a)))


def conv_strip(ext, taps, aux, j):
    n = ext.shape[0] - 8
    lanes = slice(j * 128, (j + 1) * 128)
    total = taps[4:5, lanes] + taps[3:4, lanes] * ext[8 : 8 + n, lanes]
    for back in (1, 2, 3):
        total += taps[3 - back : 4 - back, lanes] * (
            aux[:, back - 1 : back] * ext[8 - back : 8 - back + n, lanes]
        )
    return total


def two_parts(value):
    high = value.astype(BF16)
    return jnp.concatenate([high, (value - high.astype(F32)).astype(BF16)], 1)


def spread_heads(cols, table):
    return dot(two_parts(cols), table)


def scan_forward_kernel(tok, rows, gate_w, out_a, out_b, weights_a, weights_b, weights_c, taps, heads, chan, gain, spread, aux, segrow, pre_out, scan_low, state_out, gate_low, mixed_low, sums_out, ext, act, carry, fed, scan_out, gate_out, mixed_out):
    n = tok.shape[0]
    pairs = carry.shape[1] // 128

    @pl.when(pl.program_id(0) == 0)
    def _():
        carry[...] = jnp.zeros_like(carry)
        ext[0:8, :] = jnp.zeros((8, ext.shape[1]), F32)

    pre = jnp.concatenate([dot(tok[...], w[...]) for w in (weights_a, weights_b, weights_c)], 1)
    pre_out[...] = pre
    wide = ext.shape[1]
    ext[8:, :] = pre[:, :wide]
    marks = aux[...]
    for j in range(wide // 128):
        total = conv_strip(ext, taps, marks, j)
        act[:, j * 128 : (j + 1) * 128] = total * sigmoid(total)
    ext[0:8, :] = ext[n : n + 8, :]

    step = softplus(pre[:, wide:] + heads[0:1, :])
    log_step = -step * heads[1:2, :]
    row = lax.broadcasted_iota(jnp.int32, (n, n), 0)
    col = lax.broadcasted_iota(jnp.int32, (n, n), 1)
    lower = (row >= col).astype(F32)
    cum = jnp.dot(lower, log_step, precision=HIGH, preferred_element_type=F32)
    cum_t = cum.T
    write = act[:, pairs * 128 : (pairs + 1) * 128]
    read = act[:, (pairs + 1) * 128 : (pairs + 2) * 128].astype(BF16)
    write_t = write.T.astype(BF16)
    allowed = (row >= col) & (marks[:, 8:9] == segrow[0:1, :])
    inner = jnp.where(allowed, dot(read, write_t), 0.0)
    last = cum[n - 1 : n, :]
    enters = jnp.exp(cum) * marks[:, 3:4]
    to_end = jnp.exp(last - cum) * marks[:, 4:5]
    keep = jnp.exp(last) * marks[n - 1 : n, 3:4]
    wide_cols = spread_heads(jnp.concatenate([step, enters, to_end, jnp.broadcast_to(keep, (8, 128))], 0), spread[...])
    held = carry[...]
    held_low = held.astype(BF16)
    state_out[0] = held_low
    from_state = dot(read, held_low)
    low_half = lax.broadcasted_iota(jnp.int32, (1, 128), 1) < 64
    for j in range(pairs):
        lanes = slice(j * 128, (j + 1) * 128)
        x = act[:, lanes]
        xdt = x * wide_cols[:n, lanes]
        parts = []
        for h in (2 * j, 2 * j + 1):
            decay = jnp.exp(jnp.minimum(cum[:, h : h + 1] - cum_t[h : h + 1, :], 0.0))
            parts.append((decay * inner).astype(BF16))
        xdt_low = xdt.astype(BF16)
        zero = jnp.zeros_like(xdt_low)
        pair = jnp.concatenate([jnp.where(low_half, xdt_low, zero), jnp.where(low_half, zero, xdt_low)], 0)
        y = dot(jnp.concatenate(parts, 1), pair)
        if j % 2 == 0:
            block = slice(128 * j, 128 * j + 256)
            gate_out[:, block] = dot(tok[...], gate_w[:, block])
        else:
            spot = 256 * (j // 2)
            out_w = (out_a[:, 0:256], jnp.concatenate([out_a[:, 256:], out_b[:, :128]], 1), out_b[:, 128:])[j // 2]
            mixed_out[:, spot : spot + 256] = dot(rows[...], out_w)
        y += wide_cols[n : 2 * n, lanes] * from_state[:, lanes] + chan[0:1, lanes] * x
        scan_out[:, lanes] = y
        fed[:, lanes] = (xdt * wide_cols[2 * n : 3 * n, lanes]).astype(BF16)
        carry[:, lanes] = held[:, lanes] * wide_cols[3 * n : 3 * n + 1, lanes]
    carry[...] += dot(write_t, fed[...])

    gate_pre = gate_out[...]
    grad_mixed = mixed_out[...]
    scanned = scan_out[...]
    gate_low[...] = gate_pre.astype(BF16)
    mixed_low[...] = grad_mixed.astype(BF16)
    scan_low[...] = scanned.astype(BF16)
    gated = scanned * (gate_pre * sigmoid(gate_pre))
    square = jnp.sum(gated * gated, axis=1, keepdims=True)
    inner = jnp.sum(grad_mixed * gain[0:1, :] * gated, axis=1, keepdims=True)
    lane = lax.broadcasted_iota(jnp.int32, (1, 128), 1)
    cols = jnp.where(lane == 0, square, jnp.where(lane == 1, inner, 0.0))
    sums_out[...] = cols.T[0:8, :]


def small_rows(value):
    high = value.astype(BF16)
    return jnp.concatenate([high, (value - high.astype(F32)).astype(BF16)], 0)


def read_small(rows):
    return rows[:16, :].astype(F32) + rows[16:, :].astype(F32)


def scan_backward_kernel(me, pre, pre_before, taps, heads, chan, sums, spread, aux, segrow, grad, state, tok, grad_gate, weights, norm_gain, gain_sums, *rest):
    row_outs, outs_a, outs_b = rest[:4], rest[4:8], rest[8:12]
    ext, gext, act, slope, carry, fed, back, rows, low_out, taps_out, heads_out, gains, all_tok, all_low, split, packed = rest[12:]
    n = pre.shape[0]
    pairs = carry.shape[1] // 128
    wide = ext.shape[1]
    gate_width = grad_gate.shape[1]

    @pl.when(pl.program_id(0) == 0)
    def _():
        carry[...] = jnp.zeros_like(carry)
        gext[n:, :] = jnp.zeros((8, wide), F32)
        taps_out[...] = jnp.zeros_like(taps_out)
        heads_out[...] = jnp.zeros_like(heads_out)
        rows[...] = jnp.zeros_like(rows)
        gains[...] = jnp.zeros_like(gains)

    marks = aux[...]
    ext[0:8, :] = pre_before[:, :wide]
    ext[8:, :] = pre[:, :wide]
    for j in range(wide // 128):
        lanes = slice(j * 128, (j + 1) * 128)
        total = conv_strip(ext, taps, marks, j)
        sig = sigmoid(total)
        value = total * sig
        act[:, lanes] = value
        slope[:, lanes] = sig + value * (1.0 - sig)

    step_arg = pre[:, wide:] + heads[0:1, :]
    step = softplus(step_arg)
    rate = heads[1:2, :]
    row = lax.broadcasted_iota(jnp.int32, (n, n), 0)
    col = lax.broadcasted_iota(jnp.int32, (n, n), 1)
    lower = (row >= col).astype(F32)
    cum = jnp.dot(lower, -step * rate, precision=HIGH, preferred_element_type=F32)
    cum_t = cum.T
    write = act[:, pairs * 128 : (pairs + 1) * 128]
    read = act[:, (pairs + 1) * 128 : (pairs + 2) * 128]
    read_t = read.T.astype(BF16)
    write_low = write.astype(BF16)
    read_low = read.astype(BF16)
    allowed = (row <= col) & (marks[:, 8:9] == segrow[0:1, :])
    inner_t = jnp.where(allowed, dot(write_low, read_t), 0.0)
    last = cum[n - 1 : n, :]
    enters = jnp.exp(cum) * marks[:, 9:10]
    to_end = jnp.exp(last - cum) * marks[:, 10:11]
    keep = jnp.exp(last) * marks[n - 1 : n, 9:10]
    wide_cols = spread_heads(jnp.concatenate([step, enters, to_end, jnp.broadcast_to(keep, (8, 128))], 0), spread[...])
    held = state[0]
    later = carry[...]
    later_low = later.astype(BF16)
    from_state = dot(read_low, held)
    from_later = dot(write_low, later_low)
    low_half = lax.broadcasted_iota(jnp.int32, (1, 128), 1) < 64
    head_lane = lax.broadcasted_iota(jnp.int32, (1, 128), 1)
    grad_inner = jnp.zeros((n, n), F32)
    col_sums = jnp.zeros((n, 128), F32)
    to_end_part = jnp.zeros((n, 128), F32)
    enter_part = jnp.zeros((n, 128), F32)
    step_part = jnp.zeros((n, 128), F32)
    skip_part = jnp.zeros((n, 128), F32)
    keep_part = jnp.zeros((8, 128), F32)

    def head_sums(value, j):
        return dot(two_parts(value), sums[j])

    for j in range(pairs):
        lanes = slice(j * 128, (j + 1) * 128)
        x = act[:, lanes]
        dy = grad[:, lanes].astype(F32)
        step_wide = wide_cols[:n, lanes]
        xdt = x * step_wide
        xdt_low = xdt.astype(BF16)
        dy_low = dy.astype(BF16)
        zero = jnp.zeros_like(xdt_low)
        products = dot_nt(
            jnp.concatenate([jnp.where(low_half, xdt_low, zero), jnp.where(low_half, zero, xdt_low)], 0),
            dy_low,
        )
        parts = []
        for k, h in enumerate((2 * j, 2 * j + 1)):
            product = products[k * n : (k + 1) * n, :]
            decay = jnp.exp(jnp.minimum(cum_t[h : h + 1, :] - cum[:, h : h + 1], 0.0))
            scaled = decay * product
            grad_inner += scaled
            weighted = scaled * inner_t
            rows[h : h + 1, :] = jnp.sum(weighted, axis=0, keepdims=True)
            col_sums += jnp.where(head_lane == h, jnp.sum(weighted, axis=1, keepdims=True), 0.0)
            parts.append((decay * inner_t).astype(BF16))
        grad_pair = jnp.concatenate([jnp.where(low_half, dy_low, zero), jnp.where(low_half, zero, dy_low)], 0)
        grad_xdt = dot(jnp.concatenate(parts, 1), grad_pair)
        end_wide = wide_cols[2 * n : 3 * n, lanes]
        enter_wide = wide_cols[n : 2 * n, lanes]
        later_part = end_wide * from_later[:, lanes]
        grad_xdt += later_part
        to_end_part += head_sums(later_part * xdt, j)
        fed[:, lanes] = (xdt * end_wide).astype(BF16)
        grad_enter = dy * enter_wide
        back[:, lanes] = grad_enter.astype(BF16)
        enter_part += head_sums(grad_enter * from_state[:, lanes], j)
        step_part += head_sums(grad_xdt * x, j)
        skip_part += head_sums(dy * x, j)
        kept = jnp.sum(held[:, lanes].astype(F32) * later[:, lanes], axis=0, keepdims=True)
        keep_part += head_sums(jnp.broadcast_to(kept, (8, 128)), j)
        act[:, lanes] = grad_xdt * step_wide + chan[0:1, lanes] * dy
        carry[:, lanes] = later[:, lanes] * wide_cols[3 * n : 3 * n + 1, lanes]

    grad_cum = rows[...].T - col_sums + enter_part - to_end_part
    grad_last = jnp.sum(to_end_part, axis=0, keepdims=True) + keep * keep_part[0:1, :]
    upper = (row <= col).astype(F32)
    grad_log = jnp.dot(upper, grad_cum, precision=HIGH, preferred_element_type=F32) + grad_last
    grad_step = (step_part - rate * grad_log) * sigmoid(step_arg)
    heads_out[0:1, :] += jnp.sum(grad_step, axis=0, keepdims=True)
    heads_out[1:2, :] += -rate * jnp.sum(step * grad_log, axis=0, keepdims=True)
    heads_out[2:3, :] += jnp.sum(skip_part, axis=0, keepdims=True)
    low_out[:, gate_width + wide :] = grad_step.astype(BF16)

    grad_inner = jnp.where(allowed, grad_inner, 0.0)
    act[:, pairs * 128 : (pairs + 1) * 128] = dot(grad_inner.astype(BF16), read_low) + dot_nt(fed[...], later_low)
    act[:, (pairs + 1) * 128 : (pairs + 2) * 128] = dot(grad_inner.T.astype(BF16), write_low) + dot_nt(back[...], held)
    carry[...] += dot(read_t, back[...])

    for j in range(wide // 128):
        lanes = slice(j * 128, (j + 1) * 128)
        grad_pre = act[:, lanes] * slope[:, lanes]
        gext[0:n, lanes] = grad_pre
        total = taps[3:4, lanes] * grad_pre
        taps_out[3:4, lanes] += jnp.sum(grad_pre * ext[8 : 8 + n, lanes], axis=0, keepdims=True)
        taps_out[4:5, lanes] += jnp.sum(grad_pre, axis=0, keepdims=True)
        for by in (1, 2, 3):
            total += taps[3 - by : 4 - by, lanes] * (marks[:, 4 + by : 5 + by] * gext[by : by + n, lanes])
            taps_out[3 - by : 4 - by, lanes] += jnp.sum(
                grad_pre * (marks[:, by - 1 : by] * ext[8 - by : 8 - by + n, lanes]), axis=0, keepdims=True
            )
        low_out[:, gate_width + j * 128 : gate_width + (j + 1) * 128] = total.astype(BF16)
    gext[n:, :] = gext[0:8, :]

    step_id = pl.program_id(0)
    low_out[:, : grad_gate.shape[1]] = grad_gate[...]
    token_grad = dot_nt(low_out[...], weights[...])
    gains[0:1, :] += jnp.sum(token_grad * tok[...].astype(F32), axis=0, keepdims=True)
    place = pl.ds(pl.multiple_of((3 - step_id) * n, n), n)
    all_tok[place, :] = tok[...]
    all_low[place, :] = low_out[:, grad_gate.shape[1] :]
    token_low = token_grad.astype(BF16)
    for k in range(4):

        @pl.when((me[0] ^ (3 - k)) == 3 - step_id)
        def _():
            row_outs[k][...] = token_low

    @pl.when(step_id == 3)
    def _():
        cut = outs_a[0].shape[2]
        deep = outs_a[0].shape[1]
        for k in range(4):
            first = pl.multiple_of(((me[1] + k) % 4) * (4 * deep), 128)
            grad_rows = lax.dot_general(
                all_tok[:, pl.ds(first, 4 * deep)], all_low[...], TN, preferred_element_type=F32
            ).astype(BF16)
            outs_a[k][...] = grad_rows[:, :cut].reshape(outs_a[k].shape)
            split[...] = grad_rows[:, cut:]
            y = (me[1] + k) % 4
            for d in range(4):
                start = pl.multiple_of(((me[2] + d) % 4) * deep, 16)
                outs_b[d][pl.ds(pl.multiple_of(y * deep, 16), deep), :] = split[pl.ds(start, deep), :]
        width = gain_sums.shape[1]
        by_gain = gains[0:1, :] / norm_gain[0:1, :]
        packed[0:5, :] = taps_out[0:5, :]
        packed[5:6, :width] = gain_sums[0:1, :]
        packed[5:6, width:] = jnp.zeros((1, 1024 - width), F32)
        packed[6:7, :] = by_gain[:, :1024]
        packed[7:8, :512] = by_gain[:, 1024:]
        for r in range(3):
            packed[7:8, 512 + 128 * r : 640 + 128 * r] = heads_out[r : r + 1, :]
        packed[7:8, 896:] = jnp.zeros((1, 128), F32)
        sums_low = small_rows(jnp.concatenate([packed[:, :512], packed[:, 512:]], 0))
        for k in range(4):
            outs_b[k][4 * deep :, :512] = sums_low
            outs_b[k][4 * deep :, 512:] = jnp.zeros((32, outs_b[k].shape[1] - 512), BF16)


def scan_marks(segments):
    length = segments.shape[0]

    def same(by):
        if by > 0:
            other = jnp.concatenate([jnp.full((by,), -1, jnp.int32), segments[:-by]], 0)
        else:
            other = jnp.concatenate([segments[-by:], jnp.full((-by,), -1, jnp.int32)], 0)
        return other == segments

    def ends(size):
        blocks = segments.reshape(-1, size)
        before = jnp.concatenate([jnp.full((1,), -1, jnp.int32), blocks[:-1, -1]], 0)
        return [(blocks == before[:, None]).reshape(-1), (blocks == blocks[:, -1:]).reshape(-1)]

    cols = [same(1), same(2), same(3), *ends(FORWARD_BLOCK)]
    cols += [same(-1), same(-2), same(-3), segments, *ends(BACKWARD_BLOCK)]
    marks = jnp.stack([c.astype(F32) for c in cols], 1)
    return jnp.pad(marks, ((0, 0), (0, 128 - len(cols)))), jnp.broadcast_to(segments.astype(F32), (8, length))


def scan_forward(tokens, grad_rows, weights, taps, heads, chan, gain, spread, marks, segrow):
    length, model = tokens.shape
    cols = 1152
    inner = cols - 384
    wide = cols - 128
    n = FORWARD_BLOCK
    blocks = length // n


    return pl.pallas_call(
        scan_forward_kernel,
        grid=(blocks,),
        in_specs=[
            pl.BlockSpec((n, model), lambda i: (i, 0)),
            pl.BlockSpec((n, model), lambda i: (i, 0)),
            column_block(model, inner, 0),
            *out_specs_of(model),
            *first_specs(model),
            whole((8, wide)),
            whole((8, 128)),
            whole((8, inner)),
            whole((8, inner)),
            whole((256, inner)),
            pl.BlockSpec((n, 128), lambda i: (i, 0)),
            pl.BlockSpec((8, n), lambda i: (0, i)),
        ],
        out_specs=[
            pl.BlockSpec((n, cols), lambda i: (i, 0)),
            pl.BlockSpec((n, inner), lambda i: (i, 0)),
            pl.BlockSpec((1, 128, inner), lambda i: (i, 0, 0)),
            pl.BlockSpec((n, inner), lambda i: (i, 0)),
            pl.BlockSpec((n, inner), lambda i: (i, 0)),
            pl.BlockSpec((8, n), lambda i: (0, i)),
        ],
        out_shape=[
            jax.ShapeDtypeStruct((length, cols), F32),
            jax.ShapeDtypeStruct((length, inner), BF16),
            jax.ShapeDtypeStruct((blocks, 128, inner), BF16),
            jax.ShapeDtypeStruct((length, inner), BF16),
            jax.ShapeDtypeStruct((length, inner), BF16),
            jax.ShapeDtypeStruct((8, length), F32),
        ],
        scratch_shapes=[
            pltpu.VMEM((n + 8, wide), F32),
            pltpu.VMEM((n, wide), F32),
            pltpu.VMEM((128, inner), F32),
            pltpu.VMEM((n, inner), BF16),
            pltpu.VMEM((n, inner), F32),
            pltpu.VMEM((n, inner), F32),
            pltpu.VMEM((n, inner), F32),
        ],
        compiler_params=PARAMS,
        cost_estimate=cost(20),
        name="scan_forward",
    )(tokens, grad_rows, weights, weights, weights, weights, weights, weights, taps, heads, chan, gain, spread, marks, segrow)


def scan_backward(pre, taps, heads, chan, sums, spread, marks, segrow, grad, states, tokens, grad_gate, weights, norm_gain, gain_sums, me):
    length, cols = pre.shape
    model = tokens.shape[1]
    inner = cols - 384
    wide = cols - 128
    n = BACKWARD_BLOCK
    blocks = length // n
    cut = 512
    shape_a, shape_b = (4, model // 16, cut), (model // 4 + 32, cols - cut)

    def rev(i):
        return blocks - 1 - i

    def rows(width):
        return pl.BlockSpec((n, width), lambda i, me: (rev(i), 0))

    return pl.pallas_call(
        scan_backward_kernel,
        grid_spec=pltpu.PrefetchScalarGridSpec(
            num_scalar_prefetch=1,
            grid=(blocks,),
            in_specs=[
                rows(cols),
                pl.BlockSpec((8, cols), lambda i, me: (jnp.maximum(rev(i) * (n // 8) - 1, 0), 0)),
                whole((8, wide)),
                whole((8, 128)),
                whole((8, inner)),
                whole((inner // 128, 256, 128)),
                whole((256, inner)),
                rows(128),
                pl.BlockSpec((8, n), lambda i, me: (0, rev(i))),
                rows(inner),
                pl.BlockSpec((1, 128, inner), lambda i, me: (rev(i) * (n // FORWARD_BLOCK), 0, 0)),
                rows(model),
                rows(inner),
                column_block(model, inner + cols, 0),
                whole(norm_gain.shape),
                whole(gain_sums.shape),
            ],
            out_specs=[whole((n, model))] * 4 + [whole(shape_a)] * 4 + [whole(shape_b)] * 4,
            scratch_shapes=[
                pltpu.VMEM((n + 8, wide), F32),
                pltpu.VMEM((n + 8, wide), F32),
                pltpu.VMEM((n, wide), F32),
                pltpu.VMEM((n, wide), F32),
                pltpu.VMEM((128, inner), F32),
                pltpu.VMEM((n, inner), BF16),
                pltpu.VMEM((n, inner), BF16),
                pltpu.VMEM((128, n), F32),
                pltpu.VMEM((n, inner + cols), BF16),
                pltpu.VMEM((8, wide), F32),
                pltpu.VMEM((8, 128), F32),
                pltpu.VMEM((8, model), F32),
                pltpu.VMEM((length, model), BF16),
                pltpu.VMEM((length, cols), BF16),
                pltpu.VMEM((model // 4, cols - cut), BF16),
                pltpu.VMEM((8, 1024), F32),
            ],
        ),
        out_shape=[jax.ShapeDtypeStruct((n, model), BF16)] * 4
        + [jax.ShapeDtypeStruct(shape_a, BF16)] * 4
        + [jax.ShapeDtypeStruct(shape_b, BF16)] * 4,
        compiler_params=PARAMS,
        cost_estimate=cost(30),
        name="scan_backward",
    )(me, pre, pre, taps, heads, chan, sums, spread, marks, segrow, grad, states, tokens, grad_gate, weights, norm_gain, gain_sums)


def spread_table(inner):
    head = jnp.arange(inner) // 64
    return (jnp.arange(256)[:, None] % 128 == head[None, :]).astype(BF16)


def head_sum_table(inner):
    pairs = inner // 128
    lane = jnp.arange(256) % 128
    head = 2 * jnp.arange(pairs)[:, None] + (lane >= 64)[None, :]
    return (head[:, :, None] == jnp.arange(128)[None, None, :]).astype(BF16)


def store_block(value, outs):
    for k, out in enumerate(outs):

        @pl.when(pl.program_id(0) == k)
        def _():
            out[...] = value


def mix_second_kernel(channels, me, sums, gate, grad_mixed_in, scanned_in, out_a, out_b, gain, tok, rows, grad_scan, grad_gate, gain_out, grads_out, *rest):
    outs, all_gate, all_mixed = rest[:4], rest[4], rest[5]
    step = pl.program_id(0)
    n, width = gate.shape

    @pl.when(step == 0)
    def _():
        gain_out[...] = jnp.zeros_like(gain_out)

    @pl.when(step < 4)
    def _():
        cols = jnp.concatenate([sums[...], jnp.zeros((120, n), F32)], 0).T
        scale = lax.rsqrt(cols[:, 0:1] / channels + EPS)
        pull = scale * scale * scale * (cols[:, 1:2] / channels)
        gate_pre = gate[...].astype(F32)
        grad_mixed = grad_mixed_in[...].astype(F32)
        scanned = scanned_in[...].astype(F32)
        sig = sigmoid(gate_pre)
        silu = gate_pre * sig
        gated = scanned * silu
        scaled = gated * scale
        mixed = (scaled * gain[0:1, :]).astype(BF16)
        place = pl.ds(pl.multiple_of((me[0] ^ (3 - step)) * n, n), n)
        all_mixed[place, :] = mixed
        gain_out[0:1, :] += jnp.sum(grad_mixed * scaled, axis=0, keepdims=True)
        grad_gated = scale * gain[0:1, :] * grad_mixed - gated * pull
        grad_scan[...] = (grad_gated * silu).astype(BF16)
        grad_gate_low = (grad_gated * scanned * (sig + silu * (1.0 - sig))).astype(BF16)
        grad_gate[...] = grad_gate_low
        all_gate[place, :] = grad_gate_low
        projected = dot_nt(mixed[:, :384], out_a[...]) + dot_nt(mixed[:, 384:], out_b[...])
        store_block(projected.astype(BF16), outs)

    @pl.when(step >= 4)
    def _():
        gate_part = lax.dot_general(tok[...], all_gate[...], TN, preferred_element_type=F32)
        out_part = lax.dot_general(rows[...], all_mixed[...], TN, preferred_element_type=F32)
        grads_out[:, :width] = gate_part.astype(BF16)
        grads_out[:, width:] = out_part.astype(BF16)


def mix_second(sums, gate, grad_mixed, scanned, second, gain, tokens, grad_rows, channels, spot):
    length, width = gate.shape
    model = second.shape[0]
    n = 256
    m = model // 4

    def token_block(i, me):
        return me[0] ^ (3 - jnp.minimum(i, 3))

    def rows(cols):
        return pl.BlockSpec((n, cols), lambda i, me: (token_block(i, me), 0))

    def cols():
        return pl.BlockSpec((length, m), lambda i, me: (0, jnp.maximum(i - 4, 0)))

    return pl.pallas_call(
        lambda *refs: mix_second_kernel(channels, *refs),
        grid_spec=pltpu.PrefetchScalarGridSpec(
            num_scalar_prefetch=1,
            grid=(8,),
            in_specs=[
                pl.BlockSpec((8, n), lambda i, me: (0, token_block(i, me))),
                rows(width),
                rows(width),
                rows(width),
                *out_specs_of(model),
                whole((8, width)),
                cols(),
                cols(),
            ],
            out_specs=[
                rows(width),
                rows(width),
                whole((8, width)),
                pl.BlockSpec((m, 2 * width), lambda i, me: (jnp.maximum(i - 4, 0), 0)),
            ]
            + [whole((n, model))] * 4,
            scratch_shapes=[pltpu.VMEM((length, width), BF16), pltpu.VMEM((length, width), BF16)],
        ),
        out_shape=[
            jax.ShapeDtypeStruct((length, width), BF16),
            jax.ShapeDtypeStruct((length, width), BF16),
            jax.ShapeDtypeStruct((8, width), F32),
            jax.ShapeDtypeStruct((model, 2 * width), BF16),
        ]
        + [jax.ShapeDtypeStruct((n, model), BF16)] * 4,
        compiler_params=PARAMS,
        cost_estimate=cost(11),
        name="mix_second",
    )(spot, sums, gate, grad_mixed, scanned, second, second, gain, tokens, grad_rows)


def four_sum(own, ahead, across, behind):
    return (own.astype(F32) + across.astype(F32)) + (ahead.astype(F32) + behind.astype(F32))


def add_split_kernel(me, *refs):
    parts_a, parts_b, outs_a, outs_b = refs[:4], refs[4:8], refs[8:12], refs[12:]
    deep = outs_a[0].shape[0]
    sums = small_rows(four_sum(*[read_small(part[4 * deep :, :512]) for part in parts_b]))
    for d in range(4):
        e = (me[0] + d) % 4
        outs_a[d][...] = four_sum(*[part[e] for part in parts_a]).astype(BF16)
        place = pl.ds(pl.multiple_of(((me[1] + d) % 4) * deep, 16), deep)
        outs_b[d][:deep, :] = four_sum(*[part[place, :] for part in parts_b]).astype(BF16)
        outs_b[d][deep:, :512] = sums
        outs_b[d][deep:, 512:] = jnp.zeros((32, outs_b[d].shape[1] - 512), BF16)


def add_split(parts_a, parts_b, me):
    deep, width_a = parts_a[0].shape[1:]
    width_b = parts_b[0].shape[1]
    outs = pl.pallas_call(
        add_split_kernel,
        in_specs=[pl.BlockSpec(memory_space=pltpu.SMEM)] + [VMEM_SPEC] * 8,
        out_specs=[VMEM_SPEC] * 8,
        out_shape=[jax.ShapeDtypeStruct((deep, width_a), BF16)] * 4 + [jax.ShapeDtypeStruct((deep + 32, width_b), BF16)] * 4,
        compiler_params=PARAMS,
        name="add_split",
    )(me, *parts_a, *parts_b)
    return outs[:4], outs[4:]


def add_halve_kernel(me, *refs):
    ins, (keep, sums, give, total) = refs[:8], refs[8:]
    rows, cut = ins[0].shape
    total[:, :cut] = four_sum(*[part[...] for part in ins[:4]])
    total[:, cut:] = four_sum(*[part[:rows, :] for part in ins[4:]])
    n = keep.shape[0]
    keep[...] = total[pl.ds(pl.multiple_of(me[0] * n, 16), n), :]
    give[:n, :] = total[pl.ds(pl.multiple_of((1 - me[0]) * n, 16), n), :].astype(BF16)
    low = small_rows(four_sum(*[read_small(part[rows:, :512]) for part in ins[4:]]))
    give[n:, :512] = low
    give[n:, 512:] = jnp.zeros((32, give.shape[1] - 512), BF16)
    sums[...] = read_small(low)


def add_halve(parts_a, parts_b, me):
    rows = parts_a[0].shape[0]
    width = parts_a[0].shape[1] + parts_b[0].shape[1]
    return pl.pallas_call(
        add_halve_kernel,
        in_specs=[pl.BlockSpec(memory_space=pltpu.SMEM)] + [VMEM_SPEC] * 8,
        out_specs=[VMEM_SPEC] * 3,
        out_shape=[
            jax.ShapeDtypeStruct((rows // 2, width), F32),
            jax.ShapeDtypeStruct((16, 512), F32),
            jax.ShapeDtypeStruct((rows // 2 + 32, width), BF16),
        ],
        scratch_shapes=[pltpu.VMEM((rows, width), F32)],
        compiler_params=PARAMS,
        name="add_halve",
    )(me, *parts_a, *parts_b)


def place_kernel(me, *refs):
    out = refs[-1]
    for k, part in enumerate(refs[:-1]):

        @pl.when(pl.program_id(0) == k)
        def _():
            out[...] = part[...].reshape(out.shape)


def place(parts, index, me, shape, block, name):
    return pl.pallas_call(
        place_kernel,
        grid_spec=pltpu.PrefetchScalarGridSpec(
            num_scalar_prefetch=1,
            grid=(len(parts),),
            in_specs=[whole(p.shape) for p in parts],
            out_specs=pl.BlockSpec(block, lambda i, me: index(i, me[0])),
        ),
        out_shape=jax.ShapeDtypeStruct(shape, parts[0].dtype),
        compiler_params=PARAMS,
        cost_estimate=cost(2),
        name=name,
    )(me, *parts)


def shift(value, axis, by):
    n = SIZES[axis]
    return lax.ppermute(value, axis, [(i, (i - by) % n) for i in range(n)])


def swap(value, axis):
    return shift(value, axis, 1)


def ring(value, axis):
    return [value, shift(value, axis, 1), shift(value, axis, 2), shift(value, axis, -1)]


def sends(blocks, axis, in_turn=False):
    ahead, behind = shift(blocks[1], axis, -1), shift(blocks[3], axis, 1)
    opposite = after(blocks[2], ahead, behind) if in_turn else blocks[2]
    return [blocks[0], ahead, shift(opposite, axis, 2), behind]


def tensor_xor(value, by):
    return lax.ppermute(value, TENSOR, [(i, i ^ by) for i in range(4)])


def sum_ring(value, axis):
    own, ahead, across, behind = ring(value, axis)
    return (own + across) + (ahead + behind)


def sum_pair(value, axis):
    return value + swap(value, axis)


def after(value, *others):
    return lax.optimization_barrier((value,) + others)[0]


def index_of(axis):
    return lax.axis_index(axis).reshape(1).astype(jnp.int32)


def pair_kernel(me, main, other_main, side, other_side, out):
    cut, middle = 1536, side.shape[1]
    for k, (left, right) in enumerate(((main, side), (other_main, other_side))):

        @pl.when(pl.program_id(0) == k)
        def _():
            out[:, :cut] = left[:, :cut]
            out[:, cut : cut + middle] = right[...]
            out[:, cut + middle :] = left[:, cut:]


def pair_rows(main, side):
    rows = main.shape[0]
    width = main.shape[1] + side.shape[1]
    parts = [main, swap(main, "zl"), side, swap(side, "zl")]
    return pl.pallas_call(
        pair_kernel,
        grid_spec=pltpu.PrefetchScalarGridSpec(
            num_scalar_prefetch=1,
            grid=(2,),
            in_specs=[whole(p.shape) for p in parts],
            out_specs=pl.BlockSpec((rows, width), lambda i, me: ((me[0] + i) % 2, 0)),
        ),
        out_shape=jax.ShapeDtypeStruct((2 * rows, width), BF16),
        compiler_params=PARAMS,
        name="pair_rows",
    )(index_of("zl"), *parts)


def token_place(own, near, far, both, me):
    rows, width = own.shape
    return place([own, near, far, both], lambda i, me: (me ^ i, 0), me, (4 * rows, width), (rows, width), "place_tokens")


def per_device(
    hidden_in,
    norm_gain,
    proj_zx,
    proj_shared,
    proj_step,
    conv_inner,
    conv_shared,
    step_bias,
    decay_log,
    skip_gain,
    gated_gain,
    proj_out,
    out_grad,
    segments,
):
    model_width = hidden_in.shape[1]
    width = proj_zx.shape[2]
    heads = step_bias.shape[0]
    me = {axis: index_of(axis) for axis in DP + TENSOR}
    spot = 2 * me["zh"] + me["c"]

    shared_parts = [proj_shared] + [tensor_xor(proj_shared, by) for by in (1, 2, 3)]
    shared_rows = jnp.zeros((48, 256), BF16)
    for by, part in enumerate(shared_parts):
        shared_rows = lax.dynamic_update_slice(shared_rows, part, (((spot[0] ^ by) * 12), jnp.int32(0)))
    side_rows = jnp.concatenate([shared_rows, jnp.pad(proj_step, ((0, 0), (0, 128 - heads)))], 1)
    main_rows = jnp.concatenate([proj_zx[:, 0, :], proj_zx[:, 1, :], proj_out.T], 1)
    weights = lax.all_gather(pair_rows(main_rows, side_rows), ("y", "x"), axis=0, tiled=True)

    residual_in = hidden_in.astype(F32)
    scale_in = lax.rsqrt(jnp.mean(residual_in * residual_in, axis=-1, keepdims=True) + EPS)
    normed_low = (residual_in * scale_in * norm_gain).astype(BF16)
    normed_far = swap(normed_low, "zh")
    normed_near = swap(normed_low, "c")

    normed_both = swap(normed_far, "c")
    tokens = token_place(normed_low, normed_near, normed_far, normed_both, spot)
    grad_far = swap(after(out_grad, normed_far), "zh")
    grad_near = swap(after(out_grad, normed_far), "c")
    grad_both = swap(grad_far, "c")

    pad = (0, 128 - heads)
    head_rows = jnp.stack([jnp.pad(step_bias, pad), jnp.pad(jnp.exp(decay_log), pad)], 0)
    head_rows = jnp.pad(head_rows, ((0, 6), (0, 0)))
    taps = jnp.pad(jnp.concatenate([conv_inner, conv_shared], 1), ((0, 3), (0, 0)))
    chan = jnp.broadcast_to(jnp.repeat(skip_gain, width // heads), (8, width))
    gain = jnp.broadcast_to(gated_gain, (8, width))
    norm_rows = jnp.broadcast_to(norm_gain, (8, model_width))
    marks, segrow = scan_marks(segments)
    spread = spread_table(width)
    sum_table = head_sum_table(width)
    late, head_rows, taps, chan, gain, norm_rows, marks, segrow, spread, sum_table = lax.optimization_barrier(
        (spot, head_rows, taps, chan, gain, norm_rows, marks, segrow, spread, sum_table)
    )
    grad_rows = token_place(out_grad, grad_near, grad_far, grad_both, late)
    tokens, grad_rows = lax.optimization_barrier((tokens, grad_rows))
    pre, scanned, states, gate_pre, grad_mixed, sums = scan_forward(
        tokens, grad_rows, weights, taps, head_rows, chan, gain, spread, marks, segrow
    )

    sums = sum_pair(sum_pair(sums, "c"), "zh")
    grad_scanned, gate_grad_low, gain_sums, second_total, *out_blocks = mix_second(
        sums, gate_pre, grad_mixed, scanned, weights, gain, tokens, grad_rows, 4 * width, spot
    )
    out_far = (out_blocks[1].astype(F32) + swap(out_blocks[0], "c").astype(F32)).astype(BF16)
    out_near = swap(out_blocks[2], "c")
    second_sum = lax.psum_scatter(second_total, ("y", "x"), scatter_dimension=0, tiled=True)
    out_far_got = swap(out_far, "zh")

    grad_scanned = after(grad_scanned, out_far, second_total)
    sent = scan_backward(
        pre,
        taps,
        head_rows,
        chan,
        sum_table,
        spread,
        marks,
        segrow,
        grad_scanned,
        states,
        tokens,
        gate_grad_low,
        weights,
        norm_rows,
        gain_sums,
        jnp.concatenate([spot, me["y"], me["x"]]),
    )
    row_blocks = [after(block, out_far_got, out_near) for block in sent[:4]]
    far_got = swap(row_blocks[0], "c")
    row_far = (row_blocks[1].astype(F32) + far_got.astype(F32)).astype(BF16)
    row_far_got = swap(row_far, "zh")
    parts_b = sends([after(block, row_far) for block in sent[8:]], "x")
    parts_a = sends([after(block, row_far) for block in sent[4:8]], "y", in_turn=True)
    half_a, half_b = add_split(parts_a, parts_b, jnp.concatenate([me["x"], me["y"]]))
    near_got = swap(after(row_blocks[2], *half_a), "c")

    hidden_out = (
        residual_in + (out_blocks[3].astype(F32) + out_near.astype(F32) + out_far_got.astype(F32))
    ).astype(BF16)
    grad_normed = row_blocks[3].astype(F32) + near_got.astype(F32) + row_far_got.astype(F32)
    weighted = jnp.sum(grad_normed * norm_gain * residual_in, axis=-1, keepdims=True)
    grad_hidden = (
        out_grad.astype(F32)
        + scale_in * norm_gain * grad_normed
        - residual_in * scale_in**3 * weighted / model_width
    ).astype(BF16)
    parts_a = [after(part, row_far_got, second_sum) for part in sends(half_a, "x")]
    parts_b = [after(part, row_far_got, second_sum) for part in sends(half_b, "y", in_turn=True)]
    first_keep, small, first_give = add_halve(parts_a, parts_b, me["zl"])
    first_got = swap(first_give, "zl")
    first_mine = first_keep + first_got[:48].astype(F32)
    small = small + read_small(first_got[48:, :512])
    second_pairs = second_sum.reshape(2, 48, 2 * width)
    second_keep = lax.dynamic_index_in_dim(second_pairs, me["zl"][0], 0, keepdims=False)
    second_mine = second_keep.astype(F32) + swap(
        lax.dynamic_index_in_dim(second_pairs, 1 - me["zl"][0], 0, keepdims=False), "zl"
    ).astype(F32)
    grad_proj_out = second_mine[:, width:].T
    grad_proj_zx = jnp.stack([second_mine[:, :width], first_mine[:, :width]], 1)
    grad_proj_step = first_mine[:, width + 256 : width + 256 + heads]

    def quarter(by):
        part = lax.dynamic_slice(first_mine, ((spot[0] ^ by) * 12, jnp.int32(width)), (12, 256))
        return jnp.concatenate([small, jnp.pad(part, ((0, 0), (0, 256)))], 0)

    summed = (quarter(0) + tensor_xor(quarter(1), 1)) + (tensor_xor(quarter(2), 2) + tensor_xor(quarter(3), 3))
    rest = width - 512
    return (
        hidden_out,
        grad_hidden,
        jnp.concatenate([summed[6], summed[14], summed[7]]),
        grad_proj_zx,
        summed[16:, :256],
        grad_proj_step,
        jnp.concatenate([small[:5], small[8:13, :rest]], 1),
        summed[8:13, rest:],
        small[15, :heads],
        small[15, 128 : 128 + heads],
        small[15, 256 : 256 + heads],
        jnp.concatenate([small[5], small[13, :rest]]),
        grad_proj_out,
    )


def solution(mesh):
    fine = Mesh(mesh.devices.reshape(4, 4, 2, 2, 2), DP + TENSOR)
    both = DP + TENSOR
    return jax.shard_map(
        per_device,
        mesh=fine,
        in_specs=(
            P(both, None),
            P(),
            P(DP, None, TENSOR),
            P(both, None),
            P(DP, TENSOR),
            P(None, TENSOR),
            P(),
            P(TENSOR),
            P(TENSOR),
            P(TENSOR),
            P(TENSOR),
            P(TENSOR, DP),
            P(both, None),
            P(DP),
        ),
        out_specs=(
            P(both, None),
            P(both, None),
            P(),
            P(DP, None, TENSOR),
            P(both, None),
            P(DP, TENSOR),
            P(None, TENSOR),
            P(),
            P(TENSOR),
            P(TENSOR),
            P(TENSOR),
            P(TENSOR),
            P(TENSOR, DP),
        ),
        check_vma=False,
    )
```

```python
import jax
import jax.numpy as jnp
from jax import lax
from jax.experimental import pallas as pl
from jax.experimental.pallas import tpu as pltpu
from jax.sharding import Mesh
from jax.sharding import PartitionSpec as P

EPS = 1e-05
DP = ("y", "x", "zl")
TENSOR = ("zh", "c")
SIZES = {"y": 4, "x": 4, "zl": 2, "zh": 2, "c": 2}

F32 = jnp.float32
BF16 = jnp.bfloat16
HIGH = lax.Precision.HIGHEST
FORWARD_BLOCK = 128
BACKWARD_BLOCK = 256
VMEM = 56 * 1024 * 1024
PARAMS = pltpu.CompilerParams(vmem_limit_bytes=VMEM)
NT = (((1,), (1,)), ((), ()))
TN = (((0,), (0,)), ((), ()))
VMEM_SPEC = pl.BlockSpec(memory_space=pltpu.VMEM)


def cost(us):
    return pl.CostEstimate(flops=int(us * 1e6), transcendentals=0, bytes_accessed=int(us * 3e3))


def whole(shape):
    return pl.BlockSpec(shape, lambda *i: (0,) * len(shape))


def column_block(rows, width, index):
    return pl.BlockSpec((rows, width), lambda *i: (0, index))


def first_specs(rows):
    return [column_block(rows, 384, index) for index in (2, 3, 4)]


def out_specs_of(rows):
    return [column_block(rows, 384, index) for index in (5, 6)]


def dot(a, b):
    return jnp.dot(a, b, preferred_element_type=F32)


def dot_nt(a, b):
    return lax.dot_general(a, b, NT, preferred_element_type=F32)


def sigmoid(a):
    return 0.5 * jnp.tanh(0.5 * a) + 0.5


def softplus(a):
    return jnp.maximum(a, 0.0) + jnp.log1p(jnp.exp(-jnp.abs(a)))


def conv_strip(ext, taps, aux, j):
    n = ext.shape[0] - 8
    lanes = slice(j * 128, (j + 1) * 128)
    total = taps[4:5, lanes] + taps[3:4, lanes] * ext[8 : 8 + n, lanes]
    for back in (1, 2, 3):
        total += taps[3 - back : 4 - back, lanes] * (
            aux[:, back - 1 : back] * ext[8 - back : 8 - back + n, lanes]
        )
    return total


def two_parts(value):
    high = value.astype(BF16)
    return jnp.concatenate([high, (value - high.astype(F32)).astype(BF16)], 1)


def spread_heads(cols, table):
    return dot(two_parts(cols), table)


def scan_forward_kernel(tok, rows, gate_w, out_a, out_b, weights_a, weights_b, weights_c, taps, heads, chan, gain, spread, aux, segrow, pre_out, scan_low, state_out, gate_low, mixed_low, sums_out, ext, act, carry, fed, scan_out, gate_out, mixed_out):
    n = tok.shape[0]
    pairs = carry.shape[1] // 128

    @pl.when(pl.program_id(0) == 0)
    def _():
        carry[...] = jnp.zeros_like(carry)
        ext[0:8, :] = jnp.zeros((8, ext.shape[1]), F32)

    pre = jnp.concatenate([dot(tok[...], w[...]) for w in (weights_a, weights_b, weights_c)], 1)
    pre_out[...] = pre
    wide = ext.shape[1]
    ext[8:, :] = pre[:, :wide]
    marks = aux[...]
    for j in range(wide // 128):
        total = conv_strip(ext, taps, marks, j)
        act[:, j * 128 : (j + 1) * 128] = total * sigmoid(total)
    ext[0:8, :] = ext[n : n + 8, :]

    step = softplus(pre[:, wide:] + heads[0:1, :])
    log_step = -step * heads[1:2, :]
    row = lax.broadcasted_iota(jnp.int32, (n, n), 0)
    col = lax.broadcasted_iota(jnp.int32, (n, n), 1)
    lower = (row >= col).astype(F32)
    cum = jnp.dot(lower, log_step, precision=HIGH, preferred_element_type=F32)
    cum_t = cum.T
    write = act[:, pairs * 128 : (pairs + 1) * 128]
    read = act[:, (pairs + 1) * 128 : (pairs + 2) * 128].astype(BF16)
    write_t = write.T.astype(BF16)
    allowed = (row >= col) & (marks[:, 8:9] == segrow[0:1, :])
    inner = jnp.where(allowed, dot(read, write_t), 0.0)
    last = cum[n - 1 : n, :]
    enters = jnp.exp(cum) * marks[:, 3:4]
    to_end = jnp.exp(last - cum) * marks[:, 4:5]
    keep = jnp.exp(last) * marks[n - 1 : n, 3:4]
    wide_cols = spread_heads(jnp.concatenate([step, enters, to_end, jnp.broadcast_to(keep, (8, 128))], 0), spread[...])
    held = carry[...]
    held_low = held.astype(BF16)
    state_out[0] = held_low
    from_state = dot(read, held_low)
    low_half = lax.broadcasted_iota(jnp.int32, (1, 128), 1) < 64
    for j in range(pairs):
        lanes = slice(j * 128, (j + 1) * 128)
        x = act[:, lanes]
        xdt = x * wide_cols[:n, lanes]
        parts = []
        for h in (2 * j, 2 * j + 1):
            decay = jnp.exp(jnp.minimum(cum[:, h : h + 1] - cum_t[h : h + 1, :], 0.0))
            parts.append((decay * inner).astype(BF16))
        xdt_low = xdt.astype(BF16)
        zero = jnp.zeros_like(xdt_low)
        pair = jnp.concatenate([jnp.where(low_half, xdt_low, zero), jnp.where(low_half, zero, xdt_low)], 0)
        y = dot(jnp.concatenate(parts, 1), pair)
        if j % 2 == 0:
            block = slice(128 * j, 128 * j + 256)
            gate_out[:, block] = dot(tok[...], gate_w[:, block])
        else:
            spot = 256 * (j // 2)
            out_w = (out_a[:, 0:256], jnp.concatenate([out_a[:, 256:], out_b[:, :128]], 1), out_b[:, 128:])[j // 2]
            mixed_out[:, spot : spot + 256] = dot(rows[...], out_w)
        y += wide_cols[n : 2 * n, lanes] * from_state[:, lanes] + chan[0:1, lanes] * x
        scan_out[:, lanes] = y
        fed[:, lanes] = (xdt * wide_cols[2 * n : 3 * n, lanes]).astype(BF16)
        carry[:, lanes] = held[:, lanes] * wide_cols[3 * n : 3 * n + 1, lanes]
    carry[...] += dot(write_t, fed[...])

    gate_pre = gate_out[...]
    grad_mixed = mixed_out[...]
    scanned = scan_out[...]
    gate_low[...] = gate_pre.astype(BF16)
    mixed_low[...] = grad_mixed.astype(BF16)
    scan_low[...] = scanned.astype(BF16)
    gated = scanned * (gate_pre * sigmoid(gate_pre))
    square = jnp.sum(gated * gated, axis=1, keepdims=True)
    inner = jnp.sum(grad_mixed * gain[0:1, :] * gated, axis=1, keepdims=True)
    lane = lax.broadcasted_iota(jnp.int32, (1, 128), 1)
    cols = jnp.where(lane == 0, square, jnp.where(lane == 1, inner, 0.0))
    sums_out[...] = cols.T[0:8, :]


def small_rows(value):
    high = value.astype(BF16)
    return jnp.concatenate([high, (value - high.astype(F32)).astype(BF16)], 0)


def read_small(rows):
    return rows[:16, :].astype(F32) + rows[16:, :].astype(F32)


def scan_backward_kernel(me, pre, pre_before, taps, heads, chan, sums, spread, aux, segrow, grad, state, tok, grad_gate, weights, norm_gain, gain_sums, *rest):
    row_outs, outs_a, outs_b = rest[:4], rest[4:8], rest[8:12]
    ext, gext, act, slope, carry, fed, back, rows, low_out, taps_out, heads_out, gains, all_tok, all_low, split, packed = rest[12:]
    n = pre.shape[0]
    pairs = carry.shape[1] // 128
    wide = ext.shape[1]
    gate_width = grad_gate.shape[1]

    @pl.when(pl.program_id(0) == 0)
    def _():
        carry[...] = jnp.zeros_like(carry)
        gext[n:, :] = jnp.zeros((8, wide), F32)
        taps_out[...] = jnp.zeros_like(taps_out)
        heads_out[...] = jnp.zeros_like(heads_out)
        rows[...] = jnp.zeros_like(rows)
        gains[...] = jnp.zeros_like(gains)

    marks = aux[...]
    ext[0:8, :] = pre_before[:, :wide]
    ext[8:, :] = pre[:, :wide]
    for j in range(wide // 128):
        lanes = slice(j * 128, (j + 1) * 128)
        total = conv_strip(ext, taps, marks, j)
        sig = sigmoid(total)
        value = total * sig
        act[:, lanes] = value
        slope[:, lanes] = sig + value * (1.0 - sig)

    step_arg = pre[:, wide:] + heads[0:1, :]
    step = softplus(step_arg)
    rate = heads[1:2, :]
    row = lax.broadcasted_iota(jnp.int32, (n, n), 0)
    col = lax.broadcasted_iota(jnp.int32, (n, n), 1)
    lower = (row >= col).astype(F32)
    cum = jnp.dot(lower, -step * rate, precision=HIGH, preferred_element_type=F32)
    cum_t = cum.T
    write = act[:, pairs * 128 : (pairs + 1) * 128]
    read = act[:, (pairs + 1) * 128 : (pairs + 2) * 128]
    read_t = read.T.astype(BF16)
    write_low = write.astype(BF16)
    read_low = read.astype(BF16)
    allowed = (row <= col) & (marks[:, 8:9] == segrow[0:1, :])
    inner_t = jnp.where(allowed, dot(write_low, read_t), 0.0)
    last = cum[n - 1 : n, :]
    enters = jnp.exp(cum) * marks[:, 9:10]
    to_end = jnp.exp(last - cum) * marks[:, 10:11]
    keep = jnp.exp(last) * marks[n - 1 : n, 9:10]
    wide_cols = spread_heads(jnp.concatenate([step, enters, to_end, jnp.broadcast_to(keep, (8, 128))], 0), spread[...])
    held = state[0]
    later = carry[...]
    later_low = later.astype(BF16)
    from_state = dot(read_low, held)
    from_later = dot(write_low, later_low)
    low_half = lax.broadcasted_iota(jnp.int32, (1, 128), 1) < 64
    head_lane = lax.broadcasted_iota(jnp.int32, (1, 128), 1)
    grad_inner = jnp.zeros((n, n), F32)
    col_sums = jnp.zeros((n, 128), F32)
    to_end_part = jnp.zeros((n, 128), F32)
    enter_part = jnp.zeros((n, 128), F32)
    step_part = jnp.zeros((n, 128), F32)
    skip_part = jnp.zeros((n, 128), F32)
    keep_part = jnp.zeros((8, 128), F32)

    def head_sums(value, j):
        return dot(two_parts(value), sums[j])

    for j in range(pairs):
        lanes = slice(j * 128, (j + 1) * 128)
        x = act[:, lanes]
        dy = grad[:, lanes].astype(F32)
        step_wide = wide_cols[:n, lanes]
        xdt = x * step_wide
        xdt_low = xdt.astype(BF16)
        dy_low = dy.astype(BF16)
        zero = jnp.zeros_like(xdt_low)
        products = dot_nt(
            jnp.concatenate([jnp.where(low_half, xdt_low, zero), jnp.where(low_half, zero, xdt_low)], 0),
            dy_low,
        )
        parts = []
        for k, h in enumerate((2 * j, 2 * j + 1)):
            product = products[k * n : (k + 1) * n, :]
            decay = jnp.exp(jnp.minimum(cum_t[h : h + 1, :] - cum[:, h : h + 1], 0.0))
            scaled = decay * product
            grad_inner += scaled
            weighted = scaled * inner_t
            rows[h : h + 1, :] = jnp.sum(weighted, axis=0, keepdims=True)
            col_sums += jnp.where(head_lane == h, jnp.sum(weighted, axis=1, keepdims=True), 0.0)
            parts.append((decay * inner_t).astype(BF16))
        grad_pair = jnp.concatenate([jnp.where(low_half, dy_low, zero), jnp.where(low_half, zero, dy_low)], 0)
        grad_xdt = dot(jnp.concatenate(parts, 1), grad_pair)
        end_wide = wide_cols[2 * n : 3 * n, lanes]
        enter_wide = wide_cols[n : 2 * n, lanes]
        later_part = end_wide * from_later[:, lanes]
        grad_xdt += later_part
        to_end_part += head_sums(later_part * xdt, j)
        fed[:, lanes] = (xdt * end_wide).astype(BF16)
        grad_enter = dy * enter_wide
        back[:, lanes] = grad_enter.astype(BF16)
        enter_part += head_sums(grad_enter * from_state[:, lanes], j)
        step_part += head_sums(grad_xdt * x, j)
        skip_part += head_sums(dy * x, j)
        kept = jnp.sum(held[:, lanes].astype(F32) * later[:, lanes], axis=0, keepdims=True)
        keep_part += head_sums(jnp.broadcast_to(kept, (8, 128)), j)
        act[:, lanes] = grad_xdt * step_wide + chan[0:1, lanes] * dy
        carry[:, lanes] = later[:, lanes] * wide_cols[3 * n : 3 * n + 1, lanes]

    grad_cum = rows[...].T - col_sums + enter_part - to_end_part
    grad_last = jnp.sum(to_end_part, axis=0, keepdims=True) + keep * keep_part[0:1, :]
    upper = (row <= col).astype(F32)
    grad_log = jnp.dot(upper, grad_cum, precision=HIGH, preferred_element_type=F32) + grad_last
    grad_step = (step_part - rate * grad_log) * sigmoid(step_arg)
    heads_out[0:1, :] += jnp.sum(grad_step, axis=0, keepdims=True)
    heads_out[1:2, :] += -rate * jnp.sum(step * grad_log, axis=0, keepdims=True)
    heads_out[2:3, :] += jnp.sum(skip_part, axis=0, keepdims=True)
    low_out[:, gate_width + wide :] = grad_step.astype(BF16)

    grad_inner = jnp.where(allowed, grad_inner, 0.0)
    act[:, pairs * 128 : (pairs + 1) * 128] = dot(grad_inner.astype(BF16), read_low) + dot_nt(fed[...], later_low)
    act[:, (pairs + 1) * 128 : (pairs + 2) * 128] = dot(grad_inner.T.astype(BF16), write_low) + dot_nt(back[...], held)
    carry[...] += dot(read_t, back[...])

    for j in range(wide // 128):
        lanes = slice(j * 128, (j + 1) * 128)
        grad_pre = act[:, lanes] * slope[:, lanes]
        gext[0:n, lanes] = grad_pre
        total = taps[3:4, lanes] * grad_pre
        taps_out[3:4, lanes] += jnp.sum(grad_pre * ext[8 : 8 + n, lanes], axis=0, keepdims=True)
        taps_out[4:5, lanes] += jnp.sum(grad_pre, axis=0, keepdims=True)
        for by in (1, 2, 3):
            total += taps[3 - by : 4 - by, lanes] * (marks[:, 4 + by : 5 + by] * gext[by : by + n, lanes])
            taps_out[3 - by : 4 - by, lanes] += jnp.sum(
                grad_pre * (marks[:, by - 1 : by] * ext[8 - by : 8 - by + n, lanes]), axis=0, keepdims=True
            )
        low_out[:, gate_width + j * 128 : gate_width + (j + 1) * 128] = total.astype(BF16)
    gext[n:, :] = gext[0:8, :]

    step_id = pl.program_id(0)
    low_out[:, : grad_gate.shape[1]] = grad_gate[...]
    token_grad = dot_nt(low_out[...], weights[...])
    gains[0:1, :] += jnp.sum(token_grad * tok[...].astype(F32), axis=0, keepdims=True)
    place = pl.ds(pl.multiple_of((3 - step_id) * n, n), n)
    all_tok[place, :] = tok[...]
    all_low[place, :] = low_out[:, grad_gate.shape[1] :]
    token_low = token_grad.astype(BF16)
    for k in range(4):

        @pl.when((me[0] ^ (3 - k)) == 3 - step_id)
        def _():
            row_outs[k][...] = token_low

    @pl.when(step_id == 3)
    def _():
        cut = outs_a[0].shape[2]
        deep = outs_a[0].shape[1]
        for k in range(4):
            first = pl.multiple_of(((me[1] + k) % 4) * (4 * deep), 128)
            grad_rows = lax.dot_general(
                all_tok[:, pl.ds(first, 4 * deep)], all_low[...], TN, preferred_element_type=F32
            ).astype(BF16)
            outs_a[k][...] = grad_rows[:, :cut].reshape(outs_a[k].shape)
            split[...] = grad_rows[:, cut:]
            y = (me[1] + k) % 4
            for d in range(4):
                start = pl.multiple_of(((me[2] + d) % 4) * deep, 16)
                outs_b[d][pl.ds(pl.multiple_of(y * deep, 16), deep), :] = split[pl.ds(start, deep), :]
        width = gain_sums.shape[1]
        by_gain = gains[0:1, :] / norm_gain[0:1, :]
        packed[0:5, :] = taps_out[0:5, :]
        packed[5:6, :width] = gain_sums[0:1, :]
        packed[5:6, width:] = jnp.zeros((1, 1024 - width), F32)
        packed[6:7, :] = by_gain[:, :1024]
        packed[7:8, :512] = by_gain[:, 1024:]
        for r in range(3):
            packed[7:8, 512 + 128 * r : 640 + 128 * r] = heads_out[r : r + 1, :]
        packed[7:8, 896:] = jnp.zeros((1, 128), F32)
        sums_low = small_rows(jnp.concatenate([packed[:, :512], packed[:, 512:]], 0))
        for k in range(4):
            outs_b[k][4 * deep :, :512] = sums_low


def scan_marks(segments):
    length = segments.shape[0]

    def same(by):
        if by > 0:
            other = jnp.concatenate([jnp.full((by,), -1, jnp.int32), segments[:-by]], 0)
        else:
            other = jnp.concatenate([segments[-by:], jnp.full((-by,), -1, jnp.int32)], 0)
        return other == segments

    def ends(size):
        blocks = segments.reshape(-1, size)
        before = jnp.concatenate([jnp.full((1,), -1, jnp.int32), blocks[:-1, -1]], 0)
        return [(blocks == before[:, None]).reshape(-1), (blocks == blocks[:, -1:]).reshape(-1)]

    cols = [same(1), same(2), same(3), *ends(FORWARD_BLOCK)]
    cols += [same(-1), same(-2), same(-3), segments, *ends(BACKWARD_BLOCK)]
    marks = jnp.stack([c.astype(F32) for c in cols], 1)
    return jnp.pad(marks, ((0, 0), (0, 128 - len(cols)))), jnp.broadcast_to(segments.astype(F32), (8, length))


def scan_forward(tokens, grad_rows, weights, taps, heads, chan, gain, spread, marks, segrow):
    length, model = tokens.shape
    cols = 1152
    inner = cols - 384
    wide = cols - 128
    n = FORWARD_BLOCK
    blocks = length // n


    return pl.pallas_call(
        scan_forward_kernel,
        grid=(blocks,),
        in_specs=[
            pl.BlockSpec((n, model), lambda i: (i, 0)),
            pl.BlockSpec((n, model), lambda i: (i, 0)),
            column_block(model, inner, 0),
            *out_specs_of(model),
            *first_specs(model),
            whole((8, wide)),
            whole((8, 128)),
            whole((8, inner)),
            whole((8, inner)),
            whole((256, inner)),
            pl.BlockSpec((n, 128), lambda i: (i, 0)),
            pl.BlockSpec((8, n), lambda i: (0, i)),
        ],
        out_specs=[
            pl.BlockSpec((n, cols), lambda i: (i, 0)),
            pl.BlockSpec((n, inner), lambda i: (i, 0)),
            pl.BlockSpec((1, 128, inner), lambda i: (i, 0, 0)),
            pl.BlockSpec((n, inner), lambda i: (i, 0)),
            pl.BlockSpec((n, inner), lambda i: (i, 0)),
            pl.BlockSpec((8, n), lambda i: (0, i)),
        ],
        out_shape=[
            jax.ShapeDtypeStruct((length, cols), F32),
            jax.ShapeDtypeStruct((length, inner), BF16),
            jax.ShapeDtypeStruct((blocks, 128, inner), BF16),
            jax.ShapeDtypeStruct((length, inner), BF16),
            jax.ShapeDtypeStruct((length, inner), BF16),
            jax.ShapeDtypeStruct((8, length), F32),
        ],
        scratch_shapes=[
            pltpu.VMEM((n + 8, wide), F32),
            pltpu.VMEM((n, wide), F32),
            pltpu.VMEM((128, inner), F32),
            pltpu.VMEM((n, inner), BF16),
            pltpu.VMEM((n, inner), F32),
            pltpu.VMEM((n, inner), F32),
            pltpu.VMEM((n, inner), F32),
        ],
        compiler_params=PARAMS,
        cost_estimate=cost(20),
        name="scan_forward",
    )(tokens, grad_rows, weights, weights, weights, weights, weights, weights, taps, heads, chan, gain, spread, marks, segrow)


def scan_backward(pre, taps, heads, chan, sums, spread, marks, segrow, grad, states, tokens, grad_gate, weights, norm_gain, gain_sums, me):
    length, cols = pre.shape
    model = tokens.shape[1]
    inner = cols - 384
    wide = cols - 128
    n = BACKWARD_BLOCK
    blocks = length // n
    cut = 640
    shape_a, shape_b = (4, model // 16, cut), (model // 4 + 32, cols - cut)

    def rev(i):
        return blocks - 1 - i

    def rows(width):
        return pl.BlockSpec((n, width), lambda i, me: (rev(i), 0))

    return pl.pallas_call(
        scan_backward_kernel,
        grid_spec=pltpu.PrefetchScalarGridSpec(
            num_scalar_prefetch=1,
            grid=(blocks,),
            in_specs=[
                rows(cols),
                pl.BlockSpec((8, cols), lambda i, me: (jnp.maximum(rev(i) * (n // 8) - 1, 0), 0)),
                whole((8, wide)),
                whole((8, 128)),
                whole((8, inner)),
                whole((inner // 128, 256, 128)),
                whole((256, inner)),
                rows(128),
                pl.BlockSpec((8, n), lambda i, me: (0, rev(i))),
                rows(inner),
                pl.BlockSpec((1, 128, inner), lambda i, me: (rev(i) * (n // FORWARD_BLOCK), 0, 0)),
                rows(model),
                rows(inner),
                column_block(model, inner + cols, 0),
                whole(norm_gain.shape),
                whole(gain_sums.shape),
            ],
            out_specs=[whole((n, model))] * 4 + [whole(shape_a)] * 4 + [whole(shape_b)] * 4,
            scratch_shapes=[
                pltpu.VMEM((n + 8, wide), F32),
                pltpu.VMEM((n + 8, wide), F32),
                pltpu.VMEM((n, wide), F32),
                pltpu.VMEM((n, wide), F32),
                pltpu.VMEM((128, inner), F32),
                pltpu.VMEM((n, inner), BF16),
                pltpu.VMEM((n, inner), BF16),
                pltpu.VMEM((128, n), F32),
                pltpu.VMEM((n, inner + cols), BF16),
                pltpu.VMEM((8, wide), F32),
                pltpu.VMEM((8, 128), F32),
                pltpu.VMEM((8, model), F32),
                pltpu.VMEM((length, model), BF16),
                pltpu.VMEM((length, cols), BF16),
                pltpu.VMEM((model // 4, cols - cut), BF16),
                pltpu.VMEM((8, 1024), F32),
            ],
        ),
        out_shape=[jax.ShapeDtypeStruct((n, model), BF16)] * 4
        + [jax.ShapeDtypeStruct(shape_a, BF16)] * 4
        + [jax.ShapeDtypeStruct(shape_b, BF16)] * 4,
        compiler_params=PARAMS,
        cost_estimate=cost(30),
        name="scan_backward",
    )(me, pre, pre, taps, heads, chan, sums, spread, marks, segrow, grad, states, tokens, grad_gate, weights, norm_gain, gain_sums)


def spread_table(inner):
    head = jnp.arange(inner) // 64
    return (jnp.arange(256)[:, None] % 128 == head[None, :]).astype(BF16)


def head_sum_table(inner):
    pairs = inner // 128
    lane = jnp.arange(256) % 128
    head = 2 * jnp.arange(pairs)[:, None] + (lane >= 64)[None, :]
    return (head[:, :, None] == jnp.arange(128)[None, None, :]).astype(BF16)


def store_block(value, outs):
    for k, out in enumerate(outs):

        @pl.when(pl.program_id(0) == k)
        def _():
            out[...] = value


def mix_second_kernel(channels, me, sums, gate, grad_mixed_in, scanned_in, out_a, out_b, gain, tok, rows, grad_scan, grad_gate, gain_out, grads_out, *rest):
    outs, all_gate, all_mixed = rest[:4], rest[4], rest[5]
    step = pl.program_id(0)
    n, width = gate.shape

    @pl.when(step == 0)
    def _():
        gain_out[...] = jnp.zeros_like(gain_out)

    @pl.when(step < 4)
    def _():
        cols = jnp.concatenate([sums[...], jnp.zeros((120, n), F32)], 0).T
        scale = lax.rsqrt(cols[:, 0:1] / channels + EPS)
        pull = scale * scale * scale * (cols[:, 1:2] / channels)
        gate_pre = gate[...].astype(F32)
        grad_mixed = grad_mixed_in[...].astype(F32)
        scanned = scanned_in[...].astype(F32)
        sig = sigmoid(gate_pre)
        silu = gate_pre * sig
        gated = scanned * silu
        scaled = gated * scale
        mixed = (scaled * gain[0:1, :]).astype(BF16)
        place = pl.ds(pl.multiple_of((me[0] ^ (3 - step)) * n, n), n)
        all_mixed[place, :] = mixed
        gain_out[0:1, :] += jnp.sum(grad_mixed * scaled, axis=0, keepdims=True)
        grad_gated = scale * gain[0:1, :] * grad_mixed - gated * pull
        grad_scan[...] = (grad_gated * silu).astype(BF16)
        grad_gate_low = (grad_gated * scanned * (sig + silu * (1.0 - sig))).astype(BF16)
        grad_gate[...] = grad_gate_low
        all_gate[place, :] = grad_gate_low
        projected = dot_nt(mixed[:, :384], out_a[...]) + dot_nt(mixed[:, 384:], out_b[...])
        store_block(projected.astype(BF16), outs)

    @pl.when(step >= 4)
    def _():
        gate_part = lax.dot_general(tok[...], all_gate[...], TN, preferred_element_type=F32)
        out_part = lax.dot_general(rows[...], all_mixed[...], TN, preferred_element_type=F32)
        grads_out[:, :width] = gate_part.astype(BF16)
        grads_out[:, width:] = out_part.astype(BF16)


def mix_second(sums, gate, grad_mixed, scanned, second, gain, tokens, grad_rows, channels, spot):
    length, width = gate.shape
    model = second.shape[0]
    n = 256
    m = model // 4

    def token_block(i, me):
        return me[0] ^ (3 - jnp.minimum(i, 3))

    def rows(cols):
        return pl.BlockSpec((n, cols), lambda i, me: (token_block(i, me), 0))

    def cols():
        return pl.BlockSpec((length, m), lambda i, me: (0, jnp.maximum(i - 4, 0)))

    return pl.pallas_call(
        lambda *refs: mix_second_kernel(channels, *refs),
        grid_spec=pltpu.PrefetchScalarGridSpec(
            num_scalar_prefetch=1,
            grid=(8,),
            in_specs=[
                pl.BlockSpec((8, n), lambda i, me: (0, token_block(i, me))),
                rows(width),
                rows(width),
                rows(width),
                *out_specs_of(model),
                whole((8, width)),
                cols(),
                cols(),
            ],
            out_specs=[
                rows(width),
                rows(width),
                whole((8, width)),
                pl.BlockSpec((m, 2 * width), lambda i, me: (jnp.maximum(i - 4, 0), 0)),
            ]
            + [whole((n, model))] * 4,
            scratch_shapes=[pltpu.VMEM((length, width), BF16), pltpu.VMEM((length, width), BF16)],
        ),
        out_shape=[
            jax.ShapeDtypeStruct((length, width), BF16),
            jax.ShapeDtypeStruct((length, width), BF16),
            jax.ShapeDtypeStruct((8, width), F32),
            jax.ShapeDtypeStruct((model, 2 * width), BF16),
        ]
        + [jax.ShapeDtypeStruct((n, model), BF16)] * 4,
        compiler_params=PARAMS,
        cost_estimate=cost(11),
        name="mix_second",
    )(spot, sums, gate, grad_mixed, scanned, second, second, gain, tokens, grad_rows)


def four_sum(own, ahead, across, behind):
    return (own.astype(F32) + across.astype(F32)) + (ahead.astype(F32) + behind.astype(F32))


def add_split_kernel(me, *refs):
    parts_a, parts_b, outs_a, outs_b = refs[:4], refs[4:8], refs[8:12], refs[12:]
    deep = outs_a[0].shape[0]
    sums = small_rows(four_sum(*[read_small(part[4 * deep :, :512]) for part in parts_b]))
    for d in range(4):
        e = (me[0] + d) % 4
        outs_a[d][...] = four_sum(*[part[e] for part in parts_a]).astype(BF16)
        place = pl.ds(pl.multiple_of(((me[1] + d) % 4) * deep, 16), deep)
        outs_b[d][:deep, :] = four_sum(*[part[place, :] for part in parts_b]).astype(BF16)
        outs_b[d][deep:, :512] = sums


def add_split(parts_a, parts_b, me):
    deep, width_a = parts_a[0].shape[1:]
    width_b = parts_b[0].shape[1]
    outs = pl.pallas_call(
        add_split_kernel,
        in_specs=[pl.BlockSpec(memory_space=pltpu.SMEM)] + [VMEM_SPEC] * 8,
        out_specs=[VMEM_SPEC] * 8,
        out_shape=[jax.ShapeDtypeStruct((deep, width_a), BF16)] * 4 + [jax.ShapeDtypeStruct((deep + 32, width_b), BF16)] * 4,
        compiler_params=PARAMS,
        name="add_split",
    )(me, *parts_a, *parts_b)
    return outs[:4], outs[4:]


def add_halve_kernel(me, *refs):
    ins, (keep, sums, give, total) = refs[:8], refs[8:]
    rows, cut = ins[0].shape
    total[:, :cut] = four_sum(*[part[...] for part in ins[:4]])
    total[:, cut:] = four_sum(*[part[:rows, :] for part in ins[4:]])
    n = keep.shape[0]
    keep[...] = total[pl.ds(pl.multiple_of(me[0] * n, 16), n), :]
    give[:n, :] = total[pl.ds(pl.multiple_of((1 - me[0]) * n, 16), n), :].astype(BF16)
    low = small_rows(four_sum(*[read_small(part[rows:, :512]) for part in ins[4:]]))
    give[n:, :512] = low
    give[n:, 512:] = jnp.zeros((32, give.shape[1] - 512), BF16)
    sums[...] = read_small(low)


def add_halve(parts_a, parts_b, me):
    rows = parts_a[0].shape[0]
    width = parts_a[0].shape[1] + parts_b[0].shape[1]
    return pl.pallas_call(
        add_halve_kernel,
        in_specs=[pl.BlockSpec(memory_space=pltpu.SMEM)] + [VMEM_SPEC] * 8,
        out_specs=[VMEM_SPEC] * 3,
        out_shape=[
            jax.ShapeDtypeStruct((rows // 2, width), F32),
            jax.ShapeDtypeStruct((16, 512), F32),
            jax.ShapeDtypeStruct((rows // 2 + 32, width), BF16),
        ],
        scratch_shapes=[pltpu.VMEM((rows, width), F32)],
        compiler_params=PARAMS,
        name="add_halve",
    )(me, *parts_a, *parts_b)


def place_kernel(me, *refs):
    out = refs[-1]
    for k, part in enumerate(refs[:-1]):

        @pl.when(pl.program_id(0) == k)
        def _():
            out[...] = part[...].reshape(out.shape)


def place(parts, index, me, shape, block, name):
    return pl.pallas_call(
        place_kernel,
        grid_spec=pltpu.PrefetchScalarGridSpec(
            num_scalar_prefetch=1,
            grid=(len(parts),),
            in_specs=[whole(p.shape) for p in parts],
            out_specs=pl.BlockSpec(block, lambda i, me: index(i, me[0])),
        ),
        out_shape=jax.ShapeDtypeStruct(shape, parts[0].dtype),
        compiler_params=PARAMS,
        cost_estimate=cost(2),
        name=name,
    )(me, *parts)


def shift(value, axis, by):
    n = SIZES[axis]
    return lax.ppermute(value, axis, [(i, (i - by) % n) for i in range(n)])


def swap(value, axis):
    return shift(value, axis, 1)


def ring(value, axis):
    return [value, shift(value, axis, 1), shift(value, axis, 2), shift(value, axis, -1)]


def sends(blocks, axis, in_turn=False):
    ahead, behind = shift(blocks[1], axis, -1), shift(blocks[3], axis, 1)
    opposite = after(blocks[2], ahead, behind) if in_turn else blocks[2]
    return [blocks[0], ahead, shift(opposite, axis, 2), behind]


def tensor_xor(value, by):
    return lax.ppermute(value, TENSOR, [(i, i ^ by) for i in range(4)])


def sum_ring(value, axis):
    own, ahead, across, behind = ring(value, axis)
    return (own + across) + (ahead + behind)


def sum_pair(value, axis):
    return value + swap(value, axis)


def after(value, *others):
    return lax.optimization_barrier((value,) + others)[0]


def index_of(axis):
    return lax.axis_index(axis).reshape(1).astype(jnp.int32)


def pair_kernel(me, main, other_main, side, other_side, out):
    cut, middle = 1536, side.shape[1]
    for k, (left, right) in enumerate(((main, side), (other_main, other_side))):

        @pl.when(pl.program_id(0) == k)
        def _():
            out[:, :cut] = left[:, :cut]
            out[:, cut : cut + middle] = right[...]
            out[:, cut + middle :] = left[:, cut:]


def pair_rows(main, side):
    rows = main.shape[0]
    width = main.shape[1] + side.shape[1]
    parts = [main, swap(main, "zl"), side, swap(side, "zl")]
    return pl.pallas_call(
        pair_kernel,
        grid_spec=pltpu.PrefetchScalarGridSpec(
            num_scalar_prefetch=1,
            grid=(2,),
            in_specs=[whole(p.shape) for p in parts],
            out_specs=pl.BlockSpec((rows, width), lambda i, me: ((me[0] + i) % 2, 0)),
        ),
        out_shape=jax.ShapeDtypeStruct((2 * rows, width), BF16),
        compiler_params=PARAMS,
        name="pair_rows",
    )(index_of("zl"), *parts)


def token_place(own, near, far, both, me):
    rows, width = own.shape
    return place([own, near, far, both], lambda i, me: (me ^ i, 0), me, (4 * rows, width), (rows, width), "place_tokens")


def per_device(
    hidden_in,
    norm_gain,
    proj_zx,
    proj_shared,
    proj_step,
    conv_inner,
    conv_shared,
    step_bias,
    decay_log,
    skip_gain,
    gated_gain,
    proj_out,
    out_grad,
    segments,
):
    model_width = hidden_in.shape[1]
    width = proj_zx.shape[2]
    heads = step_bias.shape[0]
    me = {axis: index_of(axis) for axis in DP + TENSOR}
    spot = 2 * me["zh"] + me["c"]

    shared_parts = [proj_shared] + [tensor_xor(proj_shared, by) for by in (1, 2, 3)]
    shared_rows = jnp.zeros((48, 256), BF16)
    for by, part in enumerate(shared_parts):
        shared_rows = lax.dynamic_update_slice(shared_rows, part, (((spot[0] ^ by) * 12), jnp.int32(0)))
    side_rows = jnp.concatenate([shared_rows, jnp.pad(proj_step, ((0, 0), (0, 128 - heads)))], 1)
    main_rows = jnp.concatenate([proj_zx[:, 0, :], proj_zx[:, 1, :], proj_out.T], 1)
    weights = lax.all_gather(pair_rows(main_rows, side_rows), ("y", "x"), axis=0, tiled=True)

    residual_in = hidden_in.astype(F32)
    scale_in = lax.rsqrt(jnp.mean(residual_in * residual_in, axis=-1, keepdims=True) + EPS)
    normed_low = (residual_in * scale_in * norm_gain).astype(BF16)
    normed_far = swap(normed_low, "zh")
    normed_near = swap(normed_low, "c")

    normed_both = swap(normed_far, "c")
    tokens = token_place(normed_low, normed_near, normed_far, normed_both, spot)
    grad_far = swap(after(out_grad, normed_far), "zh")
    grad_near = swap(after(out_grad, normed_far), "c")
    grad_both = swap(grad_far, "c")

    pad = (0, 128 - heads)
    head_rows = jnp.stack([jnp.pad(step_bias, pad), jnp.pad(jnp.exp(decay_log), pad)], 0)
    head_rows = jnp.pad(head_rows, ((0, 6), (0, 0)))
    taps = jnp.pad(jnp.concatenate([conv_inner, conv_shared], 1), ((0, 3), (0, 0)))
    chan = jnp.broadcast_to(jnp.repeat(skip_gain, width // heads), (8, width))
    gain = jnp.broadcast_to(gated_gain, (8, width))
    norm_rows = jnp.broadcast_to(norm_gain, (8, model_width))
    marks, segrow = scan_marks(segments)
    spread = spread_table(width)
    sum_table = head_sum_table(width)
    late, head_rows, taps, chan, gain, norm_rows, marks, segrow, spread, sum_table = lax.optimization_barrier(
        (spot, head_rows, taps, chan, gain, norm_rows, marks, segrow, spread, sum_table)
    )
    grad_rows = token_place(out_grad, grad_near, grad_far, grad_both, late)
    tokens, grad_rows = lax.optimization_barrier((tokens, grad_rows))
    pre, scanned, states, gate_pre, grad_mixed, sums = scan_forward(
        tokens, grad_rows, weights, taps, head_rows, chan, gain, spread, marks, segrow
    )

    sums = sum_pair(sum_pair(sums, "c"), "zh")
    grad_scanned, gate_grad_low, gain_sums, second_total, *out_blocks = mix_second(
        sums, gate_pre, grad_mixed, scanned, weights, gain, tokens, grad_rows, 4 * width, spot
    )
    out_far = (out_blocks[1].astype(F32) + swap(out_blocks[0], "c").astype(F32)).astype(BF16)
    out_near = swap(out_blocks[2], "c")
    second_sum = lax.psum_scatter(second_total, ("y", "x"), scatter_dimension=0, tiled=True)
    out_far_got = swap(out_far, "zh")

    grad_scanned = after(grad_scanned, out_far, second_total)
    sent = scan_backward(
        pre,
        taps,
        head_rows,
        chan,
        sum_table,
        spread,
        marks,
        segrow,
        grad_scanned,
        states,
        tokens,
        gate_grad_low,
        weights,
        norm_rows,
        gain_sums,
        jnp.concatenate([spot, me["y"], me["x"]]),
    )
    row_blocks = [after(block, out_far_got, out_near) for block in sent[:4]]
    far_got = swap(row_blocks[0], "c")
    row_far = (row_blocks[1].astype(F32) + far_got.astype(F32)).astype(BF16)
    row_far_got = swap(row_far, "zh")
    parts_b = sends([after(block, row_far) for block in sent[8:]], "x", in_turn=True)
    parts_a = sends([after(block, row_far) for block in sent[4:8]], "y")
    half_a, half_b = add_split(parts_a, parts_b, jnp.concatenate([me["x"], me["y"]]))
    near_got = swap(after(row_blocks[2], *half_a), "c")

    hidden_out = (
        residual_in + (out_blocks[3].astype(F32) + out_near.astype(F32) + out_far_got.astype(F32))
    ).astype(BF16)
    grad_normed = row_blocks[3].astype(F32) + near_got.astype(F32) + row_far_got.astype(F32)
    weighted = jnp.sum(grad_normed * norm_gain * residual_in, axis=-1, keepdims=True)
    grad_hidden = (
        out_grad.astype(F32)
        + scale_in * norm_gain * grad_normed
        - residual_in * scale_in**3 * weighted / model_width
    ).astype(BF16)
    parts_a = [after(part, row_far_got, second_sum) for part in sends(half_a, "x")]
    parts_b = [after(part, row_far_got, second_sum) for part in sends(half_b, "y", in_turn=True)]
    first_keep, small, first_give = add_halve(parts_a, parts_b, me["zl"])
    first_got = swap(first_give, "zl")
    first_mine = first_keep + first_got[:48].astype(F32)
    small = small + read_small(first_got[48:, :512])
    second_pairs = second_sum.reshape(2, 48, 2 * width)
    second_keep = lax.dynamic_index_in_dim(second_pairs, me["zl"][0], 0, keepdims=False)
    second_mine = second_keep.astype(F32) + swap(
        lax.dynamic_index_in_dim(second_pairs, 1 - me["zl"][0], 0, keepdims=False), "zl"
    ).astype(F32)
    grad_proj_out = second_mine[:, width:].T
    grad_proj_zx = jnp.stack([second_mine[:, :width], first_mine[:, :width]], 1)
    grad_proj_step = first_mine[:, width + 256 : width + 256 + heads]

    def quarter(by):
        part = lax.dynamic_slice(first_mine, ((spot[0] ^ by) * 12, jnp.int32(width)), (12, 256))
        return jnp.concatenate([small, jnp.pad(part, ((0, 0), (0, 256)))], 0)

    summed = (quarter(0) + tensor_xor(quarter(1), 1)) + (tensor_xor(quarter(2), 2) + tensor_xor(quarter(3), 3))
    rest = width - 512
    return (
        hidden_out,
        grad_hidden,
        jnp.concatenate([summed[6], summed[14], summed[7]]),
        grad_proj_zx,
        summed[16:, :256],
        grad_proj_step,
        jnp.concatenate([small[:5], small[8:13, :rest]], 1),
        summed[8:13, rest:],
        small[15, :heads],
        small[15, 128 : 128 + heads],
        small[15, 256 : 256 + heads],
        jnp.concatenate([small[5], small[13, :rest]]),
        grad_proj_out,
    )


def solution(mesh):
    fine = Mesh(mesh.devices.reshape(4, 4, 2, 2, 2), DP + TENSOR)
    both = DP + TENSOR
    return jax.shard_map(
        per_device,
        mesh=fine,
        in_specs=(
            P(both, None),
            P(),
            P(DP, None, TENSOR),
            P(both, None),
            P(DP, TENSOR),
            P(None, TENSOR),
            P(),
            P(TENSOR),
            P(TENSOR),
            P(TENSOR),
            P(TENSOR),
            P(TENSOR, DP),
            P(both, None),
            P(DP),
        ),
        out_specs=(
            P(both, None),
            P(both, None),
            P(),
            P(DP, None, TENSOR),
            P(both, None),
            P(DP, TENSOR),
            P(None, TENSOR),
            P(),
            P(TENSOR),
            P(TENSOR),
            P(TENSOR),
            P(TENSOR),
            P(TENSOR, DP),
        ),
        check_vma=False,
    )
```
